32 devices in a mesh: ctx: 4 (over y, x), fsdp: 8 (over z, core).
Axes of the slice: x: 2, y: 2, z: 4, core: 2. Of those that a mesh axis runs over, the one named last changes fastest.
Arguments:
- tokens: bfloat16 [16384, 2048], P(('ctx', 'fsdp')), may hold values from -6 to 6
- cotangent: float32 [16384, 2048], P(('ctx', 'fsdp')), may hold values from -6 to 6
- lengths: int32 [8, 2], P('fsdp'), may hold values from 8 to 8, as said below
- span_place: int32 [8, 16], P('fsdp'), may hold values from 0 to 15, as said below
- ln1_gain: float32 [2048], P('fsdp'), may hold values from 0.1 to 1.9
- ln1_shift: float32 [2048], P('fsdp'), may hold values from -2.5 to 2.5
- qkv_weight: float32 [2048, 6144], P('fsdp'), may hold values from -0.125 to 0.125
- q_bias: float32 [2048], P('fsdp'), may hold values from -2.5 to 2.5
- v_bias: float32 [2048], P('fsdp'), may hold values from -2.5 to 2.5
- out_weight: float32 [2048, 2048], P('fsdp'), may hold values from -0.5 to 0.5
- out_bias: float32 [2048], P('fsdp'), may hold values from -2.5 to 2.5
- ln2_gain: float32 [2048], P('fsdp'), may hold values from 0.1 to 1.9
- ln2_shift: float32 [2048], P('fsdp'), may hold values from -2.5 to 2.5
- up_weight: float32 [2048, 8192], P('fsdp'), may hold values from -0.125 to 0.125
- up_bias: float32 [8192], P('fsdp'), may hold values from -3 to 3
- down_weight: float32 [8192, 2048], P('fsdp'), may hold values from -0.0625 to 0.0625
- down_bias: float32 [2048], P('fsdp'), may hold values from -2.5 to 2.5
Outputs:
- mixed: float32 [16384, 2048], P(('ctx', 'fsdp'))
- input_grad: float32 [16384, 2048], P(('ctx', 'fsdp'))
- ln1_gain_grad: float32 [2048], P('fsdp')
- ln1_shift_grad: float32 [2048], P('fsdp')
- qkv_weight_grad: float32 [2048, 6144], P('fsdp')
- q_bias_grad: float32 [2048], P('fsdp')
- v_bias_grad: float32 [2048], P('fsdp')
- out_weight_grad: float32 [2048, 2048], P('fsdp')
- out_bias_grad: float32 [2048], P('fsdp')
- ln2_gain_grad: float32 [2048], P('fsdp')
- ln2_shift_grad: float32 [2048], P('fsdp')
- up_weight_grad: float32 [2048, 8192], P('fsdp')
- up_bias_grad: float32 [8192], P('fsdp')
- down_weight_grad: float32 [8192, 2048], P('fsdp')
- down_bias_grad: float32 [2048], P('fsdp')
The draws below stay inside these ranges and needn't reach their ends.
Inputs may be any that keep to these rules, and one draw needn't show every extreme that they name: Each row holds two lengths in blocks, each 8 or more, that sum to 16; the first is at least as long as the second; in some row the first is exactly 8. `span_place`: each row is a permutation of the 16 blocks of a group.
All inputs are finite; a program needn't handle non-finite values.
Results may differ from the reference program's by a relative error of at most 0.02.
Values may be sent and summed in bfloat16 or wider, within the bound.
A program may use at most 512 MiB of HBM per device.

```python
import math
from functools import partial
import jax
import jax.numpy as jnp
from jax import lax

D = 2048
FF = 8192
HEADS = 16
HEAD_DIM = 128
SPAN = 128
MIN_SEQ = 8
CH_DEV = 4
TOK_DEV = 512
GCH = 16
TOKENS = 16384
N_CTX = 4
N_FSDP = 8


def draw_lengths(key, part):
    key = jax.random.fold_in(key, 11)
    first_key, second_key = jax.random.split(key)
    low_end = GCH // 2
    high_end = GCH - MIN_SEQ
    first = jax.random.randint(first_key, (N_FSDP,), low_end, high_end + 1).astype(jnp.int32)
    chosen = jax.random.randint(second_key, (), 0, N_FSDP).astype(jnp.int32)
    first = jnp.where(jnp.arange(N_FSDP, dtype=jnp.int32) == chosen, high_end, first).astype(jnp.int32)
    return jnp.stack([first, GCH - first], axis=1).astype(jnp.int32)


def draw_span_place(key, part):
    key = jax.random.fold_in(key, 23)
    width = N_CTX
    order = jnp.arange(GCH, dtype=jnp.int32)
    rounds = order // (2 * width)
    offset = order % (2 * width)
    device = jnp.where(offset < width, offset, 2 * width - 1 - offset)
    slot = 2 * rounds + (offset >= width).astype(jnp.int32)

    def one_group(sub):
        relabel = jax.random.permutation(sub, width).astype(jnp.int32)
        target = relabel[device] * CH_DEV + slot
        return jnp.zeros((GCH,), jnp.int32).at[target].set(order)
    return jax.vmap(one_group)(jax.random.split(key, N_FSDP))


def level_of(key, shape, cuts, least, high):
    level, own = 1.0, jax.random.fold_in(key, 6)
    for axis_at, shards_of in cuts:
        heights = jnp.exp(jax.random.uniform(jax.random.fold_in(own, axis_at), (shards_of,), jnp.float32, least / len(cuts), high / len(cuts)))
        level = level * jnp.repeat(heights, shape[axis_at] // shards_of).reshape([-1 if axis == axis_at else 1 for axis in range(len(shape))])
    return level


def bell_draw(key, dims, deviation, reach, pieces=(), kind=jnp.bfloat16):
    factor_of = level_of(key, dims, pieces, -0.22, 0.18) if pieces else 1.0
    array = jax.random.normal(key, dims, jnp.float32) * deviation * factor_of
    return jnp.minimum(jnp.maximum(array, -reach), reach).astype(kind)


def setup_inputs(seed: int = 0) -> dict:
    arg_keys = jax.random.split(jax.random.key(seed), 18)
    tokens = bell_draw(arg_keys[0], (TOKENS, D), 1.0, 6.0, ((0, 32),))
    cotangent = bell_draw(arg_keys[1], (TOKENS, D), 1.0, 6.0, ((0, 32),), jnp.float32)
    lengths = draw_lengths(jax.random.fold_in(arg_keys[17], 71), 0)
    span_place = draw_span_place(jax.random.fold_in(arg_keys[17], 71), 0)
    ln1_gain = jnp.clip(1.0 + 0.18 * jax.random.normal(arg_keys[4], (D,), jnp.float32), 0.1, 1.9)
    ln1_shift = bell_draw(arg_keys[5], (D,), 0.3, 2.5, ((0, 8),), jnp.float32)
    qkv_weight = bell_draw(arg_keys[6], (D, 3 * D), D ** -0.5, 0.125, ((0, 8),), jnp.float32)
    q_bias = bell_draw(arg_keys[7], (D,), 0.3, 2.5, ((0, 8),), jnp.float32)
    v_bias = bell_draw(arg_keys[8], (D,), 0.3, 2.5, ((0, 8),), jnp.float32)
    out_weight = bell_draw(arg_keys[9], (D, D), (D // 16) ** -0.5, 0.5, ((0, 8),), jnp.float32)
    out_bias = bell_draw(arg_keys[10], (D,), 0.3, 2.5, ((0, 8),), jnp.float32)
    ln2_gain = jnp.clip(1.0 + 0.18 * jax.random.normal(arg_keys[11], (D,), jnp.float32), 0.1, 1.9)
    ln2_shift = bell_draw(arg_keys[12], (D,), 0.3, 2.5, ((0, 8),), jnp.float32)
    up_weight = bell_draw(arg_keys[13], (D, FF), D ** -0.5, 0.125, ((0, 8),), jnp.float32)
    up_bias = bell_draw(arg_keys[14], (FF,), 0.5, 3.0, ((0, 8),), jnp.float32)
    down_weight = bell_draw(arg_keys[15], (FF, D), FF ** -0.5, 0.0625, ((0, 8),), jnp.float32)
    down_bias = bell_draw(arg_keys[16], (D,), 0.3, 2.5, ((0, 8),), jnp.float32)
    return {"tokens": tokens, "cotangent": cotangent, "lengths": lengths, "span_place": span_place, "ln1_gain": ln1_gain, "ln1_shift": ln1_shift, "qkv_weight": qkv_weight, "q_bias": q_bias, "v_bias": v_bias, "out_weight": out_weight, "out_bias": out_bias, "ln2_gain": ln2_gain, "ln2_shift": ln2_shift, "up_weight": up_weight, "up_bias": up_bias, "down_weight": down_weight, "down_bias": down_bias}


@jax.custom_vjp
def low(v):
    return lax.optimization_barrier(v.astype(jnp.bfloat16)).astype(jnp.float32)

@jax.custom_vjp
def low_back(v):
    return v

def low_keep(v):
    return (low(v), None)

def low_pass(kept, grad):
    return (grad,)

def back_keep(v):
    return (v, None)

def back_low(kept, grad):
    return (low(grad),)
low.defvjp(low_keep, low_pass)
low_back.defvjp(back_keep, back_low)
norm_eps = 1e-05
gelu_coef = 0.7978845608028654

def matmul(left, right):
    return jnp.dot(left, right, precision=lax.Precision.HIGHEST, preferred_element_type=jnp.float32)

def layer_norm(values, gain, shift):
    center = values - lax.optimization_barrier(jnp.mean(values, axis=-1, keepdims=True))
    spread = lax.optimization_barrier(jnp.mean(center * center, axis=-1, keepdims=True))
    return center * lax.rsqrt(spread + norm_eps) * gain + shift

def gelu_tanh(values):
    return 0.5 * values * (1.0 + jnp.tanh(gelu_coef * (values + 0.044715 * values * values * values)))

def head_slopes():
    return 2.0 ** (-8.0 * (jnp.arange(HEADS, dtype=jnp.float32) + 1.0) / HEADS)

def token_places(place_row, len_row):
    index = jnp.arange(place_row.shape[0] * SPAN, dtype=jnp.int32)
    packed = place_row[index // SPAN] * SPAN + index % SPAN
    starts = (jnp.cumsum(len_row) - len_row) * SPAN
    member = lax.optimization_barrier(jnp.sum((packed[:, None] >= starts[None, :]).astype(jnp.int32), axis=1))
    return (packed.astype(jnp.int32), member.astype(jnp.int32))

def one_head(items, packed, member):
    queries, keys, values, slope = items
    scale = 1.0 / math.sqrt(HEAD_DIM)
    gap = (packed[:, None] - packed[None, :]).astype(jnp.float32)
    scores = low_back(matmul(queries, keys.T) * scale - slope * gap)
    allowed = (member[:, None] == member[None, :]) & (packed[None, :] <= packed[:, None])
    scores = jnp.where(allowed, scores, -1e+30)
    row_top = lax.optimization_barrier(jnp.max(scores, axis=1, keepdims=True))
    weights = jnp.exp(scores - row_top)
    probs = weights / lax.optimization_barrier(jnp.sum(weights, axis=1, keepdims=True))
    return matmul(low(probs), values)

def attend(queries, keys, values, places, members):
    group_rows = TOK_DEV * N_CTX

    def by_heads(block):
        return block.reshape(group_rows, HEADS, HEAD_DIM).transpose(1, 0, 2)

    def group_part(items):
        group_q, group_k, group_v, packed, member = items
        head_fn = jax.checkpoint(partial(one_head, packed=packed, member=member))
        result = lax.map(head_fn, (by_heads(group_q), by_heads(group_k), by_heads(group_v), head_slopes()))
        return result.transpose(1, 0, 2).reshape(group_rows, D)
    stacked = (queries.reshape(N_FSDP, group_rows, D), keys.reshape(N_FSDP, group_rows, D), values.reshape(N_FSDP, group_rows, D), places, members)
    return lax.map(group_part, stacked).reshape(TOKENS, D)

def layer(start, ln1_gain, ln1_shift, qkv_weight, q_bias, v_bias, out_weight, out_bias, ln2_gain, ln2_shift, up_weight, up_bias, down_weight, down_bias, places, members):
    hidden_one = low(layer_norm(start, low(ln1_gain), low(ln1_shift)))
    blank = jnp.zeros_like(q_bias)
    joint_bias = jnp.concatenate([low(q_bias), blank, low(v_bias)])
    joined = low_back(low(matmul(hidden_one, low(qkv_weight)) + joint_bias))
    queries = joined[:, :D]
    keys = joined[:, D:2 * D]
    values = joined[:, 2 * D:]
    attended = low_back(low(attend(queries, keys, values, places, members)))
    branch_one = low_back(matmul(attended, low(out_weight)) + low(out_bias))
    middle = start + branch_one
    hidden_two = low(layer_norm(middle, low(ln2_gain), low(ln2_shift)))
    upward = low_back(matmul(hidden_two, low(up_weight)) + low(up_bias))
    activated = low_back(low(gelu_tanh(upward)))
    branch_two = low_back(matmul(activated, low(down_weight)) + low(down_bias))
    return middle + branch_two

def to_groups(values):
    width = values.shape[-1]
    return values.reshape(N_CTX, N_FSDP, TOK_DEV, width).transpose(1, 0, 2, 3).reshape(TOKENS, width)

def from_groups(values):
    width = values.shape[-1]
    return values.reshape(N_FSDP, N_CTX, TOK_DEV, width).transpose(1, 0, 2, 3).reshape(TOKENS, width)

def reference(tokens, cotangent, lengths, span_place, ln1_gain, ln1_shift, qkv_weight, q_bias, v_bias, out_weight, out_bias, ln2_gain, ln2_shift, up_weight, up_bias, down_weight, down_bias):
    places, members = jax.vmap(token_places)(span_place, lengths)
    start = to_groups(tokens.astype(jnp.float32))
    seed_grad = to_groups(cotangent)
    forward = partial(layer, places=places, members=members)
    mixed, pull = jax.vjp(forward, start, ln1_gain, ln1_shift, qkv_weight, q_bias, v_bias, out_weight, out_bias, ln2_gain, ln2_shift, up_weight, up_bias, down_weight, down_bias)
    grads = pull(seed_grad)
    return (from_groups(mixed), from_groups(grads[0]), grads[1], grads[2], grads[3], grads[4], grads[5], grads[6], grads[7], grads[8], grads[9], grads[10], grads[11], grads[12], grads[13])
```

```python
import functools
import math

import jax
import jax.numpy as jnp
from jax import lax
from jax.experimental import pallas as pl
from jax.experimental.pallas import tpu as pltpu
from jax.sharding import PartitionSpec as P

HEADS = 16
SPAN = 128
SEQ_BLOCKS = 8

norm_eps = 1e-05
gelu_coef = 0.7978845608028654
LOG2E = 1.4426950408889634

half = jnp.bfloat16
single = jnp.float32


def dot_nn(a, b):
    return lax.dot_general(a, b, (((1,), (0,)), ((), ())), preferred_element_type=single)


def dot_nt(a, b):
    return lax.dot_general(a, b, (((1,), (1,)), ((), ())), preferred_element_type=single)


def dot_tn(a, b):
    return lax.dot_general(a, b, (((0,), (0,)), ((), ())), preferred_element_type=single)


def norm_parts(values):
    center = values - jnp.mean(values, axis=-1, keepdims=True)
    spread = jnp.mean(center * center, axis=-1, keepdims=True)
    inv = lax.rsqrt(spread + norm_eps)
    return center * inv, inv


def norm_back(normed, inv, gain, grad):
    dn = grad * gain
    return inv * (
        dn
        - jnp.mean(dn, axis=-1, keepdims=True)
        - normed * jnp.mean(dn * normed, axis=-1, keepdims=True)
    )


def gelu_both(v):
    t = jnp.tanh(gelu_coef * (v + 0.044715 * v * v * v))
    value = 0.5 * v * (1.0 + t)
    slope = 0.5 * (1.0 + t) + 0.5 * v * (1.0 - t * t) * gelu_coef * (1.0 + 3 * 0.044715 * v * v)
    return value, slope


def swap(x, mask):
    n = lax.axis_size("ctx")
    return lax.ppermute(x, "ctx", [(i, i ^ mask) for i in range(n)])


def gather_ctx(x):
    n = x.shape[0] // 2
    count = lax.axis_size("ctx")
    if count != 4:
        c = lax.axis_index("ctx")
        whole = lax.all_gather(x, "ctx", axis=0)
        parts = [lax.dynamic_index_in_dim(whole, c ^ j, 0, keepdims=False) for j in range(count)]
        return [(p[:n], p[n:]) for p in parts]
    lo, hi = x[:n], x[n:]
    x_lo = swap(lo, 1)
    y_hi = swap(hi, 2)
    x_hi = swap(hi, 1)
    y_lo = swap(lo, 2)
    d_lo = swap(x_lo, 2)
    d_hi = swap(y_hi, 1)
    return [(lo, hi), (x_lo, x_hi), (y_lo, y_hi), (d_lo, d_hi)]


def scatter_ctx(pieces):
    if len(pieces) != 4:
        c = lax.axis_index("ctx")
        ordered = xor_order([p.astype(half) for p in pieces], c)
        whole = jnp.concatenate(ordered, axis=0)
        return lax.psum_scatter(whole, "ctx", scatter_dimension=0, tiled=True).astype(single)
    p0, p1, p2, p3 = pieces
    n = p0.shape[0] // 2
    from_x = swap(p3[:n], 1)
    from_y = swap(p3[n:], 2)
    p2_lo = (p2[:n].astype(single) + from_x.astype(single)).astype(half)
    p1_hi = (p1[n:].astype(single) + from_y.astype(single)).astype(half)
    x_lo = swap(p1[:n], 1)
    y_hi = swap(p2[n:], 2)
    x_hi = swap(p1_hi, 1)
    y_lo = swap(p2_lo, 2)
    lo = p0[:n].astype(single) + x_lo.astype(single) + y_lo.astype(single)
    hi = p0[n:].astype(single) + x_hi.astype(single) + y_hi.astype(single)
    return jnp.concatenate([lo, hi], axis=0)


def xor_order(items, c):
    bit = 1
    while bit < len(items):
        on = (c & bit) == bit
        items = [jnp.where(on, items[i ^ bit], items[i]) for i in range(len(items))]
        bit *= 2
    return items


TILE = 256


def attn_scores(q_refs, k_refs, i, scale, slope):
    q = jnp.concatenate([q_refs[2 * i][...], q_refs[2 * i + 1][...]], axis=0)
    k = jnp.concatenate([r[...] for r in k_refs[: 2 * i + 2]], axis=0)
    n = TILE * (i + 1)
    col = lax.broadcasted_iota(jnp.int32, (1, n), 1) - (n - 1)
    s = dot_nt(q, k) * (scale * LOG2E) + (slope * LOG2E) * col.astype(single)
    row_at = lax.broadcasted_iota(jnp.int32, (TILE, TILE), 0)
    col_at = lax.broadcasted_iota(jnp.int32, (TILE, TILE), 1)
    last = jnp.where(col_at <= row_at, s[:, n - TILE :], -1e30)
    s = last if i == 0 else jnp.concatenate([s[:, : n - TILE], last], axis=1)
    e = jnp.exp2(s - jnp.max(s, axis=1, keepdims=True))
    return q, k, e, 1.0 / jnp.sum(e, axis=1, keepdims=True)


def attn_fwd_kernel(scale, inv_ref, slope_ref, *refs):
    q_refs, k_refs, v_refs = refs[:8], refs[8:16], refs[16:24]
    o_ref = refs[24]
    slope = slope_ref[pl.program_id(1)]
    for i in range(4):
        q, k, e, r = attn_scores(q_refs, k_refs, i, scale, slope)
        v = jnp.concatenate([x[...] for x in v_refs[: 2 * i + 2]], axis=0)
        o = dot_nn((e * r).astype(half), v)
        o_ref[TILE * i : TILE * (i + 1), :] = o.astype(half)


def attn_bwd_kernel(scale, inv_ref, slope_ref, *refs):
    q_refs, k_refs, v_refs, g_refs = refs[:8], refs[8:16], refs[16:24], refs[24:32]
    dq_ref, dk_ref, dv_ref, dk_acc, dv_acc = refs[32:]
    slope = slope_ref[pl.program_id(1)]
    for i in (3, 2, 1, 0):
        q, k, e, r = attn_scores(q_refs, k_refs, i, scale, slope)
        n = TILE * (i + 1)
        v = jnp.concatenate([x[...] for x in v_refs[: 2 * i + 2]], axis=0)
        g = jnp.concatenate([g_refs[2 * i][...], g_refs[2 * i + 1][...]], axis=0)
        p = e * r
        dp = dot_nt(g, v)
        delta = jnp.sum(p * dp, axis=1, keepdims=True)
        ds = (p * (dp - delta)).astype(half)
        pb = p.astype(half)
        dq_ref[TILE * i : TILE * (i + 1), :] = (dot_nn(ds, k) * scale).astype(half)
        dk = dot_tn(ds, q)
        dv = dot_tn(pb, g)
        if i == 3:
            dk_acc[...] = dk
            dv_acc[...] = dv
        else:
            dk_acc[:n, :] += dk
            dv_acc[:n, :] += dv
    dk_ref[...] = (dk_acc[...] * scale).astype(half)
    dv_ref[...] = dv_acc[...].astype(half)


def block_specs(offset):
    def one(j):
        return pl.BlockSpec(
            (SPAN, 128), lambda s, h, inv, slope: (inv[s * SEQ_BLOCKS + j], offset + h)
        )

    return [one(j) for j in range(SEQ_BLOCKS)]


def attn_forward(joined, inv, slopes, heads, scale):
    rows = joined.shape[0]
    specs = block_specs(0) + block_specs(heads) + block_specs(2 * heads)
    out = pl.BlockSpec((rows // 2, 128), lambda s, h, inv, slope: (s, h))
    return pl.pallas_call(
        functools.partial(attn_fwd_kernel, scale),
        grid_spec=pltpu.PrefetchScalarGridSpec(
            num_scalar_prefetch=2, grid=(2, heads), in_specs=specs, out_specs=out
        ),
        out_shape=jax.ShapeDtypeStruct((rows, heads * 128), half),
        compiler_params=pltpu.CompilerParams(vmem_limit_bytes=48 * 1024 * 1024),
        cost_estimate=pl.CostEstimate(
            flops=20 * 10**9, bytes_accessed=rows * heads * 128 * 8, transcendentals=0
        ),
        name="attn_forward",
    )(inv, slopes, *([joined] * 24))


def attn_backward(joined, grad, inv, slopes, heads, scale):
    rows = joined.shape[0]
    specs = block_specs(0) + block_specs(heads) + block_specs(2 * heads) + block_specs(0)
    out = pl.BlockSpec((rows // 2, 128), lambda s, h, inv, slope: (s, h))
    shape = jax.ShapeDtypeStruct((rows, heads * 128), half)
    return pl.pallas_call(
        functools.partial(attn_bwd_kernel, scale),
        grid_spec=pltpu.PrefetchScalarGridSpec(
            num_scalar_prefetch=2,
            grid=(2, heads),
            in_specs=specs,
            out_specs=[out] * 3,
            scratch_shapes=[pltpu.VMEM((rows // 2, 128), single)] * 2,
        ),
        out_shape=[shape] * 3,
        compiler_params=pltpu.CompilerParams(vmem_limit_bytes=48 * 1024 * 1024),
        cost_estimate=pl.CostEstimate(
            flops=40 * 10**9, bytes_accessed=rows * heads * 128 * 14, transcendentals=0
        ),
        name="attn_backward",
    )(inv, slopes, *([joined] * 24), *([grad] * 8))


def per_device(
    tokens,
    cotangent,
    lengths,
    span_place,
    ln1_gain,
    ln1_shift,
    qkv_weight,
    q_bias,
    v_bias,
    out_weight,
    out_bias,
    ln2_gain,
    ln2_shift,
    up_weight,
    up_bias,
    down_weight,
    down_bias,
):
    rows, width = tokens.shape
    CTX = lax.axis_size("ctx")
    c = lax.axis_index("ctx")
    f = lax.axis_index("fsdp")
    nf = lax.axis_size("fsdp")
    wide = up_weight.shape[1]
    part = width // CTX
    heads = HEADS // CTX
    scale = 1.0 / math.sqrt(width // HEADS)
    shard = width // nf
    fpart = wide // nf // CTX
    wpart = wide // CTX

    def pick(x, axis):
        return lax.dynamic_index_in_dim(x, c, axis, keepdims=False)

    def gather_f(x):
        return lax.all_gather(x, "fsdp", axis=0, tiled=True)

    qkv_own = pick(qkv_weight.reshape(shard, 3, CTX, part), 2).reshape(shard, 3 * part)
    up_own = pick(up_weight.reshape(shard, nf, CTX, fpart), 2).reshape(shard, wpart)
    down_own = pick(down_weight.reshape(CTX, fpart, width), 0)
    w_qkv = gather_f(qkv_own.astype(half))
    small = jnp.concatenate(
        [ln1_gain, ln1_shift, q_bias, v_bias, out_bias, ln2_gain, ln2_shift, down_bias, up_bias]
    ).astype(half)
    small_all = lax.all_gather(small, "fsdp", axis=0).astype(single)

    def vector(k):
        return small_all[:, k * shard : (k + 1) * shard].reshape(width)

    gain1, shift1, bias_q, bias_v, bias_o, gain2, shift2, bias_d = [vector(k) for k in range(8)]
    bias_u = pick(small_all[:, 8 * shard :].reshape(nf, CTX, fpart), 1).reshape(wpart)
    bias_qkv = jnp.concatenate(
        [pick(bias_q.reshape(CTX, part), 0), jnp.zeros((part,), single), pick(bias_v.reshape(CTX, part), 0)]
    )
    w_out = gather_f(out_weight.astype(half))
    w_down = gather_f(down_own.astype(half))
    w_up = gather_f(up_own.astype(half))

    per = rows // SPAN
    table = jnp.arange(CTX * per, dtype=jnp.int32)
    source = ((table // per) ^ c) * per + table % per
    place = jnp.sum(jnp.where(source[:, None] == table[None, :], span_place[0][None, :], 0), axis=1)
    inv = jnp.sum(jnp.where(place[None, :] == table[:, None], table[None, :], 0), axis=1)
    slopes = 2.0 ** (-8.0 * ((c * heads + jnp.arange(heads)).astype(single) + 1.0) / HEADS)

    def to_rows(x):
        return jnp.concatenate(
            [lax.dynamic_slice_in_dim(x, place[r] * SPAN, SPAN, axis=0) for r in range(CTX * per)]
        )

    def join(pieces):
        return jnp.concatenate([h for p in pieces for h in p], axis=0)

    tok_all = join(gather_ctx(tokens))
    normed1, _ = norm_parts(tok_all.astype(single))
    a1 = (normed1 * gain1 + shift1).astype(half)
    joined = (dot_nn(a1, w_qkv) + bias_qkv).astype(half)
    attended = to_rows(attn_forward(joined, inv, slopes, heads, scale))

    def pieces_of(x):
        return [x[j * rows : (j + 1) * rows] for j in range(CTX)]

    mine = pieces_of(attended)
    mine = [mine[0]] + [swap(mine[j], j) for j in range(1, CTX)]
    ob = jnp.concatenate(xor_order(mine, c), axis=1)
    y1 = tokens.astype(single) + dot_nn(ob, w_out) + bias_o

    normed2, inv2 = norm_parts(y1)
    a2_pieces = gather_ctx((normed2 * gain2 + shift2).astype(half))
    dz2_own = cotangent.astype(half)
    dz2_pieces = gather_ctx(dz2_own)
    a2_pieces = [jnp.concatenate(p, axis=0) for p in a2_pieces]
    dz2_pieces = [jnp.concatenate(p, axis=0) for p in dz2_pieces]
    gb, du, dh2, mix = [], [], [None] * CTX, [None] * CTX
    for j in range(CTX):
        dgb = dot_nt(dz2_pieces[j], w_down).astype(half).astype(single)
        value, slope = gelu_both(dot_nn(a2_pieces[j], w_up) + bias_u)
        gb.append(value.astype(half))
        du.append((dgb * slope).astype(half))
    for j in reversed(range(CTX)):
        dh2[j] = dot_nt(du[j], w_up)
        if j:
            dh2[j] = dh2[j].astype(half)
    for j in reversed(range(CTX)):
        mix[j] = dot_nn(gb[j], w_down)
        if j:
            mix[j] = mix[j].astype(half)
    dh2 = scatter_ctx(dh2)
    mixed = y1 + scatter_ctx(mix) + bias_d
    gb = jnp.concatenate(gb, axis=0)
    du = jnp.concatenate(du, axis=0)
    a2 = jnp.concatenate(a2_pieces, axis=0)
    dz2 = jnp.concatenate(dz2_pieces, axis=0)
    down_grad = dot_tn(gb, dz2).astype(half)
    up_grad = dot_tn(a2, du).astype(half)
    up_bias_grad = jnp.sum(du.astype(single), axis=0)
    down_bias_grad = jnp.sum(dz2_own.astype(single), axis=0)
    gain2_grad = jnp.sum(dh2 * normed2, axis=0)
    shift2_grad = jnp.sum(dh2, axis=0)
    dy1 = cotangent + norm_back(normed2, inv2, gain2, dh2)

    dz1 = dy1.astype(half)
    out_bias_grad = jnp.sum(dz1.astype(single), axis=0)
    out_grad = dot_tn(ob, dz1).astype(half)
    dattn = dot_nt(dz1, w_out).astype(half)
    dattn = xor_order([dattn[:, s * part : (s + 1) * part] for s in range(CTX)], c)
    dattn = jnp.concatenate([dattn[0]] + [swap(dattn[j], j) for j in range(1, CTX)], axis=0)
    dqkv = jnp.concatenate(attn_backward(joined, dattn, inv, slopes, heads, scale), axis=1)
    dqkv = to_rows(dqkv)
    dh1 = [dot_nt(p, w_qkv) for p in pieces_of(dqkv)]
    dh1 = scatter_ctx(dh1[:1] + [p.astype(half) for p in dh1[1:]])
    qkv_grad = dot_tn(a1, dqkv).astype(half)
    sums = jnp.sum(dqkv.astype(single), axis=0)
    normed1_own, inv1_own = norm_parts(tokens.astype(single))
    gain1_grad = jnp.sum(dh1 * normed1_own, axis=0)
    shift1_grad = jnp.sum(dh1, axis=0)
    input_grad = dy1 + norm_back(normed1_own, inv1_own, gain1, dh1)

    def scatter_f(x):
        return lax.psum_scatter(x, "fsdp", scatter_dimension=0, tiled=True)

    def everywhere(x):
        pieces = [jnp.concatenate(p, axis=0) for p in gather_ctx(x)]
        return xor_order([p.astype(single) for p in pieces], c)

    down_out = jnp.concatenate(everywhere(scatter_f(down_grad)), axis=0)
    up_out = everywhere(scatter_f(up_grad))
    up_out = jnp.stack([p.reshape(shard, nf, fpart) for p in up_out], axis=2).reshape(shard, wide)
    out_part = scatter_f(out_grad)
    bit = 1
    while bit < CTX:
        out_part = out_part.astype(half)
        out_part = out_part.astype(single) + swap(out_part, bit).astype(single)
        bit *= 2
    out_out = out_part
    qkv_out = everywhere(scatter_f(qkv_grad))
    qkv_out = jnp.stack([p.reshape(shard, 3, part) for p in qkv_out], axis=2)
    qkv_out = qkv_out.reshape(shard, 3 * width)

    def spread(x, inner):
        x = x.reshape(-1, 1, inner)
        mask = (jnp.arange(CTX) == c)[None, :, None]
        return jnp.where(mask, x, 0.0).reshape(-1)

    early = [out_bias_grad, gain2_grad, shift2_grad, down_bias_grad, spread(up_bias_grad, fpart)]
    late = [gain1_grad, shift1_grad, spread(sums[:part], part), spread(sums[2 * part :], part)]

    def reduced(items):
        sizes = [x.shape[0] // nf for x in items]
        x = jnp.concatenate([x.reshape(nf, -1) for x in items], axis=1)
        x = lax.psum(x, ("ctx", "fsdp"))
        x = lax.dynamic_index_in_dim(x, f, 0, keepdims=False)
        out, at = [], 0
        for n in sizes:
            out.append(x[at : at + n])
            at += n
        return out

    out_bias_out, gain2_out, shift2_out, down_bias_out, up_bias_out = reduced(early)
    gain1_out, shift1_out, q_bias_out, v_bias_out = reduced(late)
    return (
        mixed,
        input_grad,
        gain1_out,
        shift1_out,
        qkv_out,
        q_bias_out,
        v_bias_out,
        out_out,
        out_bias_out,
        gain2_out,
        shift2_out,
        up_out,
        up_bias_out,
        down_out,
        down_bias_out,
    )


def solution(mesh):
    rows, flat = P(("ctx", "fsdp"), None), P("fsdp")
    mat = P("fsdp", None)
    in_specs = (
        rows,
        rows,
        mat,
        mat,
        flat,
        flat,
        mat,
        flat,
        flat,
        mat,
        flat,
        flat,
        flat,
        mat,
        flat,
        mat,
        flat,
    )
    out_specs = (
        rows,
        rows,
        flat,
        flat,
        mat,
        flat,
        flat,
        mat,
        flat,
        flat,
        flat,
        mat,
        flat,
        mat,
        flat,
    )
    return jax.shard_map(
        per_device, mesh=mesh, in_specs=in_specs, out_specs=out_specs, check_vma=False
    )
```

```python
import functools
import math

import jax
import jax.numpy as jnp
from jax import lax
from jax.experimental import pallas as pl
from jax.experimental.pallas import tpu as pltpu
from jax.sharding import PartitionSpec as P

HEADS = 16
SPAN = 128
SEQ_BLOCKS = 8

norm_eps = 1e-05
gelu_coef = 0.7978845608028654
LOG2E = 1.4426950408889634

half = jnp.bfloat16
single = jnp.float32


def dot_nn(a, b):
    return lax.dot_general(a, b, (((1,), (0,)), ((), ())), preferred_element_type=single)


def dot_nt(a, b):
    return lax.dot_general(a, b, (((1,), (1,)), ((), ())), preferred_element_type=single)


def dot_tn(a, b):
    return lax.dot_general(a, b, (((0,), (0,)), ((), ())), preferred_element_type=single)


def norm_parts(values):
    center = values - jnp.mean(values, axis=-1, keepdims=True)
    spread = jnp.mean(center * center, axis=-1, keepdims=True)
    inv = lax.rsqrt(spread + norm_eps)
    return center * inv, inv


def norm_back(normed, inv, gain, grad):
    dn = grad * gain
    return inv * (
        dn
        - jnp.mean(dn, axis=-1, keepdims=True)
        - normed * jnp.mean(dn * normed, axis=-1, keepdims=True)
    )


def gelu_both(v):
    t = jnp.tanh(gelu_coef * (v + 0.044715 * v * v * v))
    value = 0.5 * v * (1.0 + t)
    slope = 0.5 * (1.0 + t) + 0.5 * v * (1.0 - t * t) * gelu_coef * (1.0 + 3 * 0.044715 * v * v)
    return value, slope


def swap(x, mask):
    n = lax.axis_size("ctx")
    return lax.ppermute(x, "ctx", [(i, i ^ mask) for i in range(n)])


def gather_ctx(x):
    n = x.shape[0] // 2
    count = lax.axis_size("ctx")
    if count != 4:
        c = lax.axis_index("ctx")
        whole = lax.all_gather(x, "ctx", axis=0)
        parts = [lax.dynamic_index_in_dim(whole, c ^ j, 0, keepdims=False) for j in range(count)]
        return [(p[:n], p[n:]) for p in parts]
    lo, hi = x[:n], x[n:]
    x_lo = swap(lo, 1)
    y_hi = swap(hi, 2)
    x_hi = swap(hi, 1)
    y_lo = swap(lo, 2)
    d_lo = swap(x_lo, 2)
    d_hi = swap(y_hi, 1)
    return [(lo, hi), (x_lo, x_hi), (y_lo, y_hi), (d_lo, d_hi)]


def scatter_ctx(pieces):
    if len(pieces) != 4:
        c = lax.axis_index("ctx")
        ordered = xor_order([p.astype(half) for p in pieces], c)
        whole = jnp.concatenate(ordered, axis=0)
        return lax.psum_scatter(whole, "ctx", scatter_dimension=0, tiled=True).astype(single)
    p0, p1, p2, p3 = pieces
    n = p0.shape[0] // 2
    from_x = swap(p3[:n], 1)
    from_y = swap(p3[n:], 2)
    p2_lo = (p2[:n].astype(single) + from_x.astype(single)).astype(half)
    p1_hi = (p1[n:].astype(single) + from_y.astype(single)).astype(half)
    x_lo = swap(p1[:n], 1)
    y_hi = swap(p2[n:], 2)
    x_hi = swap(p1_hi, 1)
    y_lo = swap(p2_lo, 2)
    lo = p0[:n].astype(single) + x_lo.astype(single) + y_lo.astype(single)
    hi = p0[n:].astype(single) + x_hi.astype(single) + y_hi.astype(single)
    return jnp.concatenate([lo, hi], axis=0)


def xor_order(items, c):
    bit = 1
    while bit < len(items):
        on = (c & bit) == bit
        items = [jnp.where(on, items[i ^ bit], items[i]) for i in range(len(items))]
        bit *= 2
    return items


TILE = 256


def attn_scores(q_refs, k_refs, i, scale, slope):
    q = jnp.concatenate([q_refs[2 * i][...], q_refs[2 * i + 1][...]], axis=0)
    k = jnp.concatenate([r[...] for r in k_refs[: 2 * i + 2]], axis=0)
    n = TILE * (i + 1)
    col = lax.broadcasted_iota(jnp.int32, (1, n), 1) - (n - 1)
    s = dot_nt(q, k) * (scale * LOG2E) + (slope * LOG2E) * col.astype(single)
    row_at = lax.broadcasted_iota(jnp.int32, (TILE, TILE), 0)
    col_at = lax.broadcasted_iota(jnp.int32, (TILE, TILE), 1)
    last = jnp.where(col_at <= row_at, s[:, n - TILE :], -1e30)
    s = last if i == 0 else jnp.concatenate([s[:, : n - TILE], last], axis=1)
    e = jnp.exp2(s - jnp.max(s, axis=1, keepdims=True))
    return q, k, e, 1.0 / jnp.sum(e, axis=1, keepdims=True)


def attn_fwd_kernel(scale, inv_ref, slope_ref, *refs):
    q_refs, k_refs, v_refs = refs[:8], refs[8:16], refs[16:24]
    o_ref = refs[24]
    slope = slope_ref[pl.program_id(1)]
    for i in range(4):
        q, k, e, r = attn_scores(q_refs, k_refs, i, scale, slope)
        v = jnp.concatenate([x[...] for x in v_refs[: 2 * i + 2]], axis=0)
        o = dot_nn((e * r).astype(half), v)
        o_ref[TILE * i : TILE * (i + 1), :] = o.astype(half)


def attn_bwd_kernel(scale, inv_ref, slope_ref, *refs):
    q_refs, k_refs, v_refs, g_refs = refs[:8], refs[8:16], refs[16:24], refs[24:32]
    dq_ref, dk_ref, dv_ref, dk_acc, dv_acc = refs[32:]
    slope = slope_ref[pl.program_id(1)]
    for i in (3, 2, 1, 0):
        q, k, e, r = attn_scores(q_refs, k_refs, i, scale, slope)
        n = TILE * (i + 1)
        v = jnp.concatenate([x[...] for x in v_refs[: 2 * i + 2]], axis=0)
        g = jnp.concatenate([g_refs[2 * i][...], g_refs[2 * i + 1][...]], axis=0)
        p = e * r
        dp = dot_nt(g, v)
        delta = jnp.sum(p * dp, axis=1, keepdims=True)
        ds = (p * (dp - delta)).astype(half)
        pb = p.astype(half)
        dq_ref[TILE * i : TILE * (i + 1), :] = (dot_nn(ds, k) * scale).astype(half)
        dk = dot_tn(ds, q)
        dv = dot_tn(pb, g)
        if i == 3:
            dk_acc[...] = dk
            dv_acc[...] = dv
        else:
            dk_acc[:n, :] += dk
            dv_acc[:n, :] += dv
    dk_ref[...] = (dk_acc[...] * scale).astype(half)
    dv_ref[...] = dv_acc[...].astype(half)


def block_specs(offset):
    def one(j):
        return pl.BlockSpec(
            (SPAN, 128), lambda s, h, inv, slope: (inv[s * SEQ_BLOCKS + j], offset + h)
        )

    return [one(j) for j in range(SEQ_BLOCKS)]


def attn_forward(joined, inv, slopes, heads, scale):
    rows = joined.shape[0]
    specs = block_specs(0) + block_specs(heads) + block_specs(2 * heads)
    out = pl.BlockSpec((rows // 2, 128), lambda s, h, inv, slope: (s, h))
    return pl.pallas_call(
        functools.partial(attn_fwd_kernel, scale),
        grid_spec=pltpu.PrefetchScalarGridSpec(
            num_scalar_prefetch=2, grid=(2, heads), in_specs=specs, out_specs=out
        ),
        out_shape=jax.ShapeDtypeStruct((rows, heads * 128), half),
        compiler_params=pltpu.CompilerParams(vmem_limit_bytes=48 * 1024 * 1024),
        cost_estimate=pl.CostEstimate(
            flops=20 * 10**9, bytes_accessed=rows * heads * 128 * 8, transcendentals=0
        ),
        name="attn_forward",
    )(inv, slopes, *([joined] * 24))


def attn_backward(joined, grad, inv, slopes, heads, scale):
    rows = joined.shape[0]
    specs = block_specs(0) + block_specs(heads) + block_specs(2 * heads) + block_specs(0)
    out = pl.BlockSpec((rows // 2, 128), lambda s, h, inv, slope: (s, h))
    shape = jax.ShapeDtypeStruct((rows, heads * 128), half)
    return pl.pallas_call(
        functools.partial(attn_bwd_kernel, scale),
        grid_spec=pltpu.PrefetchScalarGridSpec(
            num_scalar_prefetch=2,
            grid=(2, heads),
            in_specs=specs,
            out_specs=[out] * 3,
            scratch_shapes=[pltpu.VMEM((rows // 2, 128), single)] * 2,
        ),
        out_shape=[shape] * 3,
        compiler_params=pltpu.CompilerParams(vmem_limit_bytes=48 * 1024 * 1024),
        cost_estimate=pl.CostEstimate(
            flops=40 * 10**9, bytes_accessed=rows * heads * 128 * 14, transcendentals=0
        ),
        name="attn_backward",
    )(inv, slopes, *([joined] * 24), *([grad] * 8))


def gather_small_kernel(nf, x_ref, o_ref, send_sem, recv_sem):
    f = lax.axis_index("fsdp")
    barrier = pltpu.get_barrier_semaphore()
    for d in range(1, nf):
        pl.semaphore_signal(
            barrier,
            inc=1,
            device_id={"fsdp": lax.rem(f + d, nf)},
            device_id_type=pl.DeviceIdType.MESH,
        )
    pl.semaphore_wait(barrier, nf - 1)
    copies = []
    for d in range(1, nf):
        copies.append(
            pltpu.make_async_remote_copy(
                src_ref=x_ref,
                dst_ref=o_ref.at[f],
                send_sem=send_sem.at[d],
                recv_sem=recv_sem.at[d],
                device_id={"fsdp": lax.rem(f + d, nf)},
                device_id_type=pl.DeviceIdType.MESH,
            )
        )
        copies[-1].start()
    o_ref[f] = x_ref[...]
    for copy in copies:
        copy.wait()


def gather_small(x, nf):
    return pl.pallas_call(
        functools.partial(gather_small_kernel, nf),
        out_shape=jax.ShapeDtypeStruct((nf,) + x.shape, single),
        in_specs=[pl.BlockSpec(memory_space=pltpu.VMEM)],
        out_specs=pl.BlockSpec(memory_space=pltpu.VMEM),
        scratch_shapes=[pltpu.SemaphoreType.DMA((nf,)), pltpu.SemaphoreType.DMA((nf,))],
        compiler_params=pltpu.CompilerParams(collective_id=1, has_side_effects=True),
        name="gather_small",
    )(x)


def reduce_small_kernel(nf, nc, x_ref, o_ref, land, stage, send_sem, recv_sem):
    f = lax.axis_index("fsdp")
    c = lax.axis_index("ctx")
    barrier = pltpu.get_barrier_semaphore()
    for d in range(1, nf):
        pl.semaphore_signal(
            barrier,
            inc=1,
            device_id={"fsdp": lax.rem(f + d, nf)},
            device_id_type=pl.DeviceIdType.MESH,
        )
    for d in range(1, nc):
        pl.semaphore_signal(
            barrier,
            inc=1,
            device_id={"ctx": lax.rem(c + d, nc)},
            device_id_type=pl.DeviceIdType.MESH,
        )
    pl.semaphore_wait(barrier, nf + nc - 2)
    copies = []
    for d in range(1, nf):
        to = lax.rem(f + d, nf)
        copies.append(
            pltpu.make_async_remote_copy(
                src_ref=x_ref.at[to],
                dst_ref=land.at[d],
                send_sem=send_sem.at[d],
                recv_sem=recv_sem.at[d],
                device_id={"fsdp": to},
                device_id_type=pl.DeviceIdType.MESH,
            )
        )
        copies[-1].start()
    total = x_ref[f]
    for d in range(1, nf):
        copies[d - 1].wait()
        total = total + land[d]
    stage[0] = total
    copies = []
    for d in range(1, nc):
        copies.append(
            pltpu.make_async_remote_copy(
                src_ref=stage.at[0],
                dst_ref=stage.at[d],
                send_sem=send_sem.at[nf + d],
                recv_sem=recv_sem.at[nf + d],
                device_id={"ctx": lax.rem(c + d, nc)},
                device_id_type=pl.DeviceIdType.MESH,
            )
        )
        copies[-1].start()
    for d in range(1, nc):
        copies[d - 1].wait()
        total = total + stage[d]
    o_ref[...] = total


def reduce_small(x, nf, nc, call):
    block = x.shape[1:]
    sems = pltpu.SemaphoreType.DMA((nf + nc,))
    return pl.pallas_call(
        functools.partial(reduce_small_kernel, nf, nc),
        out_shape=jax.ShapeDtypeStruct(block, single),
        in_specs=[pl.BlockSpec(memory_space=pltpu.VMEM)],
        out_specs=pl.BlockSpec(memory_space=pltpu.VMEM),
        scratch_shapes=[
            pltpu.VMEM((nf,) + block, single),
            pltpu.VMEM((nc,) + block, single),
            sems,
            sems,
        ],
        compiler_params=pltpu.CompilerParams(collective_id=call, has_side_effects=True),
        name="reduce_small",
    )(x)


def per_device(
    tokens,
    cotangent,
    lengths,
    span_place,
    ln1_gain,
    ln1_shift,
    qkv_weight,
    q_bias,
    v_bias,
    out_weight,
    out_bias,
    ln2_gain,
    ln2_shift,
    up_weight,
    up_bias,
    down_weight,
    down_bias,
):
    rows, width = tokens.shape
    CTX = lax.axis_size("ctx")
    c = lax.axis_index("ctx")
    f = lax.axis_index("fsdp")
    nf = lax.axis_size("fsdp")
    wide = up_weight.shape[1]
    part = width // CTX
    heads = HEADS // CTX
    scale = 1.0 / math.sqrt(width // HEADS)
    shard = width // nf
    fpart = wide // nf // CTX
    wpart = wide // CTX

    def columns(x, width_each, stride, count):
        return jnp.concatenate(
            [
                lax.dynamic_slice_in_dim(x, k * stride + c * width_each, width_each, axis=1)
                for k in range(count)
            ],
            axis=1,
        )

    def after(x, *others):
        return lax.optimization_barrier((x, others))[0]

    def pick(x, axis):
        return lax.dynamic_index_in_dim(x, c, axis, keepdims=False)

    def gather_f(x):
        return lax.all_gather(x, "fsdp", axis=0, tiled=True)

    qkv_own = columns(qkv_weight, part, width, 3)
    up_own = columns(up_weight, fpart, wide // nf, nf)
    down_own = lax.dynamic_slice_in_dim(down_weight, c * fpart, fpart, axis=0)
    w_qkv = gather_f(qkv_own.astype(half))
    small = jnp.concatenate(
        [ln1_gain, ln1_shift, q_bias, v_bias, out_bias, ln2_gain, ln2_shift, down_bias, up_bias]
    )
    small_len = small.shape[0]
    small = jnp.pad(small, (0, -small_len % 1024)).reshape(-1, 128)
    small_all = gather_small(small, nf).reshape(nf, -1)[:, :small_len]
    small_all = small_all.astype(half).astype(single)

    def vector(k):
        return small_all[:, k * shard : (k + 1) * shard].reshape(width)

    gain1, shift1, bias_q, bias_v, bias_o, gain2, shift2, bias_d = [vector(k) for k in range(8)]
    bias_u = pick(small_all[:, 8 * shard :].reshape(nf, CTX, fpart), 1).reshape(wpart)
    bias_qkv = jnp.concatenate(
        [pick(bias_q.reshape(CTX, part), 0), jnp.zeros((part,), single), pick(bias_v.reshape(CTX, part), 0)]
    )
    w_out = gather_f(out_weight.astype(half))

    per = rows // SPAN
    table = jnp.arange(CTX * per, dtype=jnp.int32)
    source = ((table // per) ^ c) * per + table % per
    place = jnp.sum(jnp.where(source[:, None] == table[None, :], span_place[0][None, :], 0), axis=1)
    inv = jnp.sum(jnp.where(place[None, :] == table[:, None], table[None, :], 0), axis=1)
    slopes = 2.0 ** (-8.0 * ((c * heads + jnp.arange(heads)).astype(single) + 1.0) / HEADS)

    def to_rows(x):
        return jnp.concatenate(
            [lax.dynamic_slice_in_dim(x, place[r] * SPAN, SPAN, axis=0) for r in range(CTX * per)]
        )

    def join(pieces):
        return jnp.concatenate([h for p in pieces for h in p], axis=0)

    tok_all = join(gather_ctx(tokens))
    w_down = gather_f(after(down_own.astype(half), tok_all))
    normed1, _ = norm_parts(tok_all.astype(single))
    a1 = (normed1 * gain1 + shift1).astype(half)
    joined = (dot_nn(a1, w_qkv) + bias_qkv).astype(half)
    w_up = gather_f(after(up_own.astype(half), joined))
    attended = to_rows(attn_forward(joined, inv, slopes, heads, scale))

    def pieces_of(x):
        return [x[j * rows : (j + 1) * rows] for j in range(CTX)]

    mine = pieces_of(attended)
    mine = [mine[0]] + [swap(mine[j], j) for j in range(1, CTX)]
    ob = jnp.concatenate(xor_order(mine, c), axis=1)
    y1 = tokens.astype(single) + dot_nn(ob, w_out) + bias_o

    normed2, inv2 = norm_parts(y1)
    a2_pieces = gather_ctx((normed2 * gain2 + shift2).astype(half))
    dz2_own = cotangent.astype(half)
    dz2_pieces = gather_ctx(dz2_own)
    a2_pieces = [jnp.concatenate(p, axis=0) for p in a2_pieces]
    dz2_pieces = [jnp.concatenate(p, axis=0) for p in dz2_pieces]
    gb, du, dh2, mix = [], [], [None] * CTX, [None] * CTX
    for j in range(CTX):
        dgb = dot_nt(dz2_pieces[j], w_down).astype(half).astype(single)
        value, slope = gelu_both(dot_nn(a2_pieces[j], w_up) + bias_u)
        gb.append(value.astype(half))
        du.append((dgb * slope).astype(half))
    for j in reversed(range(CTX)):
        dh2[j] = dot_nt(du[j], w_up)
        if j:
            dh2[j] = dh2[j].astype(half)
    dh2_own = dh2[0]
    dh2 = scatter_ctx(dh2)
    gb_all = jnp.concatenate(after(gb, dh2_own), axis=0)
    du = jnp.concatenate(du, axis=0)
    a2 = jnp.concatenate(a2_pieces, axis=0)
    dz2 = jnp.concatenate(dz2_pieces, axis=0)
    down_grad = dot_tn(gb_all, dz2).astype(half)
    up_grad = dot_tn(a2, du).astype(half)
    up_bias_grad = jnp.sum(du.astype(single), axis=0)
    down_bias_grad = jnp.sum(dz2_own.astype(single), axis=0)
    gb = after(gb, dh2_own)
    for j in reversed(range(CTX)):
        mix[j] = dot_nn(gb[j], w_down)
        if j:
            mix[j] = mix[j].astype(half)
    mixed = y1 + scatter_ctx(mix) + bias_d
    gain2_grad = jnp.sum(dh2 * normed2, axis=0)
    shift2_grad = jnp.sum(dh2, axis=0)
    dy1 = cotangent + norm_back(normed2, inv2, gain2, dh2)

    def scatter_f(x):
        return lax.psum_scatter(x, "fsdp", scatter_dimension=0, tiled=True)

    down_part = scatter_f(down_grad)
    dz1 = dy1.astype(half)
    out_bias_grad = jnp.sum(dz1.astype(single), axis=0)
    out_grad = dot_tn(ob, dz1).astype(half)
    up_part = scatter_f(after(up_grad, down_part))
    dattn = dot_nt(dz1, w_out).astype(half)
    dattn = xor_order([dattn[:, s * part : (s + 1) * part] for s in range(CTX)], c)
    dattn = jnp.concatenate([dattn[0]] + [swap(dattn[j], j) for j in range(1, CTX)], axis=0)
    dqkv = jnp.concatenate(attn_backward(joined, after(dattn, up_grad), inv, slopes, heads, scale), axis=1)
    dqkv = to_rows(dqkv)
    dh1 = [dot_nt(p, w_qkv) for p in pieces_of(dqkv)]
    dh1_own = dh1[0]
    dh1 = scatter_ctx(dh1[:1] + [p.astype(half) for p in dh1[1:]])
    qkv_grad = dot_tn(a1, after(dqkv, dh1_own)).astype(half)
    sums = jnp.sum(dqkv.astype(single), axis=0)
    normed1_own, inv1_own = norm_parts(tokens.astype(single))
    gain1_grad = jnp.sum(dh1 * normed1_own, axis=0)
    shift1_grad = jnp.sum(dh1, axis=0)
    input_grad = dy1 + norm_back(normed1_own, inv1_own, gain1, dh1)

    out_part = scatter_f(after(out_grad, up_part))
    qkv_part = scatter_f(after(qkv_grad, out_part))

    def everywhere(x):
        pieces = [jnp.concatenate(p, axis=0) for p in gather_ctx(x)]
        return xor_order([p.astype(single) for p in pieces], c)

    down_out = jnp.concatenate(everywhere(down_part), axis=0)
    up_out = everywhere(up_part)
    up_out = jnp.stack([p.reshape(shard, nf, fpart) for p in up_out], axis=2).reshape(shard, wide)
    bit = 1
    while bit < CTX:
        out_part = out_part.astype(half)
        out_part = out_part.astype(single) + swap(out_part, bit).astype(single)
        bit *= 2
    out_out = out_part
    qkv_out = everywhere(qkv_part)
    qkv_out = jnp.stack([p.reshape(shard, 3, part) for p in qkv_out], axis=2)
    qkv_out = qkv_out.reshape(shard, 3 * width)

    def spread(x, inner):
        x = x.reshape(-1, 1, inner)
        mask = (jnp.arange(CTX) == c)[None, :, None]
        return jnp.where(mask, x, 0.0).reshape(-1)

    early = [out_bias_grad, gain2_grad, shift2_grad, down_bias_grad, spread(up_bias_grad, fpart)]
    late = [gain1_grad, shift1_grad, spread(sums[:part], part), spread(sums[2 * part :], part)]

    def reduced(items, call):
        sizes = [x.shape[0] // nf for x in items]
        x = jnp.concatenate([x.reshape(nf, -1) for x in items], axis=1)
        x = jnp.pad(x, ((0, 0), (0, -x.shape[1] % 1024))).reshape(nf, -1, 128)
        x = reduce_small(x, nf, CTX, call).reshape(-1)
        out, at = [], 0
        for n in sizes:
            out.append(x[at : at + n])
            at += n
        return out

    out_bias_out, gain2_out, shift2_out, down_bias_out, up_bias_out = reduced(early, 2)
    gain1_out, shift1_out, q_bias_out, v_bias_out = reduced(late, 3)
    return (
        mixed,
        input_grad,
        gain1_out,
        shift1_out,
        qkv_out,
        q_bias_out,
        v_bias_out,
        out_out,
        out_bias_out,
        gain2_out,
        shift2_out,
        up_out,
        up_bias_out,
        down_out,
        down_bias_out,
    )


def solution(mesh):
    rows, flat = P(("ctx", "fsdp"), None), P("fsdp")
    mat = P("fsdp", None)
    in_specs = (
        rows,
        rows,
        mat,
        mat,
        flat,
        flat,
        mat,
        flat,
        flat,
        mat,
        flat,
        flat,
        flat,
        mat,
        flat,
        mat,
        flat,
    )
    out_specs = (
        rows,
        rows,
        flat,
        flat,
        mat,
        flat,
        flat,
        mat,
        flat,
        flat,
        flat,
        mat,
        flat,
        mat,
        flat,
    )
    return jax.shard_map(
        per_device, mesh=mesh, in_specs=in_specs, out_specs=out_specs, check_vma=False
    )
```

```python
import functools
import math

import jax
import jax.numpy as jnp
from jax import lax
from jax.experimental import pallas as pl
from jax.experimental.pallas import tpu as pltpu
from jax.sharding import PartitionSpec as P

HEADS = 16
SPAN = 128
SEQ_BLOCKS = 8

norm_eps = 1e-05
gelu_coef = 0.7978845608028654
LOG2E = 1.4426950408889634

half = jnp.bfloat16
single = jnp.float32


def dot_nn(a, b):
    return lax.dot_general(a, b, (((1,), (0,)), ((), ())), preferred_element_type=single)


def dot_nt(a, b):
    return lax.dot_general(a, b, (((1,), (1,)), ((), ())), preferred_element_type=single)


def dot_tn(a, b):
    return lax.dot_general(a, b, (((0,), (0,)), ((), ())), preferred_element_type=single)


def norm_parts(values):
    center = values - jnp.mean(values, axis=-1, keepdims=True)
    spread = jnp.mean(center * center, axis=-1, keepdims=True)
    inv = lax.rsqrt(spread + norm_eps)
    return center * inv, inv


def norm_back(normed, inv, gain, grad):
    dn = grad * gain
    return inv * (
        dn
        - jnp.mean(dn, axis=-1, keepdims=True)
        - normed * jnp.mean(dn * normed, axis=-1, keepdims=True)
    )


def gelu_both(v):
    t = jnp.tanh(gelu_coef * (v + 0.044715 * v * v * v))
    value = 0.5 * v * (1.0 + t)
    slope = 0.5 * (1.0 + t) + 0.5 * v * (1.0 - t * t) * gelu_coef * (1.0 + 3 * 0.044715 * v * v)
    return value, slope


def swap(x, mask):
    n = lax.axis_size("ctx")
    return lax.ppermute(x, "ctx", [(i, i ^ mask) for i in range(n)])


def gather_ctx(x):
    count = lax.axis_size("ctx")
    if count != 4:
        return [[x]] + [[swap(x, j)] for j in range(1, count)]
    n = x.shape[0] // 2
    one, two = swap(x, 1), swap(x, 2)
    lo, hi = swap(one[:n], 2), swap(two[n:], 1)
    return [[x], [one], [two], [lo, hi]]


def scatter_first(far):
    if lax.axis_size("ctx") != 4:
        return None
    n = far.shape[0] // 2
    return swap(far[:n], 1), swap(far[n:], 2)


def scatter_second(pieces, first):
    if first is None:
        return [swap(p, j) for j, p in enumerate(pieces) if j]
    p1, p2 = pieces[1], pieces[2]
    n = p1.shape[0] // 2
    from_x, from_y = first
    p1 = jnp.concatenate(
        [p1[:n], (p1[n:].astype(single) + from_y.astype(single)).astype(half)], axis=0
    )
    p2 = jnp.concatenate(
        [(p2[:n].astype(single) + from_x.astype(single)).astype(half), p2[n:]], axis=0
    )
    return [swap(p1, 1), swap(p2, 2)]


def total_of(own, arrived):
    for x in arrived:
        own = own + x.astype(single)
    return own


def xor_order(items, c):
    bit = 1
    while bit < len(items):
        on = (c & bit) == bit
        items = [jnp.where(on, items[i ^ bit], items[i]) for i in range(len(items))]
        bit *= 2
    return items


TILE = 256


def attn_scores(q_refs, k_refs, i, scale, slope):
    q = jnp.concatenate([q_refs[2 * i][...], q_refs[2 * i + 1][...]], axis=0)
    k = jnp.concatenate([r[...] for r in k_refs[: 2 * i + 2]], axis=0)
    n = TILE * (i + 1)
    col = lax.broadcasted_iota(jnp.int32, (1, n), 1) - (n - 1)
    s = dot_nt(q, k) * (scale * LOG2E) + (slope * LOG2E) * col.astype(single)
    row_at = lax.broadcasted_iota(jnp.int32, (TILE, TILE), 0)
    col_at = lax.broadcasted_iota(jnp.int32, (TILE, TILE), 1)
    last = jnp.where(col_at <= row_at, s[:, n - TILE :], -1e30)
    s = last if i == 0 else jnp.concatenate([s[:, : n - TILE], last], axis=1)
    e = jnp.exp2(s - jnp.max(s, axis=1, keepdims=True))
    return q, k, e, 1.0 / jnp.sum(e, axis=1, keepdims=True)


def attn_fwd_kernel(scale, inv_ref, slope_ref, *refs):
    q_refs, k_refs, v_refs = refs[:8], refs[8:16], refs[16:24]
    o_ref = refs[24]
    slope = slope_ref[pl.program_id(1)]
    for i in range(4):
        q, k, e, r = attn_scores(q_refs, k_refs, i, scale, slope)
        v = jnp.concatenate([x[...] for x in v_refs[: 2 * i + 2]], axis=0)
        o = dot_nn((e * r).astype(half), v)
        o_ref[TILE * i : TILE * (i + 1), :] = o.astype(half)


def attn_bwd_kernel(scale, inv_ref, slope_ref, *refs):
    q_refs, k_refs, v_refs, g_refs = refs[:8], refs[8:16], refs[16:24], refs[24:32]
    dq_ref, dk_ref, dv_ref, dk_acc, dv_acc = refs[32:]
    slope = slope_ref[pl.program_id(1)]
    for i in (3, 2, 1, 0):
        q, k, e, r = attn_scores(q_refs, k_refs, i, scale, slope)
        n = TILE * (i + 1)
        v = jnp.concatenate([x[...] for x in v_refs[: 2 * i + 2]], axis=0)
        g = jnp.concatenate([g_refs[2 * i][...], g_refs[2 * i + 1][...]], axis=0)
        p = e * r
        dp = dot_nt(g, v)
        delta = jnp.sum(p * dp, axis=1, keepdims=True)
        ds = (p * (dp - delta)).astype(half)
        pb = p.astype(half)
        dq_ref[TILE * i : TILE * (i + 1), :] = (dot_nn(ds, k) * scale).astype(half)
        dk = dot_tn(ds, q)
        dv = dot_tn(pb, g)
        if i == 3:
            dk_acc[...] = dk
            dv_acc[...] = dv
        else:
            dk_acc[:n, :] += dk
            dv_acc[:n, :] += dv
    dk_ref[...] = (dk_acc[...] * scale).astype(half)
    dv_ref[...] = dv_acc[...].astype(half)


def block_specs(offset):
    def one(j):
        return pl.BlockSpec(
            (SPAN, 128), lambda s, h, inv, slope: (inv[s * SEQ_BLOCKS + j], offset + h)
        )

    return [one(j) for j in range(SEQ_BLOCKS)]


def attn_forward(joined, inv, slopes, heads, scale):
    rows = joined.shape[0]
    specs = block_specs(0) + block_specs(heads) + block_specs(2 * heads)
    out = pl.BlockSpec((rows // 2, 128), lambda s, h, inv, slope: (s, h))
    return pl.pallas_call(
        functools.partial(attn_fwd_kernel, scale),
        grid_spec=pltpu.PrefetchScalarGridSpec(
            num_scalar_prefetch=2, grid=(2, heads), in_specs=specs, out_specs=out
        ),
        out_shape=jax.ShapeDtypeStruct((rows, heads * 128), half),
        compiler_params=pltpu.CompilerParams(vmem_limit_bytes=48 * 1024 * 1024),
        cost_estimate=pl.CostEstimate(
            flops=20 * 10**9, bytes_accessed=rows * heads * 128 * 8, transcendentals=0
        ),
        name="attn_forward",
    )(inv, slopes, *([joined] * 24))


def attn_backward(joined, grad, inv, slopes, heads, scale):
    rows = joined.shape[0]
    specs = block_specs(0) + block_specs(heads) + block_specs(2 * heads) + block_specs(0)
    out = pl.BlockSpec((rows // 2, 128), lambda s, h, inv, slope: (s, h))
    shape = jax.ShapeDtypeStruct((rows, heads * 128), half)
    return pl.pallas_call(
        functools.partial(attn_bwd_kernel, scale),
        grid_spec=pltpu.PrefetchScalarGridSpec(
            num_scalar_prefetch=2,
            grid=(2, heads),
            in_specs=specs,
            out_specs=[out] * 3,
            scratch_shapes=[pltpu.VMEM((rows // 2, 128), single)] * 2,
        ),
        out_shape=[shape] * 3,
        compiler_params=pltpu.CompilerParams(vmem_limit_bytes=48 * 1024 * 1024),
        cost_estimate=pl.CostEstimate(
            flops=40 * 10**9, bytes_accessed=rows * heads * 128 * 14, transcendentals=0
        ),
        name="attn_backward",
    )(inv, slopes, *([joined] * 24), *([grad] * 8))


def up_kernel(a_ref, w_ref, b_ref, g_ref, s_ref):
    u = dot_nn(a_ref[...], w_ref[...]) + b_ref[...]
    value, slope = gelu_both(u)
    g_ref[...] = value.astype(half)
    s_ref[...] = slope.astype(half)


def up_gelu(a, w, b):
    m, k = a.shape
    n = w.shape[1]
    t = min(n, 512)
    col = pl.BlockSpec((m, t), lambda i: (0, i))
    shape = jax.ShapeDtypeStruct((m, n), half)
    return pl.pallas_call(
        up_kernel,
        grid=(n // t,),
        in_specs=[
            pl.BlockSpec((m, k), lambda i: (0, 0)),
            pl.BlockSpec((k, t), lambda i: (0, i)),
            pl.BlockSpec((1, t), lambda i: (0, i)),
        ],
        out_specs=[col, col],
        out_shape=[shape, shape],
        compiler_params=pltpu.CompilerParams(vmem_limit_bytes=48 * 1024 * 1024),
        cost_estimate=pl.CostEstimate(
            flops=2 * m * n * k, bytes_accessed=2 * (m * k + n * k + 2 * m * n), transcendentals=m * n
        ),
        name="up_gelu",
    )(a, w, b.reshape(1, n))


def lay_out_kernel(axis, layout, c_ref, *refs):
    out = refs[-1]
    for (j, row), ref in zip(layout, refs):
        x = ref[...].astype(single)
        r, w = x.shape
        if axis == 0:
            n = sum(ref.shape[0] for (k, _), ref in zip(layout, refs) if k == j)
            out[pl.ds(pl.multiple_of((c_ref[0] ^ j) * n + row, r), r), :] = x
        else:
            out[row : row + r, pl.ds(pl.multiple_of((c_ref[0] ^ j) * w, w), w)] = x


def lay_out(axis, pieces, c, groups):
    count = len(pieces)
    r = sum(x.shape[0] for x in pieces[0])
    n = pieces[0][0].shape[1]
    w = n // groups
    if w % 128:
        whole = xor_order([jnp.concatenate(p, axis=0).astype(single) for p in pieces], c)
        whole = jnp.stack([p.reshape(r, groups, w) for p in whole], axis=2)
        return whole.reshape(r, count * n)
    layout, blocks = [], []
    for j, p in enumerate(pieces):
        row = 0
        for x in p:
            layout.append((j, row))
            blocks.append(x)
            row += x.shape[0]
    out = (count * r, w) if axis == 0 else (r, count * w)
    return pl.pallas_call(
        functools.partial(lay_out_kernel, axis, layout),
        grid_spec=pltpu.PrefetchScalarGridSpec(
            num_scalar_prefetch=1,
            grid=(groups,),
            in_specs=[pl.BlockSpec((x.shape[0], w), lambda k, c: (0, k)) for x in blocks],
            out_specs=pl.BlockSpec(out, lambda k, c: (0, k)),
        ),
        out_shape=jax.ShapeDtypeStruct((out[0], out[1] * groups), single),
        compiler_params=pltpu.CompilerParams(vmem_limit_bytes=48 * 1024 * 1024),
        cost_estimate=pl.CostEstimate(
            flops=0, bytes_accessed=6 * r * n * count, transcendentals=0
        ),
        name="lay_out",
    )(c.reshape(1), *blocks)


def gather_small_kernel(nf, x_ref, o_ref, send_sem, recv_sem):
    f = lax.axis_index("fsdp")
    barrier = pltpu.get_barrier_semaphore()
    for d in range(1, nf):
        pl.semaphore_signal(
            barrier,
            inc=1,
            device_id={"fsdp": lax.rem(f + d, nf)},
            device_id_type=pl.DeviceIdType.MESH,
        )
    pl.semaphore_wait(barrier, nf - 1)
    copies = []
    for d in range(1, nf):
        copies.append(
            pltpu.make_async_remote_copy(
                src_ref=x_ref,
                dst_ref=o_ref.at[f],
                send_sem=send_sem.at[d],
                recv_sem=recv_sem.at[d],
                device_id={"fsdp": lax.rem(f + d, nf)},
                device_id_type=pl.DeviceIdType.MESH,
            )
        )
        copies[-1].start()
    o_ref[f] = x_ref[...]
    for copy in copies:
        copy.wait()


def gather_small(x, nf):
    return pl.pallas_call(
        functools.partial(gather_small_kernel, nf),
        out_shape=jax.ShapeDtypeStruct((nf,) + x.shape, single),
        in_specs=[pl.BlockSpec(memory_space=pltpu.VMEM)],
        out_specs=pl.BlockSpec(memory_space=pltpu.VMEM),
        scratch_shapes=[pltpu.SemaphoreType.DMA((nf,)), pltpu.SemaphoreType.DMA((nf,))],
        compiler_params=pltpu.CompilerParams(collective_id=1, has_side_effects=True),
        name="gather_small",
    )(x)


def reduce_small_kernel(nf, nc, x_ref, o_ref, land, stage, send_sem, recv_sem):
    f = lax.axis_index("fsdp")
    c = lax.axis_index("ctx")
    barrier = pltpu.get_barrier_semaphore()
    for d in range(1, nf):
        pl.semaphore_signal(
            barrier,
            inc=1,
            device_id={"fsdp": lax.rem(f + d, nf)},
            device_id_type=pl.DeviceIdType.MESH,
        )
    for d in range(1, nc):
        pl.semaphore_signal(
            barrier,
            inc=1,
            device_id={"ctx": lax.rem(c + d, nc)},
            device_id_type=pl.DeviceIdType.MESH,
        )
    pl.semaphore_wait(barrier, nf + nc - 2)
    copies = []
    for d in range(1, nf):
        to = lax.rem(f + d, nf)
        copies.append(
            pltpu.make_async_remote_copy(
                src_ref=x_ref.at[to],
                dst_ref=land.at[d],
                send_sem=send_sem.at[d],
                recv_sem=recv_sem.at[d],
                device_id={"fsdp": to},
                device_id_type=pl.DeviceIdType.MESH,
            )
        )
        copies[-1].start()
    total = x_ref[f]
    for d in range(1, nf):
        copies[d - 1].wait()
        total = total + land[d]
    stage[0] = total
    copies = []
    for d in range(1, nc):
        copies.append(
            pltpu.make_async_remote_copy(
                src_ref=stage.at[0],
                dst_ref=stage.at[d],
                send_sem=send_sem.at[nf + d],
                recv_sem=recv_sem.at[nf + d],
                device_id={"ctx": lax.rem(c + d, nc)},
                device_id_type=pl.DeviceIdType.MESH,
            )
        )
        copies[-1].start()
    for d in range(1, nc):
        copies[d - 1].wait()
        total = total + stage[d]
    o_ref[...] = total


def reduce_small(x, nf, nc, call):
    block = x.shape[1:]
    sems = pltpu.SemaphoreType.DMA((nf + nc,))
    return pl.pallas_call(
        functools.partial(reduce_small_kernel, nf, nc),
        out_shape=jax.ShapeDtypeStruct(block, single),
        in_specs=[pl.BlockSpec(memory_space=pltpu.VMEM)],
        out_specs=pl.BlockSpec(memory_space=pltpu.VMEM),
        scratch_shapes=[
            pltpu.VMEM((nf,) + block, single),
            pltpu.VMEM((nc,) + block, single),
            sems,
            sems,
        ],
        compiler_params=pltpu.CompilerParams(collective_id=call, has_side_effects=True),
        name="reduce_small",
    )(x)


def per_device(
    tokens,
    cotangent,
    lengths,
    span_place,
    ln1_gain,
    ln1_shift,
    qkv_weight,
    q_bias,
    v_bias,
    out_weight,
    out_bias,
    ln2_gain,
    ln2_shift,
    up_weight,
    up_bias,
    down_weight,
    down_bias,
):
    rows, width = tokens.shape
    CTX = lax.axis_size("ctx")
    c = lax.axis_index("ctx")
    f = lax.axis_index("fsdp")
    nf = lax.axis_size("fsdp")
    wide = up_weight.shape[1]
    part = width // CTX
    heads = HEADS // CTX
    scale = 1.0 / math.sqrt(width // HEADS)
    shard = width // nf
    fpart = wide // nf // CTX
    wpart = wide // CTX

    def columns(x, width_each, stride, count):
        return jnp.concatenate(
            [
                lax.dynamic_slice_in_dim(x, k * stride + c * width_each, width_each, axis=1)
                for k in range(count)
            ],
            axis=1,
        )

    def after(x, *others):
        return lax.optimization_barrier((x, others))[0]

    def pick(x, axis):
        return lax.dynamic_index_in_dim(x, c, axis, keepdims=False)

    def gather_f(x):
        return lax.all_gather(x, "fsdp", axis=0, tiled=True)

    qkv_own = columns(qkv_weight, part, width, 3)
    up_own = columns(up_weight, fpart, wide // nf, nf)
    down_own = lax.dynamic_slice_in_dim(down_weight, c * fpart, fpart, axis=0)
    w_qkv = gather_f(qkv_own.astype(half))
    small = jnp.concatenate(
        [ln1_gain, ln1_shift, q_bias, v_bias, out_bias, ln2_gain, ln2_shift, down_bias, up_bias]
    )
    small_len = small.shape[0]
    small = jnp.pad(small, (0, -small_len % 1024)).reshape(-1, 128)
    small_all = gather_small(small, nf).reshape(nf, -1)[:, :small_len]
    small_all = small_all.astype(half).astype(single)

    def vector(k):
        return small_all[:, k * shard : (k + 1) * shard].reshape(width)

    gain1, shift1, bias_q, bias_v, bias_o, gain2, shift2, bias_d = [vector(k) for k in range(8)]
    bias_u = pick(small_all[:, 8 * shard :].reshape(nf, CTX, fpart), 1).reshape(wpart)
    bias_qkv = jnp.concatenate(
        [pick(bias_q.reshape(CTX, part), 0), jnp.zeros((part,), single), pick(bias_v.reshape(CTX, part), 0)]
    )
    w_out = gather_f(out_weight.astype(half))

    per = rows // SPAN
    table = jnp.arange(CTX * per, dtype=jnp.int32)
    source = ((table // per) ^ c) * per + table % per
    place = jnp.sum(jnp.where(source[:, None] == table[None, :], span_place[0][None, :], 0), axis=1)
    inv = jnp.sum(jnp.where(place[None, :] == table[:, None], table[None, :], 0), axis=1)
    slopes = 2.0 ** (-8.0 * ((c * heads + jnp.arange(heads)).astype(single) + 1.0) / HEADS)

    def to_rows(x):
        return jnp.concatenate(
            [lax.dynamic_slice_in_dim(x, place[r] * SPAN, SPAN, axis=0) for r in range(CTX * per)]
        )

    def join(pieces):
        return jnp.concatenate([x for p in pieces for x in p], axis=0)

    def pieces_of(x):
        return [x[j * rows : (j + 1) * rows] for j in range(CTX)]

    def scatter_f(x):
        return lax.psum_scatter(x, "fsdp", scatter_dimension=0, tiled=True)

    tok_all = join(gather_ctx(tokens))
    dz2_own = after(cotangent, tok_all).astype(half)
    dz2 = [jnp.concatenate(p, axis=0) for p in gather_ctx(dz2_own)]
    w_up = gather_f(after(up_own.astype(half), tok_all))
    normed1, _ = norm_parts(tok_all.astype(single))
    a1 = (normed1 * gain1 + shift1).astype(half)
    joined = (dot_nn(a1, w_qkv) + bias_qkv).astype(half)
    w_down = gather_f(after(down_own.astype(half), joined))
    attended = to_rows(attn_forward(joined, inv, slopes, heads, scale))
    mine = pieces_of(attended)
    mine = [mine[0]] + [swap(mine[j], j) for j in range(1, CTX)]
    ob = jnp.concatenate(xor_order(mine, c), axis=1)
    y1 = tokens.astype(single) + dot_nn(ob, w_out) + bias_o

    normed2, inv2 = norm_parts(y1)
    a2 = gather_ctx((normed2 * gain2 + shift2).astype(half))
    a2 = [jnp.concatenate(p, axis=0) for p in a2]
    gb, slope = zip(*[up_gelu(p, w_up, bias_u) for p in a2])
    dz2_all = jnp.concatenate(dz2, axis=0)
    down_grad = dot_tn(jnp.concatenate(gb, axis=0), dz2_all).astype(half)
    down_part = scatter_f(down_grad)
    w_down = after(w_down, down_grad)

    du, dh2, mix = [None] * CTX, [None] * CTX, [None] * CTX
    far = CTX - 1

    def hidden_grad(j, *others):
        grad = dot_nt(after(dz2[j], *others), w_down).astype(half)
        return (grad * slope[j].astype(single)).astype(half)

    du[far] = hidden_grad(far)
    dh2[far] = dot_nt(du[far], w_up).astype(half)
    first = scatter_first(dh2[far])
    last = dh2[far]
    for j in reversed(range(1, far)):
        du[j] = hidden_grad(j, last)
        last = du[j]
        if j == 1 and first is not None:
            du[j] = after(du[j], first)
        dh2[j] = last = dot_nt(du[j], w_up).astype(half)
    arrived = scatter_second(dh2, first)
    du[0] = hidden_grad(0, last)
    dh2[0] = dot_nt(du[0], w_up)
    up_grad = dot_tn(
        jnp.concatenate(a2, axis=0), jnp.concatenate(after(du, dh2[0]), axis=0)
    ).astype(half)
    up_part = scatter_f(after(up_grad, down_part))
    mix[far] = dot_nn(after(gb[far], up_grad), w_down).astype(half)
    dh2 = total_of(after(dh2[0], mix[far]), arrived)
    up_bias_grad = jnp.sum(jnp.concatenate(du, axis=0).astype(single), axis=0)
    down_bias_grad = jnp.sum(dz2_own.astype(single), axis=0)
    gain2_grad = jnp.sum(dh2 * normed2, axis=0)
    shift2_grad = jnp.sum(dh2, axis=0)
    dy1 = cotangent + norm_back(normed2, inv2, gain2, dh2)

    dz1 = dy1.astype(half)
    dattn = dot_nt(after(dz1, down_part), w_out).astype(half)
    dattn = xor_order([dattn[:, s * part : (s + 1) * part] for s in range(CTX)], c)
    out_bias_grad = jnp.sum(dz1.astype(single), axis=0)
    out_grad = dot_tn(ob, after(dz1, dattn)).astype(half)
    for j in range(1, far):
        mix[j] = dot_nn(after(gb[j], out_grad), w_down).astype(half)
    dattn = jnp.concatenate([dattn[0]] + [swap(dattn[j], j) for j in range(1, CTX)], axis=0)
    dqkv = attn_backward(joined, after(dattn, mix[1:far]), inv, slopes, heads, scale)
    down_out = gather_ctx(after(down_part, dattn))
    dqkv = to_rows(jnp.concatenate(dqkv, axis=1))
    dqkv_at = pieces_of(dqkv)
    dh1 = [None] * CTX
    for j in reversed(range(1, CTX)):
        dh1[j] = dot_nt(dqkv_at[j], w_qkv).astype(half)
    first = scatter_first(dh1[far])
    arrived = scatter_second(dh1, first)
    dh1[0] = dot_nt(after(dqkv_at[0], up_part, dh1[1:]), w_qkv)
    qkv_grad = dot_tn(a1, after(dqkv, dh1[0])).astype(half)
    mix[0] = dot_nn(after(gb[0], qkv_grad), w_down)
    dh1 = total_of(after(dh1[0], mix[0]), arrived)
    out_part = scatter_f(after(out_grad, up_part))
    qkv_part = scatter_f(after(qkv_grad, out_part, dh1))
    mix = after(mix, dh1)
    mixed = total_of(y1 + bias_d + mix[0], scatter_second(mix, scatter_first(mix[far])))
    down_out = lay_out(0, down_out, c, width // min(width, 512))
    up_out = lay_out(1, gather_ctx(after(up_part, dh1)), c, nf)
    sums = jnp.sum(dqkv.astype(single), axis=0)
    normed1_own, inv1_own = norm_parts(tokens.astype(single))
    gain1_grad = jnp.sum(dh1 * normed1_own, axis=0)
    shift1_grad = jnp.sum(dh1, axis=0)
    input_grad = dy1 + norm_back(normed1_own, inv1_own, gain1, dh1)

    bit = 1
    while bit < CTX:
        out_part = out_part.astype(half)
        out_part = out_part.astype(single) + swap(out_part, bit).astype(single)
        bit *= 2
    out_out = out_part
    qkv_out = lay_out(1, gather_ctx(qkv_part), c, 3)

    def spread(x, inner):
        x = x.reshape(-1, 1, inner)
        mask = (jnp.arange(CTX) == c)[None, :, None]
        return jnp.where(mask, x, 0.0).reshape(-1)

    early = [out_bias_grad, gain2_grad, shift2_grad, down_bias_grad, spread(up_bias_grad, fpart)]
    late = [gain1_grad, shift1_grad, spread(sums[:part], part), spread(sums[2 * part :], part)]

    def reduced(items, call):
        sizes = [x.shape[0] // nf for x in items]
        x = jnp.concatenate([x.reshape(nf, -1) for x in items], axis=1)
        x = jnp.pad(x, ((0, 0), (0, -x.shape[1] % 1024))).reshape(nf, -1, 128)
        x = reduce_small(x, nf, CTX, call).reshape(-1)
        out, at = [], 0
        for n in sizes:
            out.append(x[at : at + n])
            at += n
        return out

    out_bias_out, gain2_out, shift2_out, down_bias_out, up_bias_out = reduced(early, 2)
    gain1_out, shift1_out, q_bias_out, v_bias_out = reduced(late, 3)
    return (
        mixed,
        input_grad,
        gain1_out,
        shift1_out,
        qkv_out,
        q_bias_out,
        v_bias_out,
        out_out,
        out_bias_out,
        gain2_out,
        shift2_out,
        up_out,
        up_bias_out,
        down_out,
        down_bias_out,
    )


def solution(mesh):
    rows, flat = P(("ctx", "fsdp"), None), P("fsdp")
    mat = P("fsdp", None)
    in_specs = (
        rows,
        rows,
        mat,
        mat,
        flat,
        flat,
        mat,
        flat,
        flat,
        mat,
        flat,
        flat,
        flat,
        mat,
        flat,
        mat,
        flat,
    )
    out_specs = (
        rows,
        rows,
        flat,
        flat,
        mat,
        flat,
        flat,
        mat,
        flat,
        flat,
        flat,
        mat,
        flat,
        mat,
        flat,
    )
    return jax.shard_map(
        per_device, mesh=mesh, in_specs=in_specs, out_specs=out_specs, check_vma=False
    )
```

```python
import functools
import math

import jax
import jax.numpy as jnp
from jax import lax
from jax.experimental import pallas as pl
from jax.experimental.pallas import tpu as pltpu
from jax.sharding import PartitionSpec as P

HEADS = 16
SPAN = 128
SEQ_BLOCKS = 8

norm_eps = 1e-05
gelu_coef = 0.7978845608028654
LOG2E = 1.4426950408889634

half = jnp.bfloat16
single = jnp.float32


def dot_nn(a, b):
    return lax.dot_general(a, b, (((1,), (0,)), ((), ())), preferred_element_type=single)


def dot_nt(a, b):
    return lax.dot_general(a, b, (((1,), (1,)), ((), ())), preferred_element_type=single)


def dot_tn(a, b):
    return lax.dot_general(a, b, (((0,), (0,)), ((), ())), preferred_element_type=single)


def norm_parts(values):
    center = values - jnp.mean(values, axis=-1, keepdims=True)
    spread = jnp.mean(center * center, axis=-1, keepdims=True)
    inv = lax.rsqrt(spread + norm_eps)
    return center * inv, inv


def norm_back(normed, inv, gain, grad):
    dn = grad * gain
    return inv * (
        dn
        - jnp.mean(dn, axis=-1, keepdims=True)
        - normed * jnp.mean(dn * normed, axis=-1, keepdims=True)
    )


def gelu_both(v):
    t = jnp.tanh(gelu_coef * (v + 0.044715 * v * v * v))
    value = 0.5 * v * (1.0 + t)
    slope = 0.5 * (1.0 + t) + 0.5 * v * (1.0 - t * t) * gelu_coef * (1.0 + 3 * 0.044715 * v * v)
    return value, slope


def swap(x, mask):
    n = lax.axis_size("ctx")
    return lax.ppermute(x, "ctx", [(i, i ^ mask) for i in range(n)])


def gather_first(x):
    count = lax.axis_size("ctx")
    return [swap(x, j) for j in range(1, 3 if count == 4 else count)]


def gather_second(x, arrived):
    if lax.axis_size("ctx") != 4:
        return [[x]] + [[p] for p in arrived]
    one, two = arrived
    n = x.shape[0] // 2
    return [[x], [one], [two], [swap(one[:n], 2), swap(two[n:], 1)]]


def gather_ctx(x):
    return gather_second(x, gather_first(x))


def scatter_first(far):
    if lax.axis_size("ctx") != 4:
        return None
    return swap(far[0], 1), swap(far[1], 2)


def scatter_second(pieces, first):
    if first is None:
        return pieces[1:]
    p1, p2 = pieces[1], pieces[2]
    n = p1.shape[0] // 2
    from_x, from_y = first
    p1 = jnp.concatenate(
        [p1[:n], (p1[n:].astype(single) + from_y.astype(single)).astype(half)], axis=0
    )
    p2 = jnp.concatenate(
        [(p2[:n].astype(single) + from_x.astype(single)).astype(half), p2[n:]], axis=0
    )
    return [p1, p2]


def scatter_send(sent):
    return [swap(x, j + 1) for j, x in enumerate(sent)]


def total_of(own, arrived):
    for x in arrived:
        own = own + x.astype(single)
    return own


def xor_order(items, c):
    bit = 1
    while bit < len(items):
        on = (c & bit) == bit
        items = [jnp.where(on, items[i ^ bit], items[i]) for i in range(len(items))]
        bit *= 2
    return items


TILE = 256


def attn_scores(q_refs, k_refs, i, scale, slope):
    q = jnp.concatenate([q_refs[2 * i][...], q_refs[2 * i + 1][...]], axis=0)
    k = jnp.concatenate([r[...] for r in k_refs[: 2 * i + 2]], axis=0)
    n = TILE * (i + 1)
    col = lax.broadcasted_iota(jnp.int32, (1, n), 1) - (n - 1)
    s = dot_nt(q, k) * (scale * LOG2E) + (slope * LOG2E) * col.astype(single)
    row_at = lax.broadcasted_iota(jnp.int32, (TILE, TILE), 0)
    col_at = lax.broadcasted_iota(jnp.int32, (TILE, TILE), 1)
    last = jnp.where(col_at <= row_at, s[:, n - TILE :], -1e30)
    s = last if i == 0 else jnp.concatenate([s[:, : n - TILE], last], axis=1)
    e = jnp.exp2(s - jnp.max(s, axis=1, keepdims=True))
    return q, k, e, 1.0 / jnp.sum(e, axis=1, keepdims=True)


def attn_fwd_kernel(scale, inv_ref, slope_ref, *refs):
    q_refs, k_refs, v_refs = refs[:8], refs[8:16], refs[16:24]
    o_ref = refs[24]
    slope = slope_ref[pl.program_id(1)]
    for i in range(4):
        q, k, e, r = attn_scores(q_refs, k_refs, i, scale, slope)
        v = jnp.concatenate([x[...] for x in v_refs[: 2 * i + 2]], axis=0)
        o = dot_nn((e * r).astype(half), v)
        o_ref[TILE * i : TILE * (i + 1), :] = o.astype(half)


def attn_bwd_kernel(scale, inv_ref, slope_ref, *refs):
    q_refs, k_refs, v_refs, g_refs = refs[:8], refs[8:16], refs[16:24], refs[24:32]
    dq_ref, dk_ref, dv_ref, dk_acc, dv_acc = refs[32:]
    slope = slope_ref[pl.program_id(1)]
    for i in (3, 2, 1, 0):
        q, k, e, r = attn_scores(q_refs, k_refs, i, scale, slope)
        n = TILE * (i + 1)
        v = jnp.concatenate([x[...] for x in v_refs[: 2 * i + 2]], axis=0)
        g = jnp.concatenate([g_refs[2 * i][...], g_refs[2 * i + 1][...]], axis=0)
        p = e * r
        dp = dot_nt(g, v)
        delta = jnp.sum(p * dp, axis=1, keepdims=True)
        ds = (p * (dp - delta)).astype(half)
        pb = p.astype(half)
        dq_ref[TILE * i : TILE * (i + 1), :] = (dot_nn(ds, k) * scale).astype(half)
        dk = dot_tn(ds, q)
        dv = dot_tn(pb, g)
        if i == 3:
            dk_acc[...] = dk
            dv_acc[...] = dv
        else:
            dk_acc[:n, :] += dk
            dv_acc[:n, :] += dv
    dk_ref[...] = (dk_acc[...] * scale).astype(half)
    dv_ref[...] = dv_acc[...].astype(half)


def block_specs(offset):
    def one(j):
        return pl.BlockSpec(
            (SPAN, 128), lambda s, h, inv, slope: (inv[s * SEQ_BLOCKS + j], offset + h)
        )

    return [one(j) for j in range(SEQ_BLOCKS)]


def attn_forward(joined, inv, slopes, heads, scale):
    rows = joined.shape[0]
    specs = block_specs(0) + block_specs(heads) + block_specs(2 * heads)
    out = pl.BlockSpec((rows // 2, 128), lambda s, h, inv, slope: (s, h))
    return pl.pallas_call(
        functools.partial(attn_fwd_kernel, scale),
        grid_spec=pltpu.PrefetchScalarGridSpec(
            num_scalar_prefetch=2, grid=(2, heads), in_specs=specs, out_specs=out
        ),
        out_shape=jax.ShapeDtypeStruct((rows, heads * 128), half),
        compiler_params=pltpu.CompilerParams(vmem_limit_bytes=48 * 1024 * 1024),
        cost_estimate=hint(20 * 10**9, rows * heads * 128 * 8),
        name="attn_forward",
    )(inv, slopes, *([joined] * 24))


def attn_backward(joined, grad, inv, slopes, heads, scale):
    rows = joined.shape[0]
    specs = block_specs(0) + block_specs(heads) + block_specs(2 * heads) + block_specs(0)
    out = pl.BlockSpec((rows // 2, 128), lambda s, h, inv, slope: (s, h))
    shape = jax.ShapeDtypeStruct((rows, heads * 128), half)
    return pl.pallas_call(
        functools.partial(attn_bwd_kernel, scale),
        grid_spec=pltpu.PrefetchScalarGridSpec(
            num_scalar_prefetch=2,
            grid=(2, heads),
            in_specs=specs,
            out_specs=[out] * 3,
            scratch_shapes=[pltpu.VMEM((rows // 2, 128), single)] * 2,
        ),
        out_shape=[shape] * 3,
        compiler_params=pltpu.CompilerParams(vmem_limit_bytes=48 * 1024 * 1024),
        cost_estimate=hint(40 * 10**9, rows * heads * 128 * 14),
        name="attn_backward",
    )(inv, slopes, *([joined] * 24), *([grad] * 8))


HINT = 0.1


def block_of(x):
    return x if isinstance(x, tuple) else (x, x.shape[0], 0)


def hint(flops, bytes_accessed):
    return pl.CostEstimate(
        flops=int(HINT * flops), bytes_accessed=int(HINT * bytes_accessed), transcendentals=0
    )


def rows_kernel(dot, epilogue, count, extra, *refs):
    left, w_ref = refs[:count], refs[count]
    extras = refs[count + 1 : count + 1 + extra]
    outs = refs[count + 1 + extra :]
    for i in range(count):
        epilogue(i, dot(left[i][...], w_ref[...]), extras, outs)


def rows_matmul(blocks, w, transposed, extras, outs, epilogue, name, tile=512):
    blocks = [block_of(x) for x in blocks]
    extras = [block_of(x) for x in extras]
    n = w.shape[0] if transposed else w.shape[1]
    k = w.shape[1] if transposed else w.shape[0]
    t = math.gcd(n, tile)
    w_spec = (
        pl.BlockSpec((t, k), lambda i: (i, 0)) if transposed else pl.BlockSpec((k, t), lambda i: (0, i))
    )
    rows = sum(x[1] for x in blocks)
    return pl.pallas_call(
        functools.partial(
            rows_kernel, dot_nt if transposed else dot_nn, epilogue, len(blocks), len(extras)
        ),
        grid=(n // t,),
        in_specs=[pl.BlockSpec((x[1], k), lambda i, at=x[2]: (at, 0)) for x in blocks]
        + [w_spec]
        + [pl.BlockSpec((x[1], t), lambda i, at=x[2]: (at, i)) for x in extras],
        out_specs=[pl.BlockSpec((r, t), lambda i: (0, i)) for r, _ in outs],
        out_shape=[jax.ShapeDtypeStruct((r, n), d) for r, d in outs],
        compiler_params=pltpu.CompilerParams(vmem_limit_bytes=52 * 1024 * 1024),
        cost_estimate=hint(2 * rows * n * k, 2 * n * k + 4 * rows * (n + k)),
        name=name,
    )(*[x[0] for x in blocks], w, *[x[0] for x in extras])


def plain(blocks, w, transposed, dtype, name):
    def epilogue(i, x, extras, outs):
        outs[i][...] = x.astype(dtype)

    outs = [(block_of(x)[1], dtype) for x in blocks]
    return rows_matmul(blocks, w, transposed, [], outs, epilogue, name)


def joined_rows(blocks, w, bias, name):
    sizes = [block_of(x)[1] for x in blocks]

    def epilogue(i, x, extras, outs):
        at = sum(sizes[:i])
        outs[0][at : at + sizes[i], :] = (x + extras[0][...]).astype(half)

    bias = bias.reshape(1, -1)
    return rows_matmul(blocks, w, False, [bias], [(sum(sizes), half)], epilogue, name)[0]


def up_gelu(blocks, w, bias, name):
    count = len(blocks)

    def epilogue(i, x, extras, outs):
        value, slope = gelu_both(x + extras[0][...])
        outs[i][...] = value.astype(half)
        outs[count + i][...] = slope.astype(half)

    outs = [(block_of(x)[1], half) for x in blocks] * 2
    out = rows_matmul(blocks, w, False, [bias.reshape(1, -1)], outs, epilogue, name)
    return out[:count], out[count:]


def hidden_back(blocks, w, slopes, name):
    def epilogue(i, x, extras, outs):
        x = x.astype(half).astype(single) * extras[i][...].astype(single)
        outs[i][...] = x.astype(half)

    outs = [(block_of(x)[1], half) for x in blocks]
    return rows_matmul(blocks, w, True, slopes, outs, epilogue, name)


def outer_kernel(count, *refs):
    out = refs[-1]
    total = None
    for i in range(count):
        x = dot_tn(refs[i][...], refs[count + i][...])
        total = x if total is None else total + x
    out[...] = total.astype(half)


def outer(left, right, name):
    left = [block_of(x) for x in left]
    right = [block_of(x) for x in right]
    m, n = left[0][0].shape[1], right[0][0].shape[1]
    tm = math.gcd(m, 1024)
    tn = n // 2 if n % 256 == 0 and n > 1024 else n
    rows = sum(x[1] for x in left)
    return pl.pallas_call(
        functools.partial(outer_kernel, len(left)),
        grid=(m // tm, n // tn),
        in_specs=[pl.BlockSpec((x[1], tm), lambda i, j, at=x[2]: (at, i)) for x in left]
        + [pl.BlockSpec((x[1], tn), lambda i, j, at=x[2]: (at, j)) for x in right],
        out_specs=pl.BlockSpec((tm, tn), lambda i, j: (i, j)),
        out_shape=jax.ShapeDtypeStruct((m, n), half),
        compiler_params=pltpu.CompilerParams(vmem_limit_bytes=52 * 1024 * 1024),
        cost_estimate=hint(2 * rows * m * n, 2 * rows * (m + n) + 2 * m * n),
        name=name,
    )(*[x[0] for x in left], *[x[0] for x in right])


def lay_out_kernel(axis, layout, c_ref, *refs):
    out = refs[-1]
    for (j, row), ref in zip(layout, refs):
        x = ref[...].astype(single)
        r, w = x.shape
        if axis == 0:
            n = sum(ref.shape[0] for (k, _), ref in zip(layout, refs) if k == j)
            out[pl.ds(pl.multiple_of((c_ref[0] ^ j) * n + row, r), r), :] = x
        else:
            out[row : row + r, pl.ds(pl.multiple_of((c_ref[0] ^ j) * w, w), w)] = x


def lay_out(axis, pieces, c, groups):
    count = len(pieces)
    r = sum(x.shape[0] for x in pieces[0])
    n = pieces[0][0].shape[1]
    w = n // groups
    if w % 128:
        whole = xor_order([jnp.concatenate(p, axis=0).astype(single) for p in pieces], c)
        whole = jnp.stack([p.reshape(r, groups, w) for p in whole], axis=2)
        return whole.reshape(r, count * n)
    layout, blocks = [], []
    for j, p in enumerate(pieces):
        row = 0
        for x in p:
            layout.append((j, row))
            blocks.append(x)
            row += x.shape[0]
    out = (count * r, w) if axis == 0 else (r, count * w)
    return pl.pallas_call(
        functools.partial(lay_out_kernel, axis, layout),
        grid_spec=pltpu.PrefetchScalarGridSpec(
            num_scalar_prefetch=1,
            grid=(groups,),
            in_specs=[pl.BlockSpec((x.shape[0], w), lambda k, c: (0, k)) for x in blocks],
            out_specs=pl.BlockSpec(out, lambda k, c: (0, k)),
        ),
        out_shape=jax.ShapeDtypeStruct((out[0], out[1] * groups), single),
        compiler_params=pltpu.CompilerParams(vmem_limit_bytes=48 * 1024 * 1024),
        cost_estimate=hint(0, 6 * r * n * count),
        name="lay_out",
    )(c.reshape(1), *blocks)


def gather_small_kernel(nf, x_ref, o_ref, send_sem, recv_sem):
    f = lax.axis_index("fsdp")
    barrier = pltpu.get_barrier_semaphore()
    for d in range(1, nf):
        pl.semaphore_signal(
            barrier,
            inc=1,
            device_id={"fsdp": lax.rem(f + d, nf)},
            device_id_type=pl.DeviceIdType.MESH,
        )
    pl.semaphore_wait(barrier, nf - 1)
    copies = []
    for d in range(1, nf):
        copies.append(
            pltpu.make_async_remote_copy(
                src_ref=x_ref,
                dst_ref=o_ref.at[f],
                send_sem=send_sem.at[d],
                recv_sem=recv_sem.at[d],
                device_id={"fsdp": lax.rem(f + d, nf)},
                device_id_type=pl.DeviceIdType.MESH,
            )
        )
        copies[-1].start()
    o_ref[f] = x_ref[...]
    for copy in copies:
        copy.wait()


def gather_small(x, nf):
    return pl.pallas_call(
        functools.partial(gather_small_kernel, nf),
        out_shape=jax.ShapeDtypeStruct((nf,) + x.shape, single),
        in_specs=[pl.BlockSpec(memory_space=pltpu.VMEM)],
        out_specs=pl.BlockSpec(memory_space=pltpu.VMEM),
        scratch_shapes=[pltpu.SemaphoreType.DMA((nf,)), pltpu.SemaphoreType.DMA((nf,))],
        compiler_params=pltpu.CompilerParams(collective_id=1, has_side_effects=True),
        name="gather_small",
    )(x)


def reduce_small_kernel(nf, nc, x_ref, o_ref, land, stage, send_sem, recv_sem):
    f = lax.axis_index("fsdp")
    c = lax.axis_index("ctx")
    barrier = pltpu.get_barrier_semaphore()
    for d in range(1, nf):
        pl.semaphore_signal(
            barrier,
            inc=1,
            device_id={"fsdp": lax.rem(f + d, nf)},
            device_id_type=pl.DeviceIdType.MESH,
        )
    for d in range(1, nc):
        pl.semaphore_signal(
            barrier,
            inc=1,
            device_id={"ctx": lax.rem(c + d, nc)},
            device_id_type=pl.DeviceIdType.MESH,
        )
    pl.semaphore_wait(barrier, nf + nc - 2)
    copies = []
    for d in range(1, nf):
        to = lax.rem(f + d, nf)
        copies.append(
            pltpu.make_async_remote_copy(
                src_ref=x_ref.at[to],
                dst_ref=land.at[d],
                send_sem=send_sem.at[d],
                recv_sem=recv_sem.at[d],
                device_id={"fsdp": to},
                device_id_type=pl.DeviceIdType.MESH,
            )
        )
        copies[-1].start()
    total = x_ref[f]
    for d in range(1, nf):
        copies[d - 1].wait()
        total = total + land[d]
    stage[0] = total
    copies = []
    for d in range(1, nc):
        copies.append(
            pltpu.make_async_remote_copy(
                src_ref=stage.at[0],
                dst_ref=stage.at[d],
                send_sem=send_sem.at[nf + d],
                recv_sem=recv_sem.at[nf + d],
                device_id={"ctx": lax.rem(c + d, nc)},
                device_id_type=pl.DeviceIdType.MESH,
            )
        )
        copies[-1].start()
    for d in range(1, nc):
        copies[d - 1].wait()
        total = total + stage[d]
    o_ref[...] = total


def reduce_small(x, nf, nc, call):
    block = x.shape[1:]
    sems = pltpu.SemaphoreType.DMA((nf + nc,))
    return pl.pallas_call(
        functools.partial(reduce_small_kernel, nf, nc),
        out_shape=jax.ShapeDtypeStruct(block, single),
        in_specs=[pl.BlockSpec(memory_space=pltpu.VMEM)],
        out_specs=pl.BlockSpec(memory_space=pltpu.VMEM),
        scratch_shapes=[
            pltpu.VMEM((nf,) + block, single),
            pltpu.VMEM((nc,) + block, single),
            sems,
            sems,
        ],
        compiler_params=pltpu.CompilerParams(collective_id=call, has_side_effects=True),
        name="reduce_small",
    )(x)


def per_device(
    tokens,
    cotangent,
    lengths,
    span_place,
    ln1_gain,
    ln1_shift,
    qkv_weight,
    q_bias,
    v_bias,
    out_weight,
    out_bias,
    ln2_gain,
    ln2_shift,
    up_weight,
    up_bias,
    down_weight,
    down_bias,
):
    rows, width = tokens.shape
    CTX = lax.axis_size("ctx")
    c = lax.axis_index("ctx")
    f = lax.axis_index("fsdp")
    nf = lax.axis_size("fsdp")
    wide = up_weight.shape[1]
    part = width // CTX
    heads = HEADS // CTX
    scale = 1.0 / math.sqrt(width // HEADS)
    shard = width // nf
    fpart = wide // nf // CTX
    wpart = wide // CTX

    def columns(x, width_each, stride, count):
        return jnp.concatenate(
            [
                lax.dynamic_slice_in_dim(x, k * stride + c * width_each, width_each, axis=1)
                for k in range(count)
            ],
            axis=1,
        )

    def after(x, *others):
        return lax.optimization_barrier((x, others))[0]

    def pick(x, axis):
        return lax.dynamic_index_in_dim(x, c, axis, keepdims=False)

    def gather_f(x):
        return lax.all_gather(x, "fsdp", axis=0, tiled=True)

    qkv_own = columns(qkv_weight, part, width, 3)
    up_own = columns(up_weight, fpart, wide // nf, nf)
    down_own = lax.dynamic_slice_in_dim(down_weight, c * fpart, fpart, axis=0)
    w_qkv = gather_f(qkv_own.astype(half))
    small = jnp.concatenate(
        [ln1_gain, ln1_shift, q_bias, v_bias, out_bias, ln2_gain, ln2_shift, down_bias, up_bias]
    )
    small_len = small.shape[0]
    small = jnp.pad(small, (0, -small_len % 1024)).reshape(-1, 128)
    small_all = gather_small(small, nf).reshape(nf, -1)[:, :small_len]
    small_all = small_all.astype(half).astype(single)

    def vector(k):
        return small_all[:, k * shard : (k + 1) * shard].reshape(width)

    gain1, shift1, bias_q, bias_v, bias_o, gain2, shift2, bias_d = [vector(k) for k in range(8)]
    bias_u = pick(small_all[:, 8 * shard :].reshape(nf, CTX, fpart), 1).reshape(wpart)
    bias_qkv = jnp.concatenate(
        [pick(bias_q.reshape(CTX, part), 0), jnp.zeros((part,), single), pick(bias_v.reshape(CTX, part), 0)]
    )
    w_out = gather_f(out_weight.astype(half))

    per = rows // SPAN
    table = jnp.arange(CTX * per, dtype=jnp.int32)
    source = ((table // per) ^ c) * per + table % per
    place = jnp.sum(jnp.where(source[:, None] == table[None, :], span_place[0][None, :], 0), axis=1)
    inv = jnp.sum(jnp.where(place[None, :] == table[:, None], table[None, :], 0), axis=1)
    slopes = 2.0 ** (-8.0 * ((c * heads + jnp.arange(heads)).astype(single) + 1.0) / HEADS)

    def to_rows(x):
        return jnp.concatenate(
            [lax.dynamic_slice_in_dim(x, place[r] * SPAN, SPAN, axis=0) for r in range(CTX * per)]
        )

    def flat(pieces):
        return [x for p in pieces for x in p]

    def scatter_f(x):
        return lax.psum_scatter(x, "fsdp", scatter_dimension=0, tiled=True)

    far = CTX - 1
    mid = list(range(1, far))

    tok_near = gather_first(tokens)
    tok = flat(gather_second(tokens, after(tok_near, small_all)))
    dz2_own = after(cotangent, tok).astype(half)
    dz2_near = gather_first(dz2_own)
    w_up = gather_f(after(up_own.astype(half), tok))
    a1 = []
    for x in tok:
        normed, _ = norm_parts(x.astype(single))
        a1.append((normed * gain1 + shift1).astype(half))
    joined = joined_rows(a1, w_qkv, bias_qkv, "qkv")
    w_down = gather_f(after(down_own.astype(half), joined))
    attended = to_rows(attn_forward(joined, inv, slopes, heads, scale))
    mine = [attended[j * rows : (j + 1) * rows] for j in range(CTX)]
    mine = after(mine, dz2_near)
    mine = [mine[0]] + [swap(mine[j], j) for j in range(1, CTX)]
    ob = jnp.concatenate(xor_order(mine, c), axis=1)
    y1 = tokens.astype(single) + dot_nn(ob, w_out) + bias_o

    normed2, inv2 = norm_parts(y1)
    a2 = gather_ctx((normed2 * gain2 + shift2).astype(half))
    gb, slope = [None] * CTX, [None] * CTX
    last = ()
    for j in range(CTX):
        if j == far:
            dz2 = gather_second(dz2_own, after(dz2_near, a2[far], last))
        gb[j], slope[j] = up_gelu(after(a2[j], last), w_up, bias_u, f"up_gelu_{j}")
        last = gb[j]
    down_grad = outer(flat(gb), flat(dz2), "down_grad")
    down_part = scatter_f(down_grad)
    w_down = after(w_down, down_grad)

    du, dh2, mix = [None] * CTX, [None] * CTX, [None] * CTX
    du[far] = hidden_back(dz2[far], w_down, slope[far], "du_far")
    dh2[far] = plain(du[far], w_up, True, half, "dh2_far")
    first = scatter_first(dh2[far])
    mids = hidden_back(
        after([dz2[j][0] for j in mid], dh2[far]), w_down, [slope[j][0] for j in mid], "du_mid"
    )
    for j, x in zip(mid, mids):
        du[j] = [x]
    mids = plain(mids, w_up, True, half, "dh2_mid")
    for j, x in zip(mid, mids):
        dh2[j] = x
    if first is None:
        dh2[far] = dh2[far][0]
    sent = scatter_second(dh2, first)
    arrived = scatter_send(sent)
    du[0] = hidden_back(after(dz2[0], sent), w_down, slope[0], "du_own")
    dh2[0] = plain(du[0], w_up, True, single, "dh2_own")[0]
    up_grad = outer(flat(a2), after(flat(du), dh2[0]), "up_grad")
    up_part = scatter_f(after(up_grad, down_part))
    mix[far] = plain(after(gb[far], up_grad), w_down, False, half, "mix_far")
    dh2 = total_of(after(dh2[0], mix[far]), arrived)
    up_bias_grad = sum(jnp.sum(x.astype(single), axis=0) for x in flat(du))
    down_bias_grad = jnp.sum(dz2_own.astype(single), axis=0)
    gain2_grad = jnp.sum(dh2 * normed2, axis=0)
    shift2_grad = jnp.sum(dh2, axis=0)
    dy1 = cotangent + norm_back(normed2, inv2, gain2, dh2)

    dz1 = dy1.astype(half)
    dattn = dot_nt(after(dz1, down_part), w_out).astype(half)
    dattn = xor_order([dattn[:, s * part : (s + 1) * part] for s in range(CTX)], c)
    out_bias_grad = jnp.sum(dz1.astype(single), axis=0)
    out_grad = outer([ob], [after(dz1, dattn)], "out_grad")
    mids = plain(after([gb[j][0] for j in mid], out_grad), w_down, False, half, "mix_mid")
    for j, x in zip(mid, mids):
        mix[j] = x
    dattn = [dattn[0]] + after([swap(dattn[j], j) for j in range(1, CTX)], mids)
    dattn = jnp.concatenate(dattn, axis=0)
    dqkv = attn_backward(joined, dattn, inv, slopes, heads, scale)
    down_own = after(down_part, dattn)
    down_near = gather_first(down_own)
    dqkv = to_rows(jnp.concatenate(after(dqkv, down_near), axis=1))
    down_out = gather_second(down_own, down_near)
    dh1 = [None] * CTX
    if CTX == 4:
        dh1[far] = [(dqkv, rows // 2, 2 * far), (dqkv, rows // 2, 2 * far + 1)]
    else:
        dh1[far] = [(dqkv, rows, far)]
    dh1[far] = plain(dh1[far], w_qkv, True, half, "dh1_far")
    first = scatter_first(dh1[far])
    if first is None:
        dh1[far] = dh1[far][0]
    dqkv = after(dqkv, dh1[far])
    mids = plain([(dqkv, rows, j) for j in mid], w_qkv, True, half, "dh1_mid")
    for j, x in zip(mid, mids):
        dh1[j] = x
    dqkv = after(dqkv, up_part, down_out, mids)
    dh1[0] = plain([(dqkv, rows, 0)], w_qkv, True, single, "dh1_own")[0]
    mix[0] = plain(after(gb[0], dh1[0]), w_down, False, single, "mix_own")[0]
    if first is not None:
        first = after(first, mix[0])
    sent = scatter_second(dh1, first)
    arrived = scatter_send(sent)
    dqkv = after(dqkv, sent)
    a1_rows = [block_of(x)[1] for x in a1]
    qkv_grad = outer(
        a1,
        [(dqkv, r, sum(a1_rows[:i]) // r) for i, r in enumerate(a1_rows)],
        "qkv_grad",
    )
    dh1 = total_of(after(dh1[0], qkv_grad), arrived)
    out_part = scatter_f(after(out_grad, up_part))
    qkv_part = scatter_f(after(qkv_grad, out_part))
    mix = after(mix, dh1)
    first = scatter_first(mix[far])
    if first is None:
        mix[far] = mix[far][0]
    mixed = total_of(y1 + bias_d + mix[0], scatter_send(scatter_second(mix, first)))
    down_out = lay_out(0, down_out, c, width // min(width, 512))
    up_out = lay_out(1, gather_ctx(after(up_part, dh1)), c, nf)
    sums = jnp.sum(dqkv.astype(single), axis=0)
    normed1_own, inv1_own = norm_parts(tokens.astype(single))
    gain1_grad = jnp.sum(dh1 * normed1_own, axis=0)
    shift1_grad = jnp.sum(dh1, axis=0)
    input_grad = dy1 + norm_back(normed1_own, inv1_own, gain1, dh1)

    bit = 1
    while bit < CTX:
        out_part = out_part.astype(half)
        out_part = out_part.astype(single) + swap(out_part, bit).astype(single)
        bit *= 2
    out_out = out_part
    qkv_out = lay_out(1, gather_ctx(qkv_part), c, 3)

    def spread(x, inner):
        x = x.reshape(-1, 1, inner)
        mask = (jnp.arange(CTX) == c)[None, :, None]
        return jnp.where(mask, x, 0.0).reshape(-1)

    def reduced(items, call):
        sizes = [x.shape[0] // nf for x in items]
        x = jnp.concatenate([x.reshape(nf, -1) for x in items], axis=1)
        x = jnp.pad(x, ((0, 0), (0, -x.shape[1] % 1024))).reshape(nf, -1, 128)
        x = reduce_small(x, nf, CTX, call).reshape(-1)
        out, at = [], 0
        for n in sizes:
            out.append(x[at : at + n])
            at += n
        return out

    sums_in = [out_bias_grad, gain2_grad, shift2_grad, down_bias_grad, spread(up_bias_grad, fpart)]
    sums_in += [gain1_grad, shift1_grad, spread(sums[:part], part), spread(sums[2 * part :], part)]
    sums_in[5] = after(sums_in[5], mixed, up_out, down_out)
    sums_out = reduced(sums_in, 2)
    out_bias_out, gain2_out, shift2_out, down_bias_out, up_bias_out = sums_out[:5]
    gain1_out, shift1_out, q_bias_out, v_bias_out = sums_out[5:]
    return (
        mixed,
        input_grad,
        gain1_out,
        shift1_out,
        qkv_out,
        q_bias_out,
        v_bias_out,
        out_out,
        out_bias_out,
        gain2_out,
        shift2_out,
        up_out,
        up_bias_out,
        down_out,
        down_bias_out,
    )


def solution(mesh):
    rows, flat = P(("ctx", "fsdp"), None), P("fsdp")
    mat = P("fsdp", None)
    in_specs = (
        rows,
        rows,
        mat,
        mat,
        flat,
        flat,
        mat,
        flat,
        flat,
        mat,
        flat,
        flat,
        flat,
        mat,
        flat,
        mat,
        flat,
    )
    out_specs = (
        rows,
        rows,
        flat,
        flat,
        mat,
        flat,
        flat,
        mat,
        flat,
        flat,
        flat,
        mat,
        flat,
        mat,
        flat,
    )
    return jax.shard_map(
        per_device, mesh=mesh, in_specs=in_specs, out_specs=out_specs, check_vma=False
    )
```

```python
import functools
import math

import jax
import jax.numpy as jnp
from jax import lax
from jax.experimental import pallas as pl
from jax.experimental.pallas import tpu as pltpu
from jax.sharding import PartitionSpec as P

HEADS = 16
SPAN = 128
SEQ_BLOCKS = 8

norm_eps = 1e-05
gelu_coef = 0.7978845608028654
LOG2E = 1.4426950408889634

half = jnp.bfloat16
single = jnp.float32


def dot_nn(a, b):
    return lax.dot_general(a, b, (((1,), (0,)), ((), ())), preferred_element_type=single)


def dot_nt(a, b):
    return lax.dot_general(a, b, (((1,), (1,)), ((), ())), preferred_element_type=single)


def dot_tn(a, b):
    return lax.dot_general(a, b, (((0,), (0,)), ((), ())), preferred_element_type=single)


def norm_parts(values):
    center = values - jnp.mean(values, axis=-1, keepdims=True)
    spread = jnp.mean(center * center, axis=-1, keepdims=True)
    inv = lax.rsqrt(spread + norm_eps)
    return center * inv, inv


def norm_back(normed, inv, gain, grad):
    dn = grad * gain
    return inv * (
        dn
        - jnp.mean(dn, axis=-1, keepdims=True)
        - normed * jnp.mean(dn * normed, axis=-1, keepdims=True)
    )


def gelu_both(v):
    t = jnp.tanh(gelu_coef * (v + 0.044715 * v * v * v))
    value = 0.5 * v * (1.0 + t)
    slope = 0.5 * (1.0 + t) + 0.5 * v * (1.0 - t * t) * gelu_coef * (1.0 + 3 * 0.044715 * v * v)
    return value, slope


def swap(x, mask):
    n = lax.axis_size("ctx")
    return lax.ppermute(x, "ctx", [(i, i ^ mask) for i in range(n)])


def gather_first(x):
    count = lax.axis_size("ctx")
    return [swap(x, j) for j in range(1, 3 if count == 4 else count)]


def gather_second(x, arrived):
    if lax.axis_size("ctx") != 4:
        return [[x]] + [[p] for p in arrived]
    one, two = arrived
    n = x.shape[0] // 2
    return [[x], [one], [two], [swap(one[:n], 2), swap(two[n:], 1)]]


def gather_ctx(x):
    return gather_second(x, gather_first(x))


def scatter_first(far):
    if lax.axis_size("ctx") != 4:
        return None
    return swap(far[0], 1), swap(far[1], 2)


def scatter_second(pieces, first):
    if first is None:
        return pieces[1:]
    p1, p2 = pieces[1], pieces[2]
    n = p1.shape[0] // 2
    from_x, from_y = first
    p1 = jnp.concatenate(
        [p1[:n], (p1[n:].astype(single) + from_y.astype(single)).astype(half)], axis=0
    )
    p2 = jnp.concatenate(
        [(p2[:n].astype(single) + from_x.astype(single)).astype(half), p2[n:]], axis=0
    )
    return [p1, p2]


def scatter_send(sent):
    return [swap(x, j + 1) for j, x in enumerate(sent)]


def total_of(own, arrived):
    for x in arrived:
        own = own + x.astype(single)
    return own


def xor_order(items, c):
    bit = 1
    while bit < len(items):
        on = (c & bit) == bit
        items = [jnp.where(on, items[i ^ bit], items[i]) for i in range(len(items))]
        bit *= 2
    return items


TILE = 256


def attn_scores(q_refs, k_refs, i, scale, slope):
    q = jnp.concatenate([q_refs[2 * i][...], q_refs[2 * i + 1][...]], axis=0)
    k = jnp.concatenate([r[...] for r in k_refs[: 2 * i + 2]], axis=0)
    n = TILE * (i + 1)
    col = lax.broadcasted_iota(jnp.int32, (1, n), 1) - (n - 1)
    s = dot_nt(q, k) * (scale * LOG2E) + (slope * LOG2E) * col.astype(single)
    row_at = lax.broadcasted_iota(jnp.int32, (TILE, TILE), 0)
    col_at = lax.broadcasted_iota(jnp.int32, (TILE, TILE), 1)
    last = jnp.where(col_at <= row_at, s[:, n - TILE :], -1e30)
    s = last if i == 0 else jnp.concatenate([s[:, : n - TILE], last], axis=1)
    e = jnp.exp2(s - jnp.max(s, axis=1, keepdims=True))
    return q, k, e, 1.0 / jnp.sum(e, axis=1, keepdims=True)


def attn_fwd_kernel(scale, inv_ref, slope_ref, *refs):
    q_refs, k_refs, v_refs = refs[:8], refs[8:16], refs[16:24]
    o_ref = refs[24]
    slope = slope_ref[pl.program_id(1)]
    for i in range(4):
        q, k, e, r = attn_scores(q_refs, k_refs, i, scale, slope)
        v = jnp.concatenate([x[...] for x in v_refs[: 2 * i + 2]], axis=0)
        o = dot_nn((e * r).astype(half), v)
        o_ref[TILE * i : TILE * (i + 1), :] = o.astype(half)


def attn_bwd_kernel(scale, inv_ref, slope_ref, *refs):
    q_refs, k_refs, v_refs, g_refs = refs[:8], refs[8:16], refs[16:24], refs[24:32]
    dq_ref, dk_ref, dv_ref, dk_acc, dv_acc = refs[32:]
    slope = slope_ref[pl.program_id(1)]
    for i in (3, 2, 1, 0):
        q, k, e, r = attn_scores(q_refs, k_refs, i, scale, slope)
        n = TILE * (i + 1)
        v = jnp.concatenate([x[...] for x in v_refs[: 2 * i + 2]], axis=0)
        g = jnp.concatenate([g_refs[2 * i][...], g_refs[2 * i + 1][...]], axis=0)
        p = e * r
        dp = dot_nt(g, v)
        delta = jnp.sum(p * dp, axis=1, keepdims=True)
        ds = (p * (dp - delta)).astype(half)
        pb = p.astype(half)
        dq_ref[TILE * i : TILE * (i + 1), :] = (dot_nn(ds, k) * scale).astype(half)
        dk = dot_tn(ds, q)
        dv = dot_tn(pb, g)
        if i == 3:
            dk_acc[...] = dk
            dv_acc[...] = dv
        else:
            dk_acc[:n, :] += dk
            dv_acc[:n, :] += dv
    dk_ref[...] = (dk_acc[...] * scale).astype(half)
    dv_ref[...] = dv_acc[...].astype(half)


def block_specs(offset):
    def one(j):
        return pl.BlockSpec(
            (SPAN, 128), lambda s, h, inv, slope: (inv[s * SEQ_BLOCKS + j], offset + h)
        )

    return [one(j) for j in range(SEQ_BLOCKS)]


def attn_forward(joined, inv, slopes, heads, scale):
    rows = joined.shape[0]
    specs = block_specs(0) + block_specs(heads) + block_specs(2 * heads)
    out = pl.BlockSpec((rows // 2, 128), lambda s, h, inv, slope: (s, h))
    return pl.pallas_call(
        functools.partial(attn_fwd_kernel, scale),
        grid_spec=pltpu.PrefetchScalarGridSpec(
            num_scalar_prefetch=2, grid=(2, heads), in_specs=specs, out_specs=out
        ),
        out_shape=jax.ShapeDtypeStruct((rows, heads * 128), half),
        compiler_params=pltpu.CompilerParams(vmem_limit_bytes=48 * 1024 * 1024),
        cost_estimate=hint(20 * 10**9, rows * heads * 128 * 8),
        name="attn_forward",
    )(inv, slopes, *([joined] * 24))


def attn_backward(joined, grad, inv, slopes, heads, scale):
    rows = joined.shape[0]
    specs = block_specs(0) + block_specs(heads) + block_specs(2 * heads) + block_specs(0)
    out = pl.BlockSpec((rows // 2, 128), lambda s, h, inv, slope: (s, h))
    shape = jax.ShapeDtypeStruct((rows, heads * 128), half)
    return pl.pallas_call(
        functools.partial(attn_bwd_kernel, scale),
        grid_spec=pltpu.PrefetchScalarGridSpec(
            num_scalar_prefetch=2,
            grid=(2, heads),
            in_specs=specs,
            out_specs=[out] * 3,
            scratch_shapes=[pltpu.VMEM((rows // 2, 128), single)] * 2,
        ),
        out_shape=[shape] * 3,
        compiler_params=pltpu.CompilerParams(vmem_limit_bytes=48 * 1024 * 1024),
        cost_estimate=hint(40 * 10**9, rows * heads * 128 * 14),
        name="attn_backward",
    )(inv, slopes, *([joined] * 24), *([grad] * 8))


HINT = 0.001


def block_of(x):
    return x if isinstance(x, tuple) else (x, x.shape[0], 0)


def hint(flops, bytes_accessed):
    return pl.CostEstimate(
        flops=int(HINT * flops), bytes_accessed=int(HINT * bytes_accessed), transcendentals=0
    )


def rows_kernel(dot, epilogue, count, extra, *refs):
    left, w_ref = refs[:count], refs[count]
    extras = refs[count + 1 : count + 1 + extra]
    outs = refs[count + 1 + extra :]
    for i in range(count):
        epilogue(i, dot(left[i][...], w_ref[...]), extras, outs)


def rows_matmul(blocks, w, transposed, extras, outs, epilogue, name, tile=512):
    blocks = [block_of(x) for x in blocks]
    extras = [block_of(x) for x in extras]
    n = w.shape[0] if transposed else w.shape[1]
    k = w.shape[1] if transposed else w.shape[0]
    t = math.gcd(n, tile)
    w_spec = (
        pl.BlockSpec((t, k), lambda i: (i, 0)) if transposed else pl.BlockSpec((k, t), lambda i: (0, i))
    )
    rows = sum(x[1] for x in blocks)
    return pl.pallas_call(
        functools.partial(
            rows_kernel, dot_nt if transposed else dot_nn, epilogue, len(blocks), len(extras)
        ),
        grid=(n // t,),
        in_specs=[pl.BlockSpec((x[1], k), lambda i, at=x[2]: (at, 0)) for x in blocks]
        + [w_spec]
        + [pl.BlockSpec((x[1], t), lambda i, at=x[2]: (at, i)) for x in extras],
        out_specs=[pl.BlockSpec((r, t), lambda i: (0, i)) for r, _ in outs],
        out_shape=[jax.ShapeDtypeStruct((r, n), d) for r, d in outs],
        compiler_params=pltpu.CompilerParams(vmem_limit_bytes=52 * 1024 * 1024),
        cost_estimate=hint(2 * rows * n * k, 2 * n * k + 4 * rows * (n + k)),
        name=name,
    )(*[x[0] for x in blocks], w, *[x[0] for x in extras])


def plain(blocks, w, transposed, dtype, name):
    def epilogue(i, x, extras, outs):
        outs[i][...] = x.astype(dtype)

    outs = [(block_of(x)[1], dtype) for x in blocks]
    return rows_matmul(blocks, w, transposed, [], outs, epilogue, name)


def joined_rows(blocks, w, bias, name):
    sizes = [block_of(x)[1] for x in blocks]

    def epilogue(i, x, extras, outs):
        at = sum(sizes[:i])
        outs[0][at : at + sizes[i], :] = (x + extras[0][...]).astype(half)

    bias = bias.reshape(1, -1)
    return rows_matmul(blocks, w, False, [bias], [(sum(sizes), half)], epilogue, name)[0]


def up_gelu(blocks, w, bias, name):
    count = len(blocks)

    def epilogue(i, x, extras, outs):
        value, slope = gelu_both(x + extras[0][...])
        outs[i][...] = value.astype(half)
        outs[count + i][...] = slope.astype(half)

    outs = [(block_of(x)[1], half) for x in blocks] * 2
    out = rows_matmul(blocks, w, False, [bias.reshape(1, -1)], outs, epilogue, name)
    return out[:count], out[count:]


def hidden_back(blocks, w, slopes, name):
    def epilogue(i, x, extras, outs):
        x = x.astype(half).astype(single) * extras[i][...].astype(single)
        outs[i][...] = x.astype(half)

    outs = [(block_of(x)[1], half) for x in blocks]
    return rows_matmul(blocks, w, True, slopes, outs, epilogue, name)


def outer_kernel(count, *refs):
    out = refs[-1]
    total = None
    for i in range(count):
        x = dot_tn(refs[i][...], refs[count + i][...])
        total = x if total is None else total + x
    out[...] = total.astype(half)


def outer(left, right, name):
    left = [block_of(x) for x in left]
    right = [block_of(x) for x in right]
    m, n = left[0][0].shape[1], right[0][0].shape[1]
    tm = math.gcd(m, 1024)
    tn = n // 2 if n % 256 == 0 and n > 1024 else n
    rows = sum(x[1] for x in left)
    return pl.pallas_call(
        functools.partial(outer_kernel, len(left)),
        grid=(m // tm, n // tn),
        in_specs=[pl.BlockSpec((x[1], tm), lambda i, j, at=x[2]: (at, i)) for x in left]
        + [pl.BlockSpec((x[1], tn), lambda i, j, at=x[2]: (at, j)) for x in right],
        out_specs=pl.BlockSpec((tm, tn), lambda i, j: (i, j)),
        out_shape=jax.ShapeDtypeStruct((m, n), half),
        compiler_params=pltpu.CompilerParams(vmem_limit_bytes=52 * 1024 * 1024),
        cost_estimate=hint(2 * rows * m * n, 2 * rows * (m + n) + 2 * m * n),
        name=name,
    )(*[x[0] for x in left], *[x[0] for x in right])


def partner(mask):
    c = lax.axis_index("ctx")
    if mask == 1:
        return c + 1 - 2 * lax.rem(c, 2)
    return lax.rem(c + 2, 4) if mask == 2 else 3 - c


def greet(masks):
    barrier = pltpu.get_barrier_semaphore()
    for mask in masks:
        pl.semaphore_signal(
            barrier,
            inc=1,
            device_id={"ctx": partner(mask)},
            device_id_type=pl.DeviceIdType.MESH,
        )
    pl.semaphore_wait(barrier, len(masks))


class Moves:
    def __init__(self, send_sem, recv_sem):
        self.send_sem, self.recv_sem, self.used = send_sem, recv_sem, 0

    def start(self, src, dst, mask):
        copy = pltpu.make_async_remote_copy(
            src_ref=src,
            dst_ref=dst,
            send_sem=self.send_sem.at[self.used],
            recv_sem=self.recv_sem.at[self.used],
            device_id={"ctx": partner(mask)},
            device_id_type=pl.DeviceIdType.MESH,
        )
        self.used += 1
        copy.start()
        return copy


def multiply(lefts, w, transposed, extras, outs, epilogue, tile=512):
    k = lefts[0].shape[1]
    n = w.shape[0] if transposed else w.shape[1]
    t = math.gcd(n, tile)
    w_spec = (
        pl.BlockSpec((t, k), lambda i: (i, 0)) if transposed else pl.BlockSpec((k, t), lambda i: (0, i))
    )
    dot = dot_nt if transposed else dot_nn

    def body(*refs):
        rows_kernel(dot, epilogue, len(lefts), len(extras), *refs)

    pltpu.emit_pipeline(
        body,
        grid=(n // t,),
        in_specs=[pl.BlockSpec((x.shape[0], k), lambda i: (0, 0)) for x in lefts]
        + [w_spec]
        + [pl.BlockSpec((x.shape[0], t), lambda i: (0, i)) for x in extras],
        out_specs=[pl.BlockSpec((x.shape[0], t), lambda i: (0, i)) for x in outs],
    )(*lefts, w, *extras, *outs)


def store(i, x, extras, outs):
    outs[i][...] = x.astype(outs[i].dtype)


def store_sum(i, x, extras, outs):
    outs[i][...] = (x + extras[i][...].astype(single)).astype(outs[i].dtype)


def store_hidden(i, x, extras, outs):
    outs[i][...] = (x.astype(half).astype(single) * extras[i][...].astype(single)).astype(half)


def outer_on(lefts, rights, out):
    m, n = out.shape
    tm = math.gcd(m, 1024)
    tn = n // 2 if n % 256 == 0 and n > 1024 else n

    def body(*refs):
        outer_kernel(len(lefts), *refs)

    pltpu.emit_pipeline(
        body,
        grid=(m // tm, n // tn),
        in_specs=[pl.BlockSpec((x.shape[0], tm), lambda i, j: (0, i)) for x in lefts]
        + [pl.BlockSpec((x.shape[0], tn), lambda i, j: (0, j)) for x in rights],
        out_specs=[pl.BlockSpec((tm, tn), lambda i, j: (i, j))],
    )(*lefts, *rights, out)


def halves(ref):
    n = ref.shape[0] // 2
    return ref.at[pl.ds(0, n)], ref.at[pl.ds(n, n)]


def moving_call(kernel, operands, outs, moves, call, flops, name):
    anywhere = pl.BlockSpec(memory_space=pl.ANY)
    sems = pltpu.SemaphoreType.DMA((moves,))
    return pl.pallas_call(
        kernel,
        in_specs=[anywhere] * len(operands),
        out_specs=[anywhere] * len(outs),
        out_shape=[jax.ShapeDtypeStruct(shape, dtype) for shape, dtype in outs],
        scratch_shapes=[sems, sems],
        compiler_params=pltpu.CompilerParams(
            collective_id=call, has_side_effects=True, vmem_limit_bytes=52 * 1024 * 1024
        ),
        cost_estimate=hint(flops, 0),
        name=name,
    )(*operands)


def feed_back_kernel(*refs):
    dz, slope, a2, gb_far = refs[0:5], refs[5:10], refs[10:15], refs[15:17]
    w_down, w_up = refs[17:19]
    du, own, p3, p1, p2 = refs[19:24], refs[24], refs[25:27], refs[27], refs[28]
    from_x, from_y, land1, land2, up_grad = refs[29:34]
    mix_far = refs[34:36]
    moves = Moves(*refs[36:38])
    greet((1, 2))
    multiply(dz[3:5], w_down, True, slope[3:5], du[3:5], store_hidden)
    multiply(du[3:5], w_up, True, [], p3, store)
    first = [moves.start(p3[0], from_x, 1), moves.start(p3[1], from_y, 2)]
    multiply(dz[1:3], w_down, True, slope[1:3], du[1:3], store_hidden)
    (p1_lo, p1_hi), (p2_lo, p2_hi) = halves(p1), halves(p2)
    (du1_lo, du1_hi), (du2_lo, du2_hi) = halves(du[1]), halves(du[2])
    (land1_lo, land1_hi), (land2_lo, land2_hi) = halves(land1), halves(land2)
    multiply([du1_lo, du2_hi], w_up, True, [], [p1_lo, p2_hi], store)
    second = [moves.start(p1_lo, land1_lo, 1), moves.start(p2_hi, land2_hi, 2)]
    for copy in first:
        copy.wait()
    multiply([du1_hi, du2_lo], w_up, True, [from_y, from_x], [p1_hi, p2_lo], store_sum)
    second += [moves.start(p1_hi, land1_hi, 1), moves.start(p2_lo, land2_lo, 2)]
    multiply(dz[0:1], w_down, True, slope[0:1], du[0:1], store_hidden)
    multiply(du[0:1], w_up, True, [], [own], store)
    outer_on(a2, du, up_grad)
    multiply(gb_far, w_down, False, [], mix_far, store)
    for copy in second:
        copy.wait()


def feed_back(dz, slope, a2, gb_far, w_down, w_up):
    rows, width = dz[0].shape
    wide = w_down.shape[0]
    n = rows // 2
    sizes = [rows, rows, rows, n, n]
    outs = [((r, wide), half) for r in sizes]
    outs += [((rows, width), single)]
    outs += [((n, width), half)] * 2 + [((rows, width), half)] * 2
    outs += [((n, width), half)] * 2 + [((rows, width), half)] * 2
    outs += [((width, wide), half)] + [((n, width), half)] * 2
    out = moving_call(
        feed_back_kernel,
        [*dz, *slope, *a2, *gb_far, w_down, w_up],
        outs,
        6,
        3,
        26 * rows * width * wide,
        "feed_back",
    )
    du, own, land, up_grad, mix_far = out[0:5], out[5], out[12:14], out[14], out[15:17]
    return du, own, land, up_grad, mix_far


def heads_back_kernel(part, *refs):
    dattn, ob, dz1, gb1, gb2, w_down = refs[0:6]
    got, out_grad, mix1, mix2 = refs[6:10]
    moves = Moves(*refs[10:12])
    local = refs[12]
    rows = dattn.shape[0]
    c = lax.axis_index("ctx")

    def columns(of):
        return dattn.at[:, pl.ds(pl.multiple_of(of * part, part), part)]

    greet((1, 2, 3))
    copies = []
    for mask in (3, 1, 2):
        at = got.at[pl.ds(mask * rows, rows)]
        copies.append(moves.start(columns(partner(mask)), at, mask))
    own = pltpu.make_async_copy(columns(c), got.at[pl.ds(0, rows)], local)
    own.start()
    outer_on([ob], [dz1], out_grad)
    multiply([gb1, gb2], w_down, False, [], [mix1, mix2], store)
    own.wait()
    for copy in copies:
        copy.wait()


def heads_back(dattn, ob, dz1, gb1, gb2, w_down, part):
    rows, width = dattn.shape
    anywhere = pl.BlockSpec(memory_space=pl.ANY)
    sems = pltpu.SemaphoreType.DMA((3,))
    outs = [((4 * rows, part), half), ((width, width), half)] + [((rows, width), half)] * 2
    return pl.pallas_call(
        functools.partial(heads_back_kernel, part),
        in_specs=[anywhere] * 6,
        out_specs=[anywhere] * 4,
        out_shape=[jax.ShapeDtypeStruct(shape, dtype) for shape, dtype in outs],
        scratch_shapes=[sems, sems, pltpu.SemaphoreType.DMA],
        compiler_params=pltpu.CompilerParams(
            collective_id=4, has_side_effects=True, vmem_limit_bytes=52 * 1024 * 1024
        ),
        cost_estimate=hint(10 * rows * width * width, 0),
        name="heads_back",
    )(dattn, ob, dz1, gb1, gb2, w_down)


def qkv_back_kernel(*refs):
    dqkv, w_qkv = refs[0:2]
    a1, gb_own, w_down = refs[2:7], refs[7], refs[8]
    own, p3, p1, p2, from_x, from_y, land1, land2, qkv_grad, mix_own = refs[9:19]
    moves = Moves(*refs[19:21])
    rows = own.shape[0]
    n = rows // 2

    def block(k):
        return dqkv.at[pl.ds(k * n, n)]

    greet((1, 2))
    (p3_lo, p3_hi), (p1_lo, p1_hi), (p2_lo, p2_hi) = halves(p3), halves(p1), halves(p2)
    (land1_lo, land1_hi), (land2_lo, land2_hi) = halves(land1), halves(land2)
    multiply([block(6), block(7)], w_qkv, True, [], [p3_lo, p3_hi], store)
    first = [moves.start(p3_lo, from_x, 1), moves.start(p3_hi, from_y, 2)]
    multiply([block(2), block(5)], w_qkv, True, [], [p1_lo, p2_hi], store)
    second = [moves.start(p1_lo, land1_lo, 1), moves.start(p2_hi, land2_hi, 2)]
    multiply([dqkv.at[pl.ds(0, rows)]], w_qkv, True, [], [own], store)
    multiply([gb_own], w_down, False, [], [mix_own], store)
    for copy in first:
        copy.wait()
    multiply([block(3), block(4)], w_qkv, True, [from_y, from_x], [p1_hi, p2_lo], store_sum)
    second += [moves.start(p1_hi, land1_hi, 1), moves.start(p2_lo, land2_lo, 2)]
    rights, at = [], 0
    for x in a1:
        rights.append(dqkv.at[pl.ds(at, x.shape[0])])
        at += x.shape[0]
    outer_on(a1, rights, qkv_grad)
    for copy in second:
        copy.wait()


def qkv_back(dqkv, w_qkv, a1, gb_own, w_down):
    rows, width = a1[0].shape
    wide = gb_own.shape[1]
    n = rows // 2
    outs = [((rows, width), single)] + [((rows, width), half)] * 3
    outs += [((n, width), half)] * 2 + [((rows, width), half)] * 2
    outs += [((width, dqkv.shape[1]), half), ((rows, width), single)]
    out = moving_call(
        qkv_back_kernel,
        [dqkv, w_qkv, *a1, gb_own, w_down],
        outs,
        6,
        5,
        16 * rows * width * dqkv.shape[1] + 2 * rows * width * wide,
        "qkv_back",
    )
    return out[0], out[6:8], out[8], out[9]


def lay_out_kernel(axis, layout, c_ref, *refs):
    out = refs[-1]
    for (j, row), ref in zip(layout, refs):
        x = ref[...].astype(single)
        r, w = x.shape
        if axis == 0:
            n = sum(ref.shape[0] for (k, _), ref in zip(layout, refs) if k == j)
            out[pl.ds(pl.multiple_of((c_ref[0] ^ j) * n + row, r), r), :] = x
        else:
            out[row : row + r, pl.ds(pl.multiple_of((c_ref[0] ^ j) * w, w), w)] = x


def lay_out(axis, pieces, c, groups):
    count = len(pieces)
    r = sum(x.shape[0] for x in pieces[0])
    n = pieces[0][0].shape[1]
    w = n // groups
    if w % 128:
        whole = xor_order([jnp.concatenate(p, axis=0).astype(single) for p in pieces], c)
        whole = jnp.stack([p.reshape(r, groups, w) for p in whole], axis=2)
        return whole.reshape(r, count * n)
    layout, blocks = [], []
    for j, p in enumerate(pieces):
        row = 0
        for x in p:
            layout.append((j, row))
            blocks.append(x)
            row += x.shape[0]
    out = (count * r, w) if axis == 0 else (r, count * w)
    return pl.pallas_call(
        functools.partial(lay_out_kernel, axis, layout),
        grid_spec=pltpu.PrefetchScalarGridSpec(
            num_scalar_prefetch=1,
            grid=(groups,),
            in_specs=[pl.BlockSpec((x.shape[0], w), lambda k, c: (0, k)) for x in blocks],
            out_specs=pl.BlockSpec(out, lambda k, c: (0, k)),
        ),
        out_shape=jax.ShapeDtypeStruct((out[0], out[1] * groups), single),
        compiler_params=pltpu.CompilerParams(vmem_limit_bytes=48 * 1024 * 1024),
        cost_estimate=hint(0, 6 * r * n * count),
        name="lay_out",
    )(c.reshape(1), *blocks)


def gather_small_kernel(nf, x_ref, o_ref, send_sem, recv_sem):
    f = lax.axis_index("fsdp")
    barrier = pltpu.get_barrier_semaphore()
    for d in range(1, nf):
        pl.semaphore_signal(
            barrier,
            inc=1,
            device_id={"fsdp": lax.rem(f + d, nf)},
            device_id_type=pl.DeviceIdType.MESH,
        )
    pl.semaphore_wait(barrier, nf - 1)
    copies = []
    for d in range(1, nf):
        copies.append(
            pltpu.make_async_remote_copy(
                src_ref=x_ref,
                dst_ref=o_ref.at[f],
                send_sem=send_sem.at[d],
                recv_sem=recv_sem.at[d],
                device_id={"fsdp": lax.rem(f + d, nf)},
                device_id_type=pl.DeviceIdType.MESH,
            )
        )
        copies[-1].start()
    o_ref[f] = x_ref[...]
    for copy in copies:
        copy.wait()


def gather_small(x, nf):
    return pl.pallas_call(
        functools.partial(gather_small_kernel, nf),
        out_shape=jax.ShapeDtypeStruct((nf,) + x.shape, single),
        in_specs=[pl.BlockSpec(memory_space=pltpu.VMEM)],
        out_specs=pl.BlockSpec(memory_space=pltpu.VMEM),
        scratch_shapes=[pltpu.SemaphoreType.DMA((nf,)), pltpu.SemaphoreType.DMA((nf,))],
        compiler_params=pltpu.CompilerParams(collective_id=1, has_side_effects=True),
        name="gather_small",
    )(x)


def reduce_small_kernel(nf, nc, x_ref, o_ref, land, stage, send_sem, recv_sem):
    f = lax.axis_index("fsdp")
    c = lax.axis_index("ctx")
    barrier = pltpu.get_barrier_semaphore()
    for d in range(1, nf):
        pl.semaphore_signal(
            barrier,
            inc=1,
            device_id={"fsdp": lax.rem(f + d, nf)},
            device_id_type=pl.DeviceIdType.MESH,
        )
    for d in range(1, nc):
        pl.semaphore_signal(
            barrier,
            inc=1,
            device_id={"ctx": lax.rem(c + d, nc)},
            device_id_type=pl.DeviceIdType.MESH,
        )
    pl.semaphore_wait(barrier, nf + nc - 2)
    copies = []
    for d in range(1, nf):
        to = lax.rem(f + d, nf)
        copies.append(
            pltpu.make_async_remote_copy(
                src_ref=x_ref.at[to],
                dst_ref=land.at[d],
                send_sem=send_sem.at[d],
                recv_sem=recv_sem.at[d],
                device_id={"fsdp": to},
                device_id_type=pl.DeviceIdType.MESH,
            )
        )
        copies[-1].start()
    total = x_ref[f]
    for d in range(1, nf):
        copies[d - 1].wait()
        total = total + land[d]
    stage[0] = total
    copies = []
    for d in range(1, nc):
        copies.append(
            pltpu.make_async_remote_copy(
                src_ref=stage.at[0],
                dst_ref=stage.at[d],
                send_sem=send_sem.at[nf + d],
                recv_sem=recv_sem.at[nf + d],
                device_id={"ctx": lax.rem(c + d, nc)},
                device_id_type=pl.DeviceIdType.MESH,
            )
        )
        copies[-1].start()
    for d in range(1, nc):
        copies[d - 1].wait()
        total = total + stage[d]
    o_ref[...] = total


def reduce_small(x, nf, nc, call):
    block = x.shape[1:]
    sems = pltpu.SemaphoreType.DMA((nf + nc,))
    return pl.pallas_call(
        functools.partial(reduce_small_kernel, nf, nc),
        out_shape=jax.ShapeDtypeStruct(block, single),
        in_specs=[pl.BlockSpec(memory_space=pltpu.VMEM)],
        out_specs=pl.BlockSpec(memory_space=pltpu.VMEM),
        scratch_shapes=[
            pltpu.VMEM((nf,) + block, single),
            pltpu.VMEM((nc,) + block, single),
            sems,
            sems,
        ],
        compiler_params=pltpu.CompilerParams(collective_id=call, has_side_effects=True),
        name="reduce_small",
    )(x)


def per_device(
    tokens,
    cotangent,
    lengths,
    span_place,
    ln1_gain,
    ln1_shift,
    qkv_weight,
    q_bias,
    v_bias,
    out_weight,
    out_bias,
    ln2_gain,
    ln2_shift,
    up_weight,
    up_bias,
    down_weight,
    down_bias,
):
    rows, width = tokens.shape
    CTX = lax.axis_size("ctx")
    c = lax.axis_index("ctx")
    f = lax.axis_index("fsdp")
    nf = lax.axis_size("fsdp")
    wide = up_weight.shape[1]
    part = width // CTX
    heads = HEADS // CTX
    scale = 1.0 / math.sqrt(width // HEADS)
    shard = width // nf
    fpart = wide // nf // CTX
    wpart = wide // CTX

    def columns(x, width_each, stride, count):
        return jnp.concatenate(
            [
                lax.dynamic_slice_in_dim(x, k * stride + c * width_each, width_each, axis=1)
                for k in range(count)
            ],
            axis=1,
        )

    def after(x, *others):
        return lax.optimization_barrier((x, others))[0]

    def pick(x, axis):
        return lax.dynamic_index_in_dim(x, c, axis, keepdims=False)

    def gather_f(x):
        return lax.all_gather(x, "fsdp", axis=0, tiled=True)

    qkv_own = columns(qkv_weight, part, width, 3)
    up_own = columns(up_weight, fpart, wide // nf, nf)
    down_own = lax.dynamic_slice_in_dim(down_weight, c * fpart, fpart, axis=0)
    w_qkv = gather_f(qkv_own.astype(half))
    small = jnp.concatenate(
        [ln1_gain, ln1_shift, q_bias, v_bias, out_bias, ln2_gain, ln2_shift, down_bias, up_bias]
    )
    small_len = small.shape[0]
    small = jnp.pad(small, (0, -small_len % 1024)).reshape(-1, 128)
    small_all = gather_small(small, nf).reshape(nf, -1)[:, :small_len]
    small_all = small_all.astype(half).astype(single)

    def vector(k):
        return small_all[:, k * shard : (k + 1) * shard].reshape(width)

    gain1, shift1, bias_q, bias_v, bias_o, gain2, shift2, bias_d = [vector(k) for k in range(8)]
    bias_u = pick(small_all[:, 8 * shard :].reshape(nf, CTX, fpart), 1).reshape(wpart)
    bias_qkv = jnp.concatenate(
        [pick(bias_q.reshape(CTX, part), 0), jnp.zeros((part,), single), pick(bias_v.reshape(CTX, part), 0)]
    )
    w_out = gather_f(out_weight.astype(half))

    per = rows // SPAN
    table = jnp.arange(CTX * per, dtype=jnp.int32)
    source = ((table // per) ^ c) * per + table % per
    place = jnp.sum(jnp.where(source[:, None] == table[None, :], span_place[0][None, :], 0), axis=1)
    inv = jnp.sum(jnp.where(place[None, :] == table[:, None], table[None, :], 0), axis=1)
    slopes = 2.0 ** (-8.0 * ((c * heads + jnp.arange(heads)).astype(single) + 1.0) / HEADS)

    def to_rows(x):
        return jnp.concatenate(
            [lax.dynamic_slice_in_dim(x, place[r] * SPAN, SPAN, axis=0) for r in range(CTX * per)]
        )

    def flat(pieces):
        return [x for p in pieces for x in p]

    def scatter_f(x):
        return lax.psum_scatter(x, "fsdp", scatter_dimension=0, tiled=True)

    far = CTX - 1
    mid = list(range(1, far))

    def first_norm(x):
        normed, _ = norm_parts(x.astype(single))
        return (normed * gain1 + shift1).astype(half)

    tok_near = after(gather_first(tokens), small_all, place, inv, slopes)
    tok = gather_second(tokens, tok_near)
    near = [[first_norm(x) for x in p] for p in tok[:far]]
    tok = after(tok, near)
    dz2_own = after(cotangent, tok).astype(half)
    dz2_near = gather_first(dz2_own)
    w_up = gather_f(after(up_own.astype(half), tok))
    a1 = flat(near) + [first_norm(x) for x in tok[far]]
    joined = joined_rows(a1, w_qkv, bias_qkv, "qkv")
    w_down = gather_f(after(down_own.astype(half), joined))
    attended = to_rows(attn_forward(joined, inv, slopes, heads, scale))
    mine = [attended[j * rows : (j + 1) * rows] for j in range(CTX)]
    mine = after(mine, dz2_near)
    mine = [mine[0]] + [swap(mine[j], j) for j in range(1, CTX)]
    ob = jnp.concatenate(xor_order(mine, c), axis=1)
    y1 = tokens.astype(single) + dot_nn(ob, w_out) + bias_o

    normed2, inv2 = norm_parts(y1)
    dz2 = gather_second(dz2_own, after(dz2_near, ob))
    a2_own = (normed2 * gain2 + shift2).astype(half)
    a2 = gather_second(a2_own, gather_first(a2_own))
    gb, slope = [None] * CTX, [None] * CTX
    last = ()
    for j in range(CTX):
        gb[j], slope[j] = up_gelu(after(a2[j], last), w_up, bias_u, f"up_gelu_{j}")
        last = gb[j]
    down_grad = outer(flat(gb), flat(dz2), "down_grad")
    down_part = scatter_f(down_grad)
    w_down = after(w_down, down_grad)

    du, dh2, mix = [None] * CTX, [None] * CTX, [None] * CTX
    if CTX == 4:
        du, dh2, arrived, up_grad, mix[far] = feed_back(
            flat(dz2), flat(slope), flat(a2), gb[far], w_down, w_up
        )
        du = [du]
    else:
        for j in range(CTX):
            du[j] = hidden_back(dz2[j], w_down, slope[j], f"du_{j}")
            dh2[j] = plain(du[j], w_up, True, half if j else single, f"dh2_{j}")[0]
        arrived = scatter_send(dh2[1:])
        dh2 = dh2[0]
        up_grad = outer(flat(a2), flat(du), "up_grad")
        mix[far] = plain(gb[far], w_down, False, half, "mix_far")
    up_part = scatter_f(after(up_grad, down_part))
    dh2 = total_of(dh2, arrived)
    up_bias_grad = sum(jnp.sum(x.astype(single), axis=0) for x in flat(du))
    down_bias_grad = jnp.sum(dz2_own.astype(single), axis=0)
    gain2_grad = jnp.sum(dh2 * normed2, axis=0)
    shift2_grad = jnp.sum(dh2, axis=0)
    dy1 = cotangent + norm_back(normed2, inv2, gain2, dh2)

    dz1 = dy1.astype(half)
    dattn = dot_nt(after(dz1, down_part), w_out).astype(half)
    out_bias_grad = jnp.sum(dz1.astype(single), axis=0)
    if CTX == 4:
        dattn, out_grad, mix[1], mix[2] = heads_back(
            dattn, ob, dz1, gb[1][0], gb[2][0], w_down, part
        )
    else:
        dattn = xor_order([dattn[:, s * part : (s + 1) * part] for s in range(CTX)], c)
        dattn = [dattn[0]] + [swap(dattn[j], j) for j in range(1, CTX)]
        dattn = jnp.concatenate(dattn, axis=0)
        out_grad = outer([ob], [dz1], "out_grad")
        for j in mid:
            mix[j] = plain(gb[j], w_down, False, half, f"mix_{j}")[0]
    dqkv = attn_backward(joined, dattn, inv, slopes, heads, scale)
    down_own = after(down_part, dattn)
    down_near = gather_first(down_own)
    dqkv = to_rows(jnp.concatenate(after(dqkv, down_near), axis=1))
    if CTX == 4:
        dh1, arrived, qkv_grad, mix[0] = qkv_back(dqkv, w_qkv, a1, gb[0][0], w_down)
    else:
        dh1 = [
            plain([(dqkv, rows, j)], w_qkv, True, half if j else single, f"dh1_{j}")[0]
            for j in range(CTX)
        ]
        arrived = scatter_send(dh1[1:])
        dh1 = dh1[0]
        qkv_grad = outer(a1, [(dqkv, rows, j) for j in range(CTX)], "qkv_grad")
        mix[0] = plain(gb[0], w_down, False, single, "mix_0")[0]
    dh1 = total_of(dh1, arrived)
    out_part = scatter_f(after(out_grad, up_part, dqkv))
    qkv_part = scatter_f(after(qkv_grad, out_part))
    mix = after(mix, dh1)
    first = scatter_first(mix[far])
    if first is None:
        mix[far] = mix[far][0]
    mixed = total_of(y1 + bias_d + mix[0], scatter_send(scatter_second(mix, first)))
    down_out = gather_second(down_own, after(down_near, dh1))
    down_out = lay_out(0, down_out, c, width // min(width, 512))
    up_out = lay_out(1, gather_ctx(after(up_part, dh1)), c, nf)
    sums = jnp.sum(dqkv.astype(single), axis=0)
    normed1_own, inv1_own = norm_parts(tokens.astype(single))
    gain1_grad = jnp.sum(dh1 * normed1_own, axis=0)
    shift1_grad = jnp.sum(dh1, axis=0)
    input_grad = dy1 + norm_back(normed1_own, inv1_own, gain1, dh1)

    bit = 1
    while bit < CTX:
        out_part = out_part.astype(half)
        out_part = out_part.astype(single) + swap(out_part, bit).astype(single)
        bit *= 2
    out_out = out_part
    qkv_out = lay_out(1, gather_ctx(qkv_part), c, 3)

    def spread(x, inner):
        x = x.reshape(-1, 1, inner)
        mask = (jnp.arange(CTX) == c)[None, :, None]
        return jnp.where(mask, x, 0.0).reshape(-1)

    def reduced(items, call):
        sizes = [x.shape[0] // nf for x in items]
        x = jnp.concatenate([x.reshape(nf, -1) for x in items], axis=1)
        x = jnp.pad(x, ((0, 0), (0, -x.shape[1] % 1024))).reshape(nf, -1, 128)
        x = reduce_small(x, nf, CTX, call).reshape(-1)
        out, at = [], 0
        for n in sizes:
            out.append(x[at : at + n])
            at += n
        return out

    sums_in = [out_bias_grad, gain2_grad, shift2_grad, down_bias_grad, spread(up_bias_grad, fpart)]
    sums_in += [gain1_grad, shift1_grad, spread(sums[:part], part), spread(sums[2 * part :], part)]
    sums_in[5] = after(sums_in[5], mixed, up_out, down_out)
    sums_out = reduced(sums_in, 2)
    out_bias_out, gain2_out, shift2_out, down_bias_out, up_bias_out = sums_out[:5]
    gain1_out, shift1_out, q_bias_out, v_bias_out = sums_out[5:]
    return (
        mixed,
        input_grad,
        gain1_out,
        shift1_out,
        qkv_out,
        q_bias_out,
        v_bias_out,
        out_out,
        out_bias_out,
        gain2_out,
        shift2_out,
        up_out,
        up_bias_out,
        down_out,
        down_bias_out,
    )


def solution(mesh):
    rows, flat = P(("ctx", "fsdp"), None), P("fsdp")
    mat = P("fsdp", None)
    in_specs = (
        rows,
        rows,
        mat,
        mat,
        flat,
        flat,
        mat,
        flat,
        flat,
        mat,
        flat,
        flat,
        flat,
        mat,
        flat,
        mat,
        flat,
    )
    out_specs = (
        rows,
        rows,
        flat,
        flat,
        mat,
        flat,
        flat,
        mat,
        flat,
        flat,
        flat,
        mat,
        flat,
        mat,
        flat,
    )
    return jax.shard_map(
        per_device, mesh=mesh, in_specs=in_specs, out_specs=out_specs, check_vma=False
    )
```

```python
import functools
import math

import jax
import jax.numpy as jnp
from jax import lax
from jax.experimental import pallas as pl
from jax.experimental.pallas import tpu as pltpu
from jax.sharding import PartitionSpec as P

HEADS = 16
SPAN = 128
SEQ_BLOCKS = 8

norm_eps = 1e-05
gelu_coef = 0.7978845608028654
LOG2E = 1.4426950408889634

half = jnp.bfloat16
single = jnp.float32


def dot_nn(a, b):
    return lax.dot_general(a, b, (((1,), (0,)), ((), ())), preferred_element_type=single)


def dot_nt(a, b):
    return lax.dot_general(a, b, (((1,), (1,)), ((), ())), preferred_element_type=single)


def dot_tn(a, b):
    return lax.dot_general(a, b, (((0,), (0,)), ((), ())), preferred_element_type=single)


def norm_parts(values):
    center = values - jnp.mean(values, axis=-1, keepdims=True)
    spread = jnp.mean(center * center, axis=-1, keepdims=True)
    inv = lax.rsqrt(spread + norm_eps)
    return center * inv, inv


def norm_back(normed, inv, gain, grad):
    dn = grad * gain
    return inv * (
        dn
        - jnp.mean(dn, axis=-1, keepdims=True)
        - normed * jnp.mean(dn * normed, axis=-1, keepdims=True)
    )


def gelu_both(v):
    t = jnp.tanh(gelu_coef * (v + 0.044715 * v * v * v))
    value = 0.5 * v * (1.0 + t)
    slope = 0.5 * (1.0 + t) + 0.5 * v * (1.0 - t * t) * gelu_coef * (1.0 + 3 * 0.044715 * v * v)
    return value, slope


def swap(x, mask):
    n = lax.axis_size("ctx")
    return lax.ppermute(x, "ctx", [(i, i ^ mask) for i in range(n)])


def gather_first(x):
    count = lax.axis_size("ctx")
    return [swap(x, j) for j in range(1, 3 if count == 4 else count)]


def gather_second(x, arrived):
    if lax.axis_size("ctx") != 4:
        return [[x]] + [[p] for p in arrived]
    one, two = arrived
    n = x.shape[0] // 2
    return [[x], [one], [two], [swap(one[:n], 2), swap(two[n:], 1)]]


def gather_ctx(x):
    return gather_second(x, gather_first(x))


def scatter_first(far):
    if lax.axis_size("ctx") != 4:
        return None
    return swap(far[0], 1), swap(far[1], 2)


def scatter_second(pieces, first):
    if first is None:
        return pieces[1:]
    p1, p2 = pieces[1], pieces[2]
    n = p1.shape[0] // 2
    from_x, from_y = first
    p1 = jnp.concatenate(
        [p1[:n], (p1[n:].astype(single) + from_y.astype(single)).astype(half)], axis=0
    )
    p2 = jnp.concatenate(
        [(p2[:n].astype(single) + from_x.astype(single)).astype(half), p2[n:]], axis=0
    )
    return [p1, p2]


def scatter_send(sent):
    return [swap(x, j + 1) for j, x in enumerate(sent)]


def total_of(own, arrived):
    for x in arrived:
        own = own + x.astype(single)
    return own


def xor_order(items, c):
    bit = 1
    while bit < len(items):
        on = (c & bit) == bit
        items = [jnp.where(on, items[i ^ bit], items[i]) for i in range(len(items))]
        bit *= 2
    return items


TILE = 256


def attn_scores(q_refs, k_refs, i, scale, slope):
    q = jnp.concatenate([q_refs[2 * i][...], q_refs[2 * i + 1][...]], axis=0)
    k = jnp.concatenate([r[...] for r in k_refs[: 2 * i + 2]], axis=0)
    n = TILE * (i + 1)
    col = lax.broadcasted_iota(jnp.int32, (1, n), 1) - (n - 1)
    s = dot_nt(q, k) * (scale * LOG2E) + (slope * LOG2E) * col.astype(single)
    row_at = lax.broadcasted_iota(jnp.int32, (TILE, TILE), 0)
    col_at = lax.broadcasted_iota(jnp.int32, (TILE, TILE), 1)
    last = jnp.where(col_at <= row_at, s[:, n - TILE :], -1e30)
    s = last if i == 0 else jnp.concatenate([s[:, : n - TILE], last], axis=1)
    e = jnp.exp2(s - jnp.max(s, axis=1, keepdims=True))
    return q, k, e, 1.0 / jnp.sum(e, axis=1, keepdims=True)


class Rows:
    def __init__(self, inv_ref, stage, out, sems, kinds):
        self.inv, self.stage, self.out, self.sems, self.kinds = inv_ref, stage, out, sems, kinds
        self.heads = pl.num_programs(1)
        self.step = pl.program_id(0) * self.heads + pl.program_id(1)
        self.slot = lax.rem(self.step, 2)

    def copies(self, step):
        slot = lax.rem(step, 2)
        seq, head = step // self.heads, lax.rem(step, self.heads)
        for kind in range(self.kinds):
            col = pl.multiple_of((kind * self.heads + head) * 128, 128)
            for j in range(SEQ_BLOCKS):
                row = pl.multiple_of(self.inv[seq * SEQ_BLOCKS + j] * SPAN, SPAN)
                yield pltpu.make_async_copy(
                    self.stage.at[slot, kind, pl.ds(j * SPAN, SPAN)],
                    self.out.at[pl.ds(row, SPAN), pl.ds(col, 128)],
                    self.sems.at[slot, kind * SEQ_BLOCKS + j],
                )

    def wait(self, step):
        for copy in self.copies(step):
            copy.wait()

    def open(self):
        @pl.when(self.step >= 2)
        def _():
            self.wait(self.step - 2)

    def close(self):
        for copy in self.copies(self.step):
            copy.start()

        @pl.when(self.step == 2 * self.heads - 1)
        def _():
            self.wait(self.step - 1)
            self.wait(self.step)


def attn_fwd_kernel(scale, inv_ref, slope_ref, *refs):
    q_refs, k_refs, v_refs = refs[:8], refs[8:16], refs[16:24]
    out, stage, sems = refs[24:]
    slope = slope_ref[pl.program_id(1)]
    rows = Rows(inv_ref, stage, out, sems, 1)
    rows.open()
    for i in range(4):
        q, k, e, r = attn_scores(q_refs, k_refs, i, scale, slope)
        v = jnp.concatenate([x[...] for x in v_refs[: 2 * i + 2]], axis=0)
        o = dot_nn((e * r).astype(half), v)
        stage[rows.slot, 0, TILE * i : TILE * (i + 1), :] = o.astype(half)
    rows.close()


def attn_bwd_kernel(scale, inv_ref, slope_ref, *refs):
    q_refs, k_refs, v_refs, g_refs = refs[:8], refs[8:16], refs[16:24], refs[24:32]
    out, stage, sems, dk_acc, dv_acc = refs[32:]
    slope = slope_ref[pl.program_id(1)]
    rows = Rows(inv_ref, stage, out, sems, 3)
    rows.open()
    for i in (3, 2, 1, 0):
        q, k, e, r = attn_scores(q_refs, k_refs, i, scale, slope)
        n = TILE * (i + 1)
        v = jnp.concatenate([x[...] for x in v_refs[: 2 * i + 2]], axis=0)
        g = jnp.concatenate([g_refs[2 * i][...], g_refs[2 * i + 1][...]], axis=0)
        p = e * r
        dp = dot_nt(g, v)
        delta = jnp.sum(p * dp, axis=1, keepdims=True)
        ds = (p * (dp - delta)).astype(half)
        pb = p.astype(half)
        dq = (dot_nn(ds, k) * scale).astype(half)
        stage[rows.slot, 0, TILE * i : TILE * (i + 1), :] = dq
        dk = dot_tn(ds, q)
        dv = dot_tn(pb, g)
        if i == 3:
            dk_acc[...] = dk
            dv_acc[...] = dv
        else:
            dk_acc[:n, :] += dk
            dv_acc[:n, :] += dv
    stage[rows.slot, 1] = (dk_acc[...] * scale).astype(half)
    stage[rows.slot, 2] = dv_acc[...].astype(half)
    rows.close()


def block_specs(offset):
    def one(j):
        return pl.BlockSpec(
            (SPAN, 128), lambda s, h, inv, slope: (inv[s * SEQ_BLOCKS + j], offset + h)
        )

    return [one(j) for j in range(SEQ_BLOCKS)]


def attn_call(kernel, kinds, joined, extra, extra_specs, scratch, inv, slopes, heads, cost, name):
    rows = joined.shape[0]
    specs = block_specs(0) + block_specs(heads) + block_specs(2 * heads) + extra_specs
    return pl.pallas_call(
        kernel,
        grid_spec=pltpu.PrefetchScalarGridSpec(
            num_scalar_prefetch=2,
            grid=(2, heads),
            in_specs=specs,
            out_specs=pl.BlockSpec(memory_space=pl.ANY),
            scratch_shapes=[
                pltpu.VMEM((2, kinds, rows // 2, 128), half),
                pltpu.SemaphoreType.DMA((2, kinds * SEQ_BLOCKS)),
            ]
            + scratch,
        ),
        out_shape=jax.ShapeDtypeStruct((rows, kinds * heads * 128), half),
        compiler_params=pltpu.CompilerParams(vmem_limit_bytes=48 * 1024 * 1024),
        cost_estimate=cost,
        name=name,
    )(inv, slopes, *([joined] * 24), *extra)


def attn_forward(joined, inv, slopes, heads, scale):
    kernel = functools.partial(attn_fwd_kernel, scale)
    cost = hint(20 * 10**9, joined.shape[0] * heads * 128 * 8)
    return attn_call(
        kernel, 1, joined, [], [], [], inv, slopes, heads, cost, "attn_forward"
    )


def attn_backward(joined, grad, inv, slopes, heads, scale):
    kernel = functools.partial(attn_bwd_kernel, scale)
    cost = hint(40 * 10**9, joined.shape[0] * heads * 128 * 14)
    sums = [pltpu.VMEM((joined.shape[0] // 2, 128), single)] * 2
    return attn_call(
        kernel,
        3,
        joined,
        [grad] * 8,
        block_specs(0),
        sums,
        inv,
        slopes,
        heads,
        cost,
        "attn_backward",
    )


HINT = 0.001


def block_of(x):
    return x if isinstance(x, tuple) else (x, x.shape[0], 0)


def hint(flops, bytes_accessed):
    return pl.CostEstimate(
        flops=int(HINT * flops), bytes_accessed=int(HINT * bytes_accessed), transcendentals=0
    )


def rows_kernel(dot, epilogue, count, extra, *refs):
    left, w_ref = refs[:count], refs[count]
    extras = refs[count + 1 : count + 1 + extra]
    outs = refs[count + 1 + extra :]
    for i in range(count):
        epilogue(i, dot(left[i][...], w_ref[...]), extras, outs)


def rows_matmul(blocks, w, transposed, extras, outs, epilogue, name, tile=512):
    blocks = [block_of(x) for x in blocks]
    extras = [block_of(x) for x in extras]
    n = w.shape[0] if transposed else w.shape[1]
    k = w.shape[1] if transposed else w.shape[0]
    t = math.gcd(n, tile)
    w_spec = (
        pl.BlockSpec((t, k), lambda i: (i, 0)) if transposed else pl.BlockSpec((k, t), lambda i: (0, i))
    )
    rows = sum(x[1] for x in blocks)
    return pl.pallas_call(
        functools.partial(
            rows_kernel, dot_nt if transposed else dot_nn, epilogue, len(blocks), len(extras)
        ),
        grid=(n // t,),
        in_specs=[pl.BlockSpec((x[1], k), lambda i, at=x[2]: (at, 0)) for x in blocks]
        + [w_spec]
        + [pl.BlockSpec((x[1], t), lambda i, at=x[2]: (at, i)) for x in extras],
        out_specs=[pl.BlockSpec((r, t), lambda i: (0, i)) for r, _ in outs],
        out_shape=[jax.ShapeDtypeStruct((r, n), d) for r, d in outs],
        compiler_params=pltpu.CompilerParams(vmem_limit_bytes=52 * 1024 * 1024),
        cost_estimate=hint(2 * rows * n * k, 2 * n * k + 4 * rows * (n + k)),
        name=name,
    )(*[x[0] for x in blocks], w, *[x[0] for x in extras])


def plain(blocks, w, transposed, dtype, name):
    def epilogue(i, x, extras, outs):
        outs[i][...] = x.astype(dtype)

    outs = [(block_of(x)[1], dtype) for x in blocks]
    return rows_matmul(blocks, w, transposed, [], outs, epilogue, name)


def joined_rows(blocks, w, bias, name):
    sizes = [block_of(x)[1] for x in blocks]

    def epilogue(i, x, extras, outs):
        at = sum(sizes[:i])
        outs[0][at : at + sizes[i], :] = (x + extras[0][...]).astype(half)

    bias = bias.reshape(1, -1)
    return rows_matmul(blocks, w, False, [bias], [(sum(sizes), half)], epilogue, name)[0]


def up_gelu(blocks, w, bias, name):
    count = len(blocks)

    def epilogue(i, x, extras, outs):
        value, slope = gelu_both(x + extras[0][...])
        outs[i][...] = value.astype(half)
        outs[count + i][...] = slope.astype(half)

    outs = [(block_of(x)[1], half) for x in blocks] * 2
    out = rows_matmul(blocks, w, False, [bias.reshape(1, -1)], outs, epilogue, name)
    return out[:count], out[count:]


def hidden_back(blocks, w, slopes, name):
    def epilogue(i, x, extras, outs):
        x = x.astype(half).astype(single) * extras[i][...].astype(single)
        outs[i][...] = x.astype(half)

    outs = [(block_of(x)[1], half) for x in blocks]
    return rows_matmul(blocks, w, True, slopes, outs, epilogue, name)


def outer_kernel(count, *refs):
    out = refs[-1]
    total = None
    for i in range(count):
        x = dot_tn(refs[i][...], refs[count + i][...])
        total = x if total is None else total + x
    out[...] = total.astype(half)


def outer(left, right, name):
    left = [block_of(x) for x in left]
    right = [block_of(x) for x in right]
    m, n = left[0][0].shape[1], right[0][0].shape[1]
    tm = math.gcd(m, 1024)
    tn = n // 2 if n % 256 == 0 and n > 1024 else n
    rows = sum(x[1] for x in left)
    return pl.pallas_call(
        functools.partial(outer_kernel, len(left)),
        grid=(m // tm, n // tn),
        in_specs=[pl.BlockSpec((x[1], tm), lambda i, j, at=x[2]: (at, i)) for x in left]
        + [pl.BlockSpec((x[1], tn), lambda i, j, at=x[2]: (at, j)) for x in right],
        out_specs=pl.BlockSpec((tm, tn), lambda i, j: (i, j)),
        out_shape=jax.ShapeDtypeStruct((m, n), half),
        compiler_params=pltpu.CompilerParams(vmem_limit_bytes=52 * 1024 * 1024),
        cost_estimate=hint(2 * rows * m * n, 2 * rows * (m + n) + 2 * m * n),
        name=name,
    )(*[x[0] for x in left], *[x[0] for x in right])


def partner(mask):
    c = lax.axis_index("ctx")
    if mask == 1:
        return c + 1 - 2 * lax.rem(c, 2)
    return lax.rem(c + 2, 4) if mask == 2 else 3 - c


def greet(masks):
    barrier = pltpu.get_barrier_semaphore()
    for mask in masks:
        pl.semaphore_signal(
            barrier,
            inc=1,
            device_id={"ctx": partner(mask)},
            device_id_type=pl.DeviceIdType.MESH,
        )
    pl.semaphore_wait(barrier, len(masks))


class Moves:
    def __init__(self, send_sem, recv_sem):
        self.send_sem, self.recv_sem, self.used = send_sem, recv_sem, 0

    def start(self, src, dst, mask):
        copy = pltpu.make_async_remote_copy(
            src_ref=src,
            dst_ref=dst,
            send_sem=self.send_sem.at[self.used],
            recv_sem=self.recv_sem.at[self.used],
            device_id={"ctx": partner(mask)},
            device_id_type=pl.DeviceIdType.MESH,
        )
        self.used += 1
        copy.start()
        return copy


def multiply(lefts, w, transposed, extras, outs, epilogue, tile=512):
    k = lefts[0].shape[1]
    n = w.shape[0] if transposed else w.shape[1]
    t = math.gcd(n, tile)
    w_spec = (
        pl.BlockSpec((t, k), lambda i: (i, 0)) if transposed else pl.BlockSpec((k, t), lambda i: (0, i))
    )
    dot = dot_nt if transposed else dot_nn

    def body(*refs):
        rows_kernel(dot, epilogue, len(lefts), len(extras), *refs)

    pltpu.emit_pipeline(
        body,
        grid=(n // t,),
        in_specs=[pl.BlockSpec((x.shape[0], k), lambda i: (0, 0)) for x in lefts]
        + [w_spec]
        + [pl.BlockSpec((x.shape[0], t), lambda i: (0, i)) for x in extras],
        out_specs=[pl.BlockSpec((x.shape[0], t), lambda i: (0, i)) for x in outs],
    )(*lefts, w, *extras, *outs)


def store(i, x, extras, outs):
    outs[i][...] = x.astype(outs[i].dtype)


def store_sum(i, x, extras, outs):
    outs[i][...] = (x + extras[i][...].astype(single)).astype(outs[i].dtype)


def store_passed(i, x, extras, outs):
    if i in (1, 2):
        x = x + extras[i - 1][...].astype(single)
    outs[i][...] = x.astype(outs[i].dtype)


def store_hidden(i, x, extras, outs):
    outs[i][...] = (x.astype(half).astype(single) * extras[i][...].astype(single)).astype(half)


def outer_on(lefts, rights, out):
    m, n = out.shape
    tm = math.gcd(m, 1024)
    tn = n // 2 if n % 256 == 0 and n > 1024 else n

    def body(*refs):
        outer_kernel(len(lefts), *refs)

    pltpu.emit_pipeline(
        body,
        grid=(m // tm, n // tn),
        in_specs=[pl.BlockSpec((x.shape[0], tm), lambda i, j: (0, i)) for x in lefts]
        + [pl.BlockSpec((x.shape[0], tn), lambda i, j: (0, j)) for x in rights],
        out_specs=[pl.BlockSpec((tm, tn), lambda i, j: (i, j))],
    )(*lefts, *rights, out)


def halves(ref):
    n = ref.shape[0] // 2
    return ref.at[pl.ds(0, n)], ref.at[pl.ds(n, n)]


def moving_call(kernel, operands, outs, moves, call, flops, name):
    anywhere = pl.BlockSpec(memory_space=pl.ANY)
    sems = pltpu.SemaphoreType.DMA((moves,))
    return pl.pallas_call(
        kernel,
        in_specs=[anywhere] * len(operands),
        out_specs=[anywhere] * len(outs),
        out_shape=[jax.ShapeDtypeStruct(shape, dtype) for shape, dtype in outs],
        scratch_shapes=[sems, sems],
        compiler_params=pltpu.CompilerParams(
            collective_id=call, has_side_effects=True, vmem_limit_bytes=52 * 1024 * 1024
        ),
        cost_estimate=hint(flops, 0),
        name=name,
    )(*operands)


def feed_back_kernel(*refs):
    dz, slope, a2, gb_far = refs[0:5], refs[5:10], refs[10:15], refs[15:17]
    w_down, w_up = refs[17:19]
    du, own, p3, p1, p2 = refs[19:24], refs[24], refs[25:27], refs[27], refs[28]
    from_x, from_y, land1, land2, up_grad = refs[29:34]
    mix_far, mix_x, mix_y = refs[34:36], refs[36], refs[37]
    moves = Moves(*refs[38:40])
    greet((1, 2))
    multiply(dz[3:5], w_down, True, slope[3:5], du[3:5], store_hidden)
    multiply(du[3:5], w_up, True, [], p3, store)
    first = [moves.start(p3[0], from_x, 1), moves.start(p3[1], from_y, 2)]
    multiply(dz[1:3], w_down, True, slope[1:3], du[1:3], store_hidden)
    (p1_lo, p1_hi), (p2_lo, p2_hi) = halves(p1), halves(p2)
    (du1_lo, du1_hi), (du2_lo, du2_hi) = halves(du[1]), halves(du[2])
    (land1_lo, land1_hi), (land2_lo, land2_hi) = halves(land1), halves(land2)
    multiply([du1_lo, du2_hi], w_up, True, [], [p1_lo, p2_hi], store)
    second = [moves.start(p1_lo, land1_lo, 1), moves.start(p2_hi, land2_hi, 2)]
    for copy in first:
        copy.wait()
    multiply([du1_hi, du2_lo], w_up, True, [from_y, from_x], [p1_hi, p2_lo], store_sum)
    second += [moves.start(p1_hi, land1_hi, 1), moves.start(p2_lo, land2_lo, 2)]
    multiply(dz[0:1], w_down, True, slope[0:1], du[0:1], store_hidden)
    multiply(du[0:1], w_up, True, [], [own], store)
    multiply(gb_far, w_down, False, [], mix_far, store)
    second += [moves.start(mix_far[0], mix_x, 1), moves.start(mix_far[1], mix_y, 2)]
    outer_on(a2, du, up_grad)
    for copy in second:
        copy.wait()


def feed_back(dz, slope, a2, gb_far, w_down, w_up):
    rows, width = dz[0].shape
    wide = w_down.shape[0]
    n = rows // 2
    sizes = [rows, rows, rows, n, n]
    outs = [((r, wide), half) for r in sizes]
    outs += [((rows, width), single)]
    outs += [((n, width), half)] * 2 + [((rows, width), half)] * 2
    outs += [((n, width), half)] * 2 + [((rows, width), half)] * 2
    outs += [((width, wide), half)] + [((n, width), half)] * 4
    out = moving_call(
        feed_back_kernel,
        [*dz, *slope, *a2, *gb_far, w_down, w_up],
        outs,
        8,
        3,
        26 * rows * width * wide,
        "feed_back",
    )
    return out[0:5], out[5], out[12:14], out[14], out[17:19]


def heads_back_kernel(part, *refs):
    dattn, ob, dz1, gb1, gb2, w_down, mix_x, mix_y = refs[0:8]
    got, out_grad = refs[8:10]
    mix = refs[10:14]
    moves = Moves(*refs[14:16])
    local = refs[16]
    rows = dattn.shape[0]
    c = lax.axis_index("ctx")

    def columns(of):
        return dattn.at[:, pl.ds(pl.multiple_of(of * part, part), part)]

    greet((1, 2, 3))
    copies = []
    for mask in (3, 1, 2):
        at = got.at[pl.ds(mask * rows, rows)]
        copies.append(moves.start(columns(partner(mask)), at, mask))
    own = pltpu.make_async_copy(columns(c), got.at[pl.ds(0, rows)], local)
    own.start()
    outer_on([ob], [dz1], out_grad)
    multiply(
        [*halves(gb1), *halves(gb2)],
        w_down,
        False,
        [mix_y, mix_x],
        mix,
        store_passed,
    )
    own.wait()
    for copy in copies:
        copy.wait()


def heads_back(dattn, ob, dz1, gb1, gb2, w_down, mix_x, mix_y, part):
    rows, width = dattn.shape
    anywhere = pl.BlockSpec(memory_space=pl.ANY)
    sems = pltpu.SemaphoreType.DMA((3,))
    outs = [((4 * rows, part), half), ((width, width), half)] + [((rows // 2, width), half)] * 4
    return pl.pallas_call(
        functools.partial(heads_back_kernel, part),
        in_specs=[anywhere] * 8,
        out_specs=[anywhere] * len(outs),
        out_shape=[jax.ShapeDtypeStruct(shape, dtype) for shape, dtype in outs],
        scratch_shapes=[sems, sems, pltpu.SemaphoreType.DMA],
        compiler_params=pltpu.CompilerParams(
            collective_id=4, has_side_effects=True, vmem_limit_bytes=52 * 1024 * 1024
        ),
        cost_estimate=hint(10 * rows * width * width, 0),
        name="heads_back",
    )(dattn, ob, dz1, gb1, gb2, w_down, mix_x, mix_y)


def qkv_back_kernel(*refs):
    dqkv, w_qkv = refs[0:2]
    a1, gb_own, w_down = refs[2:7], refs[7], refs[8]
    own, p3, p1, p2, from_x, from_y, land1, land2, qkv_grad, mix_own = refs[9:19]
    moves = Moves(*refs[19:21])
    rows = own.shape[0]
    n = rows // 2

    def block(k):
        return dqkv.at[pl.ds(k * n, n)]

    greet((1, 2))
    (p3_lo, p3_hi), (p1_lo, p1_hi), (p2_lo, p2_hi) = halves(p3), halves(p1), halves(p2)
    (land1_lo, land1_hi), (land2_lo, land2_hi) = halves(land1), halves(land2)
    multiply([block(6), block(7)], w_qkv, True, [], [p3_lo, p3_hi], store)
    first = [moves.start(p3_lo, from_x, 1), moves.start(p3_hi, from_y, 2)]
    multiply([block(2), block(5)], w_qkv, True, [], [p1_lo, p2_hi], store)
    second = [moves.start(p1_lo, land1_lo, 1), moves.start(p2_hi, land2_hi, 2)]
    multiply([dqkv.at[pl.ds(0, rows)]], w_qkv, True, [], [own], store)
    multiply([gb_own], w_down, False, [], [mix_own], store)
    for copy in first:
        copy.wait()
    multiply([block(3), block(4)], w_qkv, True, [from_y, from_x], [p1_hi, p2_lo], store_sum)
    second += [moves.start(p1_hi, land1_hi, 1), moves.start(p2_lo, land2_lo, 2)]
    rights, at = [], 0
    for x in a1:
        rights.append(dqkv.at[pl.ds(at, x.shape[0])])
        at += x.shape[0]
    outer_on(a1, rights, qkv_grad)
    for copy in second:
        copy.wait()


def qkv_back(dqkv, w_qkv, a1, gb_own, w_down):
    rows, width = a1[0].shape
    wide = gb_own.shape[1]
    n = rows // 2
    outs = [((rows, width), single)] + [((rows, width), half)] * 3
    outs += [((n, width), half)] * 2 + [((rows, width), half)] * 2
    outs += [((width, dqkv.shape[1]), half), ((rows, width), single)]
    out = moving_call(
        qkv_back_kernel,
        [dqkv, w_qkv, *a1, gb_own, w_down],
        outs,
        6,
        5,
        16 * rows * width * dqkv.shape[1] + 2 * rows * width * wide,
        "qkv_back",
    )
    return out[0], out[6:8], out[8], out[9]


def lay_out_kernel(axis, layout, c_ref, *refs):
    out = refs[-1]
    for (j, row), ref in zip(layout, refs):
        x = ref[...].astype(single)
        r, w = x.shape
        if axis == 0:
            n = sum(ref.shape[0] for (k, _), ref in zip(layout, refs) if k == j)
            out[pl.ds(pl.multiple_of((c_ref[0] ^ j) * n + row, r), r), :] = x
        else:
            out[row : row + r, pl.ds(pl.multiple_of((c_ref[0] ^ j) * w, w), w)] = x


def lay_out(axis, pieces, c, groups):
    count = len(pieces)
    r = sum(x.shape[0] for x in pieces[0])
    n = pieces[0][0].shape[1]
    w = n // groups
    if w % 128:
        whole = xor_order([jnp.concatenate(p, axis=0).astype(single) for p in pieces], c)
        whole = jnp.stack([p.reshape(r, groups, w) for p in whole], axis=2)
        return whole.reshape(r, count * n)
    layout, blocks = [], []
    for j, p in enumerate(pieces):
        row = 0
        for x in p:
            layout.append((j, row))
            blocks.append(x)
            row += x.shape[0]
    out = (count * r, w) if axis == 0 else (r, count * w)
    return pl.pallas_call(
        functools.partial(lay_out_kernel, axis, layout),
        grid_spec=pltpu.PrefetchScalarGridSpec(
            num_scalar_prefetch=1,
            grid=(groups,),
            in_specs=[pl.BlockSpec((x.shape[0], w), lambda k, c: (0, k)) for x in blocks],
            out_specs=pl.BlockSpec(out, lambda k, c: (0, k)),
        ),
        out_shape=jax.ShapeDtypeStruct((out[0], out[1] * groups), single),
        compiler_params=pltpu.CompilerParams(vmem_limit_bytes=48 * 1024 * 1024),
        cost_estimate=hint(0, 6 * r * n * count),
        name="lay_out",
    )(c.reshape(1), *blocks)


def gather_small_kernel(nf, x_ref, o_ref, send_sem, recv_sem):
    f = lax.axis_index("fsdp")
    barrier = pltpu.get_barrier_semaphore()
    for d in range(1, nf):
        pl.semaphore_signal(
            barrier,
            inc=1,
            device_id={"fsdp": lax.rem(f + d, nf)},
            device_id_type=pl.DeviceIdType.MESH,
        )
    pl.semaphore_wait(barrier, nf - 1)
    copies = []
    for d in range(1, nf):
        copies.append(
            pltpu.make_async_remote_copy(
                src_ref=x_ref,
                dst_ref=o_ref.at[f],
                send_sem=send_sem.at[d],
                recv_sem=recv_sem.at[d],
                device_id={"fsdp": lax.rem(f + d, nf)},
                device_id_type=pl.DeviceIdType.MESH,
            )
        )
        copies[-1].start()
    o_ref[f] = x_ref[...]
    for copy in copies:
        copy.wait()


def gather_small(x, nf):
    return pl.pallas_call(
        functools.partial(gather_small_kernel, nf),
        out_shape=jax.ShapeDtypeStruct((nf,) + x.shape, single),
        in_specs=[pl.BlockSpec(memory_space=pltpu.VMEM)],
        out_specs=pl.BlockSpec(memory_space=pltpu.VMEM),
        scratch_shapes=[pltpu.SemaphoreType.DMA((nf,)), pltpu.SemaphoreType.DMA((nf,))],
        compiler_params=pltpu.CompilerParams(collective_id=1, has_side_effects=True),
        name="gather_small",
    )(x)


def reduce_small_kernel(nf, nc, x_ref, o_ref, land, stage, send_sem, recv_sem):
    f = lax.axis_index("fsdp")
    c = lax.axis_index("ctx")
    barrier = pltpu.get_barrier_semaphore()
    for d in range(1, nf):
        pl.semaphore_signal(
            barrier,
            inc=1,
            device_id={"fsdp": lax.rem(f + d, nf)},
            device_id_type=pl.DeviceIdType.MESH,
        )
    for d in range(1, nc):
        pl.semaphore_signal(
            barrier,
            inc=1,
            device_id={"ctx": lax.rem(c + d, nc)},
            device_id_type=pl.DeviceIdType.MESH,
        )
    pl.semaphore_wait(barrier, nf + nc - 2)
    copies = []
    for d in range(1, nf):
        to = lax.rem(f + d, nf)
        copies.append(
            pltpu.make_async_remote_copy(
                src_ref=x_ref.at[to],
                dst_ref=land.at[d],
                send_sem=send_sem.at[d],
                recv_sem=recv_sem.at[d],
                device_id={"fsdp": to},
                device_id_type=pl.DeviceIdType.MESH,
            )
        )
        copies[-1].start()
    total = x_ref[f]
    for d in range(1, nf):
        copies[d - 1].wait()
        total = total + land[d]
    stage[0] = total
    copies = []
    for d in range(1, nc):
        copies.append(
            pltpu.make_async_remote_copy(
                src_ref=stage.at[0],
                dst_ref=stage.at[d],
                send_sem=send_sem.at[nf + d],
                recv_sem=recv_sem.at[nf + d],
                device_id={"ctx": lax.rem(c + d, nc)},
                device_id_type=pl.DeviceIdType.MESH,
            )
        )
        copies[-1].start()
    for d in range(1, nc):
        copies[d - 1].wait()
        total = total + stage[d]
    o_ref[...] = total


def reduce_small(x, nf, nc, call):
    block = x.shape[1:]
    sems = pltpu.SemaphoreType.DMA((nf + nc,))
    return pl.pallas_call(
        functools.partial(reduce_small_kernel, nf, nc),
        out_shape=jax.ShapeDtypeStruct(block, single),
        in_specs=[pl.BlockSpec(memory_space=pltpu.VMEM)],
        out_specs=pl.BlockSpec(memory_space=pltpu.VMEM),
        scratch_shapes=[
            pltpu.VMEM((nf,) + block, single),
            pltpu.VMEM((nc,) + block, single),
            sems,
            sems,
        ],
        compiler_params=pltpu.CompilerParams(collective_id=call, has_side_effects=True),
        name="reduce_small",
    )(x)


def per_device(
    tokens,
    cotangent,
    lengths,
    span_place,
    ln1_gain,
    ln1_shift,
    qkv_weight,
    q_bias,
    v_bias,
    out_weight,
    out_bias,
    ln2_gain,
    ln2_shift,
    up_weight,
    up_bias,
    down_weight,
    down_bias,
):
    rows, width = tokens.shape
    CTX = lax.axis_size("ctx")
    c = lax.axis_index("ctx")
    f = lax.axis_index("fsdp")
    nf = lax.axis_size("fsdp")
    wide = up_weight.shape[1]
    part = width // CTX
    heads = HEADS // CTX
    scale = 1.0 / math.sqrt(width // HEADS)
    shard = width // nf
    fpart = wide // nf // CTX
    wpart = wide // CTX

    def columns(x, width_each, stride, count):
        return jnp.concatenate(
            [
                lax.dynamic_slice_in_dim(x, k * stride + c * width_each, width_each, axis=1)
                for k in range(count)
            ],
            axis=1,
        )

    def after(x, *others):
        return lax.optimization_barrier((x, others))[0]

    def pick(x, axis):
        return lax.dynamic_index_in_dim(x, c, axis, keepdims=False)

    def gather_f(x):
        return lax.all_gather(x, "fsdp", axis=0, tiled=True)

    qkv_own = columns(qkv_weight, part, width, 3)
    up_own = columns(up_weight, fpart, wide // nf, nf)
    down_own = lax.dynamic_slice_in_dim(down_weight, c * fpart, fpart, axis=0)
    w_qkv = gather_f(qkv_own.astype(half))
    small = jnp.concatenate(
        [ln1_gain, ln1_shift, q_bias, v_bias, out_bias, ln2_gain, ln2_shift, down_bias, up_bias]
    )
    small_len = small.shape[0]
    small = jnp.pad(small, (0, -small_len % 1024)).reshape(-1, 128)
    small_all = gather_small(small, nf).reshape(nf, -1)[:, :small_len]
    small_all = small_all.astype(half).astype(single)

    def vector(k):
        return small_all[:, k * shard : (k + 1) * shard].reshape(width)

    gain1, shift1, bias_q, bias_v, bias_o, gain2, shift2, bias_d = [vector(k) for k in range(8)]
    bias_u = pick(small_all[:, 8 * shard :].reshape(nf, CTX, fpart), 1).reshape(wpart)
    bias_qkv = jnp.concatenate(
        [pick(bias_q.reshape(CTX, part), 0), jnp.zeros((part,), single), pick(bias_v.reshape(CTX, part), 0)]
    )
    w_out = gather_f(out_weight.astype(half))

    per = rows // SPAN
    table = jnp.arange(CTX * per, dtype=jnp.int32)
    source = ((table // per) ^ c) * per + table % per
    place = jnp.sum(jnp.where(source[:, None] == table[None, :], span_place[0][None, :], 0), axis=1)
    inv = jnp.sum(jnp.where(place[None, :] == table[:, None], table[None, :], 0), axis=1)
    slopes = 2.0 ** (-8.0 * ((c * heads + jnp.arange(heads)).astype(single) + 1.0) / HEADS)

    def flat(pieces):
        return [x for p in pieces for x in p]

    def scatter_f(x):
        return lax.psum_scatter(x, "fsdp", scatter_dimension=0, tiled=True)

    far = CTX - 1
    mid = list(range(1, far))

    def first_norm(x):
        normed, _ = norm_parts(x.astype(single))
        return (normed * gain1 + shift1).astype(half)

    tok_near = after(gather_first(tokens), small_all, place, inv, slopes)
    tok = gather_second(tokens, tok_near)
    near = [[first_norm(x) for x in p] for p in tok[:far]]
    tok = after(tok, near)
    dz2_own = after(cotangent, tok).astype(half)
    dz2_near = gather_first(dz2_own)
    w_up = gather_f(after(up_own.astype(half), tok))
    a1 = flat(near) + [first_norm(x) for x in tok[far]]
    joined = joined_rows(a1, w_qkv, bias_qkv, "qkv")
    w_down = gather_f(after(down_own.astype(half), joined))
    attended = attn_forward(joined, inv, slopes, heads, scale)
    mine = [attended[j * rows : (j + 1) * rows] for j in range(CTX)]
    mine = after(mine, dz2_near)
    mine = [mine[0]] + [swap(mine[j], j) for j in range(1, CTX)]
    ob = jnp.concatenate(xor_order(mine, c), axis=1)
    y1 = tokens.astype(single) + dot_nn(ob, w_out) + bias_o

    normed2, inv2 = norm_parts(y1)
    dz2 = gather_second(dz2_own, after(dz2_near, ob))
    a2_own = (normed2 * gain2 + shift2).astype(half)
    gb, slope = [None] * CTX, [None] * CTX
    gb[0], slope[0] = up_gelu([a2_own], w_up, bias_u, "up_gelu_0")
    last = gb[0]
    a2 = gather_second(a2_own, after(gather_first(a2_own), last))
    for j in range(1, CTX):
        gb[j], slope[j] = up_gelu(after(a2[j], last), w_up, bias_u, f"up_gelu_{j}")
        last = gb[j]
    down_grad = outer(flat(gb), flat(dz2), "down_grad")
    down_part = scatter_f(down_grad)
    w_down = after(w_down, down_grad)

    du, dh2, mix = [None] * CTX, [None] * CTX, [None] * CTX
    if CTX == 4:
        du, dh2, arrived, up_grad, mix_first = feed_back(
            flat(dz2), flat(slope), flat(a2), gb[far], w_down, w_up
        )
        du = [du]
    else:
        for j in range(CTX):
            du[j] = hidden_back(dz2[j], w_down, slope[j], f"du_{j}")
            dh2[j] = plain(du[j], w_up, True, half if j else single, f"dh2_{j}")[0]
        arrived = scatter_send(dh2[1:])
        dh2 = dh2[0]
        up_grad = outer(flat(a2), flat(du), "up_grad")
        mix[far] = plain(gb[far], w_down, False, half, "mix_far")[0]
    up_part = scatter_f(up_grad)
    dh2 = total_of(dh2, arrived)
    up_bias_grad = sum(jnp.sum(x.astype(single), axis=0) for x in flat(du))
    down_bias_grad = jnp.sum(dz2_own.astype(single), axis=0)
    gain2_grad = jnp.sum(dh2 * normed2, axis=0)
    shift2_grad = jnp.sum(dh2, axis=0)
    dy1 = cotangent + norm_back(normed2, inv2, gain2, dh2)

    dz1 = dy1.astype(half)
    dattn = dot_nt(dz1, w_out).astype(half)
    out_bias_grad = jnp.sum(dz1.astype(single), axis=0)
    if CTX == 4:
        dattn, out_grad, one_lo, one_hi, two_lo, two_hi = heads_back(
            dattn, ob, dz1, gb[1][0], gb[2][0], w_down, *mix_first, part
        )
    else:
        dattn = xor_order([dattn[:, s * part : (s + 1) * part] for s in range(CTX)], c)
        dattn = [dattn[0]] + [swap(dattn[j], j) for j in range(1, CTX)]
        dattn = jnp.concatenate(dattn, axis=0)
        out_grad = outer([ob], [dz1], "out_grad")
        for j in mid:
            mix[j] = plain(gb[j], w_down, False, half, f"mix_{j}")[0]
    out_part = scatter_f(out_grad)
    down_own = after(down_part, dattn)
    down_near = gather_first(down_own)
    dqkv = attn_backward(joined, dattn, inv, slopes, heads, scale)
    if CTX == 4:
        lows = [swap(one_lo, 1), swap(two_lo, 2)]
        dqkv = after(dqkv, lows, up_part)
        dh1, arrived, qkv_grad, mix[0] = qkv_back(dqkv, w_qkv, a1, gb[0][0], w_down)
    else:
        dh1 = [
            plain([(dqkv, rows, j)], w_qkv, True, half if j else single, f"dh1_{j}")[0]
            for j in range(CTX)
        ]
        arrived = scatter_send(dh1[1:])
        dh1 = dh1[0]
        qkv_grad = outer(a1, [(dqkv, rows, j) for j in range(CTX)], "qkv_grad")
        mix[0] = plain(gb[0], w_down, False, single, "mix_0")[0]
    dh1 = total_of(after(dh1, down_near), arrived)
    down_out = gather_second(down_own, after(down_near, dh1))
    mixed = y1 + bias_d + mix[0]
    if CTX == 4:
        n = rows // 2
        one_hi, two_hi = after((one_hi, two_hi), dh1)
        lows = total_of(mixed[:n], lows)
        mixed = jnp.concatenate([lows, total_of(mixed[n:], [swap(one_hi, 1), swap(two_hi, 2)])])
    else:
        mixed = total_of(mixed, scatter_send(mix[1:]))
    down_out = lay_out(0, down_out, c, width // min(width, 512))
    up_out = gather_ctx(after(up_part, dh1))
    out_part = after(out_part, up_out)
    up_out = lay_out(1, up_out, c, nf)
    sums = jnp.sum(dqkv.astype(single), axis=0)
    normed1_own, inv1_own = norm_parts(tokens.astype(single))
    gain1_grad = jnp.sum(dh1 * normed1_own, axis=0)
    shift1_grad = jnp.sum(dh1, axis=0)
    input_grad = dy1 + norm_back(normed1_own, inv1_own, gain1, dh1)

    qkv_part = scatter_f(after(qkv_grad, input_grad))
    bit = 1
    while bit < CTX:
        out_part = out_part.astype(half)
        out_part = out_part.astype(single) + swap(out_part, bit).astype(single)
        bit *= 2
    out_out = out_part
    qkv_out = lay_out(1, gather_ctx(qkv_part), c, 3)

    def spread(x, inner):
        x = x.reshape(-1, 1, inner)
        mask = (jnp.arange(CTX) == c)[None, :, None]
        return jnp.where(mask, x, 0.0).reshape(-1)

    def reduced(items, call):
        sizes = [x.shape[0] // nf for x in items]
        x = jnp.concatenate([x.reshape(nf, -1) for x in items], axis=1)
        x = jnp.pad(x, ((0, 0), (0, -x.shape[1] % 1024))).reshape(nf, -1, 128)
        x = reduce_small(x, nf, CTX, call).reshape(-1)
        out, at = [], 0
        for n in sizes:
            out.append(x[at : at + n])
            at += n
        return out

    sums_in = [out_bias_grad, gain2_grad, shift2_grad, down_bias_grad, spread(up_bias_grad, fpart)]
    sums_in += [gain1_grad, shift1_grad, spread(sums[:part], part), spread(sums[2 * part :], part)]
    sums_out = reduced(sums_in, 2)
    out_bias_out, gain2_out, shift2_out, down_bias_out, up_bias_out = sums_out[:5]
    gain1_out, shift1_out, q_bias_out, v_bias_out = sums_out[5:]
    return (
        mixed,
        input_grad,
        gain1_out,
        shift1_out,
        qkv_out,
        q_bias_out,
        v_bias_out,
        out_out,
        out_bias_out,
        gain2_out,
        shift2_out,
        up_out,
        up_bias_out,
        down_out,
        down_bias_out,
    )


def solution(mesh):
    rows, flat = P(("ctx", "fsdp"), None), P("fsdp")
    mat = P("fsdp", None)
    in_specs = (
        rows,
        rows,
        mat,
        mat,
        flat,
        flat,
        mat,
        flat,
        flat,
        mat,
        flat,
        flat,
        flat,
        mat,
        flat,
        mat,
        flat,
    )
    out_specs = (
        rows,
        rows,
        flat,
        flat,
        mat,
        flat,
        flat,
        mat,
        flat,
        flat,
        flat,
        mat,
        flat,
        mat,
        flat,
    )
    return jax.shard_map(
        per_device, mesh=mesh, in_specs=in_specs, out_specs=out_specs, check_vma=False
    )
```

```python
import functools
import math

import jax
import jax.numpy as jnp
from jax import lax
from jax.experimental import pallas as pl
from jax.experimental.pallas import tpu as pltpu
from jax.sharding import PartitionSpec as P

HEADS = 16
SPAN = 128
SEQ_BLOCKS = 8

norm_eps = 1e-05
gelu_coef = 0.7978845608028654
LOG2E = 1.4426950408889634

half = jnp.bfloat16
single = jnp.float32


def dot_nn(a, b):
    return lax.dot_general(a, b, (((1,), (0,)), ((), ())), preferred_element_type=single)


def dot_nt(a, b):
    return lax.dot_general(a, b, (((1,), (1,)), ((), ())), preferred_element_type=single)


def dot_tn(a, b):
    return lax.dot_general(a, b, (((0,), (0,)), ((), ())), preferred_element_type=single)


def norm_parts(values):
    center = values - jnp.mean(values, axis=-1, keepdims=True)
    spread = jnp.mean(center * center, axis=-1, keepdims=True)
    inv = lax.rsqrt(spread + norm_eps)
    return center * inv, inv


def norm_back(normed, inv, gain, grad):
    dn = grad * gain
    return inv * (
        dn
        - jnp.mean(dn, axis=-1, keepdims=True)
        - normed * jnp.mean(dn * normed, axis=-1, keepdims=True)
    )


def gelu_both(v):
    t = jnp.tanh(gelu_coef * (v + 0.044715 * v * v * v))
    value = 0.5 * v * (1.0 + t)
    slope = 0.5 * (1.0 + t) + 0.5 * v * (1.0 - t * t) * gelu_coef * (1.0 + 3 * 0.044715 * v * v)
    return value, slope


def swap(x, mask):
    n = lax.axis_size("ctx")
    return lax.ppermute(x, "ctx", [(i, i ^ mask) for i in range(n)])


def gather_first(x):
    count = lax.axis_size("ctx")
    return [swap(x, j) for j in range(1, 3 if count == 4 else count)]


def gather_second(x, arrived):
    if lax.axis_size("ctx") != 4:
        return [[x]] + [[p] for p in arrived]
    one, two = arrived
    n = x.shape[0] // 2
    return [[x], [one], [two], [swap(one[:n], 2), swap(two[n:], 1)]]


def gather_ctx(x):
    return gather_second(x, gather_first(x))


def scatter_first(far):
    if lax.axis_size("ctx") != 4:
        return None
    return swap(far[0], 1), swap(far[1], 2)


def scatter_second(pieces, first):
    if first is None:
        return pieces[1:]
    p1, p2 = pieces[1], pieces[2]
    n = p1.shape[0] // 2
    from_x, from_y = first
    p1 = jnp.concatenate(
        [p1[:n], (p1[n:].astype(single) + from_y.astype(single)).astype(half)], axis=0
    )
    p2 = jnp.concatenate(
        [(p2[:n].astype(single) + from_x.astype(single)).astype(half), p2[n:]], axis=0
    )
    return [p1, p2]


def scatter_send(sent):
    return [swap(x, j + 1) for j, x in enumerate(sent)]


def total_of(own, arrived):
    for x in arrived:
        own = own + x.astype(single)
    return own


def xor_order(items, c):
    bit = 1
    while bit < len(items):
        on = (c & bit) == bit
        items = [jnp.where(on, items[i ^ bit], items[i]) for i in range(len(items))]
        bit *= 2
    return items


TILE = 256


def attn_scores(q_refs, k_refs, i, scale, slope):
    q = jnp.concatenate([q_refs[2 * i][...], q_refs[2 * i + 1][...]], axis=0)
    k = jnp.concatenate([r[...] for r in k_refs[: 2 * i + 2]], axis=0)
    n = TILE * (i + 1)
    col = lax.broadcasted_iota(jnp.int32, (1, n), 1) - (n - 1)
    s = dot_nt(q, k) * (scale * LOG2E) + (slope * LOG2E) * col.astype(single)
    row_at = lax.broadcasted_iota(jnp.int32, (TILE, TILE), 0)
    col_at = lax.broadcasted_iota(jnp.int32, (TILE, TILE), 1)
    last = jnp.where(col_at <= row_at, s[:, n - TILE :], -1e30)
    s = last if i == 0 else jnp.concatenate([s[:, : n - TILE], last], axis=1)
    e = jnp.exp2(s - jnp.max(s, axis=1, keepdims=True))
    return q, k, e, 1.0 / jnp.sum(e, axis=1, keepdims=True)


class Rows:
    def __init__(self, inv_ref, stage, out, sems, kinds):
        self.inv, self.stage, self.out, self.sems, self.kinds = inv_ref, stage, out, sems, kinds
        self.heads = pl.num_programs(1)
        self.step = pl.program_id(0) * self.heads + pl.program_id(1)
        self.slot = lax.rem(self.step, 2)

    def copies(self, step):
        slot = lax.rem(step, 2)
        seq, head = step // self.heads, lax.rem(step, self.heads)
        for kind in range(self.kinds):
            col = pl.multiple_of((kind * self.heads + head) * 128, 128)
            for j in range(SEQ_BLOCKS):
                row = pl.multiple_of(self.inv[seq * SEQ_BLOCKS + j] * SPAN, SPAN)
                yield pltpu.make_async_copy(
                    self.stage.at[slot, kind, pl.ds(j * SPAN, SPAN)],
                    self.out.at[pl.ds(row, SPAN), pl.ds(col, 128)],
                    self.sems.at[slot, kind * SEQ_BLOCKS + j],
                )

    def wait(self, step):
        for copy in self.copies(step):
            copy.wait()

    def open(self):
        @pl.when(self.step >= 2)
        def _():
            self.wait(self.step - 2)

    def close(self):
        for copy in self.copies(self.step):
            copy.start()

        @pl.when(self.step == 2 * self.heads - 1)
        def _():
            self.wait(self.step - 1)
            self.wait(self.step)


def attn_fwd_kernel(scale, inv_ref, slope_ref, *refs):
    q_refs, k_refs, v_refs = refs[:8], refs[8:16], refs[16:24]
    out, stage, sems = refs[24:]
    slope = slope_ref[pl.program_id(1)]
    rows = Rows(inv_ref, stage, out, sems, 1)
    rows.open()
    for i in range(4):
        q, k, e, r = attn_scores(q_refs, k_refs, i, scale, slope)
        v = jnp.concatenate([x[...] for x in v_refs[: 2 * i + 2]], axis=0)
        o = dot_nn((e * r).astype(half), v)
        stage[rows.slot, 0, TILE * i : TILE * (i + 1), :] = o.astype(half)
    rows.close()


def attn_bwd_kernel(scale, inv_ref, slope_ref, *refs):
    q_refs, k_refs, v_refs, g_refs = refs[:8], refs[8:16], refs[16:24], refs[24:32]
    out, stage, sems, dk_acc, dv_acc = refs[32:]
    slope = slope_ref[pl.program_id(1)]
    rows = Rows(inv_ref, stage, out, sems, 3)
    rows.open()
    for i in (3, 2, 1, 0):
        q, k, e, r = attn_scores(q_refs, k_refs, i, scale, slope)
        n = TILE * (i + 1)
        v = jnp.concatenate([x[...] for x in v_refs[: 2 * i + 2]], axis=0)
        g = jnp.concatenate([g_refs[2 * i][...], g_refs[2 * i + 1][...]], axis=0)
        p = e * r
        dp = dot_nt(g, v)
        delta = jnp.sum(p * dp, axis=1, keepdims=True)
        ds = (p * (dp - delta)).astype(half)
        pb = p.astype(half)
        dq = (dot_nn(ds, k) * scale).astype(half)
        stage[rows.slot, 0, TILE * i : TILE * (i + 1), :] = dq
        dk = dot_tn(ds, q)
        dv = dot_tn(pb, g)
        if i == 3:
            dk_acc[...] = dk
            dv_acc[...] = dv
        else:
            dk_acc[:n, :] += dk
            dv_acc[:n, :] += dv
    stage[rows.slot, 1] = (dk_acc[...] * scale).astype(half)
    stage[rows.slot, 2] = dv_acc[...].astype(half)
    rows.close()


def block_specs(offset):
    def one(j):
        return pl.BlockSpec(
            (SPAN, 128), lambda s, h, inv, slope: (inv[s * SEQ_BLOCKS + j], offset + h)
        )

    return [one(j) for j in range(SEQ_BLOCKS)]


def attn_call(kernel, kinds, joined, extra, extra_specs, scratch, inv, slopes, heads, cost, name):
    rows = joined.shape[0]
    specs = block_specs(0) + block_specs(heads) + block_specs(2 * heads) + extra_specs
    return pl.pallas_call(
        kernel,
        grid_spec=pltpu.PrefetchScalarGridSpec(
            num_scalar_prefetch=2,
            grid=(2, heads),
            in_specs=specs,
            out_specs=pl.BlockSpec(memory_space=pl.ANY),
            scratch_shapes=[
                pltpu.VMEM((2, kinds, rows // 2, 128), half),
                pltpu.SemaphoreType.DMA((2, kinds * SEQ_BLOCKS)),
            ]
            + scratch,
        ),
        out_shape=jax.ShapeDtypeStruct((rows, kinds * heads * 128), half),
        compiler_params=pltpu.CompilerParams(vmem_limit_bytes=48 * 1024 * 1024),
        cost_estimate=cost,
        name=name,
    )(inv, slopes, *([joined] * 24), *extra)


def attn_forward(joined, inv, slopes, heads, scale):
    kernel = functools.partial(attn_fwd_kernel, scale)
    cost = hint(20 * 10**9, joined.shape[0] * heads * 128 * 8)
    return attn_call(
        kernel, 1, joined, [], [], [], inv, slopes, heads, cost, "attn_forward"
    )


def attn_backward(joined, grad, inv, slopes, heads, scale):
    kernel = functools.partial(attn_bwd_kernel, scale)
    cost = hint(40 * 10**9, joined.shape[0] * heads * 128 * 14)
    sums = [pltpu.VMEM((joined.shape[0] // 2, 128), single)] * 2
    return attn_call(
        kernel,
        3,
        joined,
        [grad] * 8,
        block_specs(0),
        sums,
        inv,
        slopes,
        heads,
        cost,
        "attn_backward",
    )


HINT = 0.001


def block_of(x):
    return x if isinstance(x, tuple) else (x, x.shape[0], 0)


def hint(flops, bytes_accessed):
    return pl.CostEstimate(
        flops=int(HINT * flops), bytes_accessed=int(HINT * bytes_accessed), transcendentals=0
    )


def rows_kernel(dot, epilogue, count, extra, *refs):
    left, w_ref = refs[:count], refs[count]
    extras = refs[count + 1 : count + 1 + extra]
    outs = refs[count + 1 + extra :]
    for i in range(count):
        epilogue(i, dot(left[i][...], w_ref[...]), extras, outs)


def rows_matmul(blocks, w, transposed, extras, outs, epilogue, name, tile=512):
    blocks = [block_of(x) for x in blocks]
    extras = [block_of(x) for x in extras]
    n = w.shape[0] if transposed else w.shape[1]
    k = w.shape[1] if transposed else w.shape[0]
    t = math.gcd(n, tile)
    w_spec = (
        pl.BlockSpec((t, k), lambda i: (i, 0)) if transposed else pl.BlockSpec((k, t), lambda i: (0, i))
    )
    rows = sum(x[1] for x in blocks)
    return pl.pallas_call(
        functools.partial(
            rows_kernel, dot_nt if transposed else dot_nn, epilogue, len(blocks), len(extras)
        ),
        grid=(n // t,),
        in_specs=[pl.BlockSpec((x[1], k), lambda i, at=x[2]: (at, 0)) for x in blocks]
        + [w_spec]
        + [pl.BlockSpec((x[1], t), lambda i, at=x[2]: (at, i)) for x in extras],
        out_specs=[pl.BlockSpec((r, t), lambda i: (0, i)) for r, _ in outs],
        out_shape=[jax.ShapeDtypeStruct((r, n), d) for r, d in outs],
        compiler_params=pltpu.CompilerParams(vmem_limit_bytes=52 * 1024 * 1024),
        cost_estimate=hint(2 * rows * n * k, 2 * n * k + 4 * rows * (n + k)),
        name=name,
    )(*[x[0] for x in blocks], w, *[x[0] for x in extras])


def plain(blocks, w, transposed, dtype, name):
    def epilogue(i, x, extras, outs):
        outs[i][...] = x.astype(dtype)

    outs = [(block_of(x)[1], dtype) for x in blocks]
    return rows_matmul(blocks, w, transposed, [], outs, epilogue, name)


def joined_rows(blocks, w, bias, name):
    sizes = [block_of(x)[1] for x in blocks]

    def epilogue(i, x, extras, outs):
        at = sum(sizes[:i])
        outs[0][at : at + sizes[i], :] = (x + extras[0][...]).astype(half)

    bias = bias.reshape(1, -1)
    return rows_matmul(blocks, w, False, [bias], [(sum(sizes), half)], epilogue, name)[0]


def up_gelu(blocks, w, bias, name):
    count = len(blocks)

    def epilogue(i, x, extras, outs):
        value, slope = gelu_both(x + extras[0][...])
        outs[i][...] = value.astype(half)
        outs[count + i][...] = slope.astype(half)

    outs = [(block_of(x)[1], half) for x in blocks] * 2
    out = rows_matmul(blocks, w, False, [bias.reshape(1, -1)], outs, epilogue, name)
    return out[:count], out[count:]


def hidden_back(blocks, w, slopes, name):
    def epilogue(i, x, extras, outs):
        x = x.astype(half).astype(single) * extras[i][...].astype(single)
        outs[i][...] = x.astype(half)

    outs = [(block_of(x)[1], half) for x in blocks]
    return rows_matmul(blocks, w, True, slopes, outs, epilogue, name)


def outer_kernel(count, *refs):
    out = refs[-1]
    total = None
    for i in range(count):
        x = dot_tn(refs[i][...], refs[count + i][...])
        total = x if total is None else total + x
    out[...] = total.astype(half)


def outer(left, right, name):
    left = [block_of(x) for x in left]
    right = [block_of(x) for x in right]
    m, n = left[0][0].shape[1], right[0][0].shape[1]
    tm = math.gcd(m, 1024)
    tn = n // 2 if n % 256 == 0 and n > 1024 else n
    rows = sum(x[1] for x in left)
    return pl.pallas_call(
        functools.partial(outer_kernel, len(left)),
        grid=(m // tm, n // tn),
        in_specs=[pl.BlockSpec((x[1], tm), lambda i, j, at=x[2]: (at, i)) for x in left]
        + [pl.BlockSpec((x[1], tn), lambda i, j, at=x[2]: (at, j)) for x in right],
        out_specs=pl.BlockSpec((tm, tn), lambda i, j: (i, j)),
        out_shape=jax.ShapeDtypeStruct((m, n), half),
        compiler_params=pltpu.CompilerParams(vmem_limit_bytes=52 * 1024 * 1024),
        cost_estimate=hint(2 * rows * m * n, 2 * rows * (m + n) + 2 * m * n),
        name=name,
    )(*[x[0] for x in left], *[x[0] for x in right])


def partner(mask):
    c = lax.axis_index("ctx")
    if mask == 1:
        return c + 1 - 2 * lax.rem(c, 2)
    return lax.rem(c + 2, 4) if mask == 2 else 3 - c


def greet(masks):
    barrier = pltpu.get_barrier_semaphore()
    for mask in masks:
        pl.semaphore_signal(
            barrier,
            inc=1,
            device_id={"ctx": partner(mask)},
            device_id_type=pl.DeviceIdType.MESH,
        )
    pl.semaphore_wait(barrier, len(masks))


class Moves:
    def __init__(self, send_sem, recv_sem):
        self.send_sem, self.recv_sem, self.used = send_sem, recv_sem, 0

    def start(self, src, dst, mask):
        copy = pltpu.make_async_remote_copy(
            src_ref=src,
            dst_ref=dst,
            send_sem=self.send_sem.at[self.used],
            recv_sem=self.recv_sem.at[self.used],
            device_id={"ctx": partner(mask)},
            device_id_type=pl.DeviceIdType.MESH,
        )
        self.used += 1
        copy.start()
        return copy


def multiply(lefts, w, transposed, extras, outs, epilogue, tile=512):
    k = lefts[0].shape[1]
    n = w.shape[0] if transposed else w.shape[1]
    t = math.gcd(n, tile)
    w_spec = (
        pl.BlockSpec((t, k), lambda i: (i, 0)) if transposed else pl.BlockSpec((k, t), lambda i: (0, i))
    )
    dot = dot_nt if transposed else dot_nn

    def body(*refs):
        rows_kernel(dot, epilogue, len(lefts), len(extras), *refs)

    pltpu.emit_pipeline(
        body,
        grid=(n // t,),
        in_specs=[pl.BlockSpec((x.shape[0], k), lambda i: (0, 0)) for x in lefts]
        + [w_spec]
        + [pl.BlockSpec((x.shape[0], t), lambda i: (0, i)) for x in extras],
        out_specs=[pl.BlockSpec((x.shape[0], t), lambda i: (0, i)) for x in outs],
    )(*lefts, w, *extras, *outs)


def store(i, x, extras, outs):
    outs[i][...] = x.astype(outs[i].dtype)


def store_sum(i, x, extras, outs):
    outs[i][...] = (x + extras[i][...].astype(single)).astype(outs[i].dtype)


def store_passed(i, x, extras, outs):
    if i in (1, 2):
        x = x + extras[i - 1][...].astype(single)
    outs[i][...] = x.astype(outs[i].dtype)


def store_hidden(i, x, extras, outs):
    outs[i][...] = (x.astype(half).astype(single) * extras[i][...].astype(single)).astype(half)


def outer_on(lefts, rights, out):
    m, n = out.shape
    tm = math.gcd(m, 1024)
    tn = n // 2 if n % 256 == 0 and n > 1024 else n

    def body(*refs):
        outer_kernel(len(lefts), *refs)

    pltpu.emit_pipeline(
        body,
        grid=(m // tm, n // tn),
        in_specs=[pl.BlockSpec((x.shape[0], tm), lambda i, j: (0, i)) for x in lefts]
        + [pl.BlockSpec((x.shape[0], tn), lambda i, j: (0, j)) for x in rights],
        out_specs=[pl.BlockSpec((tm, tn), lambda i, j: (i, j))],
    )(*lefts, *rights, out)


def halves(ref):
    n = ref.shape[0] // 2
    return ref.at[pl.ds(0, n)], ref.at[pl.ds(n, n)]


def moving_call(kernel, operands, outs, moves, call, flops, name):
    anywhere = pl.BlockSpec(memory_space=pl.ANY)
    sems = pltpu.SemaphoreType.DMA((moves,))
    return pl.pallas_call(
        kernel,
        in_specs=[anywhere] * len(operands),
        out_specs=[anywhere] * len(outs),
        out_shape=[jax.ShapeDtypeStruct(shape, dtype) for shape, dtype in outs],
        scratch_shapes=[sems, sems],
        compiler_params=pltpu.CompilerParams(
            collective_id=call, has_side_effects=True, vmem_limit_bytes=52 * 1024 * 1024
        ),
        cost_estimate=hint(flops, 0),
        name=name,
    )(*operands)


def store_biased(i, x, extras, outs):
    outs[i][...] = (x + extras[0][...]).astype(half)


def qkv_kernel(*refs):
    tok, gain, shift, a1, w_qkv, bias = refs[0:2], refs[2], refs[3], refs[4:7], refs[7], refs[8]
    dz_lo, dz_hi = refs[9:11]
    joined, far, one_lo, two_hi = refs[11], refs[12:14], refs[14], refs[15]
    moves = Moves(*refs[16:18])
    n, width = tok[0].shape
    greet((1, 2))
    copies = [moves.start(dz_lo, one_lo, 1), moves.start(dz_hi, two_hi, 2)]

    def norm(x_lo, x_hi, g, s, o_lo, o_hi):
        for x, o in ((x_lo, o_lo), (x_hi, o_hi)):
            normed, _ = norm_parts(x[...].astype(single))
            o[...] = (normed * g[...] + s[...]).astype(half)

    t = math.gcd(n, 64)
    block = pl.BlockSpec((t, width), lambda i: (i, 0))
    row = pl.BlockSpec((1, width), lambda i: (0, 0))
    pltpu.emit_pipeline(
        norm, grid=(n // t,), in_specs=[block, block, row, row], out_specs=[block, block]
    )(*tok, gain, shift, *far)
    lefts, outs, at = [*a1, *far], [], 0
    for x in lefts:
        outs.append(joined.at[pl.ds(at, x.shape[0])])
        at += x.shape[0]
    multiply(lefts, w_qkv, False, [bias], outs, store_biased)
    for copy in copies:
        copy.wait()


def qkv_forward(tok, gain, shift, a1, w_qkv, bias, dz_lo, dz_hi):
    n, width = tok[0].shape
    k = w_qkv.shape[1]
    outs = [((8 * n, k), half)] + [((n, width), half)] * 4
    out = moving_call(
        qkv_kernel,
        [*tok, gain.reshape(1, -1), shift.reshape(1, -1), *a1, w_qkv, bias.reshape(1, -1), dz_lo, dz_hi],
        outs,
        2,
        7,
        16 * n * width * k,
        "qkv",
    )
    return out[0], out[1:3], out[3:5]


def feed_pass(dz, slope, w_down, w_up, du, total):
    n, width = dz[0].shape
    wide = w_down.shape[0]
    t = math.gcd(wide, 512)
    total[...] = jnp.zeros_like(total)

    def body(dz_lo, dz_hi, down, up, slope_lo, slope_hi, du_lo, du_hi):
        for i, x, s, d in ((0, dz_lo, slope_lo, du_lo), (1, dz_hi, slope_hi, du_hi)):
            grad = dot_nt(x[...], down[...]).astype(half).astype(single)
            grad = (grad * s[...].astype(single)).astype(half)
            d[...] = grad
            total[i * n : (i + 1) * n, :] += dot_nt(grad, up[...])

    pltpu.emit_pipeline(
        body,
        grid=(wide // t,),
        in_specs=[pl.BlockSpec((n, width), lambda i: (0, 0))] * 2
        + [pl.BlockSpec((t, width), lambda i: (i, 0)), pl.BlockSpec((width, t), lambda i: (0, i))]
        + [pl.BlockSpec((n, t), lambda i: (0, i))] * 2,
        out_specs=[pl.BlockSpec((n, t), lambda i: (0, i))] * 2,
    )(*dz, w_down, w_up, *slope, *du)


def feed_back_kernel(*refs):
    dz, slope, (w_down, w_up) = refs[0:8], refs[8:13], refs[13:15]
    du, own, p1_hi, p2_lo, land1_lo, land2_hi = refs[15:20], *refs[20:25]
    total, far, near, rest, from_x, from_y = refs[25:31]
    moves = Moves(*refs[31:33])
    local = refs[33]
    n = from_x.shape[0]
    lo, hi = pl.ds(0, n), pl.ds(n, n)
    (s1_lo, s1_hi), (s2_lo, s2_hi) = halves(slope[1]), halves(slope[2])
    (d1_lo, d1_hi), (d2_lo, d2_hi) = halves(du[1]), halves(du[2])
    greet((1, 2))
    feed_pass(dz[6:8], slope[3:5], w_down, w_up, du[3:5], total)
    far[...] = total[...].astype(half)
    first = [moves.start(far.at[lo], from_x, 1), moves.start(far.at[hi], from_y, 2)]
    feed_pass([dz[2], dz[5]], [s1_lo, s2_hi], w_down, w_up, [d1_lo, d2_hi], total)
    near[...] = total[...].astype(half)
    second = [moves.start(near.at[lo], land1_lo, 1), moves.start(near.at[hi], land2_hi, 2)]
    feed_pass([dz[3], dz[4]], [s1_hi, s2_lo], w_down, w_up, [d1_hi, d2_lo], total)
    for copy in first:
        copy.wait()
    rest[lo] = (total[lo] + from_y[...].astype(single)).astype(half)
    rest[hi] = (total[hi] + from_x[...].astype(single)).astype(half)
    stores = [
        pltpu.make_async_copy(rest.at[lo], p1_hi, local.at[0]),
        pltpu.make_async_copy(rest.at[hi], p2_lo, local.at[1]),
    ]
    for copy in stores:
        copy.start()
    feed_pass(dz[0:2], halves(slope[0]), w_down, w_up, halves(du[0]), total)
    stores.append(pltpu.make_async_copy(total, own, local.at[2]))
    stores[-1].start()
    for copy in second + stores:
        copy.wait()


def feed_back(dz, slope, w_down, w_up):
    n, width = dz[0].shape
    rows, wide = 2 * n, w_down.shape[0]
    anywhere = pl.BlockSpec(memory_space=pl.ANY)
    outs = [((r, wide), half) for r in (rows, rows, rows, n, n)]
    outs += [((rows, width), single)] + [((n, width), half)] * 4
    sems = pltpu.SemaphoreType.DMA((4,))
    out = pl.pallas_call(
        feed_back_kernel,
        in_specs=[anywhere] * 15,
        out_specs=[anywhere] * len(outs),
        out_shape=[jax.ShapeDtypeStruct(shape, dtype) for shape, dtype in outs],
        scratch_shapes=[pltpu.VMEM((rows, width), single)]
        + [pltpu.VMEM((rows, width), half)] * 3
        + [pltpu.VMEM((n, width), half)] * 2
        + [sems, sems, pltpu.SemaphoreType.DMA((3,))],
        compiler_params=pltpu.CompilerParams(
            collective_id=3, has_side_effects=True, vmem_limit_bytes=56 * 1024 * 1024
        ),
        cost_estimate=hint(16 * rows * width * wide, 0),
        name="feed_back",
    )(*dz, *slope, w_down, w_up)
    return out[0:5], out[5], out[6:8], out[8:10]


def up_back_kernel(*refs):
    p1_hi, p2_lo, a2, du = refs[0], refs[1], refs[2:7], refs[7:12]
    land1_hi, land2_lo, up_grad = refs[12:15]
    moves = Moves(*refs[15:17])
    greet((1, 2))
    copies = [moves.start(p1_hi, land1_hi, 1), moves.start(p2_lo, land2_lo, 2)]
    outer_on(a2, du, up_grad)
    for copy in copies:
        copy.wait()


def up_back(p1_hi, p2_lo, a2, du):
    m, n = a2[0].shape[1], du[0].shape[1]
    outs = [(p1_hi.shape, half)] * 2 + [((m, n), half)]
    flops = 8 * a2[0].shape[0] * m * n
    return moving_call(up_back_kernel, [p1_hi, p2_lo, *a2, *du], outs, 2, 6, flops, "up_back")


def heads_back_kernel(part, *refs):
    dattn, ob, dz1, gb1, gb2, w_down, mix_x, mix_y = refs[0:8]
    got, out_grad = refs[8:10]
    mix = refs[10:14]
    moves = Moves(*refs[14:16])
    local = refs[16]
    rows = dattn.shape[0]
    c = lax.axis_index("ctx")

    def columns(of):
        return dattn.at[:, pl.ds(pl.multiple_of(of * part, part), part)]

    greet((1, 2, 3))
    copies = []
    for mask in (3, 1, 2):
        at = got.at[pl.ds(mask * rows, rows)]
        copies.append(moves.start(columns(partner(mask)), at, mask))
    own = pltpu.make_async_copy(columns(c), got.at[pl.ds(0, rows)], local)
    own.start()
    outer_on([ob], [dz1], out_grad)
    multiply(
        [*halves(gb1), *halves(gb2)],
        w_down,
        False,
        [mix_y, mix_x],
        mix,
        store_passed,
    )
    own.wait()
    for copy in copies:
        copy.wait()


def heads_back(dattn, ob, dz1, gb1, gb2, w_down, mix_x, mix_y, part):
    rows, width = dattn.shape
    anywhere = pl.BlockSpec(memory_space=pl.ANY)
    sems = pltpu.SemaphoreType.DMA((3,))
    outs = [((4 * rows, part), half), ((width, width), half)] + [((rows // 2, width), half)] * 4
    return pl.pallas_call(
        functools.partial(heads_back_kernel, part),
        in_specs=[anywhere] * 8,
        out_specs=[anywhere] * len(outs),
        out_shape=[jax.ShapeDtypeStruct(shape, dtype) for shape, dtype in outs],
        scratch_shapes=[sems, sems, pltpu.SemaphoreType.DMA],
        compiler_params=pltpu.CompilerParams(
            collective_id=4, has_side_effects=True, vmem_limit_bytes=52 * 1024 * 1024
        ),
        cost_estimate=hint(10 * rows * width * width, 0),
        name="heads_back",
    )(dattn, ob, dz1, gb1, gb2, w_down, mix_x, mix_y)


def qkv_back_kernel(*refs):
    dqkv, w_qkv = refs[0:2]
    a1, gb_own, w_down = refs[2:7], refs[7], refs[8]
    own, p3, p1, p2, from_x, from_y, land1, land2, qkv_grad, mix_own = refs[9:19]
    moves = Moves(*refs[19:21])
    rows = own.shape[0]
    n = rows // 2

    def block(k):
        return dqkv.at[pl.ds(k * n, n)]

    greet((1, 2))
    (p3_lo, p3_hi), (p1_lo, p1_hi), (p2_lo, p2_hi) = halves(p3), halves(p1), halves(p2)
    (land1_lo, land1_hi), (land2_lo, land2_hi) = halves(land1), halves(land2)
    multiply([block(6), block(7)], w_qkv, True, [], [p3_lo, p3_hi], store)
    first = [moves.start(p3_lo, from_x, 1), moves.start(p3_hi, from_y, 2)]
    multiply([block(2), block(5)], w_qkv, True, [], [p1_lo, p2_hi], store)
    second = [moves.start(p1_lo, land1_lo, 1), moves.start(p2_hi, land2_hi, 2)]
    multiply([dqkv.at[pl.ds(0, rows)]], w_qkv, True, [], [own], store)
    multiply([gb_own], w_down, False, [], [mix_own], store)
    for copy in first:
        copy.wait()
    multiply([block(3), block(4)], w_qkv, True, [from_y, from_x], [p1_hi, p2_lo], store_sum)
    second += [moves.start(p1_hi, land1_hi, 1), moves.start(p2_lo, land2_lo, 2)]
    rights, at = [], 0
    for x in a1:
        rights.append(dqkv.at[pl.ds(at, x.shape[0])])
        at += x.shape[0]
    outer_on(a1, rights, qkv_grad)
    for copy in second:
        copy.wait()


def qkv_back(dqkv, w_qkv, a1, gb_own, w_down):
    rows, width = a1[0].shape
    wide = gb_own.shape[1]
    n = rows // 2
    outs = [((rows, width), single)] + [((rows, width), half)] * 3
    outs += [((n, width), half)] * 2 + [((rows, width), half)] * 2
    outs += [((width, dqkv.shape[1]), half), ((rows, width), single)]
    out = moving_call(
        qkv_back_kernel,
        [dqkv, w_qkv, *a1, gb_own, w_down],
        outs,
        6,
        5,
        16 * rows * width * dqkv.shape[1] + 2 * rows * width * wide,
        "qkv_back",
    )
    return out[0], out[6:8], out[8], out[9]


def lay_out_kernel(axis, layout, c_ref, *refs):
    out = refs[-1]
    for (j, row), ref in zip(layout, refs):
        x = ref[...].astype(single)
        r, w = x.shape
        if axis == 0:
            n = sum(ref.shape[0] for (k, _), ref in zip(layout, refs) if k == j)
            out[pl.ds(pl.multiple_of((c_ref[0] ^ j) * n + row, r), r), :] = x
        else:
            out[row : row + r, pl.ds(pl.multiple_of((c_ref[0] ^ j) * w, w), w)] = x


def lay_out(axis, pieces, c, groups):
    count = len(pieces)
    r = sum(x.shape[0] for x in pieces[0])
    n = pieces[0][0].shape[1]
    w = n // groups
    if w % 128:
        whole = xor_order([jnp.concatenate(p, axis=0).astype(single) for p in pieces], c)
        whole = jnp.stack([p.reshape(r, groups, w) for p in whole], axis=2)
        return whole.reshape(r, count * n)
    layout, blocks = [], []
    for j, p in enumerate(pieces):
        row = 0
        for x in p:
            layout.append((j, row))
            blocks.append(x)
            row += x.shape[0]
    out = (count * r, w) if axis == 0 else (r, count * w)
    return pl.pallas_call(
        functools.partial(lay_out_kernel, axis, layout),
        grid_spec=pltpu.PrefetchScalarGridSpec(
            num_scalar_prefetch=1,
            grid=(groups,),
            in_specs=[pl.BlockSpec((x.shape[0], w), lambda k, c: (0, k)) for x in blocks],
            out_specs=pl.BlockSpec(out, lambda k, c: (0, k)),
        ),
        out_shape=jax.ShapeDtypeStruct((out[0], out[1] * groups), single),
        compiler_params=pltpu.CompilerParams(vmem_limit_bytes=48 * 1024 * 1024),
        cost_estimate=hint(0, 6 * r * n * count),
        name="lay_out",
    )(c.reshape(1), *blocks)


def gather_small_kernel(nf, x_ref, o_ref, send_sem, recv_sem):
    f = lax.axis_index("fsdp")
    barrier = pltpu.get_barrier_semaphore()
    for d in range(1, nf):
        pl.semaphore_signal(
            barrier,
            inc=1,
            device_id={"fsdp": lax.rem(f + d, nf)},
            device_id_type=pl.DeviceIdType.MESH,
        )
    pl.semaphore_wait(barrier, nf - 1)
    copies = []
    for d in range(1, nf):
        copies.append(
            pltpu.make_async_remote_copy(
                src_ref=x_ref,
                dst_ref=o_ref.at[f],
                send_sem=send_sem.at[d],
                recv_sem=recv_sem.at[d],
                device_id={"fsdp": lax.rem(f + d, nf)},
                device_id_type=pl.DeviceIdType.MESH,
            )
        )
        copies[-1].start()
    o_ref[f] = x_ref[...]
    for copy in copies:
        copy.wait()


def gather_small(x, nf):
    return pl.pallas_call(
        functools.partial(gather_small_kernel, nf),
        out_shape=jax.ShapeDtypeStruct((nf,) + x.shape, single),
        in_specs=[pl.BlockSpec(memory_space=pltpu.VMEM)],
        out_specs=pl.BlockSpec(memory_space=pltpu.VMEM),
        scratch_shapes=[pltpu.SemaphoreType.DMA((nf,)), pltpu.SemaphoreType.DMA((nf,))],
        compiler_params=pltpu.CompilerParams(collective_id=1, has_side_effects=True),
        name="gather_small",
    )(x)


def reduce_small_kernel(nf, nc, x_ref, o_ref, land, stage, send_sem, recv_sem):
    f = lax.axis_index("fsdp")
    c = lax.axis_index("ctx")
    barrier = pltpu.get_barrier_semaphore()
    for d in range(1, nf):
        pl.semaphore_signal(
            barrier,
            inc=1,
            device_id={"fsdp": lax.rem(f + d, nf)},
            device_id_type=pl.DeviceIdType.MESH,
        )
    for d in range(1, nc):
        pl.semaphore_signal(
            barrier,
            inc=1,
            device_id={"ctx": lax.rem(c + d, nc)},
            device_id_type=pl.DeviceIdType.MESH,
        )
    pl.semaphore_wait(barrier, nf + nc - 2)
    copies = []
    for d in range(1, nf):
        to = lax.rem(f + d, nf)
        copies.append(
            pltpu.make_async_remote_copy(
                src_ref=x_ref.at[to],
                dst_ref=land.at[d],
                send_sem=send_sem.at[d],
                recv_sem=recv_sem.at[d],
                device_id={"fsdp": to},
                device_id_type=pl.DeviceIdType.MESH,
            )
        )
        copies[-1].start()
    total = x_ref[f]
    for d in range(1, nf):
        copies[d - 1].wait()
        total = total + land[d]
    stage[0] = total
    copies = []
    for d in range(1, nc):
        copies.append(
            pltpu.make_async_remote_copy(
                src_ref=stage.at[0],
                dst_ref=stage.at[d],
                send_sem=send_sem.at[nf + d],
                recv_sem=recv_sem.at[nf + d],
                device_id={"ctx": lax.rem(c + d, nc)},
                device_id_type=pl.DeviceIdType.MESH,
            )
        )
        copies[-1].start()
    for d in range(1, nc):
        copies[d - 1].wait()
        total = total + stage[d]
    o_ref[...] = total


def reduce_small(x, nf, nc, call):
    block = x.shape[1:]
    sems = pltpu.SemaphoreType.DMA((nf + nc,))
    return pl.pallas_call(
        functools.partial(reduce_small_kernel, nf, nc),
        out_shape=jax.ShapeDtypeStruct(block, single),
        in_specs=[pl.BlockSpec(memory_space=pltpu.VMEM)],
        out_specs=pl.BlockSpec(memory_space=pltpu.VMEM),
        scratch_shapes=[
            pltpu.VMEM((nf,) + block, single),
            pltpu.VMEM((nc,) + block, single),
            sems,
            sems,
        ],
        compiler_params=pltpu.CompilerParams(collective_id=call, has_side_effects=True),
        name="reduce_small",
    )(x)


def per_device(
    tokens,
    cotangent,
    lengths,
    span_place,
    ln1_gain,
    ln1_shift,
    qkv_weight,
    q_bias,
    v_bias,
    out_weight,
    out_bias,
    ln2_gain,
    ln2_shift,
    up_weight,
    up_bias,
    down_weight,
    down_bias,
):
    rows, width = tokens.shape
    CTX = lax.axis_size("ctx")
    c = lax.axis_index("ctx")
    f = lax.axis_index("fsdp")
    nf = lax.axis_size("fsdp")
    wide = up_weight.shape[1]
    part = width // CTX
    heads = HEADS // CTX
    scale = 1.0 / math.sqrt(width // HEADS)
    shard = width // nf
    fpart = wide // nf // CTX
    wpart = wide // CTX

    def columns(x, width_each, stride, count):
        return jnp.concatenate(
            [
                lax.dynamic_slice_in_dim(x, k * stride + c * width_each, width_each, axis=1)
                for k in range(count)
            ],
            axis=1,
        )

    def after(x, *others):
        return lax.optimization_barrier((x, others))[0]

    def pick(x, axis):
        return lax.dynamic_index_in_dim(x, c, axis, keepdims=False)

    def gather_f(x):
        return lax.all_gather(x, "fsdp", axis=0, tiled=True)

    qkv_own = columns(qkv_weight, part, width, 3)
    up_own = columns(up_weight, fpart, wide // nf, nf)
    down_own = lax.dynamic_slice_in_dim(down_weight, c * fpart, fpart, axis=0)
    w_qkv = gather_f(qkv_own.astype(half))
    small = jnp.concatenate(
        [ln1_gain, ln1_shift, q_bias, v_bias, out_bias, ln2_gain, ln2_shift, down_bias, up_bias]
    )
    small_len = small.shape[0]
    small = jnp.pad(small, (0, -small_len % 1024)).reshape(-1, 128)
    small_all = gather_small(small, nf).reshape(nf, -1)[:, :small_len]
    small_all = small_all.astype(half).astype(single)

    def vector(k):
        return small_all[:, k * shard : (k + 1) * shard].reshape(width)

    gain1, shift1, bias_q, bias_v, bias_o, gain2, shift2, bias_d = [vector(k) for k in range(8)]
    bias_u = pick(small_all[:, 8 * shard :].reshape(nf, CTX, fpart), 1).reshape(wpart)
    bias_qkv = jnp.concatenate(
        [pick(bias_q.reshape(CTX, part), 0), jnp.zeros((part,), single), pick(bias_v.reshape(CTX, part), 0)]
    )
    w_out = gather_f(out_weight.astype(half))

    per = rows // SPAN
    table = jnp.arange(CTX * per, dtype=jnp.int32)
    source = ((table // per) ^ c) * per + table % per
    place = jnp.sum(jnp.where(source[:, None] == table[None, :], span_place[0][None, :], 0), axis=1)
    inv = jnp.sum(jnp.where(place[None, :] == table[:, None], table[None, :], 0), axis=1)
    slopes = 2.0 ** (-8.0 * ((c * heads + jnp.arange(heads)).astype(single) + 1.0) / HEADS)

    def flat(pieces):
        return [x for p in pieces for x in p]

    def scatter_f(x):
        return lax.psum_scatter(x, "fsdp", scatter_dimension=0, tiled=True)

    far = CTX - 1
    mid = list(range(1, far))

    def first_norm(x):
        normed, _ = norm_parts(x.astype(single))
        return (normed * gain1 + shift1).astype(half)

    tok_near = after(gather_first(tokens), small_all, place, inv, slopes)
    tok = gather_second(tokens, tok_near)
    near = [[first_norm(x) for x in p] for p in tok[:far]]
    tok = after(tok, near)
    n = rows // 2
    if CTX == 4:
        cot = after(cotangent, tok)
        dz2_lo, dz2_hi = cot[:n].astype(half), cot[n:].astype(half)
    else:
        dz2_own = after(cotangent, tok).astype(half)
        dz2_rest = gather_first(dz2_own)
    w_up = gather_f(after(up_own.astype(half), tok))
    a1 = flat(near)
    if CTX == 4:
        joined, a1_far, dz2_first = qkv_forward(
            tok[far], gain1, shift1, a1, w_qkv, bias_qkv, dz2_lo, dz2_hi
        )
        a1 = a1 + list(a1_far)
        dz2_rest = after((dz2_hi, dz2_lo), joined)
        dz2_rest = [swap(dz2_rest[0], 1), swap(dz2_rest[1], 2)]
    else:
        a1 = a1 + [first_norm(x) for x in tok[far]]
        joined = joined_rows(a1, w_qkv, bias_qkv, "qkv")
    w_down = gather_f(after(down_own.astype(half), joined))
    attended = attn_forward(joined, inv, slopes, heads, scale)
    mine = [attended[j * rows : (j + 1) * rows] for j in range(CTX)]
    mine = after(mine, dz2_rest)
    mine = [mine[0]] + [swap(mine[j], j) for j in range(1, CTX)]
    ob = jnp.concatenate(xor_order(mine, c), axis=1)
    y1 = tokens.astype(single) + dot_nn(ob, w_out) + bias_o

    normed2, inv2 = norm_parts(y1)
    if CTX == 4:
        one_lo, two_hi = after(dz2_first, ob)
        one_hi, two_lo = dz2_rest
        dz2 = [[dz2_lo, dz2_hi], [one_lo, one_hi], [two_lo, two_hi], [swap(one_lo, 2), swap(two_hi, 1)]]
    else:
        dz2 = [[dz2_own]] + [[x] for x in dz2_rest]
    a2_own = (normed2 * gain2 + shift2).astype(half)
    gb, slope = [None] * CTX, [None] * CTX
    gb[0], slope[0] = up_gelu([a2_own], w_up, bias_u, "up_gelu_0")
    last = gb[0]
    a2 = gather_second(a2_own, after(gather_first(a2_own), last))
    for j in range(1, CTX):
        gb[j], slope[j] = up_gelu(after(a2[j], last), w_up, bias_u, f"up_gelu_{j}")
        last = gb[j]
    gb_blocks = flat(gb)
    if CTX == 4:
        gb_blocks = [(g[0], n, i) for g in gb[:far] for i in (0, 1)] + list(gb[far])
    down_grad = outer(gb_blocks, flat(dz2), "down_grad")
    down_part = scatter_f(down_grad)
    w_down = after(w_down, down_grad)

    du, dh2, mix = [None] * CTX, [None] * CTX, [None] * CTX
    if CTX == 4:
        du, dh2, (p1_hi, p2_lo), (x_lo, y_hi) = feed_back(flat(dz2), flat(slope), w_down, w_up)
        x_hi, y_lo, up_grad = up_back(p1_hi, p2_lo, flat(a2), du)
        mix_far = plain(after(gb[far], up_grad), w_down, False, half, "mix_far")
        mix_first = swap(mix_far[0], 1), swap(mix_far[1], 2)
        lows = total_of(dh2[:n], [x_lo, y_lo])
        dh2 = jnp.concatenate([lows, total_of(dh2[n:], [x_hi, y_hi])], axis=0)
        dh2 = after(dh2, mix_far)
        du = [du]
    else:
        for j in range(CTX):
            du[j] = hidden_back(dz2[j], w_down, slope[j], f"du_{j}")
            dh2[j] = plain(du[j], w_up, True, half if j else single, f"dh2_{j}")[0]
        arrived = scatter_send(dh2[1:])
        dh2 = dh2[0]
        up_grad = outer(flat(a2), flat(du), "up_grad")
        mix[far] = plain(gb[far], w_down, False, half, "mix_far")[0]
        dh2 = total_of(dh2, arrived)
    up_part = scatter_f(up_grad)
    up_bias_grad = sum(jnp.sum(x.astype(single), axis=0) for x in flat(du))
    down_bias_grad = sum(jnp.sum(x.astype(single), axis=0) for x in dz2[0])
    gain2_grad = jnp.sum(dh2 * normed2, axis=0)
    shift2_grad = jnp.sum(dh2, axis=0)
    dy1 = cotangent + norm_back(normed2, inv2, gain2, dh2)

    dz1 = dy1.astype(half)
    dattn = dot_nt(dz1, w_out).astype(half)
    out_bias_grad = jnp.sum(dz1.astype(single), axis=0)
    if CTX == 4:
        dattn, out_grad, one_lo, one_hi, two_lo, two_hi = heads_back(
            dattn, ob, dz1, gb[1][0], gb[2][0], w_down, *mix_first, part
        )
    else:
        dattn = xor_order([dattn[:, s * part : (s + 1) * part] for s in range(CTX)], c)
        dattn = [dattn[0]] + [swap(dattn[j], j) for j in range(1, CTX)]
        dattn = jnp.concatenate(dattn, axis=0)
        out_grad = outer([ob], [dz1], "out_grad")
        for j in mid:
            mix[j] = plain(gb[j], w_down, False, half, f"mix_{j}")[0]
    out_part = scatter_f(out_grad)
    down_own = after(down_part, dattn)
    down_near = gather_first(down_own)
    dqkv = attn_backward(joined, dattn, inv, slopes, heads, scale)
    if CTX == 4:
        lows = [swap(one_lo, 1), swap(two_lo, 2)]
        dqkv = after(dqkv, lows, up_part)
        dh1, arrived, qkv_grad, mix[0] = qkv_back(dqkv, w_qkv, a1, gb[0][0], w_down)
    else:
        dh1 = [
            plain([(dqkv, rows, j)], w_qkv, True, half if j else single, f"dh1_{j}")[0]
            for j in range(CTX)
        ]
        arrived = scatter_send(dh1[1:])
        dh1 = dh1[0]
        qkv_grad = outer(a1, [(dqkv, rows, j) for j in range(CTX)], "qkv_grad")
        mix[0] = plain(gb[0], w_down, False, single, "mix_0")[0]
    dh1 = total_of(after(dh1, down_near), arrived)
    down_out = gather_second(down_own, after(down_near, dh1))
    mixed = y1 + bias_d + mix[0]
    if CTX == 4:
        one_hi, two_hi = after((one_hi, two_hi), dh1)
        lows = total_of(mixed[:n], lows)
        mixed = jnp.concatenate([lows, total_of(mixed[n:], [swap(one_hi, 1), swap(two_hi, 2)])])
    else:
        mixed = total_of(mixed, scatter_send(mix[1:]))
    down_out = lay_out(0, down_out, c, width // min(width, 512))
    up_out = gather_ctx(after(up_part, dh1))
    out_part = after(out_part, up_out)
    up_out = lay_out(1, up_out, c, nf)
    sums = jnp.sum(dqkv.astype(single), axis=0)
    normed1_own, inv1_own = norm_parts(tokens.astype(single))
    gain1_grad = jnp.sum(dh1 * normed1_own, axis=0)
    shift1_grad = jnp.sum(dh1, axis=0)
    input_grad = dy1 + norm_back(normed1_own, inv1_own, gain1, dh1)

    qkv_part = scatter_f(after(qkv_grad, input_grad))
    bit = 1
    while bit < CTX:
        out_part = out_part.astype(half)
        out_part = out_part.astype(single) + swap(out_part, bit).astype(single)
        bit *= 2
    out_out = out_part
    qkv_out = lay_out(1, gather_ctx(qkv_part), c, 3)

    def spread(x, inner):
        x = x.reshape(-1, 1, inner)
        mask = (jnp.arange(CTX) == c)[None, :, None]
        return jnp.where(mask, x, 0.0).reshape(-1)

    def reduced(items, call):
        sizes = [x.shape[0] // nf for x in items]
        x = jnp.concatenate([x.reshape(nf, -1) for x in items], axis=1)
        x = jnp.pad(x, ((0, 0), (0, -x.shape[1] % 1024))).reshape(nf, -1, 128)
        x = reduce_small(x, nf, CTX, call).reshape(-1)
        out, at = [], 0
        for n in sizes:
            out.append(x[at : at + n])
            at += n
        return out

    sums_in = [out_bias_grad, gain2_grad, shift2_grad, down_bias_grad, spread(up_bias_grad, fpart)]
    gain1_grad = after(gain1_grad, qkv_part)
    sums_in += [gain1_grad, shift1_grad, spread(sums[:part], part), spread(sums[2 * part :], part)]
    sums_out = reduced(sums_in, 2)
    out_bias_out, gain2_out, shift2_out, down_bias_out, up_bias_out = sums_out[:5]
    gain1_out, shift1_out, q_bias_out, v_bias_out = sums_out[5:]
    return (
        mixed,
        input_grad,
        gain1_out,
        shift1_out,
        qkv_out,
        q_bias_out,
        v_bias_out,
        out_out,
        out_bias_out,
        gain2_out,
        shift2_out,
        up_out,
        up_bias_out,
        down_out,
        down_bias_out,
    )


def solution(mesh):
    rows, flat = P(("ctx", "fsdp"), None), P("fsdp")
    mat = P("fsdp", None)
    in_specs = (
        rows,
        rows,
        mat,
        mat,
        flat,
        flat,
        mat,
        flat,
        flat,
        mat,
        flat,
        flat,
        flat,
        mat,
        flat,
        mat,
        flat,
    )
    out_specs = (
        rows,
        rows,
        flat,
        flat,
        mat,
        flat,
        flat,
        mat,
        flat,
        flat,
        flat,
        mat,
        flat,
        mat,
        flat,
    )
    return jax.shard_map(
        per_device, mesh=mesh, in_specs=in_specs, out_specs=out_specs, check_vma=False
    )
```

```python
import functools
import math

import jax
import jax.numpy as jnp
from jax import lax
from jax.experimental import pallas as pl
from jax.experimental.pallas import tpu as pltpu
from jax.sharding import PartitionSpec as P

HEADS = 16
SPAN = 128
SEQ_BLOCKS = 8

norm_eps = 1e-05
gelu_coef = 0.7978845608028654
LOG2E = 1.4426950408889634

half = jnp.bfloat16
single = jnp.float32


def dot_nn(a, b):
    return lax.dot_general(a, b, (((1,), (0,)), ((), ())), preferred_element_type=single)


def dot_nt(a, b):
    return lax.dot_general(a, b, (((1,), (1,)), ((), ())), preferred_element_type=single)


def dot_tn(a, b):
    return lax.dot_general(a, b, (((0,), (0,)), ((), ())), preferred_element_type=single)


def norm_parts(values):
    center = values - jnp.mean(values, axis=-1, keepdims=True)
    spread = jnp.mean(center * center, axis=-1, keepdims=True)
    inv = lax.rsqrt(spread + norm_eps)
    return center * inv, inv


def norm_back(normed, inv, gain, grad):
    dn = grad * gain
    return inv * (
        dn
        - jnp.mean(dn, axis=-1, keepdims=True)
        - normed * jnp.mean(dn * normed, axis=-1, keepdims=True)
    )


def gelu_both(v):
    t = jnp.tanh(gelu_coef * (v + 0.044715 * v * v * v))
    value = 0.5 * v * (1.0 + t)
    slope = 0.5 * (1.0 + t) + 0.5 * v * (1.0 - t * t) * gelu_coef * (1.0 + 3 * 0.044715 * v * v)
    return value, slope


def swap(x, mask):
    n = lax.axis_size("ctx")
    return lax.ppermute(x, "ctx", [(i, i ^ mask) for i in range(n)])


def gather_first(x):
    count = lax.axis_size("ctx")
    return [swap(x, j) for j in range(1, 3 if count == 4 else count)]


def gather_second(x, arrived):
    if lax.axis_size("ctx") != 4:
        return [[x]] + [[p] for p in arrived]
    one, two = arrived
    n = x.shape[0] // 2
    return [[x], [one], [two], [swap(one[:n], 2), swap(two[n:], 1)]]


def gather_ctx(x):
    return gather_second(x, gather_first(x))


def scatter_first(far):
    if lax.axis_size("ctx") != 4:
        return None
    return swap(far[0], 1), swap(far[1], 2)


def scatter_second(pieces, first):
    if first is None:
        return pieces[1:]
    p1, p2 = pieces[1], pieces[2]
    n = p1.shape[0] // 2
    from_x, from_y = first
    p1 = jnp.concatenate(
        [p1[:n], (p1[n:].astype(single) + from_y.astype(single)).astype(half)], axis=0
    )
    p2 = jnp.concatenate(
        [(p2[:n].astype(single) + from_x.astype(single)).astype(half), p2[n:]], axis=0
    )
    return [p1, p2]


def scatter_send(sent):
    return [swap(x, j + 1) for j, x in enumerate(sent)]


def total_of(own, arrived):
    for x in arrived:
        own = own + x.astype(single)
    return own


def xor_order(items, c):
    bit = 1
    while bit < len(items):
        on = (c & bit) == bit
        items = [jnp.where(on, items[i ^ bit], items[i]) for i in range(len(items))]
        bit *= 2
    return items


TILE = 256


def attn_scores(q_refs, k_refs, i, scale, slope):
    q = jnp.concatenate([q_refs[2 * i][...], q_refs[2 * i + 1][...]], axis=0)
    k = jnp.concatenate([r[...] for r in k_refs[: 2 * i + 2]], axis=0)
    n = TILE * (i + 1)
    col = lax.broadcasted_iota(jnp.int32, (1, n), 1) - (n - 1)
    s = dot_nt(q, k) * (scale * LOG2E) + (slope * LOG2E) * col.astype(single)
    row_at = lax.broadcasted_iota(jnp.int32, (TILE, TILE), 0)
    col_at = lax.broadcasted_iota(jnp.int32, (TILE, TILE), 1)
    last = jnp.where(col_at <= row_at, s[:, n - TILE :], -1e30)
    s = last if i == 0 else jnp.concatenate([s[:, : n - TILE], last], axis=1)
    e = jnp.exp2(s - jnp.max(s, axis=1, keepdims=True))
    return q, k, e, 1.0 / jnp.sum(e, axis=1, keepdims=True)


class Rows:
    def __init__(self, inv_ref, stage, out, sems, kinds):
        self.inv, self.stage, self.out, self.sems, self.kinds = inv_ref, stage, out, sems, kinds
        self.heads = pl.num_programs(1)
        self.step = pl.program_id(0) * self.heads + pl.program_id(1)
        self.slot = lax.rem(self.step, 2)

    def copies(self, step):
        slot = lax.rem(step, 2)
        seq, head = step // self.heads, lax.rem(step, self.heads)
        for kind in range(self.kinds):
            col = pl.multiple_of((kind * self.heads + head) * 128, 128)
            for j in range(SEQ_BLOCKS):
                row = pl.multiple_of(self.inv[seq * SEQ_BLOCKS + j] * SPAN, SPAN)
                yield pltpu.make_async_copy(
                    self.stage.at[slot, kind, pl.ds(j * SPAN, SPAN)],
                    self.out.at[pl.ds(row, SPAN), pl.ds(col, 128)],
                    self.sems.at[slot, kind * SEQ_BLOCKS + j],
                )

    def wait(self, step):
        for copy in self.copies(step):
            copy.wait()

    def open(self):
        @pl.when(self.step >= 2)
        def _():
            self.wait(self.step - 2)

    def close(self):
        for copy in self.copies(self.step):
            copy.start()

        @pl.when(self.step == 2 * self.heads - 1)
        def _():
            self.wait(self.step - 1)
            self.wait(self.step)


def attn_fwd_kernel(scale, inv_ref, slope_ref, *refs):
    q_refs, k_refs, v_refs = refs[:8], refs[8:16], refs[16:24]
    out, stage, sems = refs[24:]
    slope = slope_ref[pl.program_id(1)]
    rows = Rows(inv_ref, stage, out, sems, 1)
    rows.open()
    for i in range(4):
        q, k, e, r = attn_scores(q_refs, k_refs, i, scale, slope)
        v = jnp.concatenate([x[...] for x in v_refs[: 2 * i + 2]], axis=0)
        o = dot_nn((e * r).astype(half), v)
        stage[rows.slot, 0, TILE * i : TILE * (i + 1), :] = o.astype(half)
    rows.close()


def attn_bwd_kernel(scale, inv_ref, slope_ref, *refs):
    q_refs, k_refs, v_refs, g_refs = refs[:8], refs[8:16], refs[16:24], refs[24:32]
    out, stage, sems, dk_acc, dv_acc = refs[32:]
    slope = slope_ref[pl.program_id(1)]
    rows = Rows(inv_ref, stage, out, sems, 3)
    rows.open()
    for i in (3, 2, 1, 0):
        q, k, e, r = attn_scores(q_refs, k_refs, i, scale, slope)
        n = TILE * (i + 1)
        v = jnp.concatenate([x[...] for x in v_refs[: 2 * i + 2]], axis=0)
        g = jnp.concatenate([g_refs[2 * i][...], g_refs[2 * i + 1][...]], axis=0)
        p = e * r
        dp = dot_nt(g, v)
        delta = jnp.sum(p * dp, axis=1, keepdims=True)
        ds = (p * (dp - delta)).astype(half)
        pb = p.astype(half)
        dq = (dot_nn(ds, k) * scale).astype(half)
        stage[rows.slot, 0, TILE * i : TILE * (i + 1), :] = dq
        dk = dot_tn(ds, q)
        dv = dot_tn(pb, g)
        if i == 3:
            dk_acc[...] = dk
            dv_acc[...] = dv
        else:
            dk_acc[:n, :] += dk
            dv_acc[:n, :] += dv
    stage[rows.slot, 1] = (dk_acc[...] * scale).astype(half)
    stage[rows.slot, 2] = dv_acc[...].astype(half)
    rows.close()


def block_specs(offset):
    def one(j):
        return pl.BlockSpec(
            (SPAN, 128), lambda s, h, inv, slope: (inv[s * SEQ_BLOCKS + j], offset + h)
        )

    return [one(j) for j in range(SEQ_BLOCKS)]


def attn_call(kernel, kinds, joined, extra, extra_specs, scratch, inv, slopes, heads, cost, name):
    rows = joined.shape[0]
    specs = block_specs(0) + block_specs(heads) + block_specs(2 * heads) + extra_specs
    return pl.pallas_call(
        kernel,
        grid_spec=pltpu.PrefetchScalarGridSpec(
            num_scalar_prefetch=2,
            grid=(2, heads),
            in_specs=specs,
            out_specs=pl.BlockSpec(memory_space=pl.ANY),
            scratch_shapes=[
                pltpu.VMEM((2, kinds, rows // 2, 128), half),
                pltpu.SemaphoreType.DMA((2, kinds * SEQ_BLOCKS)),
            ]
            + scratch,
        ),
        out_shape=jax.ShapeDtypeStruct((rows, kinds * heads * 128), half),
        compiler_params=pltpu.CompilerParams(vmem_limit_bytes=48 * 1024 * 1024),
        cost_estimate=cost,
        name=name,
    )(inv, slopes, *([joined] * 24), *extra)


def attn_forward(joined, inv, slopes, heads, scale):
    kernel = functools.partial(attn_fwd_kernel, scale)
    cost = hint(20 * 10**9, joined.shape[0] * heads * 128 * 8)
    return attn_call(
        kernel, 1, joined, [], [], [], inv, slopes, heads, cost, "attn_forward"
    )


def attn_backward(joined, grad, inv, slopes, heads, scale):
    kernel = functools.partial(attn_bwd_kernel, scale)
    cost = hint(40 * 10**9, joined.shape[0] * heads * 128 * 14)
    sums = [pltpu.VMEM((joined.shape[0] // 2, 128), single)] * 2
    return attn_call(
        kernel,
        3,
        joined,
        [grad] * 8,
        block_specs(0),
        sums,
        inv,
        slopes,
        heads,
        cost,
        "attn_backward",
    )


HINT = 0.001


def block_of(x):
    return x if isinstance(x, tuple) else (x, x.shape[0], 0)


def hint(flops, bytes_accessed):
    return pl.CostEstimate(
        flops=int(HINT * flops), bytes_accessed=int(HINT * bytes_accessed), transcendentals=0
    )


def rows_kernel(dot, epilogue, count, extra, *refs):
    left, w_ref = refs[:count], refs[count]
    extras = refs[count + 1 : count + 1 + extra]
    outs = refs[count + 1 + extra :]
    for i in range(count):
        epilogue(i, dot(left[i][...], w_ref[...]), extras, outs)


def rows_matmul(blocks, w, transposed, extras, outs, epilogue, name, tile=512):
    blocks = [block_of(x) for x in blocks]
    extras = [block_of(x) for x in extras]
    n = w.shape[0] if transposed else w.shape[1]
    k = w.shape[1] if transposed else w.shape[0]
    t = math.gcd(n, tile)
    w_spec = (
        pl.BlockSpec((t, k), lambda i: (i, 0)) if transposed else pl.BlockSpec((k, t), lambda i: (0, i))
    )
    rows = sum(x[1] for x in blocks)
    return pl.pallas_call(
        functools.partial(
            rows_kernel, dot_nt if transposed else dot_nn, epilogue, len(blocks), len(extras)
        ),
        grid=(n // t,),
        in_specs=[pl.BlockSpec((x[1], k), lambda i, at=x[2]: (at, 0)) for x in blocks]
        + [w_spec]
        + [pl.BlockSpec((x[1], t), lambda i, at=x[2]: (at, i)) for x in extras],
        out_specs=[pl.BlockSpec((r, t), lambda i: (0, i)) for r, _ in outs],
        out_shape=[jax.ShapeDtypeStruct((r, n), d) for r, d in outs],
        compiler_params=pltpu.CompilerParams(vmem_limit_bytes=52 * 1024 * 1024),
        cost_estimate=hint(2 * rows * n * k, 2 * n * k + 4 * rows * (n + k)),
        name=name,
    )(*[x[0] for x in blocks], w, *[x[0] for x in extras])


def plain(blocks, w, transposed, dtype, name):
    def epilogue(i, x, extras, outs):
        outs[i][...] = x.astype(dtype)

    outs = [(block_of(x)[1], dtype) for x in blocks]
    return rows_matmul(blocks, w, transposed, [], outs, epilogue, name)


def joined_rows(blocks, w, bias, name):
    sizes = [block_of(x)[1] for x in blocks]

    def epilogue(i, x, extras, outs):
        at = sum(sizes[:i])
        outs[0][at : at + sizes[i], :] = (x + extras[0][...]).astype(half)

    bias = bias.reshape(1, -1)
    return rows_matmul(blocks, w, False, [bias], [(sum(sizes), half)], epilogue, name)[0]


def up_gelu(blocks, w, bias, name):
    count = len(blocks)

    def epilogue(i, x, extras, outs):
        value, slope = gelu_both(x + extras[0][...])
        outs[i][...] = value.astype(half)
        outs[count + i][...] = slope.astype(half)

    outs = [(block_of(x)[1], half) for x in blocks] * 2
    out = rows_matmul(blocks, w, False, [bias.reshape(1, -1)], outs, epilogue, name)
    return out[:count], out[count:]


def hidden_back(blocks, w, slopes, name):
    def epilogue(i, x, extras, outs):
        x = x.astype(half).astype(single) * extras[i][...].astype(single)
        outs[i][...] = x.astype(half)

    outs = [(block_of(x)[1], half) for x in blocks]
    return rows_matmul(blocks, w, True, slopes, outs, epilogue, name)


def outer_kernel(count, *refs):
    out = refs[-1]
    total = None
    for i in range(count):
        x = dot_tn(refs[i][...], refs[count + i][...])
        total = x if total is None else total + x
    out[...] = total.astype(half)


def outer(left, right, name):
    left = [block_of(x) for x in left]
    right = [block_of(x) for x in right]
    m, n = left[0][0].shape[1], right[0][0].shape[1]
    tm = math.gcd(m, 1024)
    tn = n // 2 if n % 256 == 0 and n > 1024 else n
    rows = sum(x[1] for x in left)
    return pl.pallas_call(
        functools.partial(outer_kernel, len(left)),
        grid=(m // tm, n // tn),
        in_specs=[pl.BlockSpec((x[1], tm), lambda i, j, at=x[2]: (at, i)) for x in left]
        + [pl.BlockSpec((x[1], tn), lambda i, j, at=x[2]: (at, j)) for x in right],
        out_specs=pl.BlockSpec((tm, tn), lambda i, j: (i, j)),
        out_shape=jax.ShapeDtypeStruct((m, n), half),
        compiler_params=pltpu.CompilerParams(vmem_limit_bytes=52 * 1024 * 1024),
        cost_estimate=hint(2 * rows * m * n, 2 * rows * (m + n) + 2 * m * n),
        name=name,
    )(*[x[0] for x in left], *[x[0] for x in right])


def partner(mask):
    c = lax.axis_index("ctx")
    if mask == 1:
        return c + 1 - 2 * lax.rem(c, 2)
    return lax.rem(c + 2, 4) if mask == 2 else 3 - c


def greet(masks):
    barrier = pltpu.get_barrier_semaphore()
    for mask in masks:
        pl.semaphore_signal(
            barrier,
            inc=1,
            device_id={"ctx": partner(mask)},
            device_id_type=pl.DeviceIdType.MESH,
        )
    pl.semaphore_wait(barrier, len(masks))


class Moves:
    def __init__(self, send_sem, recv_sem):
        self.send_sem, self.recv_sem, self.used = send_sem, recv_sem, 0

    def start(self, src, dst, mask):
        copy = pltpu.make_async_remote_copy(
            src_ref=src,
            dst_ref=dst,
            send_sem=self.send_sem.at[self.used],
            recv_sem=self.recv_sem.at[self.used],
            device_id={"ctx": partner(mask)},
            device_id_type=pl.DeviceIdType.MESH,
        )
        self.used += 1
        copy.start()
        return copy


def multiply(lefts, w, transposed, extras, outs, epilogue, tile=512):
    k = lefts[0].shape[1]
    n = w.shape[0] if transposed else w.shape[1]
    t = math.gcd(n, tile)
    w_spec = (
        pl.BlockSpec((t, k), lambda i: (i, 0)) if transposed else pl.BlockSpec((k, t), lambda i: (0, i))
    )
    dot = dot_nt if transposed else dot_nn

    def body(*refs):
        rows_kernel(dot, epilogue, len(lefts), len(extras), *refs)

    pltpu.emit_pipeline(
        body,
        grid=(n // t,),
        in_specs=[pl.BlockSpec((x.shape[0], k), lambda i: (0, 0)) for x in lefts]
        + [w_spec]
        + [pl.BlockSpec((x.shape[0], t), lambda i: (0, i)) for x in extras],
        out_specs=[pl.BlockSpec((x.shape[0], t), lambda i: (0, i)) for x in outs],
    )(*lefts, w, *extras, *outs)


def store(i, x, extras, outs):
    outs[i][...] = x.astype(outs[i].dtype)


def store_sum(i, x, extras, outs):
    outs[i][...] = (x + extras[i][...].astype(single)).astype(outs[i].dtype)


def store_passed(i, x, extras, outs):
    if i in (1, 2):
        x = x + extras[i - 1][...].astype(single)
    outs[i][...] = x.astype(outs[i].dtype)


def store_hidden(i, x, extras, outs):
    outs[i][...] = (x.astype(half).astype(single) * extras[i][...].astype(single)).astype(half)


def outer_on(lefts, rights, out):
    m, n = out.shape
    tm = math.gcd(m, 1024)
    tn = n // 2 if n % 256 == 0 and n > 1024 else n

    def body(*refs):
        outer_kernel(len(lefts), *refs)

    pltpu.emit_pipeline(
        body,
        grid=(m // tm, n // tn),
        in_specs=[pl.BlockSpec((x.shape[0], tm), lambda i, j: (0, i)) for x in lefts]
        + [pl.BlockSpec((x.shape[0], tn), lambda i, j: (0, j)) for x in rights],
        out_specs=[pl.BlockSpec((tm, tn), lambda i, j: (i, j))],
    )(*lefts, *rights, out)


def halves(ref):
    n = ref.shape[0] // 2
    return ref.at[pl.ds(0, n)], ref.at[pl.ds(n, n)]


def moving_call(kernel, operands, outs, moves, call, flops, name):
    anywhere = pl.BlockSpec(memory_space=pl.ANY)
    sems = pltpu.SemaphoreType.DMA((moves,))
    return pl.pallas_call(
        kernel,
        in_specs=[anywhere] * len(operands),
        out_specs=[anywhere] * len(outs),
        out_shape=[jax.ShapeDtypeStruct(shape, dtype) for shape, dtype in outs],
        scratch_shapes=[sems, sems],
        compiler_params=pltpu.CompilerParams(
            collective_id=call, has_side_effects=True, vmem_limit_bytes=52 * 1024 * 1024
        ),
        cost_estimate=hint(flops, 0),
        name=name,
    )(*operands)


def store_biased(i, x, extras, outs):
    outs[i][...] = (x + extras[0][...]).astype(half)


def qkv_kernel(*refs):
    tok, gain, shift, a1, w_qkv, bias = refs[0:2], refs[2], refs[3], refs[4:7], refs[7], refs[8]
    dz_lo, dz_hi = refs[9:11]
    joined, far, one_lo, two_hi = refs[11], refs[12:14], refs[14], refs[15]
    moves = Moves(*refs[16:18])
    n, width = tok[0].shape
    greet((1, 2))
    copies = [moves.start(dz_lo, one_lo, 1), moves.start(dz_hi, two_hi, 2)]

    def norm(x_lo, x_hi, g, s, o_lo, o_hi):
        for x, o in ((x_lo, o_lo), (x_hi, o_hi)):
            normed, _ = norm_parts(x[...].astype(single))
            o[...] = (normed * g[...] + s[...]).astype(half)

    t = math.gcd(n, 64)
    block = pl.BlockSpec((t, width), lambda i: (i, 0))
    row = pl.BlockSpec((1, width), lambda i: (0, 0))
    pltpu.emit_pipeline(
        norm, grid=(n // t,), in_specs=[block, block, row, row], out_specs=[block, block]
    )(*tok, gain, shift, *far)
    lefts, outs, at = [*a1, *far], [], 0
    for x in lefts:
        outs.append(joined.at[pl.ds(at, x.shape[0])])
        at += x.shape[0]
    multiply(lefts, w_qkv, False, [bias], outs, store_biased)
    for copy in copies:
        copy.wait()


def qkv_forward(tok, gain, shift, a1, w_qkv, bias, dz_lo, dz_hi):
    n, width = tok[0].shape
    k = w_qkv.shape[1]
    outs = [((8 * n, k), half)] + [((n, width), half)] * 4
    out = moving_call(
        qkv_kernel,
        [*tok, gain.reshape(1, -1), shift.reshape(1, -1), *a1, w_qkv, bias.reshape(1, -1), dz_lo, dz_hi],
        outs,
        2,
        7,
        16 * n * width * k,
        "qkv",
    )
    return out[0], out[1:3], out[3:5]


def feed_pass(dz, slope, w_down, w_up, du, total):
    n, width = dz[0].shape
    wide = w_down.shape[0]
    t = math.gcd(wide, 512)
    total[...] = jnp.zeros_like(total)

    def body(dz_lo, dz_hi, down, up, slope_lo, slope_hi, du_lo, du_hi):
        for i, x, s, d in ((0, dz_lo, slope_lo, du_lo), (1, dz_hi, slope_hi, du_hi)):
            grad = dot_nt(x[...], down[...]).astype(half).astype(single)
            grad = (grad * s[...].astype(single)).astype(half)
            d[...] = grad
            total[i * n : (i + 1) * n, :] += dot_nt(grad, up[...])

    pltpu.emit_pipeline(
        body,
        grid=(wide // t,),
        in_specs=[pl.BlockSpec((n, width), lambda i: (0, 0))] * 2
        + [pl.BlockSpec((t, width), lambda i: (i, 0)), pl.BlockSpec((width, t), lambda i: (0, i))]
        + [pl.BlockSpec((n, t), lambda i: (0, i))] * 2,
        out_specs=[pl.BlockSpec((n, t), lambda i: (0, i))] * 2,
    )(*dz, w_down, w_up, *slope, *du)


def feed_back_kernel(*refs):
    dz, slope, (w_down, w_up) = refs[0:8], refs[8:13], refs[13:15]
    a2, gb_far = refs[15:20], refs[20:22]
    du, own, land1, land2, up_grad, mix_x, mix_y = refs[22:27], *refs[27:33]
    total, far, near, rest, from_x, from_y = refs[33:39]
    moves = Moves(*refs[39:41])
    local = refs[41]
    n = from_x.shape[0]
    lo, hi = pl.ds(0, n), pl.ds(n, n)
    (s1_lo, s1_hi), (s2_lo, s2_hi) = halves(slope[1]), halves(slope[2])
    (d1_lo, d1_hi), (d2_lo, d2_hi) = halves(du[1]), halves(du[2])
    (land1_lo, land1_hi), (land2_lo, land2_hi) = halves(land1), halves(land2)
    greet((1, 2))
    feed_pass(dz[6:8], slope[3:5], w_down, w_up, du[3:5], total)
    far[...] = total[...].astype(half)
    first = [moves.start(far.at[lo], from_x, 1), moves.start(far.at[hi], from_y, 2)]
    feed_pass([dz[2], dz[5]], [s1_lo, s2_hi], w_down, w_up, [d1_lo, d2_hi], total)
    near[...] = total[...].astype(half)
    second = [moves.start(near.at[lo], land1_lo, 1), moves.start(near.at[hi], land2_hi, 2)]
    feed_pass([dz[3], dz[4]], [s1_hi, s2_lo], w_down, w_up, [d1_hi, d2_lo], total)
    for copy in first:
        copy.wait()
    rest[lo] = (total[lo] + from_y[...].astype(single)).astype(half)
    rest[hi] = (total[hi] + from_x[...].astype(single)).astype(half)
    second += [moves.start(rest.at[lo], land1_hi, 1), moves.start(rest.at[hi], land2_lo, 2)]
    wide, width = w_down.shape
    t = math.gcd(width, 512)

    def mix(x_lo, x_hi, w):
        at = pl.ds(pl.multiple_of(pl.program_id(0) * t, t), t)
        far[0:n, at] = dot_nn(x_lo[...], w[...]).astype(half)
        far[n : 2 * n, at] = dot_nn(x_hi[...], w[...]).astype(half)

    pltpu.emit_pipeline(
        mix,
        grid=(width // t,),
        in_specs=[pl.BlockSpec((n, wide), lambda i: (0, 0))] * 2
        + [pl.BlockSpec((wide, t), lambda i: (0, i))],
    )(*gb_far, w_down)
    second += [moves.start(far.at[lo], mix_x, 1), moves.start(far.at[hi], mix_y, 2)]
    feed_pass(dz[0:2], halves(slope[0]), w_down, w_up, halves(du[0]), total)
    store_own = pltpu.make_async_copy(total, own, local)
    store_own.start()
    outer_on(a2, du, up_grad)
    store_own.wait()
    for copy in second:
        copy.wait()


def feed_back(dz, slope, w_down, w_up, a2, gb_far):
    n, width = dz[0].shape
    rows, wide = 2 * n, w_down.shape[0]
    anywhere = pl.BlockSpec(memory_space=pl.ANY)
    outs = [((r, wide), half) for r in (rows, rows, rows, n, n)]
    outs += [((rows, width), single)] + [((rows, width), half)] * 2
    outs += [((width, wide), half)] + [((n, width), half)] * 2
    sems = pltpu.SemaphoreType.DMA((8,))
    out = pl.pallas_call(
        feed_back_kernel,
        in_specs=[anywhere] * 22,
        out_specs=[anywhere] * len(outs),
        out_shape=[jax.ShapeDtypeStruct(shape, dtype) for shape, dtype in outs],
        scratch_shapes=[pltpu.VMEM((rows, width), single)]
        + [pltpu.VMEM((rows, width), half)] * 3
        + [pltpu.VMEM((n, width), half)] * 2
        + [sems, sems, pltpu.SemaphoreType.DMA],
        compiler_params=pltpu.CompilerParams(
            collective_id=3, has_side_effects=True, vmem_limit_bytes=56 * 1024 * 1024
        ),
        cost_estimate=hint(26 * rows * width * wide, 0),
        name="feed_back",
    )(*dz, *slope, w_down, w_up, *a2, *gb_far)
    return out[0:5], out[5:8], out[8], out[9:11]


def heads_back_kernel(part, *refs):
    own, land1, land2, cot, y1, gain, w_out = refs[0:7]
    ob, gb1, gb2, w_down, mix_x, mix_y, down = refs[7:14]
    dy1, dz1, sums, got, out_grad = refs[14:19]
    mix, down1, down2 = refs[19:23], refs[23], refs[24]
    dz, w, stage = refs[25:28]
    moves = Moves(*refs[28:30])
    local = refs[30]
    rows, width = own.shape
    greet((1, 2, 3))
    load = pltpu.make_async_copy(w_out, w, local.at[0])
    load.start()
    copies = [moves.start(down, down1, 1), moves.start(down, down2, 2)]
    t = math.gcd(rows, 64)

    def norm(own, one, two, cot, y1, gain, dy1, dz1, sums):
        step = pl.program_id(0)
        grad = own[...] + one[...].astype(single) + two[...].astype(single)
        normed, inv = norm_parts(y1[...])
        dy = cot[...] + norm_back(normed, inv, gain[...], grad)
        low = dy.astype(half)
        dy1[...] = dy
        dz1[...] = low
        dz[pl.ds(pl.multiple_of(step * t, t), t), :] = low

        @pl.when(step == 0)
        def _():
            sums[...] = jnp.zeros_like(sums)

        sums[0:1] += jnp.sum(grad * normed, axis=0, keepdims=True)
        sums[1:2] += jnp.sum(grad, axis=0, keepdims=True)
        sums[2:3] += jnp.sum(low.astype(single), axis=0, keepdims=True)

    block = pl.BlockSpec((t, width), lambda i: (i, 0))
    pltpu.emit_pipeline(
        norm,
        grid=(rows // t,),
        in_specs=[block] * 5 + [pl.BlockSpec((1, width), lambda i: (0, 0))],
        out_specs=[block] * 2 + [pl.BlockSpec((8, width), lambda i: (0, 0))],
    )(own, land1, land2, cot, y1, gain, dy1, dz1, sums)
    load.wait()
    for mask in (3, 1, 2, 0):
        of = partner(mask) if mask else lax.axis_index("ctx")
        heads = w[pl.ds(pl.multiple_of(of * part, part), part), :]
        stage[mask] = dot_nt(dz[...], heads).astype(half)
        at = got.at[pl.ds(mask * rows, rows)]
        if mask:
            copies.append(moves.start(stage.at[mask], at, mask))
        else:
            keep = pltpu.make_async_copy(stage.at[0], at, local.at[1])
            keep.start()
    outer_on([ob], [dz1], out_grad)
    multiply(
        [*halves(gb1), *halves(gb2)],
        w_down,
        False,
        [mix_y, mix_x],
        mix,
        store_passed,
    )
    keep.wait()
    for copy in copies:
        copy.wait()


def heads_back(terms, cot, y1, gain, w_out, ob, gb1, gb2, w_down, mix_first, down):
    rows, width = cot.shape
    part = width // 4
    anywhere = pl.BlockSpec(memory_space=pl.ANY)
    sems = pltpu.SemaphoreType.DMA((5,))
    outs = [((rows, width), single), ((rows, width), half), ((8, width), single)]
    outs += [((4 * rows, part), half), ((width, width), half)]
    outs += [((rows // 2, width), half)] * 4 + [(down.shape, half)] * 2
    out = pl.pallas_call(
        functools.partial(heads_back_kernel, part),
        in_specs=[anywhere] * 14,
        out_specs=[anywhere] * len(outs),
        out_shape=[jax.ShapeDtypeStruct(shape, dtype) for shape, dtype in outs],
        scratch_shapes=[
            pltpu.VMEM((rows, width), half),
            pltpu.VMEM((width, width), half),
            pltpu.VMEM((4, rows, part), half),
            sems,
            sems,
            pltpu.SemaphoreType.DMA((2,)),
        ],
        compiler_params=pltpu.CompilerParams(
            collective_id=4, has_side_effects=True, vmem_limit_bytes=56 * 1024 * 1024
        ),
        cost_estimate=hint(10 * rows * width * width, 0),
        name="heads_back",
    )(*terms, cot, y1, gain.reshape(1, -1), w_out, ob, gb1, gb2, w_down, *mix_first, down)
    return out[0], out[2], out[3], out[4], out[5:9], out[9:11]


def qkv_back_kernel(*refs):
    dqkv, w_qkv = refs[0:2]
    a1, gb_own, w_down = refs[2:7], refs[7], refs[8]
    own, p3, p1, p2, from_x, from_y, land1, land2, qkv_grad, mix_own = refs[9:19]
    moves = Moves(*refs[19:21])
    rows = own.shape[0]
    n = rows // 2

    def block(k):
        return dqkv.at[pl.ds(k * n, n)]

    greet((1, 2))
    (p3_lo, p3_hi), (p1_lo, p1_hi), (p2_lo, p2_hi) = halves(p3), halves(p1), halves(p2)
    (land1_lo, land1_hi), (land2_lo, land2_hi) = halves(land1), halves(land2)
    multiply([block(6), block(7)], w_qkv, True, [], [p3_lo, p3_hi], store)
    first = [moves.start(p3_lo, from_x, 1), moves.start(p3_hi, from_y, 2)]
    multiply([block(2), block(5)], w_qkv, True, [], [p1_lo, p2_hi], store)
    second = [moves.start(p1_lo, land1_lo, 1), moves.start(p2_hi, land2_hi, 2)]
    multiply([dqkv.at[pl.ds(0, rows)]], w_qkv, True, [], [own], store)
    multiply([gb_own], w_down, False, [], [mix_own], store)
    for copy in first:
        copy.wait()
    multiply([block(3), block(4)], w_qkv, True, [from_y, from_x], [p1_hi, p2_lo], store_sum)
    second += [moves.start(p1_hi, land1_hi, 1), moves.start(p2_lo, land2_lo, 2)]
    rights, at = [], 0
    for x in a1:
        rights.append(dqkv.at[pl.ds(at, x.shape[0])])
        at += x.shape[0]
    outer_on(a1, rights, qkv_grad)
    for copy in second:
        copy.wait()


def qkv_back(dqkv, w_qkv, a1, gb_own, w_down):
    rows, width = a1[0].shape
    wide = gb_own.shape[1]
    n = rows // 2
    outs = [((rows, width), single)] + [((rows, width), half)] * 3
    outs += [((n, width), half)] * 2 + [((rows, width), half)] * 2
    outs += [((width, dqkv.shape[1]), half), ((rows, width), single)]
    out = moving_call(
        qkv_back_kernel,
        [dqkv, w_qkv, *a1, gb_own, w_down],
        outs,
        6,
        5,
        16 * rows * width * dqkv.shape[1] + 2 * rows * width * wide,
        "qkv_back",
    )
    return out[0], out[6:8], out[8], out[9]


def lay_out_kernel(axis, layout, c_ref, *refs):
    out = refs[-1]
    for (j, row), ref in zip(layout, refs):
        x = ref[...].astype(single)
        r, w = x.shape
        if axis == 0:
            n = sum(ref.shape[0] for (k, _), ref in zip(layout, refs) if k == j)
            out[pl.ds(pl.multiple_of((c_ref[0] ^ j) * n + row, r), r), :] = x
        else:
            out[row : row + r, pl.ds(pl.multiple_of((c_ref[0] ^ j) * w, w), w)] = x


def lay_out(axis, pieces, c, groups):
    count = len(pieces)
    r = sum(x.shape[0] for x in pieces[0])
    n = pieces[0][0].shape[1]
    w = n // groups
    if w % 128:
        whole = xor_order([jnp.concatenate(p, axis=0).astype(single) for p in pieces], c)
        whole = jnp.stack([p.reshape(r, groups, w) for p in whole], axis=2)
        return whole.reshape(r, count * n)
    layout, blocks = [], []
    for j, p in enumerate(pieces):
        row = 0
        for x in p:
            layout.append((j, row))
            blocks.append(x)
            row += x.shape[0]
    out = (count * r, w) if axis == 0 else (r, count * w)
    return pl.pallas_call(
        functools.partial(lay_out_kernel, axis, layout),
        grid_spec=pltpu.PrefetchScalarGridSpec(
            num_scalar_prefetch=1,
            grid=(groups,),
            in_specs=[pl.BlockSpec((x.shape[0], w), lambda k, c: (0, k)) for x in blocks],
            out_specs=pl.BlockSpec(out, lambda k, c: (0, k)),
        ),
        out_shape=jax.ShapeDtypeStruct((out[0], out[1] * groups), single),
        compiler_params=pltpu.CompilerParams(vmem_limit_bytes=48 * 1024 * 1024),
        cost_estimate=hint(0, 6 * r * n * count),
        name="lay_out",
    )(c.reshape(1), *blocks)


def gather_small_kernel(nf, x_ref, o_ref, send_sem, recv_sem):
    f = lax.axis_index("fsdp")
    barrier = pltpu.get_barrier_semaphore()
    for d in range(1, nf):
        pl.semaphore_signal(
            barrier,
            inc=1,
            device_id={"fsdp": lax.rem(f + d, nf)},
            device_id_type=pl.DeviceIdType.MESH,
        )
    pl.semaphore_wait(barrier, nf - 1)
    copies = []
    for d in range(1, nf):
        copies.append(
            pltpu.make_async_remote_copy(
                src_ref=x_ref,
                dst_ref=o_ref.at[f],
                send_sem=send_sem.at[d],
                recv_sem=recv_sem.at[d],
                device_id={"fsdp": lax.rem(f + d, nf)},
                device_id_type=pl.DeviceIdType.MESH,
            )
        )
        copies[-1].start()
    o_ref[f] = x_ref[...]
    for copy in copies:
        copy.wait()


def gather_small(x, nf):
    return pl.pallas_call(
        functools.partial(gather_small_kernel, nf),
        out_shape=jax.ShapeDtypeStruct((nf,) + x.shape, single),
        in_specs=[pl.BlockSpec(memory_space=pltpu.VMEM)],
        out_specs=pl.BlockSpec(memory_space=pltpu.VMEM),
        scratch_shapes=[pltpu.SemaphoreType.DMA((nf,)), pltpu.SemaphoreType.DMA((nf,))],
        compiler_params=pltpu.CompilerParams(collective_id=1, has_side_effects=True),
        name="gather_small",
    )(x)


def reduce_small_kernel(nf, nc, moving, x_ref, *refs):
    if moving:
        piece, o_ref, one, two, far_lo, far_hi, land, stage, send_sem, recv_sem = refs[:10]
        moves = Moves(refs[10], refs[11])
    else:
        o_ref, land, stage, send_sem, recv_sem = refs
    f = lax.axis_index("fsdp")
    c = lax.axis_index("ctx")
    barrier = pltpu.get_barrier_semaphore()
    for d in range(1, nf):
        pl.semaphore_signal(
            barrier,
            inc=1,
            device_id={"fsdp": lax.rem(f + d, nf)},
            device_id_type=pl.DeviceIdType.MESH,
        )
    for d in range(1, nc):
        pl.semaphore_signal(
            barrier,
            inc=1,
            device_id={"ctx": lax.rem(c + d, nc)},
            device_id_type=pl.DeviceIdType.MESH,
        )
    pl.semaphore_wait(barrier, nf + nc - 2)
    if moving:
        lo, hi = halves(piece)
        (one_lo, one_hi), (two_lo, two_hi) = halves(one), halves(two)
        first = [moves.start(lo, one_lo, 1), moves.start(hi, two_hi, 2)]
        rest = [moves.start(hi, one_hi, 1), moves.start(lo, two_lo, 2)]
    copies = []
    for d in range(1, nf):
        to = lax.rem(f + d, nf)
        copies.append(
            pltpu.make_async_remote_copy(
                src_ref=x_ref.at[to],
                dst_ref=land.at[d],
                send_sem=send_sem.at[d],
                recv_sem=recv_sem.at[d],
                device_id={"fsdp": to},
                device_id_type=pl.DeviceIdType.MESH,
            )
        )
        copies[-1].start()
    if moving:
        for copy in first:
            copy.wait()
        rest += [moves.start(one_lo, far_lo, 2), moves.start(two_hi, far_hi, 1)]
    total = x_ref[f]
    for d in range(1, nf):
        copies[d - 1].wait()
        total = total + land[d]
    stage[0] = total
    copies = []
    for d in range(1, nc):
        copies.append(
            pltpu.make_async_remote_copy(
                src_ref=stage.at[0],
                dst_ref=stage.at[d],
                send_sem=send_sem.at[nf + d],
                recv_sem=recv_sem.at[nf + d],
                device_id={"ctx": lax.rem(c + d, nc)},
                device_id_type=pl.DeviceIdType.MESH,
            )
        )
        copies[-1].start()
    for d in range(1, nc):
        copies[d - 1].wait()
        total = total + stage[d]
    o_ref[...] = total
    if moving:
        for copy in rest:
            copy.wait()


def reduce_small(x, nf, nc, call, piece=None):
    block = x.shape[1:]
    sems = pltpu.SemaphoreType.DMA((nf + nc,))
    moving = piece is not None
    vmem = pl.BlockSpec(memory_space=pltpu.VMEM)
    anywhere = pl.BlockSpec(memory_space=pl.ANY)
    outs = [jax.ShapeDtypeStruct(block, single)]
    scratch = [
        pltpu.VMEM((nf,) + block, single),
        pltpu.VMEM((nc,) + block, single),
        sems,
        sems,
    ]
    if moving:
        n = piece.shape[0] // 2
        shapes = [piece.shape, piece.shape, (n, piece.shape[1]), (n, piece.shape[1])]
        outs += [jax.ShapeDtypeStruct(shape, half) for shape in shapes]
        scratch += [pltpu.SemaphoreType.DMA((6,))] * 2
    out = pl.pallas_call(
        functools.partial(reduce_small_kernel, nf, nc, moving),
        out_shape=outs,
        in_specs=[vmem] + [anywhere] * moving,
        out_specs=[vmem] + [anywhere] * (len(outs) - 1),
        scratch_shapes=scratch,
        compiler_params=pltpu.CompilerParams(collective_id=call, has_side_effects=True),
        name="reduce_small",
    )(x, *([piece] if moving else []))
    return out[0], [[piece], [out[1]], [out[2]], [out[3], out[4]]] if moving else None


def per_device(
    tokens,
    cotangent,
    lengths,
    span_place,
    ln1_gain,
    ln1_shift,
    qkv_weight,
    q_bias,
    v_bias,
    out_weight,
    out_bias,
    ln2_gain,
    ln2_shift,
    up_weight,
    up_bias,
    down_weight,
    down_bias,
):
    rows, width = tokens.shape
    CTX = lax.axis_size("ctx")
    c = lax.axis_index("ctx")
    f = lax.axis_index("fsdp")
    nf = lax.axis_size("fsdp")
    wide = up_weight.shape[1]
    part = width // CTX
    heads = HEADS // CTX
    scale = 1.0 / math.sqrt(width // HEADS)
    shard = width // nf
    fpart = wide // nf // CTX
    wpart = wide // CTX

    def columns(x, width_each, stride, count):
        return jnp.concatenate(
            [
                lax.dynamic_slice_in_dim(x, k * stride + c * width_each, width_each, axis=1)
                for k in range(count)
            ],
            axis=1,
        )

    def after(x, *others):
        return lax.optimization_barrier((x, others))[0]

    def pick(x, axis):
        return lax.dynamic_index_in_dim(x, c, axis, keepdims=False)

    def gather_f(x):
        return lax.all_gather(x, "fsdp", axis=0, tiled=True)

    qkv_own = columns(qkv_weight, part, width, 3)
    up_own = columns(up_weight, fpart, wide // nf, nf)
    down_own = lax.dynamic_slice_in_dim(down_weight, c * fpart, fpart, axis=0)
    w_qkv = gather_f(qkv_own.astype(half))
    small = jnp.concatenate(
        [ln1_gain, ln1_shift, q_bias, v_bias, out_bias, ln2_gain, ln2_shift, down_bias, up_bias]
    )
    small_len = small.shape[0]
    small = jnp.pad(small, (0, -small_len % 1024)).reshape(-1, 128)
    small_all = gather_small(small, nf).reshape(nf, -1)[:, :small_len]
    small_all = small_all.astype(half).astype(single)

    def vector(k):
        return small_all[:, k * shard : (k + 1) * shard].reshape(width)

    gain1, shift1, bias_q, bias_v, bias_o, gain2, shift2, bias_d = [vector(k) for k in range(8)]
    bias_u = pick(small_all[:, 8 * shard :].reshape(nf, CTX, fpart), 1).reshape(wpart)
    bias_qkv = jnp.concatenate(
        [pick(bias_q.reshape(CTX, part), 0), jnp.zeros((part,), single), pick(bias_v.reshape(CTX, part), 0)]
    )
    w_out = gather_f(out_weight.astype(half))

    per = rows // SPAN
    table = jnp.arange(CTX * per, dtype=jnp.int32)
    source = ((table // per) ^ c) * per + table % per
    place = jnp.sum(jnp.where(source[:, None] == table[None, :], span_place[0][None, :], 0), axis=1)
    inv = jnp.sum(jnp.where(place[None, :] == table[:, None], table[None, :], 0), axis=1)
    slopes = 2.0 ** (-8.0 * ((c * heads + jnp.arange(heads)).astype(single) + 1.0) / HEADS)

    def flat(pieces):
        return [x for p in pieces for x in p]

    def scatter_f(x):
        return lax.psum_scatter(x, "fsdp", scatter_dimension=0, tiled=True)

    far = CTX - 1
    mid = list(range(1, far))

    def first_norm(x):
        normed, _ = norm_parts(x.astype(single))
        return (normed * gain1 + shift1).astype(half)

    tok_near = after(gather_first(tokens), small_all, place, inv, slopes)
    tok = gather_second(tokens, tok_near)
    near = [[first_norm(x) for x in p] for p in tok[:far]]
    tok = after(tok, near)
    n = rows // 2
    if CTX == 4:
        cot = after(cotangent, tok)
        dz2_lo, dz2_hi = cot[:n].astype(half), cot[n:].astype(half)
    else:
        dz2_own = after(cotangent, tok).astype(half)
        dz2_rest = gather_first(dz2_own)
    w_up = gather_f(after(up_own.astype(half), tok))
    a1 = flat(near)
    if CTX == 4:
        joined, a1_far, dz2_first = qkv_forward(
            tok[far], gain1, shift1, a1, w_qkv, bias_qkv, dz2_lo, dz2_hi
        )
        a1 = a1 + list(a1_far)
        dz2_rest = after((dz2_hi, dz2_lo), joined)
        dz2_rest = [swap(dz2_rest[0], 1), swap(dz2_rest[1], 2)]
    else:
        a1 = a1 + [first_norm(x) for x in tok[far]]
        joined = joined_rows(a1, w_qkv, bias_qkv, "qkv")
    w_down = gather_f(after(down_own.astype(half), joined))
    attended = attn_forward(joined, inv, slopes, heads, scale)
    mine = [attended[j * rows : (j + 1) * rows] for j in range(CTX)]
    mine = after(mine, dz2_rest)
    mine = [mine[0]] + [swap(mine[j], j) for j in range(1, CTX)]
    ob = jnp.concatenate(xor_order(mine, c), axis=1)
    y1 = tokens.astype(single) + dot_nn(ob, w_out) + bias_o

    normed2, inv2 = norm_parts(y1)
    if CTX == 4:
        one_lo, two_hi = after(dz2_first, ob)
        one_hi, two_lo = dz2_rest
        dz2 = [[dz2_lo, dz2_hi], [one_lo, one_hi], [two_lo, two_hi], [swap(one_lo, 2), swap(two_hi, 1)]]
    else:
        dz2 = [[dz2_own]] + [[x] for x in dz2_rest]
    a2_own = (normed2 * gain2 + shift2).astype(half)
    gb, slope = [None] * CTX, [None] * CTX
    gb[0], slope[0] = up_gelu([a2_own], w_up, bias_u, "up_gelu_0")
    last = gb[0]
    a2 = gather_second(a2_own, after(gather_first(a2_own), last))
    for j in range(1, CTX):
        gb[j], slope[j] = up_gelu(after(a2[j], last), w_up, bias_u, f"up_gelu_{j}")
        last = gb[j]
    gb_blocks = flat(gb)
    if CTX == 4:
        gb_blocks = [(g[0], n, i) for g in gb[:far] for i in (0, 1)] + list(gb[far])
    down_grad = outer(gb_blocks, flat(dz2), "down_grad")
    down_part = scatter_f(down_grad)
    w_down = after(w_down, down_grad)

    du, dh2, mix = [None] * CTX, [None] * CTX, [None] * CTX
    if CTX == 4:
        du, dh2, up_grad, mix_first = feed_back(
            flat(dz2), flat(slope), w_down, w_up, flat(a2), gb[far]
        )
        du = [du]
    else:
        for j in range(CTX):
            du[j] = hidden_back(dz2[j], w_down, slope[j], f"du_{j}")
            dh2[j] = plain(du[j], w_up, True, half if j else single, f"dh2_{j}")[0]
        arrived = scatter_send(dh2[1:])
        dh2 = dh2[0]
        up_grad = outer(flat(a2), flat(du), "up_grad")
        mix[far] = plain(gb[far], w_down, False, half, "mix_far")[0]
        dh2 = total_of(dh2, arrived)
    up_part = scatter_f(up_grad)
    up_bias_grad = sum(jnp.sum(x.astype(single), axis=0) for x in flat(du))
    down_bias_grad = sum(jnp.sum(x.astype(single), axis=0) for x in dz2[0])
    if CTX == 4:
        dy1, sums2, dattn, out_grad, mix, down_near = heads_back(
            dh2, cotangent, y1, gain2, w_out, ob, gb[1][0], gb[2][0], w_down, mix_first, down_part
        )
        one_lo, one_hi, two_lo, two_hi = mix
        gain2_grad, shift2_grad, out_bias_grad = sums2[0], sums2[1], sums2[2]
    else:
        gain2_grad = jnp.sum(dh2 * normed2, axis=0)
        shift2_grad = jnp.sum(dh2, axis=0)
        dy1 = cotangent + norm_back(normed2, inv2, gain2, dh2)
        dz1 = dy1.astype(half)
        dattn = dot_nt(dz1, w_out).astype(half)
        out_bias_grad = jnp.sum(dz1.astype(single), axis=0)
        dattn = xor_order([dattn[:, s * part : (s + 1) * part] for s in range(CTX)], c)
        dattn = [dattn[0]] + [swap(dattn[j], j) for j in range(1, CTX)]
        dattn = jnp.concatenate(dattn, axis=0)
        out_grad = outer([ob], [dz1], "out_grad")
        for j in mid:
            mix[j] = plain(gb[j], w_down, False, half, f"mix_{j}")[0]
        down_near = gather_first(down_part)
    out_part = scatter_f(out_grad)
    dqkv = attn_backward(joined, dattn, inv, slopes, heads, scale)
    if CTX == 4:
        lows = [swap(one_lo, 1), swap(two_lo, 2)]
        dqkv = after(dqkv, lows, up_part)
        highs = [swap(one_hi, 1), swap(two_hi, 2)]
        dh1, arrived, qkv_grad, mix_own = qkv_back(dqkv, w_qkv, a1, gb[0][0], w_down)
        dh1 = after(dh1, highs)
        mixed = y1 + bias_d + mix_own
        mixed = jnp.concatenate([total_of(mixed[:n], lows), total_of(mixed[n:], highs)])
    else:
        dh1 = [
            plain([(dqkv, rows, j)], w_qkv, True, half if j else single, f"dh1_{j}")[0]
            for j in range(CTX)
        ]
        arrived = scatter_send(dh1[1:])
        dh1 = dh1[0]
        qkv_grad = outer(a1, [(dqkv, rows, j) for j in range(CTX)], "qkv_grad")
        mix_own = plain(gb[0], w_down, False, single, "mix_0")[0]
        mixed = total_of(y1 + bias_d + mix_own, scatter_send(mix[1:]))
    dh1 = total_of(dh1, arrived)
    down_out = gather_second(down_part, after(down_near, dh1))
    down_out = lay_out(0, down_out, c, width // min(width, 512))
    up_out = lay_out(1, gather_ctx(after(up_part, dh1)), c, nf)
    sums = jnp.sum(dqkv.astype(single), axis=0)
    normed1_own, inv1_own = norm_parts(tokens.astype(single))
    gain1_grad = jnp.sum(dh1 * normed1_own, axis=0)
    shift1_grad = jnp.sum(dh1, axis=0)
    input_grad = dy1 + norm_back(normed1_own, inv1_own, gain1, dh1)

    qkv_part = scatter_f(after(qkv_grad, input_grad))
    bit = 1
    while bit < CTX:
        out_part = out_part.astype(half)
        out_part = out_part.astype(single) + swap(out_part, bit).astype(single)
        bit *= 2
    out_out = out_part

    def spread(x, inner):
        x = x.reshape(-1, 1, inner)
        mask = (jnp.arange(CTX) == c)[None, :, None]
        return jnp.where(mask, x, 0.0).reshape(-1)

    def reduced(items, call):
        sizes = [x.shape[0] // nf for x in items]
        x = jnp.concatenate([x.reshape(nf, -1) for x in items], axis=1)
        x = jnp.pad(x, ((0, 0), (0, -x.shape[1] % 1024))).reshape(nf, -1, 128)
        x, qkv_all = reduce_small(x, nf, CTX, call, qkv_part if CTX == 4 else None)
        x = x.reshape(-1)
        out, at = [], 0
        for n in sizes:
            out.append(x[at : at + n])
            at += n
        return out, qkv_all

    sums_in = [out_bias_grad, gain2_grad, shift2_grad, down_bias_grad, spread(up_bias_grad, fpart)]
    gain1_grad = after(gain1_grad, qkv_part)
    sums_in += [gain1_grad, shift1_grad, spread(sums[:part], part), spread(sums[2 * part :], part)]
    sums_out, qkv_all = reduced(sums_in, 2)
    qkv_out = lay_out(1, qkv_all or gather_ctx(qkv_part), c, 3)
    out_bias_out, gain2_out, shift2_out, down_bias_out, up_bias_out = sums_out[:5]
    gain1_out, shift1_out, q_bias_out, v_bias_out = sums_out[5:]
    return (
        mixed,
        input_grad,
        gain1_out,
        shift1_out,
        qkv_out,
        q_bias_out,
        v_bias_out,
        out_out,
        out_bias_out,
        gain2_out,
        shift2_out,
        up_out,
        up_bias_out,
        down_out,
        down_bias_out,
    )


def solution(mesh):
    rows, flat = P(("ctx", "fsdp"), None), P("fsdp")
    mat = P("fsdp", None)
    in_specs = (
        rows,
        rows,
        mat,
        mat,
        flat,
        flat,
        mat,
        flat,
        flat,
        mat,
        flat,
        flat,
        flat,
        mat,
        flat,
        mat,
        flat,
    )
    out_specs = (
        rows,
        rows,
        flat,
        flat,
        mat,
        flat,
        flat,
        mat,
        flat,
        flat,
        flat,
        mat,
        flat,
        mat,
        flat,
    )
    return jax.shard_map(
        per_device, mesh=mesh, in_specs=in_specs, out_specs=out_specs, check_vma=False
    )
```

```python
import functools
import math

import jax
import jax.numpy as jnp
from jax import lax
from jax.experimental import pallas as pl
from jax.experimental.pallas import tpu as pltpu
from jax.sharding import PartitionSpec as P

HEADS = 16
SPAN = 128
SEQ_BLOCKS = 8

norm_eps = 1e-05
gelu_coef = 0.7978845608028654
LOG2E = 1.4426950408889634

half = jnp.bfloat16
single = jnp.float32


def dot_nn(a, b):
    return lax.dot_general(a, b, (((1,), (0,)), ((), ())), preferred_element_type=single)


def dot_nt(a, b):
    return lax.dot_general(a, b, (((1,), (1,)), ((), ())), preferred_element_type=single)


def dot_tn(a, b):
    return lax.dot_general(a, b, (((0,), (0,)), ((), ())), preferred_element_type=single)


def norm_parts(values):
    center = values - jnp.mean(values, axis=-1, keepdims=True)
    spread = jnp.mean(center * center, axis=-1, keepdims=True)
    inv = lax.rsqrt(spread + norm_eps)
    return center * inv, inv


def norm_back(normed, inv, gain, grad):
    dn = grad * gain
    return inv * (
        dn
        - jnp.mean(dn, axis=-1, keepdims=True)
        - normed * jnp.mean(dn * normed, axis=-1, keepdims=True)
    )


def gelu_both(v):
    t = jnp.tanh(gelu_coef * (v + 0.044715 * v * v * v))
    value = 0.5 * v * (1.0 + t)
    slope = 0.5 * (1.0 + t) + 0.5 * v * (1.0 - t * t) * gelu_coef * (1.0 + 3 * 0.044715 * v * v)
    return value, slope


def swap(x, mask):
    n = lax.axis_size("ctx")
    return lax.ppermute(x, "ctx", [(i, i ^ mask) for i in range(n)])


def gather_first(x):
    count = lax.axis_size("ctx")
    return [swap(x, j) for j in range(1, 3 if count == 4 else count)]


def gather_second(x, arrived):
    if lax.axis_size("ctx") != 4:
        return [[x]] + [[p] for p in arrived]
    one, two = arrived
    n = x.shape[0] // 2
    return [[x], [one], [two], [swap(one[:n], 2), swap(two[n:], 1)]]


def gather_ctx(x):
    return gather_second(x, gather_first(x))


def scatter_first(far):
    if lax.axis_size("ctx") != 4:
        return None
    return swap(far[0], 1), swap(far[1], 2)


def scatter_second(pieces, first):
    if first is None:
        return pieces[1:]
    p1, p2 = pieces[1], pieces[2]
    n = p1.shape[0] // 2
    from_x, from_y = first
    p1 = jnp.concatenate(
        [p1[:n], (p1[n:].astype(single) + from_y.astype(single)).astype(half)], axis=0
    )
    p2 = jnp.concatenate(
        [(p2[:n].astype(single) + from_x.astype(single)).astype(half), p2[n:]], axis=0
    )
    return [p1, p2]


def scatter_send(sent):
    return [swap(x, j + 1) for j, x in enumerate(sent)]


def total_of(own, arrived):
    for x in arrived:
        own = own + x.astype(single)
    return own


def xor_order(items, c):
    bit = 1
    while bit < len(items):
        on = (c & bit) == bit
        items = [jnp.where(on, items[i ^ bit], items[i]) for i in range(len(items))]
        bit *= 2
    return items


TILE = 256


def attn_scores(q_refs, k_refs, i, scale, slope):
    q = jnp.concatenate([q_refs[2 * i][...], q_refs[2 * i + 1][...]], axis=0)
    k = jnp.concatenate([r[...] for r in k_refs[: 2 * i + 2]], axis=0)
    n = TILE * (i + 1)
    col = lax.broadcasted_iota(jnp.int32, (1, n), 1) - (n - 1)
    s = dot_nt(q, k) * (scale * LOG2E) + (slope * LOG2E) * col.astype(single)
    row_at = lax.broadcasted_iota(jnp.int32, (TILE, TILE), 0)
    col_at = lax.broadcasted_iota(jnp.int32, (TILE, TILE), 1)
    last = jnp.where(col_at <= row_at, s[:, n - TILE :], -1e30)
    s = last if i == 0 else jnp.concatenate([s[:, : n - TILE], last], axis=1)
    e = jnp.exp2(s - jnp.max(s, axis=1, keepdims=True))
    return q, k, e, 1.0 / jnp.sum(e, axis=1, keepdims=True)


class Rows:
    def __init__(self, inv_ref, stage, out, sems, kinds):
        self.inv, self.stage, self.out, self.sems, self.kinds = inv_ref, stage, out, sems, kinds
        self.heads = pl.num_programs(1)
        self.step = pl.program_id(0) * self.heads + pl.program_id(1)
        self.slot = lax.rem(self.step, 2)

    def copies(self, step):
        slot = lax.rem(step, 2)
        seq, head = step // self.heads, lax.rem(step, self.heads)
        for kind in range(self.kinds):
            col = pl.multiple_of((kind * self.heads + head) * 128, 128)
            for j in range(SEQ_BLOCKS):
                row = pl.multiple_of(self.inv[seq * SEQ_BLOCKS + j] * SPAN, SPAN)
                yield pltpu.make_async_copy(
                    self.stage.at[slot, kind, pl.ds(j * SPAN, SPAN)],
                    self.out.at[pl.ds(row, SPAN), pl.ds(col, 128)],
                    self.sems.at[slot, kind * SEQ_BLOCKS + j],
                )

    def wait(self, step):
        for copy in self.copies(step):
            copy.wait()

    def open(self):
        @pl.when(self.step >= 2)
        def _():
            self.wait(self.step - 2)

    def close(self):
        for copy in self.copies(self.step):
            copy.start()

        @pl.when(self.step == 2 * self.heads - 1)
        def _():
            self.wait(self.step - 1)
            self.wait(self.step)


def attn_fwd_kernel(scale, inv_ref, slope_ref, *refs):
    q_refs, k_refs, v_refs = refs[:8], refs[8:16], refs[16:24]
    out, stage, sems = refs[24:]
    slope = slope_ref[pl.program_id(1)]
    rows = Rows(inv_ref, stage, out, sems, 1)
    rows.open()
    for i in range(4):
        q, k, e, r = attn_scores(q_refs, k_refs, i, scale, slope)
        v = jnp.concatenate([x[...] for x in v_refs[: 2 * i + 2]], axis=0)
        o = dot_nn((e * r).astype(half), v)
        stage[rows.slot, 0, TILE * i : TILE * (i + 1), :] = o.astype(half)
    rows.close()


def attn_bwd_kernel(scale, inv_ref, slope_ref, *refs):
    q_refs, k_refs, v_refs, g_refs = refs[:8], refs[8:16], refs[16:24], refs[24:32]
    out, stage, sems, dk_acc, dv_acc = refs[32:]
    slope = slope_ref[pl.program_id(1)]
    rows = Rows(inv_ref, stage, out, sems, 3)
    rows.open()
    for i in (3, 2, 1, 0):
        q, k, e, r = attn_scores(q_refs, k_refs, i, scale, slope)
        n = TILE * (i + 1)
        v = jnp.concatenate([x[...] for x in v_refs[: 2 * i + 2]], axis=0)
        g = jnp.concatenate([g_refs[2 * i][...], g_refs[2 * i + 1][...]], axis=0)
        p = e * r
        dp = dot_nt(g, v)
        delta = jnp.sum(p * dp, axis=1, keepdims=True)
        ds = (p * (dp - delta)).astype(half)
        pb = p.astype(half)
        dq = (dot_nn(ds, k) * scale).astype(half)
        stage[rows.slot, 0, TILE * i : TILE * (i + 1), :] = dq
        dk = dot_tn(ds, q)
        dv = dot_tn(pb, g)
        if i == 3:
            dk_acc[...] = dk
            dv_acc[...] = dv
        else:
            dk_acc[:n, :] += dk
            dv_acc[:n, :] += dv
    stage[rows.slot, 1] = (dk_acc[...] * scale).astype(half)
    stage[rows.slot, 2] = dv_acc[...].astype(half)
    rows.close()


def block_specs(offset):
    def one(j):
        return pl.BlockSpec(
            (SPAN, 128), lambda s, h, inv, slope: (inv[s * SEQ_BLOCKS + j], offset + h)
        )

    return [one(j) for j in range(SEQ_BLOCKS)]


def attn_call(kernel, kinds, joined, extra, extra_specs, scratch, inv, slopes, heads, cost, name):
    rows = joined.shape[0]
    specs = block_specs(0) + block_specs(heads) + block_specs(2 * heads) + extra_specs
    return pl.pallas_call(
        kernel,
        grid_spec=pltpu.PrefetchScalarGridSpec(
            num_scalar_prefetch=2,
            grid=(2, heads),
            in_specs=specs,
            out_specs=pl.BlockSpec(memory_space=pl.ANY),
            scratch_shapes=[
                pltpu.VMEM((2, kinds, rows // 2, 128), half),
                pltpu.SemaphoreType.DMA((2, kinds * SEQ_BLOCKS)),
            ]
            + scratch,
        ),
        out_shape=jax.ShapeDtypeStruct((rows, kinds * heads * 128), half),
        compiler_params=pltpu.CompilerParams(vmem_limit_bytes=48 * 1024 * 1024),
        cost_estimate=cost,
        name=name,
    )(inv, slopes, *([joined] * 24), *extra)


def attn_forward(joined, inv, slopes, heads, scale):
    kernel = functools.partial(attn_fwd_kernel, scale)
    cost = hint(20 * 10**9, joined.shape[0] * heads * 128 * 8)
    return attn_call(
        kernel, 1, joined, [], [], [], inv, slopes, heads, cost, "attn_forward"
    )


def attn_backward(joined, grad, inv, slopes, heads, scale):
    kernel = functools.partial(attn_bwd_kernel, scale)
    cost = hint(40 * 10**9, joined.shape[0] * heads * 128 * 14)
    sums = [pltpu.VMEM((joined.shape[0] // 2, 128), single)] * 2
    return attn_call(
        kernel,
        3,
        joined,
        [grad] * 8,
        block_specs(0),
        sums,
        inv,
        slopes,
        heads,
        cost,
        "attn_backward",
    )


HINT = 0.001


def block_of(x):
    return x if isinstance(x, tuple) else (x, x.shape[0], 0)


def hint(flops, bytes_accessed):
    return pl.CostEstimate(
        flops=int(HINT * flops), bytes_accessed=int(HINT * bytes_accessed), transcendentals=0
    )


def rows_kernel(dot, epilogue, count, extra, *refs):
    left, w_ref = refs[:count], refs[count]
    extras = refs[count + 1 : count + 1 + extra]
    outs = refs[count + 1 + extra :]
    for i in range(count):
        epilogue(i, dot(left[i][...], w_ref[...]), extras, outs)


def rows_matmul(blocks, w, transposed, extras, outs, epilogue, name, tile=512):
    blocks = [block_of(x) for x in blocks]
    extras = [block_of(x) for x in extras]
    n = w.shape[0] if transposed else w.shape[1]
    k = w.shape[1] if transposed else w.shape[0]
    t = math.gcd(n, tile)
    w_spec = (
        pl.BlockSpec((t, k), lambda i: (i, 0)) if transposed else pl.BlockSpec((k, t), lambda i: (0, i))
    )
    rows = sum(x[1] for x in blocks)
    return pl.pallas_call(
        functools.partial(
            rows_kernel, dot_nt if transposed else dot_nn, epilogue, len(blocks), len(extras)
        ),
        grid=(n // t,),
        in_specs=[pl.BlockSpec((x[1], k), lambda i, at=x[2]: (at, 0)) for x in blocks]
        + [w_spec]
        + [pl.BlockSpec((x[1], t), lambda i, at=x[2]: (at, i)) for x in extras],
        out_specs=[pl.BlockSpec((r, t), lambda i: (0, i)) for r, _ in outs],
        out_shape=[jax.ShapeDtypeStruct((r, n), d) for r, d in outs],
        compiler_params=pltpu.CompilerParams(vmem_limit_bytes=52 * 1024 * 1024),
        cost_estimate=hint(2 * rows * n * k, 2 * n * k + 4 * rows * (n + k)),
        name=name,
    )(*[x[0] for x in blocks], w, *[x[0] for x in extras])


def plain(blocks, w, transposed, dtype, name):
    def epilogue(i, x, extras, outs):
        outs[i][...] = x.astype(dtype)

    outs = [(block_of(x)[1], dtype) for x in blocks]
    return rows_matmul(blocks, w, transposed, [], outs, epilogue, name)


def joined_rows(blocks, w, bias, name):
    sizes = [block_of(x)[1] for x in blocks]

    def epilogue(i, x, extras, outs):
        at = sum(sizes[:i])
        outs[0][at : at + sizes[i], :] = (x + extras[0][...]).astype(half)

    bias = bias.reshape(1, -1)
    return rows_matmul(blocks, w, False, [bias], [(sum(sizes), half)], epilogue, name)[0]


def up_gelu(blocks, w, bias, name):
    count = len(blocks)

    def epilogue(i, x, extras, outs):
        value, slope = gelu_both(x + extras[0][...])
        outs[i][...] = value.astype(half)
        outs[count + i][...] = slope.astype(half)

    outs = [(block_of(x)[1], half) for x in blocks] * 2
    out = rows_matmul(blocks, w, False, [bias.reshape(1, -1)], outs, epilogue, name)
    return out[:count], out[count:]


def hidden_back(blocks, w, slopes, name):
    def epilogue(i, x, extras, outs):
        x = x.astype(half).astype(single) * extras[i][...].astype(single)
        outs[i][...] = x.astype(half)

    outs = [(block_of(x)[1], half) for x in blocks]
    return rows_matmul(blocks, w, True, slopes, outs, epilogue, name)


def outer_kernel(count, *refs):
    out = refs[-1]
    total = None
    for i in range(count):
        x = dot_tn(refs[i][...], refs[count + i][...])
        total = x if total is None else total + x
    out[...] = total.astype(half)


def outer(left, right, name):
    left = [block_of(x) for x in left]
    right = [block_of(x) for x in right]
    m, n = left[0][0].shape[1], right[0][0].shape[1]
    tm = math.gcd(m, 1024)
    tn = n // 2 if n % 256 == 0 and n > 1024 else n
    rows = sum(x[1] for x in left)
    return pl.pallas_call(
        functools.partial(outer_kernel, len(left)),
        grid=(m // tm, n // tn),
        in_specs=[pl.BlockSpec((x[1], tm), lambda i, j, at=x[2]: (at, i)) for x in left]
        + [pl.BlockSpec((x[1], tn), lambda i, j, at=x[2]: (at, j)) for x in right],
        out_specs=pl.BlockSpec((tm, tn), lambda i, j: (i, j)),
        out_shape=jax.ShapeDtypeStruct((m, n), half),
        compiler_params=pltpu.CompilerParams(vmem_limit_bytes=52 * 1024 * 1024),
        cost_estimate=hint(2 * rows * m * n, 2 * rows * (m + n) + 2 * m * n),
        name=name,
    )(*[x[0] for x in left], *[x[0] for x in right])


def partner(mask):
    c = lax.axis_index("ctx")
    if mask == 1:
        return c + 1 - 2 * lax.rem(c, 2)
    return lax.rem(c + 2, 4) if mask == 2 else 3 - c


def greet(masks):
    barrier = pltpu.get_barrier_semaphore()
    for mask in masks:
        pl.semaphore_signal(
            barrier,
            inc=1,
            device_id={"ctx": partner(mask)},
            device_id_type=pl.DeviceIdType.MESH,
        )
    pl.semaphore_wait(barrier, len(masks))


class Moves:
    def __init__(self, send_sem, recv_sem):
        self.send_sem, self.recv_sem, self.used = send_sem, recv_sem, 0

    def start(self, src, dst, mask):
        copy = pltpu.make_async_remote_copy(
            src_ref=src,
            dst_ref=dst,
            send_sem=self.send_sem.at[self.used],
            recv_sem=self.recv_sem.at[self.used],
            device_id={"ctx": partner(mask)},
            device_id_type=pl.DeviceIdType.MESH,
        )
        self.used += 1
        copy.start()
        return copy


def multiply(lefts, w, transposed, extras, outs, epilogue, tile=512):
    k = lefts[0].shape[1]
    n = w.shape[0] if transposed else w.shape[1]
    t = math.gcd(n, tile)
    w_spec = (
        pl.BlockSpec((t, k), lambda i: (i, 0)) if transposed else pl.BlockSpec((k, t), lambda i: (0, i))
    )
    dot = dot_nt if transposed else dot_nn

    def body(*refs):
        rows_kernel(dot, epilogue, len(lefts), len(extras), *refs)

    pltpu.emit_pipeline(
        body,
        grid=(n // t,),
        in_specs=[pl.BlockSpec((x.shape[0], k), lambda i: (0, 0)) for x in lefts]
        + [w_spec]
        + [pl.BlockSpec((x.shape[0], t), lambda i: (0, i)) for x in extras],
        out_specs=[pl.BlockSpec((x.shape[0], t), lambda i: (0, i)) for x in outs],
    )(*lefts, w, *extras, *outs)


def store(i, x, extras, outs):
    outs[i][...] = x.astype(outs[i].dtype)


def store_sum(i, x, extras, outs):
    outs[i][...] = (x + extras[i][...].astype(single)).astype(outs[i].dtype)


def store_passed(i, x, extras, outs):
    if i in (1, 2):
        x = x + extras[i - 1][...].astype(single)
    outs[i][...] = x.astype(outs[i].dtype)


def store_hidden(i, x, extras, outs):
    outs[i][...] = (x.astype(half).astype(single) * extras[i][...].astype(single)).astype(half)


def outer_on(lefts, rights, out):
    m, n = out.shape
    tm = math.gcd(m, 1024)
    tn = n // 2 if n % 256 == 0 and n > 1024 else n

    def body(*refs):
        outer_kernel(len(lefts), *refs)

    pltpu.emit_pipeline(
        body,
        grid=(m // tm, n // tn),
        in_specs=[pl.BlockSpec((x.shape[0], tm), lambda i, j: (0, i)) for x in lefts]
        + [pl.BlockSpec((x.shape[0], tn), lambda i, j: (0, j)) for x in rights],
        out_specs=[pl.BlockSpec((tm, tn), lambda i, j: (i, j))],
    )(*lefts, *rights, out)


def halves(ref):
    n = ref.shape[0] // 2
    return ref.at[pl.ds(0, n)], ref.at[pl.ds(n, n)]


def moving_call(kernel, operands, outs, moves, call, flops, name):
    anywhere = pl.BlockSpec(memory_space=pl.ANY)
    sems = pltpu.SemaphoreType.DMA((moves,))
    return pl.pallas_call(
        kernel,
        in_specs=[anywhere] * len(operands),
        out_specs=[anywhere] * len(outs),
        out_shape=[jax.ShapeDtypeStruct(shape, dtype) for shape, dtype in outs],
        scratch_shapes=[sems, sems],
        compiler_params=pltpu.CompilerParams(
            collective_id=call, has_side_effects=True, vmem_limit_bytes=52 * 1024 * 1024
        ),
        cost_estimate=hint(flops, 0),
        name=name,
    )(*operands)


def store_biased(i, x, extras, outs):
    outs[i][...] = (x + extras[0][...]).astype(half)


def qkv_kernel(*refs):
    tok, gain, shift, a1, w_qkv, bias = refs[0:2], refs[2], refs[3], refs[4:7], refs[7], refs[8]
    dz_lo, dz_hi = refs[9:11]
    joined, far, one_lo, two_hi = refs[11], refs[12:14], refs[14], refs[15]
    moves = Moves(*refs[16:18])
    n, width = tok[0].shape
    greet((1, 2))
    copies = [moves.start(dz_lo, one_lo, 1), moves.start(dz_hi, two_hi, 2)]

    def norm(x_lo, x_hi, g, s, o_lo, o_hi):
        for x, o in ((x_lo, o_lo), (x_hi, o_hi)):
            normed, _ = norm_parts(x[...].astype(single))
            o[...] = (normed * g[...] + s[...]).astype(half)

    t = math.gcd(n, 64)
    block = pl.BlockSpec((t, width), lambda i: (i, 0))
    row = pl.BlockSpec((1, width), lambda i: (0, 0))
    pltpu.emit_pipeline(
        norm, grid=(n // t,), in_specs=[block, block, row, row], out_specs=[block, block]
    )(*tok, gain, shift, *far)
    lefts, outs, at = [*a1, *far], [], 0
    for x in lefts:
        outs.append(joined.at[pl.ds(at, x.shape[0])])
        at += x.shape[0]
    multiply(lefts, w_qkv, False, [bias], outs, store_biased)
    for copy in copies:
        copy.wait()


def qkv_forward(tok, gain, shift, a1, w_qkv, bias, dz_lo, dz_hi):
    n, width = tok[0].shape
    k = w_qkv.shape[1]
    outs = [((8 * n, k), half)] + [((n, width), half)] * 4
    out = moving_call(
        qkv_kernel,
        [*tok, gain.reshape(1, -1), shift.reshape(1, -1), *a1, w_qkv, bias.reshape(1, -1), dz_lo, dz_hi],
        outs,
        2,
        7,
        16 * n * width * k,
        "qkv",
    )
    return out[0], out[1:3], out[3:5]


def feed_pass(dz, slope, w_down, w_up, du, total):
    n, width = dz[0].shape
    wide = w_down.shape[0]
    t = math.gcd(wide, 512)
    total[...] = jnp.zeros_like(total)

    def body(dz_lo, dz_hi, down, up, slope_lo, slope_hi, du_lo, du_hi):
        for i, x, s, d in ((0, dz_lo, slope_lo, du_lo), (1, dz_hi, slope_hi, du_hi)):
            grad = dot_nt(x[...], down[...]).astype(half).astype(single)
            grad = (grad * s[...].astype(single)).astype(half)
            d[...] = grad
            total[i * n : (i + 1) * n, :] += dot_nt(grad, up[...])

    pltpu.emit_pipeline(
        body,
        grid=(wide // t,),
        in_specs=[pl.BlockSpec((n, width), lambda i: (0, 0))] * 2
        + [pl.BlockSpec((t, width), lambda i: (i, 0)), pl.BlockSpec((width, t), lambda i: (0, i))]
        + [pl.BlockSpec((n, t), lambda i: (0, i))] * 2,
        out_specs=[pl.BlockSpec((n, t), lambda i: (0, i))] * 2,
    )(*dz, w_down, w_up, *slope, *du)


def feed_back_kernel(*refs):
    dz, slope, (w_down, w_up) = refs[0:8], refs[8:13], refs[13:15]
    a2, gb_far = refs[15:20], refs[20:22]
    du, own, land1, land2, up_grad, mix_x, mix_y = refs[22:27], *refs[27:33]
    total, far, near, rest, from_x, from_y, mixed = refs[33:40]
    moves = Moves(*refs[40:42])
    local = refs[42]
    n = from_x.shape[0]
    lo, hi = pl.ds(0, n), pl.ds(n, n)
    (s1_lo, s1_hi), (s2_lo, s2_hi) = halves(slope[1]), halves(slope[2])
    (d1_lo, d1_hi), (d2_lo, d2_hi) = halves(du[1]), halves(du[2])
    (land1_lo, land1_hi), (land2_lo, land2_hi) = halves(land1), halves(land2)
    greet((1, 2))
    wide, width = w_down.shape
    t = math.gcd(width, 512)

    def mix(x_lo, x_hi, w):
        at = pl.ds(pl.multiple_of(pl.program_id(0) * t, t), t)
        mixed[0:n, at] = dot_nn(x_lo[...], w[...]).astype(half)
        mixed[n : 2 * n, at] = dot_nn(x_hi[...], w[...]).astype(half)

    pltpu.emit_pipeline(
        mix,
        grid=(width // t,),
        in_specs=[pl.BlockSpec((n, wide), lambda i: (0, 0))] * 2
        + [pl.BlockSpec((wide, t), lambda i: (0, i))],
    )(*gb_far, w_down)
    second = [moves.start(mixed.at[lo], mix_x, 1), moves.start(mixed.at[hi], mix_y, 2)]
    feed_pass(dz[6:8], slope[3:5], w_down, w_up, du[3:5], total)
    far[...] = total[...].astype(half)
    first = [moves.start(far.at[lo], from_x, 1), moves.start(far.at[hi], from_y, 2)]
    feed_pass([dz[2], dz[5]], [s1_lo, s2_hi], w_down, w_up, [d1_lo, d2_hi], total)
    near[...] = total[...].astype(half)
    second += [moves.start(near.at[lo], land1_lo, 1), moves.start(near.at[hi], land2_hi, 2)]
    feed_pass([dz[3], dz[4]], [s1_hi, s2_lo], w_down, w_up, [d1_hi, d2_lo], total)
    for copy in first:
        copy.wait()
    rest[lo] = (total[lo] + from_y[...].astype(single)).astype(half)
    rest[hi] = (total[hi] + from_x[...].astype(single)).astype(half)
    second += [moves.start(rest.at[lo], land1_hi, 1), moves.start(rest.at[hi], land2_lo, 2)]
    feed_pass(dz[0:2], halves(slope[0]), w_down, w_up, halves(du[0]), total)
    store_own = pltpu.make_async_copy(total, own, local)
    store_own.start()
    outer_on(a2, du, up_grad)
    store_own.wait()
    for copy in second:
        copy.wait()


def feed_back(dz, slope, w_down, w_up, a2, gb_far):
    n, width = dz[0].shape
    rows, wide = 2 * n, w_down.shape[0]
    anywhere = pl.BlockSpec(memory_space=pl.ANY)
    outs = [((r, wide), half) for r in (rows, rows, rows, n, n)]
    outs += [((rows, width), single)] + [((rows, width), half)] * 2
    outs += [((width, wide), half)] + [((n, width), half)] * 2
    sems = pltpu.SemaphoreType.DMA((8,))
    out = pl.pallas_call(
        feed_back_kernel,
        in_specs=[anywhere] * 22,
        out_specs=[anywhere] * len(outs),
        out_shape=[jax.ShapeDtypeStruct(shape, dtype) for shape, dtype in outs],
        scratch_shapes=[pltpu.VMEM((rows, width), single)]
        + [pltpu.VMEM((rows, width), half)] * 3
        + [pltpu.VMEM((n, width), half)] * 2
        + [pltpu.VMEM((rows, width), half)]
        + [sems, sems, pltpu.SemaphoreType.DMA],
        compiler_params=pltpu.CompilerParams(
            collective_id=3, has_side_effects=True, vmem_limit_bytes=56 * 1024 * 1024
        ),
        cost_estimate=hint(26 * rows * width * wide, 0),
        name="feed_back",
    )(*dz, *slope, w_down, w_up, *a2, *gb_far)
    return out[0:5], out[5:8], out[8], out[9:11]


def heads_back_kernel(part, *refs):
    own, land1, land2, cot, y1, gain, w_out = refs[0:7]
    ob, gb1, gb2, w_down, mix_x, mix_y, down = refs[7:14]
    dy1, dz1, sums, got, out_grad = refs[14:19]
    mix, down1, down2 = refs[19:23], refs[23], refs[24]
    dz, w, stage = refs[25:28]
    moves = Moves(*refs[28:30])
    local = refs[30]
    rows, width = own.shape
    greet((1, 2, 3))
    load = pltpu.make_async_copy(w_out, w, local.at[0])
    load.start()
    copies = [moves.start(down, down1, 1), moves.start(down, down2, 2)]
    t = math.gcd(rows, 64)

    def norm(own, one, two, cot, y1, gain, dy1, dz1, sums):
        step = pl.program_id(0)
        grad = own[...] + one[...].astype(single) + two[...].astype(single)
        normed, inv = norm_parts(y1[...])
        dy = cot[...] + norm_back(normed, inv, gain[...], grad)
        low = dy.astype(half)
        dy1[...] = dy
        dz1[...] = low
        dz[pl.ds(pl.multiple_of(step * t, t), t), :] = low

        @pl.when(step == 0)
        def _():
            sums[...] = jnp.zeros_like(sums)

        sums[0:1] += jnp.sum(grad * normed, axis=0, keepdims=True)
        sums[1:2] += jnp.sum(grad, axis=0, keepdims=True)
        sums[2:3] += jnp.sum(low.astype(single), axis=0, keepdims=True)

    block = pl.BlockSpec((t, width), lambda i: (i, 0))
    pltpu.emit_pipeline(
        norm,
        grid=(rows // t,),
        in_specs=[block] * 5 + [pl.BlockSpec((1, width), lambda i: (0, 0))],
        out_specs=[block] * 2 + [pl.BlockSpec((8, width), lambda i: (0, 0))],
    )(own, land1, land2, cot, y1, gain, dy1, dz1, sums)
    load.wait()
    for mask in (3, 1, 2, 0):
        of = partner(mask) if mask else lax.axis_index("ctx")
        heads = w[pl.ds(pl.multiple_of(of * part, part), part), :]
        stage[mask] = dot_nt(dz[...], heads).astype(half)
        at = got.at[pl.ds(mask * rows, rows)]
        if mask:
            copies.append(moves.start(stage.at[mask], at, mask))
        else:
            keep = pltpu.make_async_copy(stage.at[0], at, local.at[1])
            keep.start()
    outer_on([ob], [dz1], out_grad)
    multiply(
        [*halves(gb1), *halves(gb2)],
        w_down,
        False,
        [mix_y, mix_x],
        mix,
        store_passed,
    )
    keep.wait()
    for copy in copies:
        copy.wait()


def heads_back(terms, cot, y1, gain, w_out, ob, gb1, gb2, w_down, mix_first, down):
    rows, width = cot.shape
    part = width // 4
    anywhere = pl.BlockSpec(memory_space=pl.ANY)
    sems = pltpu.SemaphoreType.DMA((5,))
    outs = [((rows, width), single), ((rows, width), half), ((8, width), single)]
    outs += [((4 * rows, part), half), ((width, width), half)]
    outs += [((rows // 2, width), half)] * 4 + [(down.shape, half)] * 2
    out = pl.pallas_call(
        functools.partial(heads_back_kernel, part),
        in_specs=[anywhere] * 14,
        out_specs=[anywhere] * len(outs),
        out_shape=[jax.ShapeDtypeStruct(shape, dtype) for shape, dtype in outs],
        scratch_shapes=[
            pltpu.VMEM((rows, width), half),
            pltpu.VMEM((width, width), half),
            pltpu.VMEM((4, rows, part), half),
            sems,
            sems,
            pltpu.SemaphoreType.DMA((2,)),
        ],
        compiler_params=pltpu.CompilerParams(
            collective_id=4, has_side_effects=True, vmem_limit_bytes=56 * 1024 * 1024
        ),
        cost_estimate=hint(10 * rows * width * width, 0),
        name="heads_back",
    )(*terms, cot, y1, gain.reshape(1, -1), w_out, ob, gb1, gb2, w_down, *mix_first, down)
    return out[0], out[2], out[3], out[4], out[5:9], out[9:11]


def qkv_back_kernel(*refs):
    dqkv, w_qkv = refs[0:2]
    a1, gb_own, w_down, one_hi, two_hi = refs[2:7], *refs[7:11]
    own, p3, p1, p2, from_x, from_y, land1, land2, qkv_grad, mix_own = refs[11:21]
    x_hi, y_hi = refs[21:23]
    moves = Moves(*refs[23:25])
    rows = own.shape[0]
    n = rows // 2

    def block(k):
        return dqkv.at[pl.ds(k * n, n)]

    greet((1, 2))
    output = [moves.start(one_hi, x_hi, 1), moves.start(two_hi, y_hi, 2)]
    (p3_lo, p3_hi), (p1_lo, p1_hi), (p2_lo, p2_hi) = halves(p3), halves(p1), halves(p2)
    (land1_lo, land1_hi), (land2_lo, land2_hi) = halves(land1), halves(land2)
    multiply([block(6), block(7)], w_qkv, True, [], [p3_lo, p3_hi], store)
    first = [moves.start(p3_lo, from_x, 1), moves.start(p3_hi, from_y, 2)]
    multiply([block(2), block(5)], w_qkv, True, [], [p1_lo, p2_hi], store)
    second = [moves.start(p1_lo, land1_lo, 1), moves.start(p2_hi, land2_hi, 2)]
    multiply([dqkv.at[pl.ds(0, rows)]], w_qkv, True, [], [own], store)
    multiply([gb_own], w_down, False, [], [mix_own], store)
    for copy in first:
        copy.wait()
    multiply([block(3), block(4)], w_qkv, True, [from_y, from_x], [p1_hi, p2_lo], store_sum)
    second += [moves.start(p1_hi, land1_hi, 1), moves.start(p2_lo, land2_lo, 2)]
    rights, at = [], 0
    for x in a1:
        rights.append(dqkv.at[pl.ds(at, x.shape[0])])
        at += x.shape[0]
    outer_on(a1, rights, qkv_grad)
    for copy in output + second:
        copy.wait()


def qkv_back(dqkv, w_qkv, a1, gb_own, w_down, one_hi, two_hi):
    rows, width = a1[0].shape
    wide = gb_own.shape[1]
    n = rows // 2
    outs = [((rows, width), single)] + [((rows, width), half)] * 3
    outs += [((n, width), half)] * 2 + [((rows, width), half)] * 2
    outs += [((width, dqkv.shape[1]), half), ((rows, width), single)] + [((n, width), half)] * 2
    out = moving_call(
        qkv_back_kernel,
        [dqkv, w_qkv, *a1, gb_own, w_down, one_hi, two_hi],
        outs,
        8,
        5,
        16 * rows * width * dqkv.shape[1] + 2 * rows * width * wide,
        "qkv_back",
    )
    return out[0], out[6:8], out[8], out[9], out[10:12]


def lay_out_kernel(axis, layout, c_ref, *refs):
    out = refs[-1]
    for (j, row), ref in zip(layout, refs):
        x = ref[...].astype(single)
        r, w = x.shape
        if axis == 0:
            n = sum(ref.shape[0] for (k, _), ref in zip(layout, refs) if k == j)
            out[pl.ds(pl.multiple_of((c_ref[0] ^ j) * n + row, r), r), :] = x
        else:
            out[row : row + r, pl.ds(pl.multiple_of((c_ref[0] ^ j) * w, w), w)] = x


def lay_out(axis, pieces, c, groups):
    count = len(pieces)
    r = sum(x.shape[0] for x in pieces[0])
    n = pieces[0][0].shape[1]
    w = n // groups
    if w % 128:
        whole = xor_order([jnp.concatenate(p, axis=0).astype(single) for p in pieces], c)
        whole = jnp.stack([p.reshape(r, groups, w) for p in whole], axis=2)
        return whole.reshape(r, count * n)
    layout, blocks = [], []
    for j, p in enumerate(pieces):
        row = 0
        for x in p:
            layout.append((j, row))
            blocks.append(x)
            row += x.shape[0]
    out = (count * r, w) if axis == 0 else (r, count * w)
    return pl.pallas_call(
        functools.partial(lay_out_kernel, axis, layout),
        grid_spec=pltpu.PrefetchScalarGridSpec(
            num_scalar_prefetch=1,
            grid=(groups,),
            in_specs=[pl.BlockSpec((x.shape[0], w), lambda k, c: (0, k)) for x in blocks],
            out_specs=pl.BlockSpec(out, lambda k, c: (0, k)),
        ),
        out_shape=jax.ShapeDtypeStruct((out[0], out[1] * groups), single),
        compiler_params=pltpu.CompilerParams(vmem_limit_bytes=48 * 1024 * 1024),
        cost_estimate=hint(0, 6 * r * n * count),
        name="lay_out",
    )(c.reshape(1), *blocks)


def gather_small_kernel(nf, x_ref, o_ref, send_sem, recv_sem):
    f = lax.axis_index("fsdp")
    barrier = pltpu.get_barrier_semaphore()
    for d in range(1, nf):
        pl.semaphore_signal(
            barrier,
            inc=1,
            device_id={"fsdp": lax.rem(f + d, nf)},
            device_id_type=pl.DeviceIdType.MESH,
        )
    pl.semaphore_wait(barrier, nf - 1)
    copies = []
    for d in range(1, nf):
        copies.append(
            pltpu.make_async_remote_copy(
                src_ref=x_ref,
                dst_ref=o_ref.at[f],
                send_sem=send_sem.at[d],
                recv_sem=recv_sem.at[d],
                device_id={"fsdp": lax.rem(f + d, nf)},
                device_id_type=pl.DeviceIdType.MESH,
            )
        )
        copies[-1].start()
    o_ref[f] = x_ref[...]
    for copy in copies:
        copy.wait()


def gather_small(x, nf):
    return pl.pallas_call(
        functools.partial(gather_small_kernel, nf),
        out_shape=jax.ShapeDtypeStruct((nf,) + x.shape, single),
        in_specs=[pl.BlockSpec(memory_space=pltpu.VMEM)],
        out_specs=pl.BlockSpec(memory_space=pltpu.VMEM),
        scratch_shapes=[pltpu.SemaphoreType.DMA((nf,)), pltpu.SemaphoreType.DMA((nf,))],
        compiler_params=pltpu.CompilerParams(collective_id=1, has_side_effects=True),
        name="gather_small",
    )(x)


def reduce_small_kernel(nf, nc, x_ref, o_ref, land, stage, send_sem, recv_sem):
    f = lax.axis_index("fsdp")
    c = lax.axis_index("ctx")
    barrier = pltpu.get_barrier_semaphore()
    for d in range(1, nf):
        pl.semaphore_signal(
            barrier,
            inc=1,
            device_id={"fsdp": lax.rem(f + d, nf)},
            device_id_type=pl.DeviceIdType.MESH,
        )
    for d in range(1, nc):
        pl.semaphore_signal(
            barrier,
            inc=1,
            device_id={"ctx": lax.rem(c + d, nc)},
            device_id_type=pl.DeviceIdType.MESH,
        )
    pl.semaphore_wait(barrier, nf + nc - 2)
    copies = []
    for d in range(1, nf):
        to = lax.rem(f + d, nf)
        copies.append(
            pltpu.make_async_remote_copy(
                src_ref=x_ref.at[to],
                dst_ref=land.at[d],
                send_sem=send_sem.at[d],
                recv_sem=recv_sem.at[d],
                device_id={"fsdp": to},
                device_id_type=pl.DeviceIdType.MESH,
            )
        )
        copies[-1].start()
    total = x_ref[f]
    for d in range(1, nf):
        copies[d - 1].wait()
        total = total + land[d]
    stage[0] = total
    copies = []
    for d in range(1, nc):
        copies.append(
            pltpu.make_async_remote_copy(
                src_ref=stage.at[0],
                dst_ref=stage.at[d],
                send_sem=send_sem.at[nf + d],
                recv_sem=recv_sem.at[nf + d],
                device_id={"ctx": lax.rem(c + d, nc)},
                device_id_type=pl.DeviceIdType.MESH,
            )
        )
        copies[-1].start()
    for d in range(1, nc):
        copies[d - 1].wait()
        total = total + stage[d]
    o_ref[...] = total


def reduce_small(x, nf, nc, call):
    block = x.shape[1:]
    sems = pltpu.SemaphoreType.DMA((nf + nc,))
    return pl.pallas_call(
        functools.partial(reduce_small_kernel, nf, nc),
        out_shape=jax.ShapeDtypeStruct(block, single),
        in_specs=[pl.BlockSpec(memory_space=pltpu.VMEM)],
        out_specs=pl.BlockSpec(memory_space=pltpu.VMEM),
        scratch_shapes=[
            pltpu.VMEM((nf,) + block, single),
            pltpu.VMEM((nc,) + block, single),
            sems,
            sems,
        ],
        compiler_params=pltpu.CompilerParams(collective_id=call, has_side_effects=True),
        name="reduce_small",
    )(x)


def per_device(
    tokens,
    cotangent,
    lengths,
    span_place,
    ln1_gain,
    ln1_shift,
    qkv_weight,
    q_bias,
    v_bias,
    out_weight,
    out_bias,
    ln2_gain,
    ln2_shift,
    up_weight,
    up_bias,
    down_weight,
    down_bias,
):
    rows, width = tokens.shape
    CTX = lax.axis_size("ctx")
    c = lax.axis_index("ctx")
    f = lax.axis_index("fsdp")
    nf = lax.axis_size("fsdp")
    wide = up_weight.shape[1]
    part = width // CTX
    heads = HEADS // CTX
    scale = 1.0 / math.sqrt(width // HEADS)
    shard = width // nf
    fpart = wide // nf // CTX
    wpart = wide // CTX

    def columns(x, width_each, stride, count):
        return jnp.concatenate(
            [
                lax.dynamic_slice_in_dim(x, k * stride + c * width_each, width_each, axis=1)
                for k in range(count)
            ],
            axis=1,
        )

    def after(x, *others):
        return lax.optimization_barrier((x, others))[0]

    def pick(x, axis):
        return lax.dynamic_index_in_dim(x, c, axis, keepdims=False)

    def gather_f(x):
        return lax.all_gather(x, "fsdp", axis=0, tiled=True)

    qkv_own = columns(qkv_weight, part, width, 3)
    up_own = columns(up_weight, fpart, wide // nf, nf)
    down_own = lax.dynamic_slice_in_dim(down_weight, c * fpart, fpart, axis=0)
    w_qkv = gather_f(qkv_own.astype(half))
    up_own, down_own = up_own.astype(half), down_own.astype(half)
    small = jnp.concatenate(
        [ln1_gain, ln1_shift, q_bias, v_bias, out_bias, ln2_gain, ln2_shift, down_bias, up_bias]
    )
    small_len = small.shape[0]
    small = jnp.pad(small, (0, -small_len % 1024)).reshape(-1, 128)
    small_all = gather_small(small, nf).reshape(nf, -1)[:, :small_len]
    small_all = small_all.astype(half).astype(single)

    def vector(k):
        return small_all[:, k * shard : (k + 1) * shard].reshape(width)

    gain1, shift1, bias_q, bias_v, bias_o, gain2, shift2, bias_d = [vector(k) for k in range(8)]
    bias_u = pick(small_all[:, 8 * shard :].reshape(nf, CTX, fpart), 1).reshape(wpart)
    bias_qkv = jnp.concatenate(
        [pick(bias_q.reshape(CTX, part), 0), jnp.zeros((part,), single), pick(bias_v.reshape(CTX, part), 0)]
    )
    w_out = gather_f(out_weight.astype(half))

    per = rows // SPAN
    table = jnp.arange(CTX * per, dtype=jnp.int32)
    source = ((table // per) ^ c) * per + table % per
    place = jnp.sum(jnp.where(source[:, None] == table[None, :], span_place[0][None, :], 0), axis=1)
    inv = jnp.sum(jnp.where(place[None, :] == table[:, None], table[None, :], 0), axis=1)
    slopes = 2.0 ** (-8.0 * ((c * heads + jnp.arange(heads)).astype(single) + 1.0) / HEADS)

    def flat(pieces):
        return [x for p in pieces for x in p]

    def scatter_f(x):
        return lax.psum_scatter(x, "fsdp", scatter_dimension=0, tiled=True)

    far = CTX - 1
    mid = list(range(1, far))

    def first_norm(x):
        normed, _ = norm_parts(x.astype(single))
        return (normed * gain1 + shift1).astype(half)

    n = rows // 2
    dz2_lo, dz2_hi = cotangent[:n].astype(half), cotangent[n:].astype(half)
    early = (small_all, place, inv, slopes, up_own, down_own, dz2_lo, dz2_hi)
    early, tok_near = after((early, gather_first(tokens)))
    small_all, place, inv, slopes, up_own, down_own, dz2_lo, dz2_hi = early
    tok = gather_second(tokens, tok_near)
    near = [[first_norm(x) for x in p] for p in tok[:far]]
    tok = after(tok, near)
    if CTX != 4:
        dz2_own = jnp.concatenate([dz2_lo, dz2_hi], axis=0)
        dz2_rest = gather_first(dz2_own)
    w_up = gather_f(after(up_own, tok))
    a1 = flat(near)
    if CTX == 4:
        joined, a1_far, dz2_first = qkv_forward(
            tok[far], gain1, shift1, a1, w_qkv, bias_qkv, dz2_lo, dz2_hi
        )
        a1 = a1 + list(a1_far)
        dz2_rest = after((dz2_hi, dz2_lo), joined)
        dz2_rest = [swap(dz2_rest[0], 1), swap(dz2_rest[1], 2)]
    else:
        a1 = a1 + [first_norm(x) for x in tok[far]]
        joined = joined_rows(a1, w_qkv, bias_qkv, "qkv")
    w_down = gather_f(after(down_own, joined))
    attended = attn_forward(joined, inv, slopes, heads, scale)
    mine = [attended[j * rows : (j + 1) * rows] for j in range(CTX)]
    mine = after(mine, dz2_rest)
    mine = [mine[0]] + [swap(mine[j], j) for j in range(1, CTX)]
    ob = jnp.concatenate(xor_order(mine, c), axis=1)
    y1 = tokens.astype(single) + dot_nn(ob, w_out) + bias_o

    normed2, inv2 = norm_parts(y1)
    if CTX == 4:
        one_lo, two_hi = after(dz2_first, ob)
        one_hi, two_lo = dz2_rest
        dz2 = [[dz2_lo, dz2_hi], [one_lo, one_hi], [two_lo, two_hi], [swap(one_lo, 2), swap(two_hi, 1)]]
    else:
        dz2 = [[dz2_own]] + [[x] for x in dz2_rest]
    a2_own = (normed2 * gain2 + shift2).astype(half)
    gb, slope = [None] * CTX, [None] * CTX
    gb[0], slope[0] = up_gelu([a2_own], w_up, bias_u, "up_gelu_0")
    last = gb[0]
    a2 = gather_second(a2_own, after(gather_first(a2_own), last))
    for j in range(1, CTX):
        gb[j], slope[j] = up_gelu(after(a2[j], last), w_up, bias_u, f"up_gelu_{j}")
        last = gb[j]
    gb_blocks = flat(gb)
    if CTX == 4:
        gb_blocks = [(g[0], n, i) for g in gb[:far] for i in (0, 1)] + list(gb[far])
    down_grad = outer(gb_blocks, flat(dz2), "down_grad")
    down_part = scatter_f(down_grad)
    w_down = after(w_down, down_grad)

    du, dh2, mix = [None] * CTX, [None] * CTX, [None] * CTX
    if CTX == 4:
        du, dh2, up_grad, mix_first = feed_back(
            flat(dz2), flat(slope), w_down, w_up, flat(a2), gb[far]
        )
        du = [du]
    else:
        for j in range(CTX):
            du[j] = hidden_back(dz2[j], w_down, slope[j], f"du_{j}")
            dh2[j] = plain(du[j], w_up, True, half if j else single, f"dh2_{j}")[0]
        arrived = scatter_send(dh2[1:])
        dh2 = dh2[0]
        up_grad = outer(flat(a2), flat(du), "up_grad")
        mix[far] = plain(gb[far], w_down, False, half, "mix_far")[0]
        dh2 = total_of(dh2, arrived)
    up_part = scatter_f(up_grad)
    up_bias_grad = sum(jnp.sum(x.astype(single), axis=0) for x in flat(du))
    down_bias_grad = sum(jnp.sum(x.astype(single), axis=0) for x in dz2[0])
    if CTX == 4:
        dy1, sums2, dattn, out_grad, mix, down_near = heads_back(
            dh2, cotangent, y1, gain2, w_out, ob, gb[1][0], gb[2][0], w_down, mix_first, down_part
        )
        one_lo, one_hi, two_lo, two_hi = mix
        gain2_grad, shift2_grad, out_bias_grad = sums2[0], sums2[1], sums2[2]
    else:
        gain2_grad = jnp.sum(dh2 * normed2, axis=0)
        shift2_grad = jnp.sum(dh2, axis=0)
        dy1 = cotangent + norm_back(normed2, inv2, gain2, dh2)
        dz1 = dy1.astype(half)
        dattn = dot_nt(dz1, w_out).astype(half)
        out_bias_grad = jnp.sum(dz1.astype(single), axis=0)
        dattn = xor_order([dattn[:, s * part : (s + 1) * part] for s in range(CTX)], c)
        dattn = [dattn[0]] + [swap(dattn[j], j) for j in range(1, CTX)]
        dattn = jnp.concatenate(dattn, axis=0)
        out_grad = outer([ob], [dz1], "out_grad")
        for j in mid:
            mix[j] = plain(gb[j], w_down, False, half, f"mix_{j}")[0]
        down_near = gather_first(down_part)
    out_part = scatter_f(out_grad)
    dqkv = attn_backward(joined, dattn, inv, slopes, heads, scale)
    if CTX == 4:
        lows = [swap(one_lo, 1), swap(two_lo, 2)]
        dqkv = after(dqkv, lows, up_part)
        dh1, arrived, qkv_grad, mix_own, highs = qkv_back(
            dqkv, w_qkv, a1, gb[0][0], w_down, one_hi, two_hi
        )
        mixed = y1 + bias_d + mix_own
        mixed = jnp.concatenate([total_of(mixed[:n], lows), total_of(mixed[n:], highs)])
    else:
        dh1 = [
            plain([(dqkv, rows, j)], w_qkv, True, half if j else single, f"dh1_{j}")[0]
            for j in range(CTX)
        ]
        arrived = scatter_send(dh1[1:])
        dh1 = dh1[0]
        qkv_grad = outer(a1, [(dqkv, rows, j) for j in range(CTX)], "qkv_grad")
        mix_own = plain(gb[0], w_down, False, single, "mix_0")[0]
        mixed = total_of(y1 + bias_d + mix_own, scatter_send(mix[1:]))
    qkv_part = scatter_f(qkv_grad)
    up_own = after(up_part, arrived)
    up_near = gather_first(up_own)
    down_out = gather_second(down_part, after(down_near, arrived))
    dh1 = total_of(after(dh1, up_near), arrived)
    up_out = gather_second(up_own, up_near)
    sums = jnp.sum(dqkv.astype(single), axis=0)
    normed1_own, inv1_own = norm_parts(tokens.astype(single))
    gain1_grad = jnp.sum(dh1 * normed1_own, axis=0)
    shift1_grad = jnp.sum(dh1, axis=0)
    dy1 = after(dy1, up_out)
    input_grad = dy1 + norm_back(normed1_own, inv1_own, gain1, dh1)

    def add_swapped(x, mask):
        return (x.astype(single) + swap(x, mask).astype(single)).astype(half)

    if CTX == 4:
        k = out_part.shape[0] // 2
        out_lo, out_hi = add_swapped(out_part[:k], 1), add_swapped(out_part[k:], 2)
        out_lo, out_hi = (out_lo, swap(out_lo, 2)), (out_hi, swap(out_hi, 1))
        out_out = [x.astype(single) + y.astype(single) for x, y in (out_lo, out_hi)]
        out_out = jnp.concatenate(out_out, axis=0)
    else:
        bit = 1
        while bit < CTX:
            out_out = out_part.astype(single) + swap(out_part, bit).astype(single)
            out_part = out_out.astype(half)
            bit *= 2

    def spread(x, inner):
        x = x.reshape(-1, 1, inner)
        mask = (jnp.arange(CTX) == c)[None, :, None]
        return jnp.where(mask, x, 0.0).reshape(-1)

    def reduced(items, call):
        sizes = [x.shape[0] // nf for x in items]
        x = jnp.concatenate([x.reshape(nf, -1) for x in items], axis=1)
        x = jnp.pad(x, ((0, 0), (0, -x.shape[1] % 1024))).reshape(nf, -1, 128)
        x = reduce_small(x, nf, CTX, call).reshape(-1)
        out, at = [], 0
        for n in sizes:
            out.append(x[at : at + n])
            at += n
        return out

    sums_in = [out_bias_grad, gain2_grad, shift2_grad, down_bias_grad, spread(up_bias_grad, fpart)]
    sums_in += [gain1_grad, shift1_grad, spread(sums[:part], part), spread(sums[2 * part :], part)]
    qkv_near = gather_first(qkv_part)
    sums_in[5] = after(sums_in[5], qkv_near)
    sums_out = reduced(sums_in, 2)
    qkv_out = lay_out(1, gather_second(qkv_part, qkv_near), c, 3)
    down_out = lay_out(0, after(down_out, qkv_part), c, width // min(width, 512))
    up_out = lay_out(1, after(up_out, qkv_part), c, nf)
    out_bias_out, gain2_out, shift2_out, down_bias_out, up_bias_out = sums_out[:5]
    gain1_out, shift1_out, q_bias_out, v_bias_out = sums_out[5:]
    return (
        mixed,
        input_grad,
        gain1_out,
        shift1_out,
        qkv_out,
        q_bias_out,
        v_bias_out,
        out_out,
        out_bias_out,
        gain2_out,
        shift2_out,
        up_out,
        up_bias_out,
        down_out,
        down_bias_out,
    )


def solution(mesh):
    rows, flat = P(("ctx", "fsdp"), None), P("fsdp")
    mat = P("fsdp", None)
    in_specs = (
        rows,
        rows,
        mat,
        mat,
        flat,
        flat,
        mat,
        flat,
        flat,
        mat,
        flat,
        flat,
        flat,
        mat,
        flat,
        mat,
        flat,
    )
    out_specs = (
        rows,
        rows,
        flat,
        flat,
        mat,
        flat,
        flat,
        mat,
        flat,
        flat,
        flat,
        mat,
        flat,
        mat,
        flat,
    )
    return jax.shard_map(
        per_device, mesh=mesh, in_specs=in_specs, out_specs=out_specs, check_vma=False
    )
```

```python
import functools
import math

import jax
import jax.numpy as jnp
from jax import lax
from jax.experimental import pallas as pl
from jax.experimental.pallas import tpu as pltpu
from jax.sharding import PartitionSpec as P

HEADS = 16
SPAN = 128
SEQ_BLOCKS = 8

norm_eps = 1e-05
gelu_coef = 0.7978845608028654
LOG2E = 1.4426950408889634

half = jnp.bfloat16
single = jnp.float32


def dot_nn(a, b):
    return lax.dot_general(a, b, (((1,), (0,)), ((), ())), preferred_element_type=single)


def dot_nt(a, b):
    return lax.dot_general(a, b, (((1,), (1,)), ((), ())), preferred_element_type=single)


def dot_tn(a, b):
    return lax.dot_general(a, b, (((0,), (0,)), ((), ())), preferred_element_type=single)


def norm_parts(values):
    center = values - jnp.mean(values, axis=-1, keepdims=True)
    spread = jnp.mean(center * center, axis=-1, keepdims=True)
    inv = lax.rsqrt(spread + norm_eps)
    return center * inv, inv


def norm_back(normed, inv, gain, grad):
    dn = grad * gain
    return inv * (
        dn
        - jnp.mean(dn, axis=-1, keepdims=True)
        - normed * jnp.mean(dn * normed, axis=-1, keepdims=True)
    )


def gelu_both(v):
    t = jnp.tanh(gelu_coef * (v + 0.044715 * v * v * v))
    value = 0.5 * v * (1.0 + t)
    slope = 0.5 * (1.0 + t) + 0.5 * v * (1.0 - t * t) * gelu_coef * (1.0 + 3 * 0.044715 * v * v)
    return value, slope


def swap(x, mask):
    n = lax.axis_size("ctx")
    return lax.ppermute(x, "ctx", [(i, i ^ mask) for i in range(n)])


def gather_first(x):
    count = lax.axis_size("ctx")
    return [swap(x, j) for j in range(1, 3 if count == 4 else count)]


def gather_second(x, arrived):
    if lax.axis_size("ctx") != 4:
        return [[x]] + [[p] for p in arrived]
    one, two = arrived
    n = x.shape[0] // 2
    return [[x], [one], [two], [swap(one[:n], 2), swap(two[n:], 1)]]


def gather_ctx(x):
    return gather_second(x, gather_first(x))


def scatter_first(far):
    if lax.axis_size("ctx") != 4:
        return None
    return swap(far[0], 1), swap(far[1], 2)


def scatter_second(pieces, first):
    if first is None:
        return pieces[1:]
    p1, p2 = pieces[1], pieces[2]
    n = p1.shape[0] // 2
    from_x, from_y = first
    p1 = jnp.concatenate(
        [p1[:n], (p1[n:].astype(single) + from_y.astype(single)).astype(half)], axis=0
    )
    p2 = jnp.concatenate(
        [(p2[:n].astype(single) + from_x.astype(single)).astype(half), p2[n:]], axis=0
    )
    return [p1, p2]


def scatter_send(sent):
    return [swap(x, j + 1) for j, x in enumerate(sent)]


def total_of(own, arrived):
    for x in arrived:
        own = own + x.astype(single)
    return own


def xor_order(items, c):
    bit = 1
    while bit < len(items):
        on = (c & bit) == bit
        items = [jnp.where(on, items[i ^ bit], items[i]) for i in range(len(items))]
        bit *= 2
    return items


TILE = 256


def attn_scores(q_refs, k_refs, i, scale, slope):
    q = jnp.concatenate([q_refs[2 * i][...], q_refs[2 * i + 1][...]], axis=0)
    k = jnp.concatenate([r[...] for r in k_refs[: 2 * i + 2]], axis=0)
    n = TILE * (i + 1)
    col = lax.broadcasted_iota(jnp.int32, (1, n), 1) - (n - 1)
    s = dot_nt(q, k) * (scale * LOG2E) + (slope * LOG2E) * col.astype(single)
    row_at = lax.broadcasted_iota(jnp.int32, (TILE, TILE), 0)
    col_at = lax.broadcasted_iota(jnp.int32, (TILE, TILE), 1)
    last = jnp.where(col_at <= row_at, s[:, n - TILE :], -1e30)
    s = last if i == 0 else jnp.concatenate([s[:, : n - TILE], last], axis=1)
    e = jnp.exp2(s - jnp.max(s, axis=1, keepdims=True))
    return q, k, e, 1.0 / jnp.sum(e, axis=1, keepdims=True)


class Rows:
    def __init__(self, inv_ref, stage, out, sems, kinds):
        self.inv, self.stage, self.out, self.sems, self.kinds = inv_ref, stage, out, sems, kinds
        self.heads = pl.num_programs(1)
        self.step = pl.program_id(0) * self.heads + pl.program_id(1)
        self.slot = lax.rem(self.step, 2)

    def copies(self, step):
        slot = lax.rem(step, 2)
        seq, head = step // self.heads, lax.rem(step, self.heads)
        for kind in range(self.kinds):
            col = pl.multiple_of((kind * self.heads + head) * 128, 128)
            for j in range(SEQ_BLOCKS):
                row = pl.multiple_of(self.inv[seq * SEQ_BLOCKS + j] * SPAN, SPAN)
                yield pltpu.make_async_copy(
                    self.stage.at[slot, kind, pl.ds(j * SPAN, SPAN)],
                    self.out.at[pl.ds(row, SPAN), pl.ds(col, 128)],
                    self.sems.at[slot, kind * SEQ_BLOCKS + j],
                )

    def wait(self, step):
        for copy in self.copies(step):
            copy.wait()

    def open(self):
        @pl.when(self.step >= 2)
        def _():
            self.wait(self.step - 2)

    def close(self):
        for copy in self.copies(self.step):
            copy.start()

        @pl.when(self.step == 2 * self.heads - 1)
        def _():
            self.wait(self.step - 1)
            self.wait(self.step)


def attn_fwd_kernel(scale, inv_ref, slope_ref, *refs):
    q_refs, k_refs, v_refs = refs[:8], refs[8:16], refs[16:24]
    out, stage, sems = refs[24:]
    slope = slope_ref[pl.program_id(1)]
    rows = Rows(inv_ref, stage, out, sems, 1)
    rows.open()
    for i in range(4):
        q, k, e, r = attn_scores(q_refs, k_refs, i, scale, slope)
        v = jnp.concatenate([x[...] for x in v_refs[: 2 * i + 2]], axis=0)
        o = dot_nn((e * r).astype(half), v)
        stage[rows.slot, 0, TILE * i : TILE * (i + 1), :] = o.astype(half)
    rows.close()


def attn_bwd_kernel(scale, inv_ref, slope_ref, *refs):
    q_refs, k_refs, v_refs, g_refs = refs[:8], refs[8:16], refs[16:24], refs[24:32]
    out, stage, sems, dk_acc, dv_acc = refs[32:]
    slope = slope_ref[pl.program_id(1)]
    rows = Rows(inv_ref, stage, out, sems, 3)
    rows.open()
    for i in (3, 2, 1, 0):
        q, k, e, r = attn_scores(q_refs, k_refs, i, scale, slope)
        n = TILE * (i + 1)
        v = jnp.concatenate([x[...] for x in v_refs[: 2 * i + 2]], axis=0)
        g = jnp.concatenate([g_refs[2 * i][...], g_refs[2 * i + 1][...]], axis=0)
        p = e * r
        dp = dot_nt(g, v)
        delta = jnp.sum(p * dp, axis=1, keepdims=True)
        ds = (p * (dp - delta)).astype(half)
        pb = p.astype(half)
        dq = (dot_nn(ds, k) * scale).astype(half)
        stage[rows.slot, 0, TILE * i : TILE * (i + 1), :] = dq
        dk = dot_tn(ds, q)
        dv = dot_tn(pb, g)
        if i == 3:
            dk_acc[...] = dk
            dv_acc[...] = dv
        else:
            dk_acc[:n, :] += dk
            dv_acc[:n, :] += dv
    stage[rows.slot, 1] = (dk_acc[...] * scale).astype(half)
    stage[rows.slot, 2] = dv_acc[...].astype(half)
    rows.close()


def block_specs(offset):
    def one(j):
        return pl.BlockSpec(
            (SPAN, 128), lambda s, h, inv, slope: (inv[s * SEQ_BLOCKS + j], offset + h)
        )

    return [one(j) for j in range(SEQ_BLOCKS)]


def attn_call(kernel, kinds, joined, extra, extra_specs, scratch, inv, slopes, heads, cost, name):
    rows = joined.shape[0]
    specs = block_specs(0) + block_specs(heads) + block_specs(2 * heads) + extra_specs
    return pl.pallas_call(
        kernel,
        grid_spec=pltpu.PrefetchScalarGridSpec(
            num_scalar_prefetch=2,
            grid=(2, heads),
            in_specs=specs,
            out_specs=pl.BlockSpec(memory_space=pl.ANY),
            scratch_shapes=[
                pltpu.VMEM((2, kinds, rows // 2, 128), half),
                pltpu.SemaphoreType.DMA((2, kinds * SEQ_BLOCKS)),
            ]
            + scratch,
        ),
        out_shape=jax.ShapeDtypeStruct((rows, kinds * heads * 128), half),
        compiler_params=pltpu.CompilerParams(vmem_limit_bytes=48 * 1024 * 1024),
        cost_estimate=cost,
        name=name,
    )(inv, slopes, *([joined] * 24), *extra)


def attn_forward(joined, inv, slopes, heads, scale):
    kernel = functools.partial(attn_fwd_kernel, scale)
    cost = hint(20 * 10**9, joined.shape[0] * heads * 128 * 8)
    return attn_call(
        kernel, 1, joined, [], [], [], inv, slopes, heads, cost, "attn_forward"
    )


def attn_backward(joined, grad, inv, slopes, heads, scale):
    kernel = functools.partial(attn_bwd_kernel, scale)
    cost = hint(40 * 10**9, joined.shape[0] * heads * 128 * 14)
    sums = [pltpu.VMEM((joined.shape[0] // 2, 128), single)] * 2
    return attn_call(
        kernel,
        3,
        joined,
        [grad] * 8,
        block_specs(0),
        sums,
        inv,
        slopes,
        heads,
        cost,
        "attn_backward",
    )


HINT = 0.001


def block_of(x):
    return x if isinstance(x, tuple) else (x, x.shape[0], 0)


def hint(flops, bytes_accessed):
    return pl.CostEstimate(
        flops=int(HINT * flops), bytes_accessed=int(HINT * bytes_accessed), transcendentals=0
    )


def rows_kernel(dot, epilogue, count, extra, *refs):
    left, w_ref = refs[:count], refs[count]
    extras = refs[count + 1 : count + 1 + extra]
    outs = refs[count + 1 + extra :]
    for i in range(count):
        epilogue(i, dot(left[i][...], w_ref[...]), extras, outs)


def rows_matmul(blocks, w, transposed, extras, outs, epilogue, name, tile=512):
    blocks = [block_of(x) for x in blocks]
    extras = [block_of(x) for x in extras]
    n = w.shape[0] if transposed else w.shape[1]
    k = w.shape[1] if transposed else w.shape[0]
    t = math.gcd(n, tile)
    w_spec = (
        pl.BlockSpec((t, k), lambda i: (i, 0)) if transposed else pl.BlockSpec((k, t), lambda i: (0, i))
    )
    rows = sum(x[1] for x in blocks)
    return pl.pallas_call(
        functools.partial(
            rows_kernel, dot_nt if transposed else dot_nn, epilogue, len(blocks), len(extras)
        ),
        grid=(n // t,),
        in_specs=[pl.BlockSpec((x[1], k), lambda i, at=x[2]: (at, 0)) for x in blocks]
        + [w_spec]
        + [pl.BlockSpec((x[1], t), lambda i, at=x[2]: (at, i)) for x in extras],
        out_specs=[pl.BlockSpec((r, t), lambda i: (0, i)) for r, _ in outs],
        out_shape=[jax.ShapeDtypeStruct((r, n), d) for r, d in outs],
        compiler_params=pltpu.CompilerParams(vmem_limit_bytes=52 * 1024 * 1024),
        cost_estimate=hint(2 * rows * n * k, 2 * n * k + 4 * rows * (n + k)),
        name=name,
    )(*[x[0] for x in blocks], w, *[x[0] for x in extras])


def plain(blocks, w, transposed, dtype, name):
    def epilogue(i, x, extras, outs):
        outs[i][...] = x.astype(dtype)

    outs = [(block_of(x)[1], dtype) for x in blocks]
    return rows_matmul(blocks, w, transposed, [], outs, epilogue, name)


def joined_rows(blocks, w, bias, name):
    sizes = [block_of(x)[1] for x in blocks]

    def epilogue(i, x, extras, outs):
        at = sum(sizes[:i])
        outs[0][at : at + sizes[i], :] = (x + extras[0][...]).astype(half)

    bias = bias.reshape(1, -1)
    return rows_matmul(blocks, w, False, [bias], [(sum(sizes), half)], epilogue, name)[0]


def up_gelu(blocks, w, bias, name):
    count = len(blocks)

    def epilogue(i, x, extras, outs):
        value, slope = gelu_both(x + extras[0][...])
        outs[i][...] = value.astype(half)
        outs[count + i][...] = slope.astype(half)

    outs = [(block_of(x)[1], half) for x in blocks] * 2
    out = rows_matmul(blocks, w, False, [bias.reshape(1, -1)], outs, epilogue, name)
    return out[:count], out[count:]


def hidden_back(blocks, w, slopes, name):
    def epilogue(i, x, extras, outs):
        x = x.astype(half).astype(single) * extras[i][...].astype(single)
        outs[i][...] = x.astype(half)

    outs = [(block_of(x)[1], half) for x in blocks]
    return rows_matmul(blocks, w, True, slopes, outs, epilogue, name)


def outer_kernel(count, *refs):
    out = refs[-1]
    total = None
    for i in range(count):
        x = dot_tn(refs[i][...], refs[count + i][...])
        total = x if total is None else total + x
    out[...] = total.astype(half)


def outer(left, right, name):
    left = [block_of(x) for x in left]
    right = [block_of(x) for x in right]
    m, n = left[0][0].shape[1], right[0][0].shape[1]
    tm = math.gcd(m, 1024)
    tn = n // 2 if n % 256 == 0 and n > 1024 else n
    rows = sum(x[1] for x in left)
    return pl.pallas_call(
        functools.partial(outer_kernel, len(left)),
        grid=(m // tm, n // tn),
        in_specs=[pl.BlockSpec((x[1], tm), lambda i, j, at=x[2]: (at, i)) for x in left]
        + [pl.BlockSpec((x[1], tn), lambda i, j, at=x[2]: (at, j)) for x in right],
        out_specs=pl.BlockSpec((tm, tn), lambda i, j: (i, j)),
        out_shape=jax.ShapeDtypeStruct((m, n), half),
        compiler_params=pltpu.CompilerParams(vmem_limit_bytes=52 * 1024 * 1024),
        cost_estimate=hint(2 * rows * m * n, 2 * rows * (m + n) + 2 * m * n),
        name=name,
    )(*[x[0] for x in left], *[x[0] for x in right])


def partner(mask):
    c = lax.axis_index("ctx")
    if mask == 1:
        return c + 1 - 2 * lax.rem(c, 2)
    return lax.rem(c + 2, 4) if mask == 2 else 3 - c


def greet(masks):
    barrier = pltpu.get_barrier_semaphore()
    for mask in masks:
        pl.semaphore_signal(
            barrier,
            inc=1,
            device_id={"ctx": partner(mask)},
            device_id_type=pl.DeviceIdType.MESH,
        )
    pl.semaphore_wait(barrier, len(masks))


class Moves:
    def __init__(self, send_sem, recv_sem):
        self.send_sem, self.recv_sem, self.used = send_sem, recv_sem, 0

    def start(self, src, dst, mask):
        copy = pltpu.make_async_remote_copy(
            src_ref=src,
            dst_ref=dst,
            send_sem=self.send_sem.at[self.used],
            recv_sem=self.recv_sem.at[self.used],
            device_id={"ctx": partner(mask)},
            device_id_type=pl.DeviceIdType.MESH,
        )
        self.used += 1
        copy.start()
        return copy


def multiply(lefts, w, transposed, extras, outs, epilogue, tile=512):
    k = lefts[0].shape[1]
    n = w.shape[0] if transposed else w.shape[1]
    t = math.gcd(n, tile)
    w_spec = (
        pl.BlockSpec((t, k), lambda i: (i, 0)) if transposed else pl.BlockSpec((k, t), lambda i: (0, i))
    )
    dot = dot_nt if transposed else dot_nn

    def body(*refs):
        rows_kernel(dot, epilogue, len(lefts), len(extras), *refs)

    pltpu.emit_pipeline(
        body,
        grid=(n // t,),
        in_specs=[pl.BlockSpec((x.shape[0], k), lambda i: (0, 0)) for x in lefts]
        + [w_spec]
        + [pl.BlockSpec((x.shape[0], t), lambda i: (0, i)) for x in extras],
        out_specs=[pl.BlockSpec((x.shape[0], t), lambda i: (0, i)) for x in outs],
    )(*lefts, w, *extras, *outs)


def store(i, x, extras, outs):
    outs[i][...] = x.astype(outs[i].dtype)


def store_sum(i, x, extras, outs):
    outs[i][...] = (x + extras[i][...].astype(single)).astype(outs[i].dtype)


def store_passed(i, x, extras, outs):
    if i in (1, 2):
        x = x + extras[i - 1][...].astype(single)
    outs[i][...] = x.astype(outs[i].dtype)


def store_hidden(i, x, extras, outs):
    outs[i][...] = (x.astype(half).astype(single) * extras[i][...].astype(single)).astype(half)


def outer_on(lefts, rights, out):
    m, n = out.shape
    tm = math.gcd(m, 1024)
    tn = n // 2 if n % 256 == 0 and n > 1024 else n

    def body(*refs):
        outer_kernel(len(lefts), *refs)

    pltpu.emit_pipeline(
        body,
        grid=(m // tm, n // tn),
        in_specs=[pl.BlockSpec((x.shape[0], tm), lambda i, j: (0, i)) for x in lefts]
        + [pl.BlockSpec((x.shape[0], tn), lambda i, j: (0, j)) for x in rights],
        out_specs=[pl.BlockSpec((tm, tn), lambda i, j: (i, j))],
    )(*lefts, *rights, out)


def halves(ref):
    n = ref.shape[0] // 2
    return ref.at[pl.ds(0, n)], ref.at[pl.ds(n, n)]


def moving_call(kernel, operands, outs, moves, call, flops, name):
    anywhere = pl.BlockSpec(memory_space=pl.ANY)
    sems = pltpu.SemaphoreType.DMA((moves,))
    return pl.pallas_call(
        kernel,
        in_specs=[anywhere] * len(operands),
        out_specs=[anywhere] * len(outs),
        out_shape=[jax.ShapeDtypeStruct(shape, dtype) for shape, dtype in outs],
        scratch_shapes=[sems, sems],
        compiler_params=pltpu.CompilerParams(
            collective_id=call, has_side_effects=True, vmem_limit_bytes=52 * 1024 * 1024
        ),
        cost_estimate=hint(flops, 0),
        name=name,
    )(*operands)


def store_biased(i, x, extras, outs):
    outs[i][...] = (x + extras[0][...]).astype(half)


def qkv_kernel(*refs):
    tok, gain, shift, a1, w_qkv, bias = refs[0:2], refs[2], refs[3], refs[4:7], refs[7], refs[8]
    dz_lo, dz_hi = refs[9:11]
    joined, far, one_lo, two_hi = refs[11], refs[12:14], refs[14], refs[15]
    moves = Moves(*refs[16:18])
    n, width = tok[0].shape
    greet((1, 2))
    copies = [moves.start(dz_lo, one_lo, 1), moves.start(dz_hi, two_hi, 2)]

    def norm(x_lo, x_hi, g, s, o_lo, o_hi):
        for x, o in ((x_lo, o_lo), (x_hi, o_hi)):
            normed, _ = norm_parts(x[...].astype(single))
            o[...] = (normed * g[...] + s[...]).astype(half)

    t = math.gcd(n, 64)
    block = pl.BlockSpec((t, width), lambda i: (i, 0))
    row = pl.BlockSpec((1, width), lambda i: (0, 0))
    pltpu.emit_pipeline(
        norm, grid=(n // t,), in_specs=[block, block, row, row], out_specs=[block, block]
    )(*tok, gain, shift, *far)
    lefts, outs, at = [*a1, *far], [], 0
    for x in lefts:
        outs.append(joined.at[pl.ds(at, x.shape[0])])
        at += x.shape[0]
    multiply(lefts, w_qkv, False, [bias], outs, store_biased)
    for copy in copies:
        copy.wait()


def qkv_forward(tok, gain, shift, a1, w_qkv, bias, dz_lo, dz_hi):
    n, width = tok[0].shape
    k = w_qkv.shape[1]
    outs = [((8 * n, k), half)] + [((n, width), half)] * 4
    out = moving_call(
        qkv_kernel,
        [*tok, gain.reshape(1, -1), shift.reshape(1, -1), *a1, w_qkv, bias.reshape(1, -1), dz_lo, dz_hi],
        outs,
        2,
        7,
        16 * n * width * k,
        "qkv",
    )
    return out[0], out[1:3], out[3:5]


def feed_pass(dz, slope, w_down, w_up, du, total):
    n, width = dz[0].shape
    wide = w_down.shape[0]
    t = math.gcd(wide, 512)
    total[...] = jnp.zeros_like(total)

    def body(dz_lo, dz_hi, down, up, slope_lo, slope_hi, du_lo, du_hi):
        for i, x, s, d in ((0, dz_lo, slope_lo, du_lo), (1, dz_hi, slope_hi, du_hi)):
            grad = dot_nt(x[...], down[...]).astype(half).astype(single)
            grad = (grad * s[...].astype(single)).astype(half)
            d[...] = grad
            total[i * n : (i + 1) * n, :] += dot_nt(grad, up[...])

    pltpu.emit_pipeline(
        body,
        grid=(wide // t,),
        in_specs=[pl.BlockSpec((n, width), lambda i: (0, 0))] * 2
        + [pl.BlockSpec((t, width), lambda i: (i, 0)), pl.BlockSpec((width, t), lambda i: (0, i))]
        + [pl.BlockSpec((n, t), lambda i: (0, i))] * 2,
        out_specs=[pl.BlockSpec((n, t), lambda i: (0, i))] * 2,
    )(*dz, w_down, w_up, *slope, *du)


def feed_back_kernel(*refs):
    dz, slope, (w_down, w_up) = refs[0:8], refs[8:13], refs[13:15]
    a2, gb_far = refs[15:20], refs[20:22]
    du, own, land1, land2, up_grad, mix_x, mix_y = refs[22:27], *refs[27:33]
    total, far, near, rest, from_x, from_y, mixed = refs[33:40]
    moves = Moves(*refs[40:42])
    local = refs[42]
    n = from_x.shape[0]
    lo, hi = pl.ds(0, n), pl.ds(n, n)
    (s1_lo, s1_hi), (s2_lo, s2_hi) = halves(slope[1]), halves(slope[2])
    (d1_lo, d1_hi), (d2_lo, d2_hi) = halves(du[1]), halves(du[2])
    (land1_lo, land1_hi), (land2_lo, land2_hi) = halves(land1), halves(land2)
    greet((1, 2))
    wide, width = w_down.shape
    t = math.gcd(width, 512)

    def mix(x_lo, x_hi, w):
        at = pl.ds(pl.multiple_of(pl.program_id(0) * t, t), t)
        mixed[0:n, at] = dot_nn(x_lo[...], w[...]).astype(half)
        mixed[n : 2 * n, at] = dot_nn(x_hi[...], w[...]).astype(half)

    pltpu.emit_pipeline(
        mix,
        grid=(width // t,),
        in_specs=[pl.BlockSpec((n, wide), lambda i: (0, 0))] * 2
        + [pl.BlockSpec((wide, t), lambda i: (0, i))],
    )(*gb_far, w_down)
    second = [moves.start(mixed.at[lo], mix_x, 1), moves.start(mixed.at[hi], mix_y, 2)]
    feed_pass(dz[6:8], slope[3:5], w_down, w_up, du[3:5], total)
    far[...] = total[...].astype(half)
    first = [moves.start(far.at[lo], from_x, 1), moves.start(far.at[hi], from_y, 2)]
    feed_pass([dz[2], dz[5]], [s1_lo, s2_hi], w_down, w_up, [d1_lo, d2_hi], total)
    near[...] = total[...].astype(half)
    second += [moves.start(near.at[lo], land1_lo, 1), moves.start(near.at[hi], land2_hi, 2)]
    feed_pass([dz[3], dz[4]], [s1_hi, s2_lo], w_down, w_up, [d1_hi, d2_lo], total)
    for copy in first:
        copy.wait()
    rest[lo] = (total[lo] + from_y[...].astype(single)).astype(half)
    rest[hi] = (total[hi] + from_x[...].astype(single)).astype(half)
    second += [moves.start(rest.at[lo], land1_hi, 1), moves.start(rest.at[hi], land2_lo, 2)]
    feed_pass(dz[0:2], halves(slope[0]), w_down, w_up, halves(du[0]), total)
    store_own = pltpu.make_async_copy(total, own, local)
    store_own.start()
    outer_on(a2, du, up_grad)
    store_own.wait()
    for copy in second:
        copy.wait()


def feed_back(dz, slope, w_down, w_up, a2, gb_far):
    n, width = dz[0].shape
    rows, wide = 2 * n, w_down.shape[0]
    anywhere = pl.BlockSpec(memory_space=pl.ANY)
    outs = [((r, wide), half) for r in (rows, rows, rows, n, n)]
    outs += [((rows, width), single)] + [((rows, width), half)] * 2
    outs += [((width, wide), half)] + [((n, width), half)] * 2
    sems = pltpu.SemaphoreType.DMA((8,))
    out = pl.pallas_call(
        feed_back_kernel,
        in_specs=[anywhere] * 22,
        out_specs=[anywhere] * len(outs),
        out_shape=[jax.ShapeDtypeStruct(shape, dtype) for shape, dtype in outs],
        scratch_shapes=[pltpu.VMEM((rows, width), single)]
        + [pltpu.VMEM((rows, width), half)] * 3
        + [pltpu.VMEM((n, width), half)] * 2
        + [pltpu.VMEM((rows, width), half)]
        + [sems, sems, pltpu.SemaphoreType.DMA],
        compiler_params=pltpu.CompilerParams(
            collective_id=3, has_side_effects=True, vmem_limit_bytes=56 * 1024 * 1024
        ),
        cost_estimate=hint(26 * rows * width * wide, 0),
        name="feed_back",
    )(*dz, *slope, w_down, w_up, *a2, *gb_far)
    return out[0:5], out[5:8], out[8], out[9:11]


def heads_back_kernel(part, *refs):
    own, land1, land2, cot, y1, gain, w_out = refs[0:7]
    ob, gb1, gb2, w_down, mix_x, mix_y, down = refs[7:14]
    dy1, dz1, sums, got, out_grad = refs[14:19]
    mix, down1, down2 = refs[19:23], refs[23], refs[24]
    dz, w, stage = refs[25:28]
    moves = Moves(*refs[28:30])
    local = refs[30]
    rows, width = own.shape
    greet((1, 2, 3))
    load = pltpu.make_async_copy(w_out, w, local.at[0])
    load.start()
    copies = [moves.start(down, down1, 1), moves.start(down, down2, 2)]
    t = math.gcd(rows, 64)

    def norm(own, one, two, cot, y1, gain, dy1, dz1, sums):
        step = pl.program_id(0)
        grad = own[...] + one[...].astype(single) + two[...].astype(single)
        normed, inv = norm_parts(y1[...])
        dy = cot[...] + norm_back(normed, inv, gain[...], grad)
        low = dy.astype(half)
        dy1[...] = dy
        dz1[...] = low
        dz[pl.ds(pl.multiple_of(step * t, t), t), :] = low

        @pl.when(step == 0)
        def _():
            sums[...] = jnp.zeros_like(sums)

        sums[0:1] += jnp.sum(grad * normed, axis=0, keepdims=True)
        sums[1:2] += jnp.sum(grad, axis=0, keepdims=True)
        sums[2:3] += jnp.sum(low.astype(single), axis=0, keepdims=True)

    block = pl.BlockSpec((t, width), lambda i: (i, 0))
    pltpu.emit_pipeline(
        norm,
        grid=(rows // t,),
        in_specs=[block] * 5 + [pl.BlockSpec((1, width), lambda i: (0, 0))],
        out_specs=[block] * 2 + [pl.BlockSpec((8, width), lambda i: (0, 0))],
    )(own, land1, land2, cot, y1, gain, dy1, dz1, sums)
    load.wait()
    for mask in (3, 1, 2, 0):
        of = partner(mask) if mask else lax.axis_index("ctx")
        heads = w[pl.ds(pl.multiple_of(of * part, part), part), :]
        stage[mask] = dot_nt(dz[...], heads).astype(half)
        at = got.at[pl.ds(mask * rows, rows)]
        if mask:
            copies.append(moves.start(stage.at[mask], at, mask))
        else:
            keep = pltpu.make_async_copy(stage.at[0], at, local.at[1])
            keep.start()
    outer_on([ob], [dz1], out_grad)
    multiply(
        [*halves(gb1), *halves(gb2)],
        w_down,
        False,
        [mix_y, mix_x],
        mix,
        store_passed,
    )
    keep.wait()
    for copy in copies:
        copy.wait()


def heads_back(terms, cot, y1, gain, w_out, ob, gb1, gb2, w_down, mix_first, down):
    rows, width = cot.shape
    part = width // 4
    anywhere = pl.BlockSpec(memory_space=pl.ANY)
    sems = pltpu.SemaphoreType.DMA((5,))
    outs = [((rows, width), single), ((rows, width), half), ((8, width), single)]
    outs += [((4 * rows, part), half), ((width, width), half)]
    outs += [((rows // 2, width), half)] * 4 + [(down.shape, half)] * 2
    out = pl.pallas_call(
        functools.partial(heads_back_kernel, part),
        in_specs=[anywhere] * 14,
        out_specs=[anywhere] * len(outs),
        out_shape=[jax.ShapeDtypeStruct(shape, dtype) for shape, dtype in outs],
        scratch_shapes=[
            pltpu.VMEM((rows, width), half),
            pltpu.VMEM((width, width), half),
            pltpu.VMEM((4, rows, part), half),
            sems,
            sems,
            pltpu.SemaphoreType.DMA((2,)),
        ],
        compiler_params=pltpu.CompilerParams(
            collective_id=4, has_side_effects=True, vmem_limit_bytes=56 * 1024 * 1024
        ),
        cost_estimate=hint(10 * rows * width * width, 0),
        name="heads_back",
    )(*terms, cot, y1, gain.reshape(1, -1), w_out, ob, gb1, gb2, w_down, *mix_first, down)
    return out[0], out[2], out[3], out[4], out[5:9], out[9:11]


def qkv_back_kernel(*refs):
    dqkv, w_qkv = refs[0:2]
    a1, gb_own, w_down, one_hi, two_hi = refs[2:7], *refs[7:11]
    own, p3, p1, p2, from_x, from_y, land1, land2, qkv_grad, mix_own = refs[11:21]
    x_hi, y_hi = refs[21:23]
    moves = Moves(*refs[23:25])
    rows = own.shape[0]
    n = rows // 2

    def block(k):
        return dqkv.at[pl.ds(k * n, n)]

    greet((1, 2))
    output = [moves.start(one_hi, x_hi, 1), moves.start(two_hi, y_hi, 2)]
    (p3_lo, p3_hi), (p1_lo, p1_hi), (p2_lo, p2_hi) = halves(p3), halves(p1), halves(p2)
    (land1_lo, land1_hi), (land2_lo, land2_hi) = halves(land1), halves(land2)
    multiply([block(6), block(7)], w_qkv, True, [], [p3_lo, p3_hi], store)
    first = [moves.start(p3_lo, from_x, 1), moves.start(p3_hi, from_y, 2)]
    multiply([block(2), block(5)], w_qkv, True, [], [p1_lo, p2_hi], store)
    second = [moves.start(p1_lo, land1_lo, 1), moves.start(p2_hi, land2_hi, 2)]
    multiply([dqkv.at[pl.ds(0, rows)]], w_qkv, True, [], [own], store)
    multiply([gb_own], w_down, False, [], [mix_own], store)
    for copy in first:
        copy.wait()
    multiply([block(3), block(4)], w_qkv, True, [from_y, from_x], [p1_hi, p2_lo], store_sum)
    second += [moves.start(p1_hi, land1_hi, 1), moves.start(p2_lo, land2_lo, 2)]
    rights, at = [], 0
    for x in a1:
        rights.append(dqkv.at[pl.ds(at, x.shape[0])])
        at += x.shape[0]
    outer_on(a1, rights, qkv_grad)
    for copy in output + second:
        copy.wait()


def qkv_back(dqkv, w_qkv, a1, gb_own, w_down, one_hi, two_hi):
    rows, width = a1[0].shape
    wide = gb_own.shape[1]
    n = rows // 2
    outs = [((rows, width), single)] + [((rows, width), half)] * 3
    outs += [((n, width), half)] * 2 + [((rows, width), half)] * 2
    outs += [((width, dqkv.shape[1]), half), ((rows, width), single)] + [((n, width), half)] * 2
    out = moving_call(
        qkv_back_kernel,
        [dqkv, w_qkv, *a1, gb_own, w_down, one_hi, two_hi],
        outs,
        8,
        5,
        16 * rows * width * dqkv.shape[1] + 2 * rows * width * wide,
        "qkv_back",
    )
    return out[0], out[6:8], out[8], out[9], out[10:12]


def lay_out_kernel(axis, layout, c_ref, *refs):
    out = refs[-1]
    for (j, row), ref in zip(layout, refs):
        x = ref[...].astype(single)
        r, w = x.shape
        if axis == 0:
            n = sum(ref.shape[0] for (k, _), ref in zip(layout, refs) if k == j)
            out[pl.ds(pl.multiple_of((c_ref[0] ^ j) * n + row, r), r), :] = x
        else:
            out[row : row + r, pl.ds(pl.multiple_of((c_ref[0] ^ j) * w, w), w)] = x


def lay_out(axis, pieces, c, groups):
    count = len(pieces)
    r = sum(x.shape[0] for x in pieces[0])
    n = pieces[0][0].shape[1]
    w = n // groups
    if w % 128:
        whole = xor_order([jnp.concatenate(p, axis=0).astype(single) for p in pieces], c)
        whole = jnp.stack([p.reshape(r, groups, w) for p in whole], axis=2)
        return whole.reshape(r, count * n)
    layout, blocks = [], []
    for j, p in enumerate(pieces):
        row = 0
        for x in p:
            layout.append((j, row))
            blocks.append(x)
            row += x.shape[0]
    out = (count * r, w) if axis == 0 else (r, count * w)
    return pl.pallas_call(
        functools.partial(lay_out_kernel, axis, layout),
        grid_spec=pltpu.PrefetchScalarGridSpec(
            num_scalar_prefetch=1,
            grid=(groups,),
            in_specs=[pl.BlockSpec((x.shape[0], w), lambda k, c: (0, k)) for x in blocks],
            out_specs=pl.BlockSpec(out, lambda k, c: (0, k)),
        ),
        out_shape=jax.ShapeDtypeStruct((out[0], out[1] * groups), single),
        compiler_params=pltpu.CompilerParams(vmem_limit_bytes=48 * 1024 * 1024),
        cost_estimate=hint(0, 6 * r * n * count),
        name="lay_out",
    )(c.reshape(1), *blocks)


def gather_small_kernel(nf, x_ref, o_ref, send_sem, recv_sem):
    f = lax.axis_index("fsdp")
    barrier = pltpu.get_barrier_semaphore()
    for d in range(1, nf):
        pl.semaphore_signal(
            barrier,
            inc=1,
            device_id={"fsdp": lax.rem(f + d, nf)},
            device_id_type=pl.DeviceIdType.MESH,
        )
    pl.semaphore_wait(barrier, nf - 1)
    copies = []
    for d in range(1, nf):
        copies.append(
            pltpu.make_async_remote_copy(
                src_ref=x_ref,
                dst_ref=o_ref.at[f],
                send_sem=send_sem.at[d],
                recv_sem=recv_sem.at[d],
                device_id={"fsdp": lax.rem(f + d, nf)},
                device_id_type=pl.DeviceIdType.MESH,
            )
        )
        copies[-1].start()
    o_ref[f] = x_ref[...]
    for copy in copies:
        copy.wait()


def gather_small(x, nf):
    return pl.pallas_call(
        functools.partial(gather_small_kernel, nf),
        out_shape=jax.ShapeDtypeStruct((nf,) + x.shape, single),
        in_specs=[pl.BlockSpec(memory_space=pltpu.VMEM)],
        out_specs=pl.BlockSpec(memory_space=pltpu.VMEM),
        scratch_shapes=[pltpu.SemaphoreType.DMA((nf,)), pltpu.SemaphoreType.DMA((nf,))],
        compiler_params=pltpu.CompilerParams(collective_id=1, has_side_effects=True),
        name="gather_small",
    )(x)


def reduce_small_kernel(nf, nc, x_ref, o_ref, land, stage, send_sem, recv_sem):
    f = lax.axis_index("fsdp")
    c = lax.axis_index("ctx")
    barrier = pltpu.get_barrier_semaphore()
    for d in range(1, nf):
        pl.semaphore_signal(
            barrier,
            inc=1,
            device_id={"fsdp": lax.rem(f + d, nf)},
            device_id_type=pl.DeviceIdType.MESH,
        )
    for d in range(1, nc):
        pl.semaphore_signal(
            barrier,
            inc=1,
            device_id={"ctx": lax.rem(c + d, nc)},
            device_id_type=pl.DeviceIdType.MESH,
        )
    pl.semaphore_wait(barrier, nf + nc - 2)
    copies = []
    for d in range(1, nf):
        to = lax.rem(f + d, nf)
        copies.append(
            pltpu.make_async_remote_copy(
                src_ref=x_ref.at[to],
                dst_ref=land.at[d],
                send_sem=send_sem.at[d],
                recv_sem=recv_sem.at[d],
                device_id={"fsdp": to},
                device_id_type=pl.DeviceIdType.MESH,
            )
        )
        copies[-1].start()
    total = x_ref[f]
    for d in range(1, nf):
        copies[d - 1].wait()
        total = total + land[d]
    stage[0] = total
    copies = []
    for d in range(1, nc):
        copies.append(
            pltpu.make_async_remote_copy(
                src_ref=stage.at[0],
                dst_ref=stage.at[d],
                send_sem=send_sem.at[nf + d],
                recv_sem=recv_sem.at[nf + d],
                device_id={"ctx": lax.rem(c + d, nc)},
                device_id_type=pl.DeviceIdType.MESH,
            )
        )
        copies[-1].start()
    for d in range(1, nc):
        copies[d - 1].wait()
        total = total + stage[d]
    o_ref[...] = total


def reduce_small(x, nf, nc, call):
    block = x.shape[1:]
    sems = pltpu.SemaphoreType.DMA((nf + nc,))
    return pl.pallas_call(
        functools.partial(reduce_small_kernel, nf, nc),
        out_shape=jax.ShapeDtypeStruct(block, single),
        in_specs=[pl.BlockSpec(memory_space=pltpu.VMEM)],
        out_specs=pl.BlockSpec(memory_space=pltpu.VMEM),
        scratch_shapes=[
            pltpu.VMEM((nf,) + block, single),
            pltpu.VMEM((nc,) + block, single),
            sems,
            sems,
        ],
        compiler_params=pltpu.CompilerParams(collective_id=call, has_side_effects=True),
        name="reduce_small",
    )(x)


def per_device(
    tokens,
    cotangent,
    lengths,
    span_place,
    ln1_gain,
    ln1_shift,
    qkv_weight,
    q_bias,
    v_bias,
    out_weight,
    out_bias,
    ln2_gain,
    ln2_shift,
    up_weight,
    up_bias,
    down_weight,
    down_bias,
):
    rows, width = tokens.shape
    CTX = lax.axis_size("ctx")
    c = lax.axis_index("ctx")
    f = lax.axis_index("fsdp")
    nf = lax.axis_size("fsdp")
    wide = up_weight.shape[1]
    part = width // CTX
    heads = HEADS // CTX
    scale = 1.0 / math.sqrt(width // HEADS)
    shard = width // nf
    fpart = wide // nf // CTX
    wpart = wide // CTX

    def columns(x, width_each, stride, count):
        return jnp.concatenate(
            [
                lax.dynamic_slice_in_dim(x, k * stride + c * width_each, width_each, axis=1)
                for k in range(count)
            ],
            axis=1,
        )

    def after(x, *others):
        return lax.optimization_barrier((x, others))[0]

    def pick(x, axis):
        return lax.dynamic_index_in_dim(x, c, axis, keepdims=False)

    def gather_f(x):
        return lax.all_gather(x, "fsdp", axis=0, tiled=True)

    qkv_own = columns(qkv_weight, part, width, 3)
    up_own = columns(up_weight, fpart, wide // nf, nf)
    down_own = lax.dynamic_slice_in_dim(down_weight, c * fpart, fpart, axis=0)
    w_qkv = gather_f(qkv_own.astype(half))
    up_own, down_own = up_own.astype(half), down_own.astype(half)
    small = jnp.concatenate(
        [ln1_gain, ln1_shift, q_bias, v_bias, out_bias, ln2_gain, ln2_shift, down_bias, up_bias]
    )
    small_len = small.shape[0]
    small = jnp.pad(small, (0, -small_len % 1024)).reshape(-1, 128)
    small_all = gather_small(small, nf).reshape(nf, -1)[:, :small_len]
    small_all = small_all.astype(half).astype(single)

    def vector(k):
        return small_all[:, k * shard : (k + 1) * shard].reshape(width)

    gain1, shift1, bias_q, bias_v, bias_o, gain2, shift2, bias_d = [vector(k) for k in range(8)]
    bias_u = pick(small_all[:, 8 * shard :].reshape(nf, CTX, fpart), 1).reshape(wpart)
    bias_qkv = jnp.concatenate(
        [pick(bias_q.reshape(CTX, part), 0), jnp.zeros((part,), single), pick(bias_v.reshape(CTX, part), 0)]
    )
    w_out = gather_f(out_weight.astype(half))

    per = rows // SPAN
    table = jnp.arange(CTX * per, dtype=jnp.int32)
    source = ((table // per) ^ c) * per + table % per
    place = jnp.sum(jnp.where(source[:, None] == table[None, :], span_place[0][None, :], 0), axis=1)
    inv = jnp.sum(jnp.where(place[None, :] == table[:, None], table[None, :], 0), axis=1)
    slopes = 2.0 ** (-8.0 * ((c * heads + jnp.arange(heads)).astype(single) + 1.0) / HEADS)

    def flat(pieces):
        return [x for p in pieces for x in p]

    def scatter_f(x):
        return lax.psum_scatter(x, "fsdp", scatter_dimension=0, tiled=True)

    far = CTX - 1
    mid = list(range(1, far))

    def first_norm(x):
        normed, _ = norm_parts(x.astype(single))
        return (normed * gain1 + shift1).astype(half)

    n = rows // 2
    dz2_lo, dz2_hi = cotangent[:n].astype(half), cotangent[n:].astype(half)
    early = (small_all, place, inv, slopes, up_own, down_own, dz2_lo, dz2_hi)
    early, tok_near = after((early, gather_first(tokens)))
    small_all, place, inv, slopes, up_own, down_own, dz2_lo, dz2_hi = early
    tok = gather_second(tokens, tok_near)
    near = [[first_norm(x) for x in p] for p in tok[:far]]
    tok = after(tok, near)
    if CTX != 4:
        dz2_own = jnp.concatenate([dz2_lo, dz2_hi], axis=0)
        dz2_rest = gather_first(dz2_own)
    w_up = gather_f(after(up_own, tok))
    a1 = flat(near)
    if CTX == 4:
        joined, a1_far, dz2_first = qkv_forward(
            tok[far], gain1, shift1, a1, w_qkv, bias_qkv, dz2_lo, dz2_hi
        )
        a1 = a1 + list(a1_far)
        dz2_rest = after((dz2_hi, dz2_lo), joined)
        dz2_rest = [swap(dz2_rest[0], 1), swap(dz2_rest[1], 2)]
    else:
        a1 = a1 + [first_norm(x) for x in tok[far]]
        joined = joined_rows(a1, w_qkv, bias_qkv, "qkv")
    w_down = gather_f(after(down_own, joined))
    attended = attn_forward(joined, inv, slopes, heads, scale)
    mine = [attended[j * rows : (j + 1) * rows] for j in range(CTX)]
    mine = after(mine, dz2_rest)
    mine = [mine[0]] + [swap(mine[j], j) for j in range(1, CTX)]
    ob = jnp.concatenate(xor_order(mine, c), axis=1)
    y1 = tokens.astype(single) + dot_nn(ob, w_out) + bias_o

    normed2, inv2 = norm_parts(y1)
    a2_own = (normed2 * gain2 + shift2).astype(half)
    gb, slope = [None] * CTX, [None] * CTX
    gb[0], slope[0] = up_gelu([a2_own], w_up, bias_u, "up_gelu_0")
    last = gb[0]
    a2_near = gather_first(a2_own)
    a2 = gather_second(a2_own, a2_near)
    if CTX == 4:
        one_lo, two_hi = after(dz2_first, a2_near)
        one_hi, two_lo = dz2_rest
        dz2 = [[dz2_lo, dz2_hi], [one_lo, one_hi], [two_lo, two_hi], [swap(one_lo, 2), swap(two_hi, 1)]]
    else:
        dz2 = [[dz2_own]] + [[x] for x in dz2_rest]
    for j in range(1, CTX):
        gb[j], slope[j] = up_gelu(after(a2[j], last), w_up, bias_u, f"up_gelu_{j}")
        last = gb[j]
    gb_blocks = flat(gb)
    if CTX == 4:
        gb_blocks = [(g[0], n, i) for g in gb[:far] for i in (0, 1)] + list(gb[far])
    down_grad = outer(gb_blocks, flat(dz2), "down_grad")
    down_part = scatter_f(down_grad)
    w_down = after(w_down, down_grad)

    du, dh2, mix = [None] * CTX, [None] * CTX, [None] * CTX
    if CTX == 4:
        du, dh2, up_grad, mix_first = feed_back(
            flat(dz2), flat(slope), w_down, w_up, flat(a2), gb[far]
        )
        du = [du]
    else:
        for j in range(CTX):
            du[j] = hidden_back(dz2[j], w_down, slope[j], f"du_{j}")
            dh2[j] = plain(du[j], w_up, True, half if j else single, f"dh2_{j}")[0]
        arrived = scatter_send(dh2[1:])
        dh2 = dh2[0]
        up_grad = outer(flat(a2), flat(du), "up_grad")
        mix[far] = plain(gb[far], w_down, False, half, "mix_far")[0]
        dh2 = total_of(dh2, arrived)
    up_part = scatter_f(up_grad)
    if CTX == 4:
        dy1, sums2, dattn, out_grad, mix, down_near = heads_back(
            dh2, cotangent, y1, gain2, w_out, ob, gb[1][0], gb[2][0], w_down, mix_first, down_part
        )
        one_lo, one_hi, two_lo, two_hi = mix
        gain2_grad, shift2_grad, out_bias_grad = sums2[0], sums2[1], sums2[2]
    else:
        gain2_grad = jnp.sum(dh2 * normed2, axis=0)
        shift2_grad = jnp.sum(dh2, axis=0)
        dy1 = cotangent + norm_back(normed2, inv2, gain2, dh2)
        dz1 = dy1.astype(half)
        dattn = dot_nt(dz1, w_out).astype(half)
        out_bias_grad = jnp.sum(dz1.astype(single), axis=0)
        dattn = xor_order([dattn[:, s * part : (s + 1) * part] for s in range(CTX)], c)
        dattn = [dattn[0]] + [swap(dattn[j], j) for j in range(1, CTX)]
        dattn = jnp.concatenate(dattn, axis=0)
        out_grad = outer([ob], [dz1], "out_grad")
        for j in mid:
            mix[j] = plain(gb[j], w_down, False, half, f"mix_{j}")[0]
        down_near = gather_first(down_part)
    out_part = scatter_f(out_grad)
    dqkv = attn_backward(joined, dattn, inv, slopes, heads, scale)
    if CTX == 4:
        lows = [swap(one_lo, 1), swap(two_lo, 2)]
        dqkv = after(dqkv, lows, up_part)
        dh1, arrived, qkv_grad, mix_own, highs = qkv_back(
            dqkv, w_qkv, a1, gb[0][0], w_down, one_hi, two_hi
        )
    else:
        dh1 = [
            plain([(dqkv, rows, j)], w_qkv, True, half if j else single, f"dh1_{j}")[0]
            for j in range(CTX)
        ]
        arrived = scatter_send(dh1[1:])
        dh1 = dh1[0]
        qkv_grad = outer(a1, [(dqkv, rows, j) for j in range(CTX)], "qkv_grad")
        mix_own = plain(gb[0], w_down, False, single, "mix_0")[0]
    qkv_part = scatter_f(qkv_grad)
    up_own = after(up_part, arrived)
    up_near = gather_first(up_own)
    out_first = []
    if CTX == 4:
        k = out_part.shape[0] // 2
        out_lo, out_hi = after(out_part, arrived)[:k], after(out_part, arrived)[k:]
        out_first = [swap(out_lo, 1), swap(out_hi, 2)]
    waiting = (dh1, dqkv, mix_own, flat(du), flat(dz2[:1]))
    dh1, dqkv, mix_own, du, dz2_own = after(waiting, up_near, out_first)
    up_bias_grad = sum(jnp.sum(x.astype(single), axis=0) for x in du)
    down_bias_grad = sum(jnp.sum(x.astype(single), axis=0) for x in dz2_own)
    dh1 = total_of(dh1, arrived)
    down_near, up_near, out_first = after((down_near, up_near, out_first))
    down_out = gather_second(down_part, down_near)
    up_out = gather_second(up_own, up_near)
    out_second = []
    if CTX == 4:
        out_lo = (out_lo.astype(single) + out_first[0].astype(single)).astype(half)
        out_hi = (out_hi.astype(single) + out_first[1].astype(single)).astype(half)
        out_second = [(out_lo, swap(out_lo, 2)), (out_hi, swap(out_hi, 1))]
        mixed = y1 + bias_d + mix_own
        mixed = jnp.concatenate([total_of(mixed[:n], lows), total_of(mixed[n:], highs)])
    else:
        mixed = total_of(y1 + bias_d + mix_own, scatter_send(mix[1:]))
    sums = jnp.sum(dqkv.astype(single), axis=0)
    normed1_own, inv1_own = norm_parts(tokens.astype(single))
    gain1_grad = jnp.sum(dh1 * normed1_own, axis=0)
    shift1_grad = jnp.sum(dh1, axis=0)
    dy1 = after(dy1, up_out, down_out, out_second)
    input_grad = dy1 + norm_back(normed1_own, inv1_own, gain1, dh1)

    if CTX == 4:
        out_out = [x.astype(single) + y.astype(single) for x, y in out_second]
        out_out = jnp.concatenate(out_out, axis=0)
    else:
        bit = 1
        while bit < CTX:
            out_out = out_part.astype(single) + swap(out_part, bit).astype(single)
            out_part = out_out.astype(half)
            bit *= 2

    def spread(x, inner):
        x = x.reshape(-1, 1, inner)
        mask = (jnp.arange(CTX) == c)[None, :, None]
        return jnp.where(mask, x, 0.0).reshape(-1)

    def reduced(items, call):
        sizes = [x.shape[0] // nf for x in items]
        x = jnp.concatenate([x.reshape(nf, -1) for x in items], axis=1)
        x = jnp.pad(x, ((0, 0), (0, -x.shape[1] % 1024))).reshape(nf, -1, 128)
        x = reduce_small(x, nf, CTX, call).reshape(-1)
        out, at = [], 0
        for n in sizes:
            out.append(x[at : at + n])
            at += n
        return out

    sums_in = [out_bias_grad, gain2_grad, shift2_grad, down_bias_grad, spread(up_bias_grad, fpart)]
    sums_in += [gain1_grad, shift1_grad, spread(sums[:part], part), spread(sums[2 * part :], part)]
    qkv_near = gather_first(qkv_part)
    sums_in[5] = after(sums_in[5], qkv_near)
    sums_out = reduced(sums_in, 2)
    qkv_out = lay_out(1, gather_second(qkv_part, qkv_near), c, 3)
    down_out = lay_out(0, after(down_out, qkv_part), c, width // min(width, 512))
    up_out = lay_out(1, after(up_out, qkv_part), c, nf)
    out_bias_out, gain2_out, shift2_out, down_bias_out, up_bias_out = sums_out[:5]
    gain1_out, shift1_out, q_bias_out, v_bias_out = sums_out[5:]
    return (
        mixed,
        input_grad,
        gain1_out,
        shift1_out,
        qkv_out,
        q_bias_out,
        v_bias_out,
        out_out,
        out_bias_out,
        gain2_out,
        shift2_out,
        up_out,
        up_bias_out,
        down_out,
        down_bias_out,
    )


def solution(mesh):
    rows, flat = P(("ctx", "fsdp"), None), P("fsdp")
    mat = P("fsdp", None)
    in_specs = (
        rows,
        rows,
        mat,
        mat,
        flat,
        flat,
        mat,
        flat,
        flat,
        mat,
        flat,
        flat,
        flat,
        mat,
        flat,
        mat,
        flat,
    )
    out_specs = (
        rows,
        rows,
        flat,
        flat,
        mat,
        flat,
        flat,
        mat,
        flat,
        flat,
        flat,
        mat,
        flat,
        mat,
        flat,
    )
    return jax.shard_map(
        per_device, mesh=mesh, in_specs=in_specs, out_specs=out_specs, check_vma=False
    )
```

```python
import functools
import math

import jax
import jax.numpy as jnp
from jax import lax
from jax.experimental import pallas as pl
from jax.experimental.pallas import tpu as pltpu
from jax.sharding import PartitionSpec as P

HEADS = 16
SPAN = 128
SEQ_BLOCKS = 8

norm_eps = 1e-05
gelu_coef = 0.7978845608028654
LOG2E = 1.4426950408889634

half = jnp.bfloat16
single = jnp.float32


def dot_nn(a, b):
    return lax.dot_general(a, b, (((1,), (0,)), ((), ())), preferred_element_type=single)


def dot_nt(a, b):
    return lax.dot_general(a, b, (((1,), (1,)), ((), ())), preferred_element_type=single)


def dot_tn(a, b):
    return lax.dot_general(a, b, (((0,), (0,)), ((), ())), preferred_element_type=single)


def norm_parts(values):
    center = values - jnp.mean(values, axis=-1, keepdims=True)
    spread = jnp.mean(center * center, axis=-1, keepdims=True)
    inv = lax.rsqrt(spread + norm_eps)
    return center * inv, inv


def norm_back(normed, inv, gain, grad):
    dn = grad * gain
    return inv * (
        dn
        - jnp.mean(dn, axis=-1, keepdims=True)
        - normed * jnp.mean(dn * normed, axis=-1, keepdims=True)
    )


def gelu_both(v):
    t = jnp.tanh(gelu_coef * (v + 0.044715 * v * v * v))
    value = 0.5 * v * (1.0 + t)
    slope = 0.5 * (1.0 + t) + 0.5 * v * (1.0 - t * t) * gelu_coef * (1.0 + 3 * 0.044715 * v * v)
    return value, slope


def swap(x, mask):
    n = lax.axis_size("ctx")
    return lax.ppermute(x, "ctx", [(i, i ^ mask) for i in range(n)])


def gather_first(x):
    count = lax.axis_size("ctx")
    return [swap(x, j) for j in range(1, 3 if count == 4 else count)]


def gather_second(x, arrived):
    if lax.axis_size("ctx") != 4:
        return [[x]] + [[p] for p in arrived]
    one, two = arrived
    n = x.shape[0] // 2
    return [[x], [one], [two], [swap(one[:n], 2), swap(two[n:], 1)]]


def gather_ctx(x):
    return gather_second(x, gather_first(x))


def scatter_first(far):
    if lax.axis_size("ctx") != 4:
        return None
    return swap(far[0], 1), swap(far[1], 2)


def scatter_second(pieces, first):
    if first is None:
        return pieces[1:]
    p1, p2 = pieces[1], pieces[2]
    n = p1.shape[0] // 2
    from_x, from_y = first
    p1 = jnp.concatenate(
        [p1[:n], (p1[n:].astype(single) + from_y.astype(single)).astype(half)], axis=0
    )
    p2 = jnp.concatenate(
        [(p2[:n].astype(single) + from_x.astype(single)).astype(half), p2[n:]], axis=0
    )
    return [p1, p2]


def scatter_send(sent):
    return [swap(x, j + 1) for j, x in enumerate(sent)]


def total_of(own, arrived):
    for x in arrived:
        own = own + x.astype(single)
    return own


def xor_order(items, c):
    bit = 1
    while bit < len(items):
        on = (c & bit) == bit
        items = [jnp.where(on, items[i ^ bit], items[i]) for i in range(len(items))]
        bit *= 2
    return items


TILE = 256


def attn_scores(q_refs, k_refs, i, scale, slope):
    q = jnp.concatenate([q_refs[2 * i][...], q_refs[2 * i + 1][...]], axis=0)
    k = jnp.concatenate([r[...] for r in k_refs[: 2 * i + 2]], axis=0)
    n = TILE * (i + 1)
    col = lax.broadcasted_iota(jnp.int32, (1, n), 1) - (n - 1)
    s = dot_nt(q, k) * (scale * LOG2E) + (slope * LOG2E) * col.astype(single)
    row_at = lax.broadcasted_iota(jnp.int32, (TILE, TILE), 0)
    col_at = lax.broadcasted_iota(jnp.int32, (TILE, TILE), 1)
    last = jnp.where(col_at <= row_at, s[:, n - TILE :], -1e30)
    s = last if i == 0 else jnp.concatenate([s[:, : n - TILE], last], axis=1)
    e = jnp.exp2(s - jnp.max(s, axis=1, keepdims=True))
    return q, k, e, 1.0 / jnp.sum(e, axis=1, keepdims=True)


class Rows:
    def __init__(self, inv_ref, stage, out, sems, kinds):
        self.inv, self.stage, self.out, self.sems, self.kinds = inv_ref, stage, out, sems, kinds
        self.heads = pl.num_programs(1)
        self.step = pl.program_id(0) * self.heads + pl.program_id(1)
        self.slot = lax.rem(self.step, 2)

    def copies(self, step):
        slot = lax.rem(step, 2)
        seq, head = step // self.heads, lax.rem(step, self.heads)
        for kind in range(self.kinds):
            col = pl.multiple_of((kind * self.heads + head) * 128, 128)
            for j in range(SEQ_BLOCKS):
                row = pl.multiple_of(self.inv[seq * SEQ_BLOCKS + j] * SPAN, SPAN)
                yield pltpu.make_async_copy(
                    self.stage.at[slot, kind, pl.ds(j * SPAN, SPAN)],
                    self.out.at[pl.ds(row, SPAN), pl.ds(col, 128)],
                    self.sems.at[slot, kind * SEQ_BLOCKS + j],
                )

    def wait(self, step):
        for copy in self.copies(step):
            copy.wait()

    def open(self):
        @pl.when(self.step >= 2)
        def _():
            self.wait(self.step - 2)

    def close(self):
        for copy in self.copies(self.step):
            copy.start()

        @pl.when(self.step == 2 * self.heads - 1)
        def _():
            self.wait(self.step - 1)
            self.wait(self.step)


def attn_fwd_kernel(scale, inv_ref, slope_ref, *refs):
    q_refs, k_refs, v_refs = refs[:8], refs[8:16], refs[16:24]
    out, stage, sems = refs[24:]
    slope = slope_ref[pl.program_id(1)]
    rows = Rows(inv_ref, stage, out, sems, 1)
    rows.open()
    for i in range(4):
        q, k, e, r = attn_scores(q_refs, k_refs, i, scale, slope)
        v = jnp.concatenate([x[...] for x in v_refs[: 2 * i + 2]], axis=0)
        o = dot_nn((e * r).astype(half), v)
        stage[rows.slot, 0, TILE * i : TILE * (i + 1), :] = o.astype(half)
    rows.close()


def attn_bwd_kernel(scale, inv_ref, slope_ref, *refs):
    q_refs, k_refs, v_refs, g_refs = refs[:8], refs[8:16], refs[16:24], refs[24:32]
    out, stage, sems, dk_acc, dv_acc = refs[32:]
    slope = slope_ref[pl.program_id(1)]
    rows = Rows(inv_ref, stage, out, sems, 3)
    rows.open()
    for i in (3, 2, 1, 0):
        q, k, e, r = attn_scores(q_refs, k_refs, i, scale, slope)
        n = TILE * (i + 1)
        v = jnp.concatenate([x[...] for x in v_refs[: 2 * i + 2]], axis=0)
        g = jnp.concatenate([g_refs[2 * i][...], g_refs[2 * i + 1][...]], axis=0)
        p = e * r
        dp = dot_nt(g, v)
        delta = jnp.sum(p * dp, axis=1, keepdims=True)
        ds = (p * (dp - delta)).astype(half)
        pb = p.astype(half)
        dq = (dot_nn(ds, k) * scale).astype(half)
        stage[rows.slot, 0, TILE * i : TILE * (i + 1), :] = dq
        dk = dot_tn(ds, q)
        dv = dot_tn(pb, g)
        if i == 3:
            dk_acc[...] = dk
            dv_acc[...] = dv
        else:
            dk_acc[:n, :] += dk
            dv_acc[:n, :] += dv
    stage[rows.slot, 1] = (dk_acc[...] * scale).astype(half)
    stage[rows.slot, 2] = dv_acc[...].astype(half)
    rows.close()


def block_specs(offset):
    def one(j):
        return pl.BlockSpec(
            (SPAN, 128), lambda s, h, inv, slope: (inv[s * SEQ_BLOCKS + j], offset + h)
        )

    return [one(j) for j in range(SEQ_BLOCKS)]


def attn_call(kernel, kinds, joined, extra, extra_specs, scratch, inv, slopes, heads, cost, name):
    rows = joined.shape[0]
    specs = block_specs(0) + block_specs(heads) + block_specs(2 * heads) + extra_specs
    return pl.pallas_call(
        kernel,
        grid_spec=pltpu.PrefetchScalarGridSpec(
            num_scalar_prefetch=2,
            grid=(2, heads),
            in_specs=specs,
            out_specs=pl.BlockSpec(memory_space=pl.ANY),
            scratch_shapes=[
                pltpu.VMEM((2, kinds, rows // 2, 128), half),
                pltpu.SemaphoreType.DMA((2, kinds * SEQ_BLOCKS)),
            ]
            + scratch,
        ),
        out_shape=jax.ShapeDtypeStruct((rows, kinds * heads * 128), half),
        compiler_params=pltpu.CompilerParams(vmem_limit_bytes=48 * 1024 * 1024),
        cost_estimate=cost,
        name=name,
    )(inv, slopes, *([joined] * 24), *extra)


def attn_forward(joined, inv, slopes, heads, scale):
    kernel = functools.partial(attn_fwd_kernel, scale)
    cost = hint(20 * 10**9, joined.shape[0] * heads * 128 * 8)
    return attn_call(
        kernel, 1, joined, [], [], [], inv, slopes, heads, cost, "attn_forward"
    )


def attn_backward(joined, grad, inv, slopes, heads, scale):
    kernel = functools.partial(attn_bwd_kernel, scale)
    cost = hint(40 * 10**9, joined.shape[0] * heads * 128 * 14)
    sums = [pltpu.VMEM((joined.shape[0] // 2, 128), single)] * 2
    return attn_call(
        kernel,
        3,
        joined,
        [grad] * 8,
        block_specs(0),
        sums,
        inv,
        slopes,
        heads,
        cost,
        "attn_backward",
    )


HINT = 0.001


def block_of(x):
    return x if isinstance(x, tuple) else (x, x.shape[0], 0)


def hint(flops, bytes_accessed):
    return pl.CostEstimate(
        flops=int(HINT * flops), bytes_accessed=int(HINT * bytes_accessed), transcendentals=0
    )


def rows_kernel(dot, epilogue, count, extra, *refs):
    left, w_ref = refs[:count], refs[count]
    extras = refs[count + 1 : count + 1 + extra]
    outs = refs[count + 1 + extra :]
    for i in range(count):
        epilogue(i, dot(left[i][...], w_ref[...]), extras, outs)


def rows_matmul(blocks, w, transposed, extras, outs, epilogue, name, tile=512):
    blocks = [block_of(x) for x in blocks]
    extras = [block_of(x) for x in extras]
    n = w.shape[0] if transposed else w.shape[1]
    k = w.shape[1] if transposed else w.shape[0]
    t = math.gcd(n, tile)
    w_spec = (
        pl.BlockSpec((t, k), lambda i: (i, 0)) if transposed else pl.BlockSpec((k, t), lambda i: (0, i))
    )
    rows = sum(x[1] for x in blocks)
    return pl.pallas_call(
        functools.partial(
            rows_kernel, dot_nt if transposed else dot_nn, epilogue, len(blocks), len(extras)
        ),
        grid=(n // t,),
        in_specs=[pl.BlockSpec((x[1], k), lambda i, at=x[2]: (at, 0)) for x in blocks]
        + [w_spec]
        + [pl.BlockSpec((x[1], t), lambda i, at=x[2]: (at, i)) for x in extras],
        out_specs=[pl.BlockSpec((r, t), lambda i: (0, i)) for r, _ in outs],
        out_shape=[jax.ShapeDtypeStruct((r, n), d) for r, d in outs],
        compiler_params=pltpu.CompilerParams(vmem_limit_bytes=52 * 1024 * 1024),
        cost_estimate=hint(2 * rows * n * k, 2 * n * k + 4 * rows * (n + k)),
        name=name,
    )(*[x[0] for x in blocks], w, *[x[0] for x in extras])


def plain(blocks, w, transposed, dtype, name):
    def epilogue(i, x, extras, outs):
        outs[i][...] = x.astype(dtype)

    outs = [(block_of(x)[1], dtype) for x in blocks]
    return rows_matmul(blocks, w, transposed, [], outs, epilogue, name)


def joined_rows(blocks, w, bias, name):
    sizes = [block_of(x)[1] for x in blocks]

    def epilogue(i, x, extras, outs):
        at = sum(sizes[:i])
        outs[0][at : at + sizes[i], :] = (x + extras[0][...]).astype(half)

    bias = bias.reshape(1, -1)
    return rows_matmul(blocks, w, False, [bias], [(sum(sizes), half)], epilogue, name)[0]


def up_gelu(blocks, w, bias, name):
    count = len(blocks)

    def epilogue(i, x, extras, outs):
        value, slope = gelu_both(x + extras[0][...])
        outs[i][...] = value.astype(half)
        outs[count + i][...] = slope.astype(half)

    outs = [(block_of(x)[1], half) for x in blocks] * 2
    out = rows_matmul(blocks, w, False, [bias.reshape(1, -1)], outs, epilogue, name)
    return out[:count], out[count:]


def hidden_back(blocks, w, slopes, name):
    def epilogue(i, x, extras, outs):
        x = x.astype(half).astype(single) * extras[i][...].astype(single)
        outs[i][...] = x.astype(half)

    outs = [(block_of(x)[1], half) for x in blocks]
    return rows_matmul(blocks, w, True, slopes, outs, epilogue, name)


def outer_kernel(count, *refs):
    out = refs[-1]
    total = None
    for i in range(count):
        x = dot_tn(refs[i][...], refs[count + i][...])
        total = x if total is None else total + x
    out[...] = total.astype(half)


def outer(left, right, name):
    left = [block_of(x) for x in left]
    right = [block_of(x) for x in right]
    m, n = left[0][0].shape[1], right[0][0].shape[1]
    tm = math.gcd(m, 1024)
    tn = n // 2 if n % 256 == 0 and n > 1024 else n
    rows = sum(x[1] for x in left)
    return pl.pallas_call(
        functools.partial(outer_kernel, len(left)),
        grid=(m // tm, n // tn),
        in_specs=[pl.BlockSpec((x[1], tm), lambda i, j, at=x[2]: (at, i)) for x in left]
        + [pl.BlockSpec((x[1], tn), lambda i, j, at=x[2]: (at, j)) for x in right],
        out_specs=pl.BlockSpec((tm, tn), lambda i, j: (i, j)),
        out_shape=jax.ShapeDtypeStruct((m, n), half),
        compiler_params=pltpu.CompilerParams(vmem_limit_bytes=52 * 1024 * 1024),
        cost_estimate=hint(2 * rows * m * n, 2 * rows * (m + n) + 2 * m * n),
        name=name,
    )(*[x[0] for x in left], *[x[0] for x in right])


def partner(mask):
    c = lax.axis_index("ctx")
    if mask == 1:
        return c + 1 - 2 * lax.rem(c, 2)
    return lax.rem(c + 2, 4) if mask == 2 else 3 - c


def greet(masks):
    barrier = pltpu.get_barrier_semaphore()
    for mask in masks:
        pl.semaphore_signal(
            barrier,
            inc=1,
            device_id={"ctx": partner(mask)},
            device_id_type=pl.DeviceIdType.MESH,
        )
    pl.semaphore_wait(barrier, len(masks))


class Moves:
    def __init__(self, send_sem, recv_sem):
        self.send_sem, self.recv_sem, self.used = send_sem, recv_sem, 0

    def start(self, src, dst, mask):
        copy = pltpu.make_async_remote_copy(
            src_ref=src,
            dst_ref=dst,
            send_sem=self.send_sem.at[self.used],
            recv_sem=self.recv_sem.at[self.used],
            device_id={"ctx": partner(mask)},
            device_id_type=pl.DeviceIdType.MESH,
        )
        self.used += 1
        copy.start()
        return copy


def multiply(lefts, w, transposed, extras, outs, epilogue, tile=512):
    k = lefts[0].shape[1]
    n = w.shape[0] if transposed else w.shape[1]
    t = math.gcd(n, tile)
    w_spec = (
        pl.BlockSpec((t, k), lambda i: (i, 0)) if transposed else pl.BlockSpec((k, t), lambda i: (0, i))
    )
    dot = dot_nt if transposed else dot_nn

    def body(*refs):
        rows_kernel(dot, epilogue, len(lefts), len(extras), *refs)

    pltpu.emit_pipeline(
        body,
        grid=(n // t,),
        in_specs=[pl.BlockSpec((x.shape[0], k), lambda i: (0, 0)) for x in lefts]
        + [w_spec]
        + [pl.BlockSpec((x.shape[0], t), lambda i: (0, i)) for x in extras],
        out_specs=[pl.BlockSpec((x.shape[0], t), lambda i: (0, i)) for x in outs],
    )(*lefts, w, *extras, *outs)


def store(i, x, extras, outs):
    outs[i][...] = x.astype(outs[i].dtype)


def store_sum(i, x, extras, outs):
    outs[i][...] = (x + extras[i][...].astype(single)).astype(outs[i].dtype)


def store_passed(i, x, extras, outs):
    if i in (1, 2):
        x = x + extras[i - 1][...].astype(single)
    outs[i][...] = x.astype(outs[i].dtype)


def store_hidden(i, x, extras, outs):
    outs[i][...] = (x.astype(half).astype(single) * extras[i][...].astype(single)).astype(half)


def outer_on(lefts, rights, out):
    m, n = out.shape
    tm = math.gcd(m, 1024)
    tn = n // 2 if n % 256 == 0 and n > 1024 else n

    def body(*refs):
        outer_kernel(len(lefts), *refs)

    pltpu.emit_pipeline(
        body,
        grid=(m // tm, n // tn),
        in_specs=[pl.BlockSpec((x.shape[0], tm), lambda i, j: (0, i)) for x in lefts]
        + [pl.BlockSpec((x.shape[0], tn), lambda i, j: (0, j)) for x in rights],
        out_specs=[pl.BlockSpec((tm, tn), lambda i, j: (i, j))],
    )(*lefts, *rights, out)


def halves(ref):
    n = ref.shape[0] // 2
    return ref.at[pl.ds(0, n)], ref.at[pl.ds(n, n)]


def moving_call(kernel, operands, outs, moves, call, flops, name):
    anywhere = pl.BlockSpec(memory_space=pl.ANY)
    sems = pltpu.SemaphoreType.DMA((moves,))
    return pl.pallas_call(
        kernel,
        in_specs=[anywhere] * len(operands),
        out_specs=[anywhere] * len(outs),
        out_shape=[jax.ShapeDtypeStruct(shape, dtype) for shape, dtype in outs],
        scratch_shapes=[sems, sems],
        compiler_params=pltpu.CompilerParams(
            collective_id=call, has_side_effects=True, vmem_limit_bytes=52 * 1024 * 1024
        ),
        cost_estimate=hint(flops, 0),
        name=name,
    )(*operands)


def store_biased(i, x, extras, outs):
    outs[i][...] = (x + extras[0][...]).astype(half)


def qkv_kernel(*refs):
    tok, gain, shift, a1, w_qkv, bias = refs[0:2], refs[2], refs[3], refs[4:7], refs[7], refs[8]
    dz_lo, dz_hi = refs[9:11]
    joined, far, one_lo, two_hi = refs[11], refs[12:14], refs[14], refs[15]
    moves = Moves(*refs[16:18])
    n, width = tok[0].shape
    greet((1, 2))
    copies = [moves.start(dz_lo, one_lo, 1), moves.start(dz_hi, two_hi, 2)]

    def norm(x_lo, x_hi, g, s, o_lo, o_hi):
        for x, o in ((x_lo, o_lo), (x_hi, o_hi)):
            normed, _ = norm_parts(x[...].astype(single))
            o[...] = (normed * g[...] + s[...]).astype(half)

    t = math.gcd(n, 64)
    block = pl.BlockSpec((t, width), lambda i: (i, 0))
    row = pl.BlockSpec((1, width), lambda i: (0, 0))
    pltpu.emit_pipeline(
        norm, grid=(n // t,), in_specs=[block, block, row, row], out_specs=[block, block]
    )(*tok, gain, shift, *far)
    lefts, outs, at = [*a1, *far], [], 0
    for x in lefts:
        outs.append(joined.at[pl.ds(at, x.shape[0])])
        at += x.shape[0]
    multiply(lefts, w_qkv, False, [bias], outs, store_biased)
    for copy in copies:
        copy.wait()


def qkv_forward(tok, gain, shift, a1, w_qkv, bias, dz_lo, dz_hi):
    n, width = tok[0].shape
    k = w_qkv.shape[1]
    outs = [((8 * n, k), half)] + [((n, width), half)] * 4
    out = moving_call(
        qkv_kernel,
        [*tok, gain.reshape(1, -1), shift.reshape(1, -1), *a1, w_qkv, bias.reshape(1, -1), dz_lo, dz_hi],
        outs,
        2,
        7,
        16 * n * width * k,
        "qkv",
    )
    return out[0], out[1:3], out[3:5]


def feed_pass(dz, slope, w_down, w_up, du, total):
    n, width = dz[0].shape
    wide = w_down.shape[0]
    t = math.gcd(wide, 512)
    total[...] = jnp.zeros_like(total)

    def body(dz_lo, dz_hi, down, up, slope_lo, slope_hi, du_lo, du_hi):
        for i, x, s, d in ((0, dz_lo, slope_lo, du_lo), (1, dz_hi, slope_hi, du_hi)):
            grad = dot_nt(x[...], down[...]).astype(half).astype(single)
            grad = (grad * s[...].astype(single)).astype(half)
            d[...] = grad
            total[i * n : (i + 1) * n, :] += dot_nt(grad, up[...])

    pltpu.emit_pipeline(
        body,
        grid=(wide // t,),
        in_specs=[pl.BlockSpec((n, width), lambda i: (0, 0))] * 2
        + [pl.BlockSpec((t, width), lambda i: (i, 0)), pl.BlockSpec((width, t), lambda i: (0, i))]
        + [pl.BlockSpec((n, t), lambda i: (0, i))] * 2,
        out_specs=[pl.BlockSpec((n, t), lambda i: (0, i))] * 2,
    )(*dz, w_down, w_up, *slope, *du)


def feed_back_kernel(*refs):
    dz, slope, (w_down, w_up) = refs[0:8], refs[8:13], refs[13:15]
    a2, gb_far = refs[15:20], refs[20:22]
    du, own, land1, land2, up_grad, mix_x, mix_y = refs[22:27], *refs[27:33]
    total, far, near, rest, from_x, from_y, mixed = refs[33:40]
    moves = Moves(*refs[40:42])
    local = refs[42]
    n = from_x.shape[0]
    lo, hi = pl.ds(0, n), pl.ds(n, n)
    (s1_lo, s1_hi), (s2_lo, s2_hi) = halves(slope[1]), halves(slope[2])
    (d1_lo, d1_hi), (d2_lo, d2_hi) = halves(du[1]), halves(du[2])
    (land1_lo, land1_hi), (land2_lo, land2_hi) = halves(land1), halves(land2)
    greet((1, 2))
    wide, width = w_down.shape
    t = math.gcd(width, 512)

    def mix(x_lo, x_hi, w):
        at = pl.ds(pl.multiple_of(pl.program_id(0) * t, t), t)
        mixed[0:n, at] = dot_nn(x_lo[...], w[...]).astype(half)
        mixed[n : 2 * n, at] = dot_nn(x_hi[...], w[...]).astype(half)

    pltpu.emit_pipeline(
        mix,
        grid=(width // t,),
        in_specs=[pl.BlockSpec((n, wide), lambda i: (0, 0))] * 2
        + [pl.BlockSpec((wide, t), lambda i: (0, i))],
    )(*gb_far, w_down)
    second = [moves.start(mixed.at[lo], mix_x, 1), moves.start(mixed.at[hi], mix_y, 2)]
    feed_pass(dz[6:8], slope[3:5], w_down, w_up, du[3:5], total)
    far[...] = total[...].astype(half)
    first = [moves.start(far.at[lo], from_x, 1), moves.start(far.at[hi], from_y, 2)]
    feed_pass([dz[2], dz[5]], [s1_lo, s2_hi], w_down, w_up, [d1_lo, d2_hi], total)
    near[...] = total[...].astype(half)
    second += [moves.start(near.at[lo], land1_lo, 1), moves.start(near.at[hi], land2_hi, 2)]
    feed_pass([dz[3], dz[4]], [s1_hi, s2_lo], w_down, w_up, [d1_hi, d2_lo], total)
    for copy in first:
        copy.wait()
    rest[lo] = (total[lo] + from_y[...].astype(single)).astype(half)
    rest[hi] = (total[hi] + from_x[...].astype(single)).astype(half)
    second += [moves.start(rest.at[lo], land1_hi, 1), moves.start(rest.at[hi], land2_lo, 2)]
    feed_pass(dz[0:2], halves(slope[0]), w_down, w_up, halves(du[0]), total)
    store_own = pltpu.make_async_copy(total, own, local)
    store_own.start()
    outer_on(a2, du, up_grad)
    store_own.wait()
    for copy in second:
        copy.wait()


def feed_back(dz, slope, w_down, w_up, a2, gb_far):
    n, width = dz[0].shape
    rows, wide = 2 * n, w_down.shape[0]
    anywhere = pl.BlockSpec(memory_space=pl.ANY)
    outs = [((r, wide), half) for r in (rows, rows, rows, n, n)]
    outs += [((rows, width), single)] + [((rows, width), half)] * 2
    outs += [((width, wide), half)] + [((n, width), half)] * 2
    sems = pltpu.SemaphoreType.DMA((8,))
    out = pl.pallas_call(
        feed_back_kernel,
        in_specs=[anywhere] * 22,
        out_specs=[anywhere] * len(outs),
        out_shape=[jax.ShapeDtypeStruct(shape, dtype) for shape, dtype in outs],
        scratch_shapes=[pltpu.VMEM((rows, width), single)]
        + [pltpu.VMEM((rows, width), half)] * 3
        + [pltpu.VMEM((n, width), half)] * 2
        + [pltpu.VMEM((rows, width), half)]
        + [sems, sems, pltpu.SemaphoreType.DMA],
        compiler_params=pltpu.CompilerParams(
            collective_id=3, has_side_effects=True, vmem_limit_bytes=56 * 1024 * 1024
        ),
        cost_estimate=hint(26 * rows * width * wide, 0),
        name="feed_back",
    )(*dz, *slope, w_down, w_up, *a2, *gb_far)
    return out[0:5], out[5:8], out[8], out[9:11]


def heads_back_kernel(part, *refs):
    own, land1, land2, cot, y1, gain, w_out = refs[0:7]
    ob, gb1, gb2, w_down, mix_x, mix_y, down = refs[7:14]
    dy1, dz1, sums, got, out_grad = refs[14:19]
    mix, down1, down2 = refs[19:23], refs[23], refs[24]
    dz, w, stage = refs[25:28]
    moves = Moves(*refs[28:30])
    local = refs[30]
    rows, width = own.shape
    greet((1, 2, 3))
    load = pltpu.make_async_copy(w_out, w, local.at[0])
    load.start()
    copies = [moves.start(down, down1, 1), moves.start(down, down2, 2)]
    t = math.gcd(rows, 64)

    def norm(own, one, two, cot, y1, gain, dy1, dz1, sums):
        step = pl.program_id(0)
        grad = own[...] + one[...].astype(single) + two[...].astype(single)
        normed, inv = norm_parts(y1[...])
        dy = cot[...] + norm_back(normed, inv, gain[...], grad)
        low = dy.astype(half)
        dy1[...] = dy
        dz1[...] = low
        dz[pl.ds(pl.multiple_of(step * t, t), t), :] = low

        @pl.when(step == 0)
        def _():
            sums[...] = jnp.zeros_like(sums)

        sums[0:1] += jnp.sum(grad * normed, axis=0, keepdims=True)
        sums[1:2] += jnp.sum(grad, axis=0, keepdims=True)
        sums[2:3] += jnp.sum(low.astype(single), axis=0, keepdims=True)

    block = pl.BlockSpec((t, width), lambda i: (i, 0))
    pltpu.emit_pipeline(
        norm,
        grid=(rows // t,),
        in_specs=[block] * 5 + [pl.BlockSpec((1, width), lambda i: (0, 0))],
        out_specs=[block] * 2 + [pl.BlockSpec((8, width), lambda i: (0, 0))],
    )(own, land1, land2, cot, y1, gain, dy1, dz1, sums)
    load.wait()
    for mask in (3, 1, 2, 0):
        of = partner(mask) if mask else lax.axis_index("ctx")
        heads = w[pl.ds(pl.multiple_of(of * part, part), part), :]
        stage[mask] = dot_nt(dz[...], heads).astype(half)
        at = got.at[pl.ds(mask * rows, rows)]
        if mask:
            copies.append(moves.start(stage.at[mask], at, mask))
        else:
            keep = pltpu.make_async_copy(stage.at[0], at, local.at[1])
            keep.start()
    outer_on([ob], [dz1], out_grad)
    multiply(
        [*halves(gb1), *halves(gb2)],
        w_down,
        False,
        [mix_y, mix_x],
        mix,
        store_passed,
    )
    keep.wait()
    for copy in copies:
        copy.wait()


def heads_back(terms, cot, y1, gain, w_out, ob, gb1, gb2, w_down, mix_first, down):
    rows, width = cot.shape
    part = width // 4
    anywhere = pl.BlockSpec(memory_space=pl.ANY)
    sems = pltpu.SemaphoreType.DMA((5,))
    outs = [((rows, width), single), ((rows, width), half), ((8, width), single)]
    outs += [((4 * rows, part), half), ((width, width), half)]
    outs += [((rows // 2, width), half)] * 4 + [(down.shape, half)] * 2
    out = pl.pallas_call(
        functools.partial(heads_back_kernel, part),
        in_specs=[anywhere] * 14,
        out_specs=[anywhere] * len(outs),
        out_shape=[jax.ShapeDtypeStruct(shape, dtype) for shape, dtype in outs],
        scratch_shapes=[
            pltpu.VMEM((rows, width), half),
            pltpu.VMEM((width, width), half),
            pltpu.VMEM((4, rows, part), half),
            sems,
            sems,
            pltpu.SemaphoreType.DMA((2,)),
        ],
        compiler_params=pltpu.CompilerParams(
            collective_id=4, has_side_effects=True, vmem_limit_bytes=56 * 1024 * 1024
        ),
        cost_estimate=hint(10 * rows * width * width, 0),
        name="heads_back",
    )(*terms, cot, y1, gain.reshape(1, -1), w_out, ob, gb1, gb2, w_down, *mix_first, down)
    return out[0], out[2], out[3], out[4], out[5:9], out[9:11]


def qkv_back_kernel(*refs):
    dqkv, w_qkv = refs[0:2]
    a1, gb_own, w_down, one_hi, two_hi = refs[2:7], *refs[7:11]
    own, p3, p1, p2, from_x, from_y, land1, land2, qkv_grad, mix_own = refs[11:21]
    x_hi, y_hi = refs[21:23]
    moves = Moves(*refs[23:25])
    rows = own.shape[0]
    n = rows // 2

    def block(k):
        return dqkv.at[pl.ds(k * n, n)]

    greet((1, 2))
    output = [moves.start(one_hi, x_hi, 1), moves.start(two_hi, y_hi, 2)]
    (p3_lo, p3_hi), (p1_lo, p1_hi), (p2_lo, p2_hi) = halves(p3), halves(p1), halves(p2)
    (land1_lo, land1_hi), (land2_lo, land2_hi) = halves(land1), halves(land2)
    multiply([block(6), block(7)], w_qkv, True, [], [p3_lo, p3_hi], store)
    first = [moves.start(p3_lo, from_x, 1), moves.start(p3_hi, from_y, 2)]
    multiply([block(2), block(5)], w_qkv, True, [], [p1_lo, p2_hi], store)
    second = [moves.start(p1_lo, land1_lo, 1), moves.start(p2_hi, land2_hi, 2)]
    multiply([dqkv.at[pl.ds(0, rows)]], w_qkv, True, [], [own], store)
    multiply([gb_own], w_down, False, [], [mix_own], store)
    for copy in first:
        copy.wait()
    multiply([block(3), block(4)], w_qkv, True, [from_y, from_x], [p1_hi, p2_lo], store_sum)
    second += [moves.start(p1_hi, land1_hi, 1), moves.start(p2_lo, land2_lo, 2)]
    rights, at = [], 0
    for x in a1:
        rights.append(dqkv.at[pl.ds(at, x.shape[0])])
        at += x.shape[0]
    outer_on(a1, rights, qkv_grad)
    for copy in output + second:
        copy.wait()


def qkv_back(dqkv, w_qkv, a1, gb_own, w_down, one_hi, two_hi):
    rows, width = a1[0].shape
    wide = gb_own.shape[1]
    n = rows // 2
    outs = [((rows, width), single)] + [((rows, width), half)] * 3
    outs += [((n, width), half)] * 2 + [((rows, width), half)] * 2
    outs += [((width, dqkv.shape[1]), half), ((rows, width), single)] + [((n, width), half)] * 2
    out = moving_call(
        qkv_back_kernel,
        [dqkv, w_qkv, *a1, gb_own, w_down, one_hi, two_hi],
        outs,
        8,
        5,
        16 * rows * width * dqkv.shape[1] + 2 * rows * width * wide,
        "qkv_back",
    )
    return out[0], out[6:8], out[8], out[9], out[10:12]


def lay_out_kernel(axis, layout, c_ref, *refs):
    out = refs[-1]
    for (j, row), ref in zip(layout, refs):
        x = ref[...].astype(single)
        r, w = x.shape
        if axis == 0:
            n = sum(ref.shape[0] for (k, _), ref in zip(layout, refs) if k == j)
            out[pl.ds(pl.multiple_of((c_ref[0] ^ j) * n + row, r), r), :] = x
        else:
            out[row : row + r, pl.ds(pl.multiple_of((c_ref[0] ^ j) * w, w), w)] = x


def lay_out(axis, pieces, c, groups):
    count = len(pieces)
    r = sum(x.shape[0] for x in pieces[0])
    n = pieces[0][0].shape[1]
    w = n // groups
    if w % 128:
        whole = xor_order([jnp.concatenate(p, axis=0).astype(single) for p in pieces], c)
        whole = jnp.stack([p.reshape(r, groups, w) for p in whole], axis=2)
        return whole.reshape(r, count * n)
    layout, blocks = [], []
    for j, p in enumerate(pieces):
        row = 0
        for x in p:
            layout.append((j, row))
            blocks.append(x)
            row += x.shape[0]
    out = (count * r, w) if axis == 0 else (r, count * w)
    return pl.pallas_call(
        functools.partial(lay_out_kernel, axis, layout),
        grid_spec=pltpu.PrefetchScalarGridSpec(
            num_scalar_prefetch=1,
            grid=(groups,),
            in_specs=[pl.BlockSpec((x.shape[0], w), lambda k, c: (0, k)) for x in blocks],
            out_specs=pl.BlockSpec(out, lambda k, c: (0, k)),
        ),
        out_shape=jax.ShapeDtypeStruct((out[0], out[1] * groups), single),
        compiler_params=pltpu.CompilerParams(vmem_limit_bytes=48 * 1024 * 1024),
        cost_estimate=hint(0, 6 * r * n * count),
        name="lay_out",
    )(c.reshape(1), *blocks)


def gather_small_kernel(nf, x_ref, o_ref, send_sem, recv_sem):
    f = lax.axis_index("fsdp")
    barrier = pltpu.get_barrier_semaphore()
    for d in range(1, nf):
        pl.semaphore_signal(
            barrier,
            inc=1,
            device_id={"fsdp": lax.rem(f + d, nf)},
            device_id_type=pl.DeviceIdType.MESH,
        )
    pl.semaphore_wait(barrier, nf - 1)
    copies = []
    for d in range(1, nf):
        copies.append(
            pltpu.make_async_remote_copy(
                src_ref=x_ref,
                dst_ref=o_ref.at[f],
                send_sem=send_sem.at[d],
                recv_sem=recv_sem.at[d],
                device_id={"fsdp": lax.rem(f + d, nf)},
                device_id_type=pl.DeviceIdType.MESH,
            )
        )
        copies[-1].start()
    o_ref[f] = x_ref[...]
    for copy in copies:
        copy.wait()


def gather_small(x, nf):
    return pl.pallas_call(
        functools.partial(gather_small_kernel, nf),
        out_shape=jax.ShapeDtypeStruct((nf,) + x.shape, single),
        in_specs=[pl.BlockSpec(memory_space=pltpu.VMEM)],
        out_specs=pl.BlockSpec(memory_space=pltpu.VMEM),
        scratch_shapes=[pltpu.SemaphoreType.DMA((nf,)), pltpu.SemaphoreType.DMA((nf,))],
        compiler_params=pltpu.CompilerParams(collective_id=1, has_side_effects=True),
        name="gather_small",
    )(x)


def reduce_small_kernel(nf, nc, x_ref, o_ref, land, stage, send_sem, recv_sem):
    f = lax.axis_index("fsdp")
    c = lax.axis_index("ctx")
    barrier = pltpu.get_barrier_semaphore()
    for d in range(1, nf):
        pl.semaphore_signal(
            barrier,
            inc=1,
            device_id={"fsdp": lax.rem(f + d, nf)},
            device_id_type=pl.DeviceIdType.MESH,
        )
    for d in range(1, nc):
        pl.semaphore_signal(
            barrier,
            inc=1,
            device_id={"ctx": lax.rem(c + d, nc)},
            device_id_type=pl.DeviceIdType.MESH,
        )
    pl.semaphore_wait(barrier, nf + nc - 2)
    copies = []
    for d in range(1, nf):
        to = lax.rem(f + d, nf)
        copies.append(
            pltpu.make_async_remote_copy(
                src_ref=x_ref.at[to],
                dst_ref=land.at[d],
                send_sem=send_sem.at[d],
                recv_sem=recv_sem.at[d],
                device_id={"fsdp": to},
                device_id_type=pl.DeviceIdType.MESH,
            )
        )
        copies[-1].start()
    total = x_ref[f]
    for d in range(1, nf):
        copies[d - 1].wait()
        total = total + land[d]
    stage[0] = total
    copies = []
    for d in range(1, nc):
        copies.append(
            pltpu.make_async_remote_copy(
                src_ref=stage.at[0],
                dst_ref=stage.at[d],
                send_sem=send_sem.at[nf + d],
                recv_sem=recv_sem.at[nf + d],
                device_id={"ctx": lax.rem(c + d, nc)},
                device_id_type=pl.DeviceIdType.MESH,
            )
        )
        copies[-1].start()
    for d in range(1, nc):
        copies[d - 1].wait()
        total = total + stage[d]
    o_ref[...] = total


def reduce_small(x, nf, nc, call):
    block = x.shape[1:]
    sems = pltpu.SemaphoreType.DMA((nf + nc,))
    return pl.pallas_call(
        functools.partial(reduce_small_kernel, nf, nc),
        out_shape=jax.ShapeDtypeStruct(block, single),
        in_specs=[pl.BlockSpec(memory_space=pltpu.VMEM)],
        out_specs=pl.BlockSpec(memory_space=pltpu.VMEM),
        scratch_shapes=[
            pltpu.VMEM((nf,) + block, single),
            pltpu.VMEM((nc,) + block, single),
            sems,
            sems,
        ],
        compiler_params=pltpu.CompilerParams(collective_id=call, has_side_effects=True),
        name="reduce_small",
    )(x)


def per_device(
    tokens,
    cotangent,
    lengths,
    span_place,
    ln1_gain,
    ln1_shift,
    qkv_weight,
    q_bias,
    v_bias,
    out_weight,
    out_bias,
    ln2_gain,
    ln2_shift,
    up_weight,
    up_bias,
    down_weight,
    down_bias,
):
    rows, width = tokens.shape
    CTX = lax.axis_size("ctx")
    c = lax.axis_index("ctx")
    f = lax.axis_index("fsdp")
    nf = lax.axis_size("fsdp")
    wide = up_weight.shape[1]
    part = width // CTX
    heads = HEADS // CTX
    scale = 1.0 / math.sqrt(width // HEADS)
    shard = width // nf
    fpart = wide // nf // CTX
    wpart = wide // CTX

    def columns(x, width_each, stride, count):
        return jnp.concatenate(
            [
                lax.dynamic_slice_in_dim(x, k * stride + c * width_each, width_each, axis=1)
                for k in range(count)
            ],
            axis=1,
        )

    def after(x, *others):
        return lax.optimization_barrier((x, others))[0]

    def pick(x, axis):
        return lax.dynamic_index_in_dim(x, c, axis, keepdims=False)

    def gather_f(x):
        return lax.all_gather(x, "fsdp", axis=0, tiled=True)

    qkv_own = columns(qkv_weight, part, width, 3)
    up_own = columns(up_weight, fpart, wide // nf, nf)
    down_own = lax.dynamic_slice_in_dim(down_weight, c * fpart, fpart, axis=0)
    w_qkv = gather_f(qkv_own.astype(half))
    up_own, down_own = up_own.astype(half), down_own.astype(half)
    small = jnp.concatenate(
        [ln1_gain, ln1_shift, q_bias, v_bias, out_bias, ln2_gain, ln2_shift, down_bias, up_bias]
    )
    small_len = small.shape[0]
    small = jnp.pad(small, (0, -small_len % 1024)).reshape(-1, 128)
    small_all = gather_small(small, nf).reshape(nf, -1)[:, :small_len]
    small_all = small_all.astype(half).astype(single)

    def vector(k):
        return small_all[:, k * shard : (k + 1) * shard].reshape(width)

    gain1, shift1, bias_q, bias_v, bias_o, gain2, shift2, bias_d = [vector(k) for k in range(8)]
    bias_u = pick(small_all[:, 8 * shard :].reshape(nf, CTX, fpart), 1).reshape(wpart)
    bias_qkv = jnp.concatenate(
        [pick(bias_q.reshape(CTX, part), 0), jnp.zeros((part,), single), pick(bias_v.reshape(CTX, part), 0)]
    )
    w_out = gather_f(out_weight.astype(half))

    per = rows // SPAN
    table = jnp.arange(CTX * per, dtype=jnp.int32)
    source = ((table // per) ^ c) * per + table % per
    place = jnp.sum(jnp.where(source[:, None] == table[None, :], span_place[0][None, :], 0), axis=1)
    inv = jnp.sum(jnp.where(place[None, :] == table[:, None], table[None, :], 0), axis=1)
    slopes = 2.0 ** (-8.0 * ((c * heads + jnp.arange(heads)).astype(single) + 1.0) / HEADS)

    def flat(pieces):
        return [x for p in pieces for x in p]

    def scatter_f(x):
        return lax.psum_scatter(x, "fsdp", scatter_dimension=0, tiled=True)

    far = CTX - 1
    mid = list(range(1, far))

    def first_norm(x):
        normed, _ = norm_parts(x.astype(single))
        return (normed * gain1 + shift1).astype(half)

    n = rows // 2
    dz2_lo, dz2_hi = cotangent[:n].astype(half), cotangent[n:].astype(half)
    early = (small_all, place, inv, slopes, up_own, down_own, dz2_lo, dz2_hi)
    early, tok_near = after((early, gather_first(tokens)))
    small_all, place, inv, slopes, up_own, down_own, dz2_lo, dz2_hi = early
    tok = gather_second(tokens, tok_near)
    near = [[first_norm(x) for x in p] for p in tok[:far]]
    tok = after(tok, near)
    if CTX != 4:
        dz2_own = jnp.concatenate([dz2_lo, dz2_hi], axis=0)
        dz2_rest = gather_first(dz2_own)
    w_up = gather_f(after(up_own, tok))
    a1 = flat(near)
    if CTX == 4:
        joined, a1_far, dz2_first = qkv_forward(
            tok[far], gain1, shift1, a1, w_qkv, bias_qkv, dz2_lo, dz2_hi
        )
        a1 = a1 + list(a1_far)
        dz2_rest = after((dz2_hi, dz2_lo), joined)
        dz2_rest = [swap(dz2_rest[0], 1), swap(dz2_rest[1], 2)]
    else:
        a1 = a1 + [first_norm(x) for x in tok[far]]
        joined = joined_rows(a1, w_qkv, bias_qkv, "qkv")
    w_down = gather_f(after(down_own, joined))
    attended = attn_forward(joined, inv, slopes, heads, scale)
    mine = [attended[j * rows : (j + 1) * rows] for j in range(CTX)]
    mine = after(mine, dz2_rest)
    mine = [mine[0]] + [swap(mine[j], j) for j in range(1, CTX)]
    ob = jnp.concatenate(xor_order(mine, c), axis=1)
    y1 = tokens.astype(single) + dot_nn(ob, w_out) + bias_o

    normed2, inv2 = norm_parts(y1)
    a2_own = (normed2 * gain2 + shift2).astype(half)
    gb, slope = [None] * CTX, [None] * CTX
    gb[0], slope[0] = up_gelu([a2_own], w_up, bias_u, "up_gelu_0")
    last = gb[0]
    a2_near = gather_first(a2_own)
    a2 = gather_second(a2_own, a2_near)
    if CTX == 4:
        one_lo, two_hi = after(dz2_first, a2_near)
        one_hi, two_lo = dz2_rest
        dz2 = [[dz2_lo, dz2_hi], [one_lo, one_hi], [two_lo, two_hi], [swap(one_lo, 2), swap(two_hi, 1)]]
    else:
        dz2 = [[dz2_own]] + [[x] for x in dz2_rest]
    for j in range(1, CTX):
        gb[j], slope[j] = up_gelu(after(a2[j], last), w_up, bias_u, f"up_gelu_{j}")
        last = gb[j]
    gb_blocks = flat(gb)
    if CTX == 4:
        gb_blocks = [(g[0], n, i) for g in gb[:far] for i in (0, 1)] + list(gb[far])
    down_grad = outer(gb_blocks, flat(dz2), "down_grad")
    down_part = scatter_f(down_grad)
    w_down = after(w_down, down_grad)

    du, dh2, mix = [None] * CTX, [None] * CTX, [None] * CTX
    if CTX == 4:
        du, dh2, up_grad, mix_first = feed_back(
            flat(dz2), flat(slope), w_down, w_up, flat(a2), gb[far]
        )
        du = [du]
    else:
        for j in range(CTX):
            du[j] = hidden_back(dz2[j], w_down, slope[j], f"du_{j}")
            dh2[j] = plain(du[j], w_up, True, half if j else single, f"dh2_{j}")[0]
        arrived = scatter_send(dh2[1:])
        dh2 = dh2[0]
        up_grad = outer(flat(a2), flat(du), "up_grad")
        mix[far] = plain(gb[far], w_down, False, half, "mix_far")[0]
        dh2 = total_of(dh2, arrived)
    up_part = scatter_f(up_grad)
    if CTX == 4:
        dy1, sums2, dattn, out_grad, mix, down_near = heads_back(
            dh2, cotangent, y1, gain2, w_out, ob, gb[1][0], gb[2][0], w_down, mix_first, down_part
        )
        one_lo, one_hi, two_lo, two_hi = mix
        gain2_grad, shift2_grad, out_bias_grad = sums2[0], sums2[1], sums2[2]
    else:
        gain2_grad = jnp.sum(dh2 * normed2, axis=0)
        shift2_grad = jnp.sum(dh2, axis=0)
        dy1 = cotangent + norm_back(normed2, inv2, gain2, dh2)
        dz1 = dy1.astype(half)
        dattn = dot_nt(dz1, w_out).astype(half)
        out_bias_grad = jnp.sum(dz1.astype(single), axis=0)
        dattn = xor_order([dattn[:, s * part : (s + 1) * part] for s in range(CTX)], c)
        dattn = [dattn[0]] + [swap(dattn[j], j) for j in range(1, CTX)]
        dattn = jnp.concatenate(dattn, axis=0)
        out_grad = outer([ob], [dz1], "out_grad")
        for j in mid:
            mix[j] = plain(gb[j], w_down, False, half, f"mix_{j}")[0]
        down_near = gather_first(down_part)
    out_part = scatter_f(out_grad)
    dqkv = attn_backward(joined, dattn, inv, slopes, heads, scale)
    if CTX == 4:
        lows = [swap(one_lo, 1), swap(two_lo, 2)]
        dqkv = after(dqkv, lows, up_part)
        dh1, arrived, qkv_grad, mix_own, highs = qkv_back(
            dqkv, w_qkv, a1, gb[0][0], w_down, one_hi, two_hi
        )
    else:
        dh1 = [
            plain([(dqkv, rows, j)], w_qkv, True, half if j else single, f"dh1_{j}")[0]
            for j in range(CTX)
        ]
        arrived = scatter_send(dh1[1:])
        dh1 = dh1[0]
        qkv_grad = outer(a1, [(dqkv, rows, j) for j in range(CTX)], "qkv_grad")
        mix_own = plain(gb[0], w_down, False, single, "mix_0")[0]
    qkv_part = scatter_f(qkv_grad)
    up_own = after(up_part, arrived)
    up_near = gather_first(up_own)
    out_first = []
    if CTX == 4:
        k = out_part.shape[0] // 2
        out_lo, out_hi = after(out_part, arrived)[:k], after(out_part, arrived)[k:]
        out_first = [swap(out_lo, 1), swap(out_hi, 2)]
    mix_own, du, dz2_own = after((mix_own, flat(du), flat(dz2[:1])), out_part)
    up_bias_grad = sum(jnp.sum(x.astype(single), axis=0) for x in du)
    down_bias_grad = sum(jnp.sum(x.astype(single), axis=0) for x in dz2_own)
    down_near, up_near, out_first = after((down_near, up_near, out_first))
    down_out = gather_second(down_part, down_near)
    up_out = gather_second(up_own, up_near)
    out_second = []
    if CTX == 4:
        out_lo = (out_lo.astype(single) + out_first[0].astype(single)).astype(half)
        out_hi = (out_hi.astype(single) + out_first[1].astype(single)).astype(half)
        out_lo, out_hi = after((out_lo, out_hi))
        dh1, dqkv = after((dh1, dqkv), out_lo, out_hi)
        out_second = [(out_lo, swap(out_lo, 2)), (out_hi, swap(out_hi, 1))]
        mixed = y1 + bias_d + mix_own
        mixed = jnp.concatenate([total_of(mixed[:n], lows), total_of(mixed[n:], highs)])
    else:
        mixed = total_of(y1 + bias_d + mix_own, scatter_send(mix[1:]))
    dh1 = total_of(dh1, arrived)
    sums = jnp.sum(dqkv.astype(single), axis=0)
    normed1_own, inv1_own = norm_parts(tokens.astype(single))
    gain1_grad = jnp.sum(dh1 * normed1_own, axis=0)
    shift1_grad = jnp.sum(dh1, axis=0)
    dy1 = after(dy1, up_out, down_out, out_second)
    input_grad = dy1 + norm_back(normed1_own, inv1_own, gain1, dh1)

    if CTX == 4:
        out_out = [x.astype(single) + y.astype(single) for x, y in out_second]
        out_out = jnp.concatenate(out_out, axis=0)
    else:
        bit = 1
        while bit < CTX:
            out_out = out_part.astype(single) + swap(out_part, bit).astype(single)
            out_part = out_out.astype(half)
            bit *= 2

    def spread(x, inner):
        x = x.reshape(-1, 1, inner)
        mask = (jnp.arange(CTX) == c)[None, :, None]
        return jnp.where(mask, x, 0.0).reshape(-1)

    def reduced(items, call):
        sizes = [x.shape[0] // nf for x in items]
        x = jnp.concatenate([x.reshape(nf, -1) for x in items], axis=1)
        x = jnp.pad(x, ((0, 0), (0, -x.shape[1] % 1024))).reshape(nf, -1, 128)
        x = reduce_small(x, nf, CTX, call).reshape(-1)
        out, at = [], 0
        for n in sizes:
            out.append(x[at : at + n])
            at += n
        return out

    sums_in = [out_bias_grad, gain2_grad, shift2_grad, down_bias_grad, spread(up_bias_grad, fpart)]
    sums_in += [gain1_grad, shift1_grad, spread(sums[:part], part), spread(sums[2 * part :], part)]
    qkv_near = gather_first(qkv_part)
    sums_in[5] = after(sums_in[5], qkv_part)
    sums_out = reduced(sums_in, 2)
    down_out = lay_out(0, after(down_out, sums_out), c, width // min(width, 512))
    qkv_near = after(qkv_near, down_out)
    qkv_out = lay_out(1, gather_second(qkv_part, qkv_near), c, 3)
    up_out = lay_out(1, after(up_out, qkv_near), c, nf)
    out_bias_out, gain2_out, shift2_out, down_bias_out, up_bias_out = sums_out[:5]
    gain1_out, shift1_out, q_bias_out, v_bias_out = sums_out[5:]
    return (
        mixed,
        input_grad,
        gain1_out,
        shift1_out,
        qkv_out,
        q_bias_out,
        v_bias_out,
        out_out,
        out_bias_out,
        gain2_out,
        shift2_out,
        up_out,
        up_bias_out,
        down_out,
        down_bias_out,
    )


def solution(mesh):
    rows, flat = P(("ctx", "fsdp"), None), P("fsdp")
    mat = P("fsdp", None)
    in_specs = (
        rows,
        rows,
        mat,
        mat,
        flat,
        flat,
        mat,
        flat,
        flat,
        mat,
        flat,
        flat,
        flat,
        mat,
        flat,
        mat,
        flat,
    )
    out_specs = (
        rows,
        rows,
        flat,
        flat,
        mat,
        flat,
        flat,
        mat,
        flat,
        flat,
        flat,
        mat,
        flat,
        mat,
        flat,
    )
    return jax.shard_map(
        per_device, mesh=mesh, in_specs=in_specs, out_specs=out_specs, check_vma=False
    )
```

```python
import functools
import math

import jax
import jax.numpy as jnp
from jax import lax
from jax.experimental import pallas as pl
from jax.experimental.pallas import tpu as pltpu
from jax.sharding import PartitionSpec as P

HEADS = 16
SPAN = 128
SEQ_BLOCKS = 8

norm_eps = 1e-05
gelu_coef = 0.7978845608028654
LOG2E = 1.4426950408889634

half = jnp.bfloat16
single = jnp.float32


def dot_nn(a, b):
    return lax.dot_general(a, b, (((1,), (0,)), ((), ())), preferred_element_type=single)


def dot_nt(a, b):
    return lax.dot_general(a, b, (((1,), (1,)), ((), ())), preferred_element_type=single)


def dot_tn(a, b):
    return lax.dot_general(a, b, (((0,), (0,)), ((), ())), preferred_element_type=single)


def norm_parts(values):
    center = values - jnp.mean(values, axis=-1, keepdims=True)
    spread = jnp.mean(center * center, axis=-1, keepdims=True)
    inv = lax.rsqrt(spread + norm_eps)
    return center * inv, inv


def norm_back(normed, inv, gain, grad):
    dn = grad * gain
    return inv * (
        dn
        - jnp.mean(dn, axis=-1, keepdims=True)
        - normed * jnp.mean(dn * normed, axis=-1, keepdims=True)
    )


def gelu_both(v):
    t = jnp.tanh(gelu_coef * (v + 0.044715 * v * v * v))
    value = 0.5 * v * (1.0 + t)
    slope = 0.5 * (1.0 + t) + 0.5 * v * (1.0 - t * t) * gelu_coef * (1.0 + 3 * 0.044715 * v * v)
    return value, slope


def swap(x, mask):
    n = lax.axis_size("ctx")
    return lax.ppermute(x, "ctx", [(i, i ^ mask) for i in range(n)])


def gather_first(x):
    count = lax.axis_size("ctx")
    return [swap(x, j) for j in range(1, 3 if count == 4 else count)]


def gather_second(x, arrived):
    if lax.axis_size("ctx") != 4:
        return [[x]] + [[p] for p in arrived]
    one, two = arrived
    n = x.shape[0] // 2
    return [[x], [one], [two], [swap(one[:n], 2), swap(two[n:], 1)]]


def gather_ctx(x):
    return gather_second(x, gather_first(x))


def scatter_first(far):
    if lax.axis_size("ctx") != 4:
        return None
    return swap(far[0], 1), swap(far[1], 2)


def scatter_second(pieces, first):
    if first is None:
        return pieces[1:]
    p1, p2 = pieces[1], pieces[2]
    n = p1.shape[0] // 2
    from_x, from_y = first
    p1 = jnp.concatenate(
        [p1[:n], (p1[n:].astype(single) + from_y.astype(single)).astype(half)], axis=0
    )
    p2 = jnp.concatenate(
        [(p2[:n].astype(single) + from_x.astype(single)).astype(half), p2[n:]], axis=0
    )
    return [p1, p2]


def scatter_send(sent):
    return [swap(x, j + 1) for j, x in enumerate(sent)]


def total_of(own, arrived):
    for x in arrived:
        own = own + x.astype(single)
    return own


def xor_order(items, c):
    bit = 1
    while bit < len(items):
        on = (c & bit) == bit
        items = [jnp.where(on, items[i ^ bit], items[i]) for i in range(len(items))]
        bit *= 2
    return items


TILE = 256


def attn_scores(q_refs, k_refs, i, scale, slope):
    q = jnp.concatenate([q_refs[2 * i][...], q_refs[2 * i + 1][...]], axis=0)
    k = jnp.concatenate([r[...] for r in k_refs[: 2 * i + 2]], axis=0)
    n = TILE * (i + 1)
    col = lax.broadcasted_iota(jnp.int32, (1, n), 1) - (n - 1)
    s = dot_nt(q, k) * (scale * LOG2E) + (slope * LOG2E) * col.astype(single)
    row_at = lax.broadcasted_iota(jnp.int32, (TILE, TILE), 0)
    col_at = lax.broadcasted_iota(jnp.int32, (TILE, TILE), 1)
    last = jnp.where(col_at <= row_at, s[:, n - TILE :], -1e30)
    s = last if i == 0 else jnp.concatenate([s[:, : n - TILE], last], axis=1)
    e = jnp.exp2(s - jnp.max(s, axis=1, keepdims=True))
    return q, k, e, 1.0 / jnp.sum(e, axis=1, keepdims=True)


class Rows:
    def __init__(self, inv_ref, stage, out, sems, kinds):
        self.inv, self.stage, self.out, self.sems, self.kinds = inv_ref, stage, out, sems, kinds
        self.heads = pl.num_programs(1)
        self.step = pl.program_id(0) * self.heads + pl.program_id(1)
        self.slot = lax.rem(self.step, 2)

    def copies(self, step):
        slot = lax.rem(step, 2)
        seq, head = step // self.heads, lax.rem(step, self.heads)
        for kind in range(self.kinds):
            col = pl.multiple_of((kind * self.heads + head) * 128, 128)
            for j in range(SEQ_BLOCKS):
                row = pl.multiple_of(self.inv[seq * SEQ_BLOCKS + j] * SPAN, SPAN)
                yield pltpu.make_async_copy(
                    self.stage.at[slot, kind, pl.ds(j * SPAN, SPAN)],
                    self.out.at[pl.ds(row, SPAN), pl.ds(col, 128)],
                    self.sems.at[slot, kind * SEQ_BLOCKS + j],
                )

    def wait(self, step):
        for copy in self.copies(step):
            copy.wait()

    def open(self):
        @pl.when(self.step >= 2)
        def _():
            self.wait(self.step - 2)

    def close(self):
        for copy in self.copies(self.step):
            copy.start()

        @pl.when(self.step == 2 * self.heads - 1)
        def _():
            self.wait(self.step - 1)
            self.wait(self.step)


def attn_fwd_kernel(scale, inv_ref, slope_ref, *refs):
    q_refs, k_refs, v_refs = refs[:8], refs[8:16], refs[16:24]
    out, stage, sems = refs[24:]
    slope = slope_ref[pl.program_id(1)]
    rows = Rows(inv_ref, stage, out, sems, 1)
    rows.open()
    for i in range(4):
        q, k, e, r = attn_scores(q_refs, k_refs, i, scale, slope)
        v = jnp.concatenate([x[...] for x in v_refs[: 2 * i + 2]], axis=0)
        o = dot_nn((e * r).astype(half), v)
        stage[rows.slot, 0, TILE * i : TILE * (i + 1), :] = o.astype(half)
    rows.close()


def attn_bwd_kernel(scale, inv_ref, slope_ref, *refs):
    q_refs, k_refs, v_refs, g_refs = refs[:8], refs[8:16], refs[16:24], refs[24:32]
    out, stage, sems, dk_acc, dv_acc = refs[32:]
    slope = slope_ref[pl.program_id(1)]
    rows = Rows(inv_ref, stage, out, sems, 3)
    rows.open()
    for i in (3, 2, 1, 0):
        q, k, e, r = attn_scores(q_refs, k_refs, i, scale, slope)
        n = TILE * (i + 1)
        v = jnp.concatenate([x[...] for x in v_refs[: 2 * i + 2]], axis=0)
        g = jnp.concatenate([g_refs[2 * i][...], g_refs[2 * i + 1][...]], axis=0)
        p = e * r
        dp = dot_nt(g, v)
        delta = jnp.sum(p * dp, axis=1, keepdims=True)
        ds = (p * (dp - delta)).astype(half)
        pb = p.astype(half)
        dq = (dot_nn(ds, k) * scale).astype(half)
        stage[rows.slot, 0, TILE * i : TILE * (i + 1), :] = dq
        dk = dot_tn(ds, q)
        dv = dot_tn(pb, g)
        if i == 3:
            dk_acc[...] = dk
            dv_acc[...] = dv
        else:
            dk_acc[:n, :] += dk
            dv_acc[:n, :] += dv
    stage[rows.slot, 1] = (dk_acc[...] * scale).astype(half)
    stage[rows.slot, 2] = dv_acc[...].astype(half)
    rows.close()


def block_specs(offset):
    def one(j):
        return pl.BlockSpec(
            (SPAN, 128), lambda s, h, inv, slope: (inv[s * SEQ_BLOCKS + j], offset + h)
        )

    return [one(j) for j in range(SEQ_BLOCKS)]


def attn_call(kernel, kinds, joined, extra, extra_specs, scratch, inv, slopes, heads, cost, name):
    rows = joined.shape[0]
    specs = block_specs(0) + block_specs(heads) + block_specs(2 * heads) + extra_specs
    return pl.pallas_call(
        kernel,
        grid_spec=pltpu.PrefetchScalarGridSpec(
            num_scalar_prefetch=2,
            grid=(2, heads),
            in_specs=specs,
            out_specs=pl.BlockSpec(memory_space=pl.ANY),
            scratch_shapes=[
                pltpu.VMEM((2, kinds, rows // 2, 128), half),
                pltpu.SemaphoreType.DMA((2, kinds * SEQ_BLOCKS)),
            ]
            + scratch,
        ),
        out_shape=jax.ShapeDtypeStruct((rows, kinds * heads * 128), half),
        compiler_params=pltpu.CompilerParams(vmem_limit_bytes=48 * 1024 * 1024),
        cost_estimate=cost,
        name=name,
    )(inv, slopes, *([joined] * 24), *extra)


def attn_forward(joined, inv, slopes, heads, scale):
    kernel = functools.partial(attn_fwd_kernel, scale)
    cost = hint(20 * 10**9, joined.shape[0] * heads * 128 * 8)
    return attn_call(
        kernel, 1, joined, [], [], [], inv, slopes, heads, cost, "attn_forward"
    )


def attn_backward(joined, grad, inv, slopes, heads, scale):
    kernel = functools.partial(attn_bwd_kernel, scale)
    cost = hint(40 * 10**9, joined.shape[0] * heads * 128 * 14)
    sums = [pltpu.VMEM((joined.shape[0] // 2, 128), single)] * 2
    return attn_call(
        kernel,
        3,
        joined,
        [grad] * 8,
        block_specs(0),
        sums,
        inv,
        slopes,
        heads,
        cost,
        "attn_backward",
    )


HINT = 0.001


def block_of(x):
    return x if isinstance(x, tuple) else (x, x.shape[0], 0)


def hint(flops, bytes_accessed):
    return pl.CostEstimate(
        flops=int(HINT * flops), bytes_accessed=int(HINT * bytes_accessed), transcendentals=0
    )


def rows_kernel(dot, epilogue, count, extra, *refs):
    left, w_ref = refs[:count], refs[count]
    extras = refs[count + 1 : count + 1 + extra]
    outs = refs[count + 1 + extra :]
    for i in range(count):
        epilogue(i, dot(left[i][...], w_ref[...]), extras, outs)


def rows_matmul(blocks, w, transposed, extras, outs, epilogue, name, tile=512):
    blocks = [block_of(x) for x in blocks]
    extras = [block_of(x) for x in extras]
    n = w.shape[0] if transposed else w.shape[1]
    k = w.shape[1] if transposed else w.shape[0]
    t = math.gcd(n, tile)
    w_spec = (
        pl.BlockSpec((t, k), lambda i: (i, 0)) if transposed else pl.BlockSpec((k, t), lambda i: (0, i))
    )
    rows = sum(x[1] for x in blocks)
    return pl.pallas_call(
        functools.partial(
            rows_kernel, dot_nt if transposed else dot_nn, epilogue, len(blocks), len(extras)
        ),
        grid=(n // t,),
        in_specs=[pl.BlockSpec((x[1], k), lambda i, at=x[2]: (at, 0)) for x in blocks]
        + [w_spec]
        + [pl.BlockSpec((x[1], t), lambda i, at=x[2]: (at, i)) for x in extras],
        out_specs=[pl.BlockSpec((r, t), lambda i: (0, i)) for r, _ in outs],
        out_shape=[jax.ShapeDtypeStruct((r, n), d) for r, d in outs],
        compiler_params=pltpu.CompilerParams(vmem_limit_bytes=52 * 1024 * 1024),
        cost_estimate=hint(2 * rows * n * k, 2 * n * k + 4 * rows * (n + k)),
        name=name,
    )(*[x[0] for x in blocks], w, *[x[0] for x in extras])


def plain(blocks, w, transposed, dtype, name):
    def epilogue(i, x, extras, outs):
        outs[i][...] = x.astype(dtype)

    outs = [(block_of(x)[1], dtype) for x in blocks]
    return rows_matmul(blocks, w, transposed, [], outs, epilogue, name)


def joined_rows(blocks, w, bias, name):
    sizes = [block_of(x)[1] for x in blocks]

    def epilogue(i, x, extras, outs):
        at = sum(sizes[:i])
        outs[0][at : at + sizes[i], :] = (x + extras[0][...]).astype(half)

    bias = bias.reshape(1, -1)
    return rows_matmul(blocks, w, False, [bias], [(sum(sizes), half)], epilogue, name)[0]


def up_gelu(blocks, w, bias, name):
    count = len(blocks)

    def epilogue(i, x, extras, outs):
        value, slope = gelu_both(x + extras[0][...])
        outs[i][...] = value.astype(half)
        outs[count + i][...] = slope.astype(half)

    outs = [(block_of(x)[1], half) for x in blocks] * 2
    out = rows_matmul(blocks, w, False, [bias.reshape(1, -1)], outs, epilogue, name)
    return out[:count], out[count:]


def hidden_back(blocks, w, slopes, name):
    def epilogue(i, x, extras, outs):
        x = x.astype(half).astype(single) * extras[i][...].astype(single)
        outs[i][...] = x.astype(half)

    outs = [(block_of(x)[1], half) for x in blocks]
    return rows_matmul(blocks, w, True, slopes, outs, epilogue, name)


def outer_kernel(count, *refs):
    out = refs[-1]
    total = None
    for i in range(count):
        x = dot_tn(refs[i][...], refs[count + i][...])
        total = x if total is None else total + x
    out[...] = total.astype(half)


def outer(left, right, name):
    left = [block_of(x) for x in left]
    right = [block_of(x) for x in right]
    m, n = left[0][0].shape[1], right[0][0].shape[1]
    tm = math.gcd(m, 1024)
    tn = n // 2 if n % 256 == 0 and n > 1024 else n
    rows = sum(x[1] for x in left)
    return pl.pallas_call(
        functools.partial(outer_kernel, len(left)),
        grid=(m // tm, n // tn),
        in_specs=[pl.BlockSpec((x[1], tm), lambda i, j, at=x[2]: (at, i)) for x in left]
        + [pl.BlockSpec((x[1], tn), lambda i, j, at=x[2]: (at, j)) for x in right],
        out_specs=pl.BlockSpec((tm, tn), lambda i, j: (i, j)),
        out_shape=jax.ShapeDtypeStruct((m, n), half),
        compiler_params=pltpu.CompilerParams(vmem_limit_bytes=52 * 1024 * 1024),
        cost_estimate=hint(2 * rows * m * n, 2 * rows * (m + n) + 2 * m * n),
        name=name,
    )(*[x[0] for x in left], *[x[0] for x in right])


def partner(mask):
    c = lax.axis_index("ctx")
    if mask == 1:
        return c + 1 - 2 * lax.rem(c, 2)
    return lax.rem(c + 2, 4) if mask == 2 else 3 - c


def greet(masks):
    barrier = pltpu.get_barrier_semaphore()
    for mask in masks:
        pl.semaphore_signal(
            barrier,
            inc=1,
            device_id={"ctx": partner(mask)},
            device_id_type=pl.DeviceIdType.MESH,
        )
    pl.semaphore_wait(barrier, len(masks))


class Moves:
    def __init__(self, send_sem, recv_sem):
        self.send_sem, self.recv_sem, self.used = send_sem, recv_sem, 0

    def start(self, src, dst, mask):
        copy = pltpu.make_async_remote_copy(
            src_ref=src,
            dst_ref=dst,
            send_sem=self.send_sem.at[self.used],
            recv_sem=self.recv_sem.at[self.used],
            device_id={"ctx": partner(mask)},
            device_id_type=pl.DeviceIdType.MESH,
        )
        self.used += 1
        copy.start()
        return copy


def multiply(lefts, w, transposed, extras, outs, epilogue, tile=512):
    k = lefts[0].shape[1]
    n = w.shape[0] if transposed else w.shape[1]
    t = math.gcd(n, tile)
    w_spec = (
        pl.BlockSpec((t, k), lambda i: (i, 0)) if transposed else pl.BlockSpec((k, t), lambda i: (0, i))
    )
    dot = dot_nt if transposed else dot_nn

    def body(*refs):
        rows_kernel(dot, epilogue, len(lefts), len(extras), *refs)

    pltpu.emit_pipeline(
        body,
        grid=(n // t,),
        in_specs=[pl.BlockSpec((x.shape[0], k), lambda i: (0, 0)) for x in lefts]
        + [w_spec]
        + [pl.BlockSpec((x.shape[0], t), lambda i: (0, i)) for x in extras],
        out_specs=[pl.BlockSpec((x.shape[0], t), lambda i: (0, i)) for x in outs],
    )(*lefts, w, *extras, *outs)


def store(i, x, extras, outs):
    outs[i][...] = x.astype(outs[i].dtype)


def store_sum(i, x, extras, outs):
    outs[i][...] = (x + extras[i][...].astype(single)).astype(outs[i].dtype)


def store_passed(i, x, extras, outs):
    if i in (1, 2):
        x = x + extras[i - 1][...].astype(single)
    outs[i][...] = x.astype(outs[i].dtype)


def store_hidden(i, x, extras, outs):
    outs[i][...] = (x.astype(half).astype(single) * extras[i][...].astype(single)).astype(half)


def outer_on(lefts, rights, out):
    m, n = out.shape
    tm = math.gcd(m, 1024)
    tn = n // 2 if n % 256 == 0 and n > 1024 else n

    def body(*refs):
        outer_kernel(len(lefts), *refs)

    pltpu.emit_pipeline(
        body,
        grid=(m // tm, n // tn),
        in_specs=[pl.BlockSpec((x.shape[0], tm), lambda i, j: (0, i)) for x in lefts]
        + [pl.BlockSpec((x.shape[0], tn), lambda i, j: (0, j)) for x in rights],
        out_specs=[pl.BlockSpec((tm, tn), lambda i, j: (i, j))],
    )(*lefts, *rights, out)


def halves(ref):
    n = ref.shape[0] // 2
    return ref.at[pl.ds(0, n)], ref.at[pl.ds(n, n)]


def moving_call(kernel, operands, outs, moves, call, flops, name):
    anywhere = pl.BlockSpec(memory_space=pl.ANY)
    sems = pltpu.SemaphoreType.DMA((moves,))
    return pl.pallas_call(
        kernel,
        in_specs=[anywhere] * len(operands),
        out_specs=[anywhere] * len(outs),
        out_shape=[jax.ShapeDtypeStruct(shape, dtype) for shape, dtype in outs],
        scratch_shapes=[sems, sems],
        compiler_params=pltpu.CompilerParams(
            collective_id=call, has_side_effects=True, vmem_limit_bytes=52 * 1024 * 1024
        ),
        cost_estimate=hint(flops, 0),
        name=name,
    )(*operands)


def store_biased(i, x, extras, outs):
    outs[i][...] = (x + extras[0][...]).astype(half)


def qkv_kernel(*refs):
    tok, gain, shift, a1, w_qkv, bias = refs[0:2], refs[2], refs[3], refs[4:7], refs[7], refs[8]
    dz_lo, dz_hi = refs[9:11]
    joined, far, one_lo, two_hi = refs[11], refs[12:14], refs[14], refs[15]
    moves = Moves(*refs[16:18])
    n, width = tok[0].shape
    greet((1, 2))
    copies = [moves.start(dz_lo, one_lo, 1), moves.start(dz_hi, two_hi, 2)]

    def norm(x_lo, x_hi, g, s, o_lo, o_hi):
        for x, o in ((x_lo, o_lo), (x_hi, o_hi)):
            normed, _ = norm_parts(x[...].astype(single))
            o[...] = (normed * g[...] + s[...]).astype(half)

    t = math.gcd(n, 64)
    block = pl.BlockSpec((t, width), lambda i: (i, 0))
    row = pl.BlockSpec((1, width), lambda i: (0, 0))
    pltpu.emit_pipeline(
        norm, grid=(n // t,), in_specs=[block, block, row, row], out_specs=[block, block]
    )(*tok, gain, shift, *far)
    lefts, outs, at = [*a1, *far], [], 0
    for x in lefts:
        outs.append(joined.at[pl.ds(at, x.shape[0])])
        at += x.shape[0]
    multiply(lefts, w_qkv, False, [bias], outs, store_biased)
    for copy in copies:
        copy.wait()


def qkv_forward(tok, gain, shift, a1, w_qkv, bias, dz_lo, dz_hi):
    n, width = tok[0].shape
    k = w_qkv.shape[1]
    outs = [((8 * n, k), half)] + [((n, width), half)] * 4
    out = moving_call(
        qkv_kernel,
        [*tok, gain.reshape(1, -1), shift.reshape(1, -1), *a1, w_qkv, bias.reshape(1, -1), dz_lo, dz_hi],
        outs,
        2,
        7,
        16 * n * width * k,
        "qkv",
    )
    return out[0], out[1:3], out[3:5]


def feed_pass(dz, slope, w_down, w_up, du, total):
    n, width = dz[0].shape
    wide = w_down.shape[0]
    t = math.gcd(wide, 512)
    total[...] = jnp.zeros_like(total)

    def body(dz_lo, dz_hi, down, up, slope_lo, slope_hi, du_lo, du_hi):
        for i, x, s, d in ((0, dz_lo, slope_lo, du_lo), (1, dz_hi, slope_hi, du_hi)):
            grad = dot_nt(x[...], down[...]).astype(half).astype(single)
            grad = (grad * s[...].astype(single)).astype(half)
            d[...] = grad
            total[i * n : (i + 1) * n, :] += dot_nt(grad, up[...])

    pltpu.emit_pipeline(
        body,
        grid=(wide // t,),
        in_specs=[pl.BlockSpec((n, width), lambda i: (0, 0))] * 2
        + [pl.BlockSpec((t, width), lambda i: (i, 0)), pl.BlockSpec((width, t), lambda i: (0, i))]
        + [pl.BlockSpec((n, t), lambda i: (0, i))] * 2,
        out_specs=[pl.BlockSpec((n, t), lambda i: (0, i))] * 2,
    )(*dz, w_down, w_up, *slope, *du)


def feed_back_kernel(*refs):
    dz, slope, (w_down, w_up) = refs[0:8], refs[8:13], refs[13:15]
    a2, gb_far = refs[15:20], refs[20:22]
    du, own, land1, land2, up_grad, mix_x, mix_y = refs[22:27], *refs[27:33]
    total, far, near, rest, from_x, from_y, mixed = refs[33:40]
    moves = Moves(*refs[40:42])
    local = refs[42]
    n = from_x.shape[0]
    lo, hi = pl.ds(0, n), pl.ds(n, n)
    (s1_lo, s1_hi), (s2_lo, s2_hi) = halves(slope[1]), halves(slope[2])
    (d1_lo, d1_hi), (d2_lo, d2_hi) = halves(du[1]), halves(du[2])
    (land1_lo, land1_hi), (land2_lo, land2_hi) = halves(land1), halves(land2)
    greet((1, 2))
    wide, width = w_down.shape
    t = math.gcd(width, 512)

    def mix(x_lo, x_hi, w):
        at = pl.ds(pl.multiple_of(pl.program_id(0) * t, t), t)
        mixed[0:n, at] = dot_nn(x_lo[...], w[...]).astype(half)
        mixed[n : 2 * n, at] = dot_nn(x_hi[...], w[...]).astype(half)

    pltpu.emit_pipeline(
        mix,
        grid=(width // t,),
        in_specs=[pl.BlockSpec((n, wide), lambda i: (0, 0))] * 2
        + [pl.BlockSpec((wide, t), lambda i: (0, i))],
    )(*gb_far, w_down)
    second = [moves.start(mixed.at[lo], mix_x, 1), moves.start(mixed.at[hi], mix_y, 2)]
    feed_pass(dz[6:8], slope[3:5], w_down, w_up, du[3:5], total)
    far[...] = total[...].astype(half)
    first = [moves.start(far.at[lo], from_x, 1), moves.start(far.at[hi], from_y, 2)]
    feed_pass([dz[2], dz[5]], [s1_lo, s2_hi], w_down, w_up, [d1_lo, d2_hi], total)
    near[...] = total[...].astype(half)
    second += [moves.start(near.at[lo], land1_lo, 1), moves.start(near.at[hi], land2_hi, 2)]
    feed_pass([dz[3], dz[4]], [s1_hi, s2_lo], w_down, w_up, [d1_hi, d2_lo], total)
    for copy in first:
        copy.wait()
    rest[lo] = (total[lo] + from_y[...].astype(single)).astype(half)
    rest[hi] = (total[hi] + from_x[...].astype(single)).astype(half)
    second += [moves.start(rest.at[lo], land1_hi, 1), moves.start(rest.at[hi], land2_lo, 2)]
    feed_pass(dz[0:2], halves(slope[0]), w_down, w_up, halves(du[0]), total)
    store_own = pltpu.make_async_copy(total, own, local)
    store_own.start()
    outer_on(a2, du, up_grad)
    store_own.wait()
    for copy in second:
        copy.wait()


def feed_back(dz, slope, w_down, w_up, a2, gb_far):
    n, width = dz[0].shape
    rows, wide = 2 * n, w_down.shape[0]
    anywhere = pl.BlockSpec(memory_space=pl.ANY)
    outs = [((r, wide), half) for r in (rows, rows, rows, n, n)]
    outs += [((rows, width), single)] + [((rows, width), half)] * 2
    outs += [((width, wide), half)] + [((n, width), half)] * 2
    sems = pltpu.SemaphoreType.DMA((8,))
    out = pl.pallas_call(
        feed_back_kernel,
        in_specs=[anywhere] * 22,
        out_specs=[anywhere] * len(outs),
        out_shape=[jax.ShapeDtypeStruct(shape, dtype) for shape, dtype in outs],
        scratch_shapes=[pltpu.VMEM((rows, width), single)]
        + [pltpu.VMEM((rows, width), half)] * 3
        + [pltpu.VMEM((n, width), half)] * 2
        + [pltpu.VMEM((rows, width), half)]
        + [sems, sems, pltpu.SemaphoreType.DMA],
        compiler_params=pltpu.CompilerParams(
            collective_id=3, has_side_effects=True, vmem_limit_bytes=56 * 1024 * 1024
        ),
        cost_estimate=hint(26 * rows * width * wide, 0),
        name="feed_back",
    )(*dz, *slope, w_down, w_up, *a2, *gb_far)
    return out[0:5], out[5:8], out[8], out[9:11]


def heads_back_kernel(part, *refs):
    own, land1, land2, cot, y1, gain, w_out = refs[0:7]
    ob, gb1, gb2, w_down, mix_x, mix_y, down = refs[7:14]
    dy1, dz1, sums, got, out_grad = refs[14:19]
    mix, down1, down2 = refs[19:23], refs[23], refs[24]
    dz, w, stage = refs[25:28]
    moves = Moves(*refs[28:30])
    local = refs[30]
    rows, width = own.shape
    greet((1, 2, 3))
    load = pltpu.make_async_copy(w_out, w, local.at[0])
    load.start()
    copies = [moves.start(down, down1, 1), moves.start(down, down2, 2)]
    t = math.gcd(rows, 64)

    def norm(own, one, two, cot, y1, gain, dy1, dz1, sums):
        step = pl.program_id(0)
        grad = own[...] + one[...].astype(single) + two[...].astype(single)
        normed, inv = norm_parts(y1[...])
        dy = cot[...] + norm_back(normed, inv, gain[...], grad)
        low = dy.astype(half)
        dy1[...] = dy
        dz1[...] = low
        dz[pl.ds(pl.multiple_of(step * t, t), t), :] = low

        @pl.when(step == 0)
        def _():
            sums[...] = jnp.zeros_like(sums)

        sums[0:1] += jnp.sum(grad * normed, axis=0, keepdims=True)
        sums[1:2] += jnp.sum(grad, axis=0, keepdims=True)
        sums[2:3] += jnp.sum(low.astype(single), axis=0, keepdims=True)

    block = pl.BlockSpec((t, width), lambda i: (i, 0))
    pltpu.emit_pipeline(
        norm,
        grid=(rows // t,),
        in_specs=[block] * 5 + [pl.BlockSpec((1, width), lambda i: (0, 0))],
        out_specs=[block] * 2 + [pl.BlockSpec((8, width), lambda i: (0, 0))],
    )(own, land1, land2, cot, y1, gain, dy1, dz1, sums)
    load.wait()
    for mask in (3, 1, 2, 0):
        of = partner(mask) if mask else lax.axis_index("ctx")
        heads = w[pl.ds(pl.multiple_of(of * part, part), part), :]
        stage[mask] = dot_nt(dz[...], heads).astype(half)
        at = got.at[pl.ds(mask * rows, rows)]
        if mask:
            copies.append(moves.start(stage.at[mask], at, mask))
        else:
            keep = pltpu.make_async_copy(stage.at[0], at, local.at[1])
            keep.start()
    outer_on([ob], [dz1], out_grad)
    multiply(
        [*halves(gb1), *halves(gb2)],
        w_down,
        False,
        [mix_y, mix_x],
        mix,
        store_passed,
    )
    keep.wait()
    for copy in copies:
        copy.wait()


def heads_back(terms, cot, y1, gain, w_out, ob, gb1, gb2, w_down, mix_first, down):
    rows, width = cot.shape
    part = width // 4
    anywhere = pl.BlockSpec(memory_space=pl.ANY)
    sems = pltpu.SemaphoreType.DMA((5,))
    outs = [((rows, width), single), ((rows, width), half), ((8, width), single)]
    outs += [((4 * rows, part), half), ((width, width), half)]
    outs += [((rows // 2, width), half)] * 4 + [(down.shape, half)] * 2
    out = pl.pallas_call(
        functools.partial(heads_back_kernel, part),
        in_specs=[anywhere] * 14,
        out_specs=[anywhere] * len(outs),
        out_shape=[jax.ShapeDtypeStruct(shape, dtype) for shape, dtype in outs],
        scratch_shapes=[
            pltpu.VMEM((rows, width), half),
            pltpu.VMEM((width, width), half),
            pltpu.VMEM((4, rows, part), half),
            sems,
            sems,
            pltpu.SemaphoreType.DMA((2,)),
        ],
        compiler_params=pltpu.CompilerParams(
            collective_id=4, has_side_effects=True, vmem_limit_bytes=56 * 1024 * 1024
        ),
        cost_estimate=hint(10 * rows * width * width, 0),
        name="heads_back",
    )(*terms, cot, y1, gain.reshape(1, -1), w_out, ob, gb1, gb2, w_down, *mix_first, down)
    return out[0], out[2], out[3], out[4], out[5:9], out[9:11]


def qkv_back_kernel(*refs):
    dqkv, w_qkv = refs[0:2]
    a1, gb_own, w_down, one_hi, two_hi, down1, down2 = refs[2:7], *refs[7:13]
    own, p3, p1, p2, from_x, from_y, land1, land2, qkv_grad, mix_own = refs[13:23]
    x_hi, y_hi, down_lo, down_hi = refs[23:27]
    moves = Moves(*refs[27:29])
    rows = own.shape[0]
    n = rows // 2

    def block(k):
        return dqkv.at[pl.ds(k * n, n)]

    greet((1, 2))
    output = [moves.start(one_hi, x_hi, 1), moves.start(two_hi, y_hi, 2)]
    (p3_lo, p3_hi), (p1_lo, p1_hi), (p2_lo, p2_hi) = halves(p3), halves(p1), halves(p2)
    (land1_lo, land1_hi), (land2_lo, land2_hi) = halves(land1), halves(land2)
    multiply([block(6), block(7)], w_qkv, True, [], [p3_lo, p3_hi], store)
    first = [moves.start(p3_lo, from_x, 1), moves.start(p3_hi, from_y, 2)]
    multiply([block(2), block(5)], w_qkv, True, [], [p1_lo, p2_hi], store)
    second = [moves.start(p1_lo, land1_lo, 1), moves.start(p2_hi, land2_hi, 2)]
    multiply([dqkv.at[pl.ds(0, rows)]], w_qkv, True, [], [own], store)
    multiply([gb_own], w_down, False, [], [mix_own], store)
    for copy in first:
        copy.wait()
    multiply([block(3), block(4)], w_qkv, True, [from_y, from_x], [p1_hi, p2_lo], store_sum)
    second += [moves.start(p1_hi, land1_hi, 1), moves.start(p2_lo, land2_lo, 2)]
    second += [moves.start(halves(down1)[0], down_lo, 2)]
    second += [moves.start(halves(down2)[1], down_hi, 1)]
    rights, at = [], 0
    for x in a1:
        rights.append(dqkv.at[pl.ds(at, x.shape[0])])
        at += x.shape[0]
    outer_on(a1, rights, qkv_grad)
    for copy in output + second:
        copy.wait()


def qkv_back(dqkv, w_qkv, a1, gb_own, w_down, one_hi, two_hi, down_near):
    rows, width = a1[0].shape
    wide = gb_own.shape[1]
    n = rows // 2
    outs = [((rows, width), single)] + [((rows, width), half)] * 3
    outs += [((n, width), half)] * 2 + [((rows, width), half)] * 2
    outs += [((width, dqkv.shape[1]), half), ((rows, width), single)] + [((n, width), half)] * 2
    outs += [((down_near[0].shape[0] // 2, width), half)] * 2
    out = moving_call(
        qkv_back_kernel,
        [dqkv, w_qkv, *a1, gb_own, w_down, one_hi, two_hi, *down_near],
        outs,
        10,
        5,
        16 * rows * width * dqkv.shape[1] + 2 * rows * width * wide,
        "qkv_back",
    )
    return out[0], out[6:8], out[8], out[9], out[10:12], out[12:14]


def lay_out_kernel(axis, layout, c_ref, *refs):
    out = refs[-1]
    for (j, row), ref in zip(layout, refs):
        x = ref[...].astype(single)
        r, w = x.shape
        if axis == 0:
            n = sum(ref.shape[0] for (k, _), ref in zip(layout, refs) if k == j)
            out[pl.ds(pl.multiple_of((c_ref[0] ^ j) * n + row, r), r), :] = x
        else:
            out[row : row + r, pl.ds(pl.multiple_of((c_ref[0] ^ j) * w, w), w)] = x


def lay_out(axis, pieces, c, groups):
    count = len(pieces)
    r = sum(x.shape[0] for x in pieces[0])
    n = pieces[0][0].shape[1]
    w = n // groups
    if w % 128:
        whole = xor_order([jnp.concatenate(p, axis=0).astype(single) for p in pieces], c)
        whole = jnp.stack([p.reshape(r, groups, w) for p in whole], axis=2)
        return whole.reshape(r, count * n)
    layout, blocks = [], []
    for j, p in enumerate(pieces):
        row = 0
        for x in p:
            layout.append((j, row))
            blocks.append(x)
            row += x.shape[0]
    out = (count * r, w) if axis == 0 else (r, count * w)
    return pl.pallas_call(
        functools.partial(lay_out_kernel, axis, layout),
        grid_spec=pltpu.PrefetchScalarGridSpec(
            num_scalar_prefetch=1,
            grid=(groups,),
            in_specs=[pl.BlockSpec((x.shape[0], w), lambda k, c: (0, k)) for x in blocks],
            out_specs=pl.BlockSpec(out, lambda k, c: (0, k)),
        ),
        out_shape=jax.ShapeDtypeStruct((out[0], out[1] * groups), single),
        compiler_params=pltpu.CompilerParams(vmem_limit_bytes=48 * 1024 * 1024),
        cost_estimate=hint(0, 6 * r * n * count),
        name="lay_out",
    )(c.reshape(1), *blocks)


def gather_small_kernel(nf, x_ref, o_ref, send_sem, recv_sem):
    f = lax.axis_index("fsdp")
    barrier = pltpu.get_barrier_semaphore()
    for d in range(1, nf):
        pl.semaphore_signal(
            barrier,
            inc=1,
            device_id={"fsdp": lax.rem(f + d, nf)},
            device_id_type=pl.DeviceIdType.MESH,
        )
    pl.semaphore_wait(barrier, nf - 1)
    copies = []
    for d in range(1, nf):
        copies.append(
            pltpu.make_async_remote_copy(
                src_ref=x_ref,
                dst_ref=o_ref.at[f],
                send_sem=send_sem.at[d],
                recv_sem=recv_sem.at[d],
                device_id={"fsdp": lax.rem(f + d, nf)},
                device_id_type=pl.DeviceIdType.MESH,
            )
        )
        copies[-1].start()
    o_ref[f] = x_ref[...]
    for copy in copies:
        copy.wait()


def gather_small(x, nf):
    return pl.pallas_call(
        functools.partial(gather_small_kernel, nf),
        out_shape=jax.ShapeDtypeStruct((nf,) + x.shape, single),
        in_specs=[pl.BlockSpec(memory_space=pltpu.VMEM)],
        out_specs=pl.BlockSpec(memory_space=pltpu.VMEM),
        scratch_shapes=[pltpu.SemaphoreType.DMA((nf,)), pltpu.SemaphoreType.DMA((nf,))],
        compiler_params=pltpu.CompilerParams(collective_id=1, has_side_effects=True),
        name="gather_small",
    )(x)


def reduce_small_kernel(nf, nc, x_ref, o_ref, land, stage, send_sem, recv_sem):
    f = lax.axis_index("fsdp")
    c = lax.axis_index("ctx")
    barrier = pltpu.get_barrier_semaphore()
    for d in range(1, nf):
        pl.semaphore_signal(
            barrier,
            inc=1,
            device_id={"fsdp": lax.rem(f + d, nf)},
            device_id_type=pl.DeviceIdType.MESH,
        )
    for d in range(1, nc):
        pl.semaphore_signal(
            barrier,
            inc=1,
            device_id={"ctx": lax.rem(c + d, nc)},
            device_id_type=pl.DeviceIdType.MESH,
        )
    pl.semaphore_wait(barrier, nf + nc - 2)
    copies = []
    for d in range(1, nf):
        to = lax.rem(f + d, nf)
        copies.append(
            pltpu.make_async_remote_copy(
                src_ref=x_ref.at[to],
                dst_ref=land.at[d],
                send_sem=send_sem.at[d],
                recv_sem=recv_sem.at[d],
                device_id={"fsdp": to},
                device_id_type=pl.DeviceIdType.MESH,
            )
        )
        copies[-1].start()
    total = x_ref[f]
    for d in range(1, nf):
        copies[d - 1].wait()
        total = total + land[d]
    stage[0] = total
    copies = []
    for d in range(1, nc):
        copies.append(
            pltpu.make_async_remote_copy(
                src_ref=stage.at[0],
                dst_ref=stage.at[d],
                send_sem=send_sem.at[nf + d],
                recv_sem=recv_sem.at[nf + d],
                device_id={"ctx": lax.rem(c + d, nc)},
                device_id_type=pl.DeviceIdType.MESH,
            )
        )
        copies[-1].start()
    for d in range(1, nc):
        copies[d - 1].wait()
        total = total + stage[d]
    o_ref[...] = total


def reduce_small(x, nf, nc, call):
    block = x.shape[1:]
    sems = pltpu.SemaphoreType.DMA((nf + nc,))
    return pl.pallas_call(
        functools.partial(reduce_small_kernel, nf, nc),
        out_shape=jax.ShapeDtypeStruct(block, single),
        in_specs=[pl.BlockSpec(memory_space=pltpu.VMEM)],
        out_specs=pl.BlockSpec(memory_space=pltpu.VMEM),
        scratch_shapes=[
            pltpu.VMEM((nf,) + block, single),
            pltpu.VMEM((nc,) + block, single),
            sems,
            sems,
        ],
        compiler_params=pltpu.CompilerParams(collective_id=call, has_side_effects=True),
        name="reduce_small",
    )(x)


def per_device(
    tokens,
    cotangent,
    lengths,
    span_place,
    ln1_gain,
    ln1_shift,
    qkv_weight,
    q_bias,
    v_bias,
    out_weight,
    out_bias,
    ln2_gain,
    ln2_shift,
    up_weight,
    up_bias,
    down_weight,
    down_bias,
):
    rows, width = tokens.shape
    CTX = lax.axis_size("ctx")
    c = lax.axis_index("ctx")
    f = lax.axis_index("fsdp")
    nf = lax.axis_size("fsdp")
    wide = up_weight.shape[1]
    part = width // CTX
    heads = HEADS // CTX
    scale = 1.0 / math.sqrt(width // HEADS)
    shard = width // nf
    fpart = wide // nf // CTX
    wpart = wide // CTX

    def columns(x, width_each, stride, count):
        return jnp.concatenate(
            [
                lax.dynamic_slice_in_dim(x, k * stride + c * width_each, width_each, axis=1)
                for k in range(count)
            ],
            axis=1,
        )

    def after(x, *others):
        return lax.optimization_barrier((x, others))[0]

    def pick(x, axis):
        return lax.dynamic_index_in_dim(x, c, axis, keepdims=False)

    def gather_f(x):
        return lax.all_gather(x, "fsdp", axis=0, tiled=True)

    qkv_own = columns(qkv_weight, part, width, 3)
    up_own = columns(up_weight, fpart, wide // nf, nf)
    down_own = lax.dynamic_slice_in_dim(down_weight, c * fpart, fpart, axis=0)
    w_qkv = gather_f(qkv_own.astype(half))
    up_own, down_own = up_own.astype(half), down_own.astype(half)
    small = jnp.concatenate(
        [ln1_gain, ln1_shift, q_bias, v_bias, out_bias, ln2_gain, ln2_shift, down_bias, up_bias]
    )
    small_len = small.shape[0]
    small = jnp.pad(small, (0, -small_len % 1024)).reshape(-1, 128)
    small_all = gather_small(small, nf).reshape(nf, -1)[:, :small_len]
    small_all = small_all.astype(half).astype(single)

    def vector(k):
        return small_all[:, k * shard : (k + 1) * shard].reshape(width)

    gain1, shift1, bias_q, bias_v, bias_o, gain2, shift2, bias_d = [vector(k) for k in range(8)]
    bias_u = pick(small_all[:, 8 * shard :].reshape(nf, CTX, fpart), 1).reshape(wpart)
    bias_qkv = jnp.concatenate(
        [pick(bias_q.reshape(CTX, part), 0), jnp.zeros((part,), single), pick(bias_v.reshape(CTX, part), 0)]
    )
    w_out = gather_f(out_weight.astype(half))

    per = rows // SPAN
    table = jnp.arange(CTX * per, dtype=jnp.int32)
    source = ((table // per) ^ c) * per + table % per
    place = jnp.sum(jnp.where(source[:, None] == table[None, :], span_place[0][None, :], 0), axis=1)
    inv = jnp.sum(jnp.where(place[None, :] == table[:, None], table[None, :], 0), axis=1)
    slopes = 2.0 ** (-8.0 * ((c * heads + jnp.arange(heads)).astype(single) + 1.0) / HEADS)

    def flat(pieces):
        return [x for p in pieces for x in p]

    def scatter_f(x):
        return lax.psum_scatter(x, "fsdp", scatter_dimension=0, tiled=True)

    far = CTX - 1
    mid = list(range(1, far))

    def first_norm(x):
        normed, _ = norm_parts(x.astype(single))
        return (normed * gain1 + shift1).astype(half)

    n = rows // 2
    dz2_lo, dz2_hi = cotangent[:n].astype(half), cotangent[n:].astype(half)
    early = (small_all, place, inv, slopes, up_own, down_own, dz2_lo, dz2_hi)
    early, tok_near = after((early, gather_first(tokens)))
    small_all, place, inv, slopes, up_own, down_own, dz2_lo, dz2_hi = early
    tok = gather_second(tokens, tok_near)
    near = [[first_norm(x) for x in p] for p in tok[:far]]
    tok = after(tok, near)
    if CTX != 4:
        dz2_own = jnp.concatenate([dz2_lo, dz2_hi], axis=0)
        dz2_rest = gather_first(dz2_own)
    w_up = gather_f(after(up_own, tok))
    a1 = flat(near)
    if CTX == 4:
        joined, a1_far, dz2_first = qkv_forward(
            tok[far], gain1, shift1, a1, w_qkv, bias_qkv, dz2_lo, dz2_hi
        )
        a1 = a1 + list(a1_far)
        dz2_rest = after((dz2_hi, dz2_lo), joined)
        dz2_rest = [swap(dz2_rest[0], 1), swap(dz2_rest[1], 2)]
    else:
        a1 = a1 + [first_norm(x) for x in tok[far]]
        joined = joined_rows(a1, w_qkv, bias_qkv, "qkv")
    w_down = gather_f(after(down_own, joined))
    attended = attn_forward(joined, inv, slopes, heads, scale)
    mine = [attended[j * rows : (j + 1) * rows] for j in range(CTX)]
    mine = after(mine, dz2_rest)
    mine = [mine[0]] + [swap(mine[j], j) for j in range(1, CTX)]
    ob = jnp.concatenate(xor_order(mine, c), axis=1)
    y1 = tokens.astype(single) + dot_nn(ob, w_out) + bias_o

    normed2, inv2 = norm_parts(y1)
    a2_own = (normed2 * gain2 + shift2).astype(half)
    gb, slope = [None] * CTX, [None] * CTX
    gb[0], slope[0] = up_gelu([a2_own], w_up, bias_u, "up_gelu_0")
    last = gb[0]
    a2_near = gather_first(a2_own)
    a2 = gather_second(a2_own, a2_near)
    if CTX == 4:
        one_lo, two_hi = after(dz2_first, a2_near)
        one_hi, two_lo = dz2_rest
        dz2 = [[dz2_lo, dz2_hi], [one_lo, one_hi], [two_lo, two_hi], [swap(one_lo, 2), swap(two_hi, 1)]]
    else:
        dz2 = [[dz2_own]] + [[x] for x in dz2_rest]
    for j in range(1, CTX):
        gb[j], slope[j] = up_gelu(after(a2[j], last), w_up, bias_u, f"up_gelu_{j}")
        last = gb[j]
    gb_blocks = flat(gb)
    if CTX == 4:
        gb_blocks = [(g[0], n, i) for g in gb[:far] for i in (0, 1)] + list(gb[far])
    down_grad = outer(gb_blocks, flat(dz2), "down_grad")
    down_part = scatter_f(down_grad)
    w_down = after(w_down, down_grad)

    du, dh2, mix = [None] * CTX, [None] * CTX, [None] * CTX
    if CTX == 4:
        du, dh2, up_grad, mix_first = feed_back(
            flat(dz2), flat(slope), w_down, w_up, flat(a2), gb[far]
        )
        du = [du]
    else:
        for j in range(CTX):
            du[j] = hidden_back(dz2[j], w_down, slope[j], f"du_{j}")
            dh2[j] = plain(du[j], w_up, True, half if j else single, f"dh2_{j}")[0]
        arrived = scatter_send(dh2[1:])
        dh2 = dh2[0]
        up_grad = outer(flat(a2), flat(du), "up_grad")
        mix[far] = plain(gb[far], w_down, False, half, "mix_far")[0]
        dh2 = total_of(dh2, arrived)
    up_part = scatter_f(up_grad)
    if CTX == 4:
        dy1, sums2, dattn, out_grad, mix, down_near = heads_back(
            dh2, cotangent, y1, gain2, w_out, ob, gb[1][0], gb[2][0], w_down, mix_first, down_part
        )
        one_lo, one_hi, two_lo, two_hi = mix
        gain2_grad, shift2_grad, out_bias_grad = sums2[0], sums2[1], sums2[2]
    else:
        gain2_grad = jnp.sum(dh2 * normed2, axis=0)
        shift2_grad = jnp.sum(dh2, axis=0)
        dy1 = cotangent + norm_back(normed2, inv2, gain2, dh2)
        dz1 = dy1.astype(half)
        dattn = dot_nt(dz1, w_out).astype(half)
        out_bias_grad = jnp.sum(dz1.astype(single), axis=0)
        dattn = xor_order([dattn[:, s * part : (s + 1) * part] for s in range(CTX)], c)
        dattn = [dattn[0]] + [swap(dattn[j], j) for j in range(1, CTX)]
        dattn = jnp.concatenate(dattn, axis=0)
        out_grad = outer([ob], [dz1], "out_grad")
        for j in mid:
            mix[j] = plain(gb[j], w_down, False, half, f"mix_{j}")[0]
        down_near = gather_first(down_part)
    out_part = scatter_f(out_grad)
    dqkv = attn_backward(joined, dattn, inv, slopes, heads, scale)
    if CTX == 4:
        lows = [swap(one_lo, 1), swap(two_lo, 2)]
        dqkv = after(dqkv, lows, up_part)
        dh1, arrived, qkv_grad, mix_own, highs, down_far = qkv_back(
            dqkv, w_qkv, a1, gb[0][0], w_down, one_hi, two_hi, down_near
        )
        down_out = [[down_part], [down_near[0]], [down_near[1]], down_far]
    else:
        dh1 = [
            plain([(dqkv, rows, j)], w_qkv, True, half if j else single, f"dh1_{j}")[0]
            for j in range(CTX)
        ]
        arrived = scatter_send(dh1[1:])
        dh1 = dh1[0]
        qkv_grad = outer(a1, [(dqkv, rows, j) for j in range(CTX)], "qkv_grad")
        mix_own = plain(gb[0], w_down, False, single, "mix_0")[0]
        down_out = gather_second(down_part, down_near)
    qkv_part = scatter_f(qkv_grad)

    up_own = after(up_part, arrived)
    up_near = gather_first(up_own)
    out_first = []
    if CTX == 4:
        k = out_part.shape[0] // 2
        out_lo, out_hi = after(out_part, arrived)[:k], after(out_part, arrived)[k:]
        out_first = [swap(out_lo, 1), swap(out_hi, 2)]
    waiting = (dh1, dqkv, mix_own, flat(du), flat(dz2[:1]), down_out)
    dh1, dqkv, mix_own, du, dz2_own, down_out = after(waiting, out_part)
    down_out = lay_out(0, down_out, c, width // min(width, 512))
    dh1 = total_of(dh1, arrived)
    if CTX == 4:
        mixed = y1 + bias_d + mix_own
        mixed = jnp.concatenate([total_of(mixed[:n], lows), total_of(mixed[n:], highs)])
    else:
        mixed = total_of(y1 + bias_d + mix_own, scatter_send(mix[1:]))
    up_bias_grad = sum(jnp.sum(x.astype(single), axis=0) for x in du)
    down_bias_grad = sum(jnp.sum(x.astype(single), axis=0) for x in dz2_own)
    sums = jnp.sum(dqkv.astype(single), axis=0)
    normed1_own, inv1_own = norm_parts(tokens.astype(single))
    gain1_grad = jnp.sum(dh1 * normed1_own, axis=0)
    shift1_grad = jnp.sum(dh1, axis=0)
    input_grad = dy1 + norm_back(normed1_own, inv1_own, gain1, dh1)

    done = (down_out, input_grad, mixed, sums, up_bias_grad, down_bias_grad, gain1_grad, shift1_grad)
    up_near, out_first = after((up_near, out_first), done)
    if CTX == 4:
        out_lo = (out_lo.astype(single) + out_first[0].astype(single)).astype(half)
        out_hi = (out_hi.astype(single) + out_first[1].astype(single)).astype(half)
        out_lo, out_hi, up_near = after((out_lo, out_hi, up_near))
        out_second = [(out_lo, swap(out_lo, 2)), (out_hi, swap(out_hi, 1))]
    up_out = gather_second(up_own, up_near)
    up_out = lay_out(1, up_out, c, nf)
    if CTX == 4:
        out_second = after(out_second, up_out)
        out_out = [x.astype(single) + y.astype(single) for x, y in out_second]
        out_out = jnp.concatenate(out_out, axis=0)
    else:
        bit = 1
        while bit < CTX:
            out_out = out_part.astype(single) + swap(out_part, bit).astype(single)
            out_part = out_out.astype(half)
            bit *= 2

    def spread(x, inner):
        x = x.reshape(-1, 1, inner)
        mask = (jnp.arange(CTX) == c)[None, :, None]
        return jnp.where(mask, x, 0.0).reshape(-1)

    def reduced(items, call):
        sizes = [x.shape[0] // nf for x in items]
        x = jnp.concatenate([x.reshape(nf, -1) for x in items], axis=1)
        x = jnp.pad(x, ((0, 0), (0, -x.shape[1] % 1024))).reshape(nf, -1, 128)
        x = reduce_small(x, nf, CTX, call).reshape(-1)
        out, at = [], 0
        for n in sizes:
            out.append(x[at : at + n])
            at += n
        return out

    sums_in = [out_bias_grad, gain2_grad, shift2_grad, down_bias_grad, spread(up_bias_grad, fpart)]
    sums_in += [gain1_grad, shift1_grad, spread(sums[:part], part), spread(sums[2 * part :], part)]
    qkv_part = after(qkv_part, out_out)
    qkv_near = gather_first(qkv_part)
    sums_in[5] = after(sums_in[5], qkv_part)
    sums_out = reduced(sums_in, 2)
    qkv_near = after(qkv_near, sums_out)
    qkv_out = lay_out(1, gather_second(qkv_part, qkv_near), c, 3)
    out_bias_out, gain2_out, shift2_out, down_bias_out, up_bias_out = sums_out[:5]
    gain1_out, shift1_out, q_bias_out, v_bias_out = sums_out[5:]
    return (
        mixed,
        input_grad,
        gain1_out,
        shift1_out,
        qkv_out,
        q_bias_out,
        v_bias_out,
        out_out,
        out_bias_out,
        gain2_out,
        shift2_out,
        up_out,
        up_bias_out,
        down_out,
        down_bias_out,
    )


def solution(mesh):
    rows, flat = P(("ctx", "fsdp"), None), P("fsdp")
    mat = P("fsdp", None)
    in_specs = (
        rows,
        rows,
        mat,
        mat,
        flat,
        flat,
        mat,
        flat,
        flat,
        mat,
        flat,
        flat,
        flat,
        mat,
        flat,
        mat,
        flat,
    )
    out_specs = (
        rows,
        rows,
        flat,
        flat,
        mat,
        flat,
        flat,
        mat,
        flat,
        flat,
        flat,
        mat,
        flat,
        mat,
        flat,
    )
    return jax.shard_map(
        per_device, mesh=mesh, in_specs=in_specs, out_specs=out_specs, check_vma=False
    )
```

```python
import functools
import math

import jax
import jax.numpy as jnp
from jax import lax
from jax.experimental import pallas as pl
from jax.experimental.pallas import tpu as pltpu
from jax.sharding import PartitionSpec as P

HEADS = 16
SPAN = 128
SEQ_BLOCKS = 8

norm_eps = 1e-05
gelu_coef = 0.7978845608028654
LOG2E = 1.4426950408889634

half = jnp.bfloat16
single = jnp.float32


def dot_nn(a, b):
    return lax.dot_general(a, b, (((1,), (0,)), ((), ())), preferred_element_type=single)


def dot_nt(a, b):
    return lax.dot_general(a, b, (((1,), (1,)), ((), ())), preferred_element_type=single)


def dot_tn(a, b):
    return lax.dot_general(a, b, (((0,), (0,)), ((), ())), preferred_element_type=single)


def norm_parts(values):
    center = values - jnp.mean(values, axis=-1, keepdims=True)
    spread = jnp.mean(center * center, axis=-1, keepdims=True)
    inv = lax.rsqrt(spread + norm_eps)
    return center * inv, inv


def norm_back(normed, inv, gain, grad):
    dn = grad * gain
    return inv * (
        dn
        - jnp.mean(dn, axis=-1, keepdims=True)
        - normed * jnp.mean(dn * normed, axis=-1, keepdims=True)
    )


def gelu_both(v):
    t = jnp.tanh(gelu_coef * (v + 0.044715 * v * v * v))
    value = 0.5 * v * (1.0 + t)
    slope = 0.5 * (1.0 + t) + 0.5 * v * (1.0 - t * t) * gelu_coef * (1.0 + 3 * 0.044715 * v * v)
    return value, slope


def swap(x, mask):
    n = lax.axis_size("ctx")
    return lax.ppermute(x, "ctx", [(i, i ^ mask) for i in range(n)])


def gather_first(x):
    count = lax.axis_size("ctx")
    return [swap(x, j) for j in range(1, 3 if count == 4 else count)]


def gather_second(x, arrived):
    if lax.axis_size("ctx") != 4:
        return [[x]] + [[p] for p in arrived]
    one, two = arrived
    n = x.shape[0] // 2
    return [[x], [one], [two], [swap(one[:n], 2), swap(two[n:], 1)]]


def gather_ctx(x):
    return gather_second(x, gather_first(x))


def scatter_first(far):
    if lax.axis_size("ctx") != 4:
        return None
    return swap(far[0], 1), swap(far[1], 2)


def scatter_second(pieces, first):
    if first is None:
        return pieces[1:]
    p1, p2 = pieces[1], pieces[2]
    n = p1.shape[0] // 2
    from_x, from_y = first
    p1 = jnp.concatenate(
        [p1[:n], (p1[n:].astype(single) + from_y.astype(single)).astype(half)], axis=0
    )
    p2 = jnp.concatenate(
        [(p2[:n].astype(single) + from_x.astype(single)).astype(half), p2[n:]], axis=0
    )
    return [p1, p2]


def scatter_send(sent):
    return [swap(x, j + 1) for j, x in enumerate(sent)]


def total_of(own, arrived):
    for x in arrived:
        own = own + x.astype(single)
    return own


def xor_order(items, c):
    bit = 1
    while bit < len(items):
        on = (c & bit) == bit
        items = [jnp.where(on, items[i ^ bit], items[i]) for i in range(len(items))]
        bit *= 2
    return items


TILE = 256


def attn_scores(q_refs, k_refs, i, scale, slope):
    q = jnp.concatenate([q_refs[2 * i][...], q_refs[2 * i + 1][...]], axis=0)
    k = jnp.concatenate([r[...] for r in k_refs[: 2 * i + 2]], axis=0)
    n = TILE * (i + 1)
    col = lax.broadcasted_iota(jnp.int32, (1, n), 1) - (n - 1)
    s = dot_nt(q, k) * (scale * LOG2E) + (slope * LOG2E) * col.astype(single)
    row_at = lax.broadcasted_iota(jnp.int32, (TILE, TILE), 0)
    col_at = lax.broadcasted_iota(jnp.int32, (TILE, TILE), 1)
    last = jnp.where(col_at <= row_at, s[:, n - TILE :], -1e30)
    s = last if i == 0 else jnp.concatenate([s[:, : n - TILE], last], axis=1)
    e = jnp.exp2(s - jnp.max(s, axis=1, keepdims=True))
    return q, k, e, 1.0 / jnp.sum(e, axis=1, keepdims=True)


class Rows:
    def __init__(self, inv_ref, stage, out, sems, kinds):
        self.inv, self.stage, self.out, self.sems, self.kinds = inv_ref, stage, out, sems, kinds
        self.heads = pl.num_programs(1)
        self.step = pl.program_id(0) * self.heads + pl.program_id(1)
        self.slot = lax.rem(self.step, 2)

    def copies(self, step):
        slot = lax.rem(step, 2)
        seq, head = step // self.heads, lax.rem(step, self.heads)
        for kind in range(self.kinds):
            col = pl.multiple_of((kind * self.heads + head) * 128, 128)
            for j in range(SEQ_BLOCKS):
                row = pl.multiple_of(self.inv[seq * SEQ_BLOCKS + j] * SPAN, SPAN)
                yield pltpu.make_async_copy(
                    self.stage.at[slot, kind, pl.ds(j * SPAN, SPAN)],
                    self.out.at[pl.ds(row, SPAN), pl.ds(col, 128)],
                    self.sems.at[slot, kind * SEQ_BLOCKS + j],
                )

    def wait(self, step):
        for copy in self.copies(step):
            copy.wait()

    def open(self):
        @pl.when(self.step >= 2)
        def _():
            self.wait(self.step - 2)

    def close(self):
        for copy in self.copies(self.step):
            copy.start()

        @pl.when(self.step == 2 * self.heads - 1)
        def _():
            self.wait(self.step - 1)
            self.wait(self.step)


def attn_fwd_kernel(scale, inv_ref, slope_ref, *refs):
    q_refs, k_refs, v_refs = refs[:8], refs[8:16], refs[16:24]
    out, stage, sems = refs[24:]
    slope = slope_ref[pl.program_id(1)]
    rows = Rows(inv_ref, stage, out, sems, 1)
    rows.open()
    for i in range(4):
        q, k, e, r = attn_scores(q_refs, k_refs, i, scale, slope)
        v = jnp.concatenate([x[...] for x in v_refs[: 2 * i + 2]], axis=0)
        o = dot_nn((e * r).astype(half), v)
        stage[rows.slot, 0, TILE * i : TILE * (i + 1), :] = o.astype(half)
    rows.close()


def attn_bwd_kernel(scale, inv_ref, slope_ref, *refs):
    q_refs, k_refs, v_refs, g_refs = refs[:8], refs[8:16], refs[16:24], refs[24:32]
    out, sum_q, sum_v, stage, sems, dk_acc, dv_acc = refs[32:]
    slope = slope_ref[pl.program_id(1)]
    rows = Rows(inv_ref, stage, out, sems, 3)
    rows.open()
    total_q = jnp.zeros((1, 128), single)
    for i in (3, 2, 1, 0):
        q, k, e, r = attn_scores(q_refs, k_refs, i, scale, slope)
        n = TILE * (i + 1)
        v = jnp.concatenate([x[...] for x in v_refs[: 2 * i + 2]], axis=0)
        g = jnp.concatenate([g_refs[2 * i][...], g_refs[2 * i + 1][...]], axis=0)
        p = e * r
        dp = dot_nt(g, v)
        delta = jnp.sum(p * dp, axis=1, keepdims=True)
        ds = (p * (dp - delta)).astype(half)
        pb = p.astype(half)
        dq = (dot_nn(ds, k) * scale).astype(half)
        stage[rows.slot, 0, TILE * i : TILE * (i + 1), :] = dq
        total_q = total_q + jnp.sum(dq.astype(single), axis=0, keepdims=True)
        dk = dot_tn(ds, q)
        dv = dot_tn(pb, g)
        if i == 3:
            dk_acc[...] = dk
            dv_acc[...] = dv
        else:
            dk_acc[:n, :] += dk
            dv_acc[:n, :] += dv
    stage[rows.slot, 1] = (dk_acc[...] * scale).astype(half)
    dv = dv_acc[...].astype(half)
    stage[rows.slot, 2] = dv
    total_v = jnp.sum(dv.astype(single), axis=0, keepdims=True)
    sum_q[...] = jnp.broadcast_to(total_q, sum_q.shape)
    sum_v[...] = jnp.broadcast_to(total_v, sum_v.shape)
    rows.close()


def block_specs(offset):
    def one(j):
        return pl.BlockSpec(
            (SPAN, 128), lambda s, h, inv, slope: (inv[s * SEQ_BLOCKS + j], offset + h)
        )

    return [one(j) for j in range(SEQ_BLOCKS)]


def attn_call(kernel, kinds, joined, extra, extra_specs, scratch, inv, slopes, heads, cost, name):
    rows = joined.shape[0]
    tops = [pl.BlockSpec((8, 128), lambda s, h, inv, slope: (s, h))] * (2 if kinds == 3 else 0)
    specs = block_specs(0) + block_specs(heads) + block_specs(2 * heads) + extra_specs
    return pl.pallas_call(
        kernel,
        grid_spec=pltpu.PrefetchScalarGridSpec(
            num_scalar_prefetch=2,
            grid=(2, heads),
            in_specs=specs,
            out_specs=[pl.BlockSpec(memory_space=pl.ANY)] + tops,
            scratch_shapes=[
                pltpu.VMEM((2, kinds, rows // 2, 128), half),
                pltpu.SemaphoreType.DMA((2, kinds * SEQ_BLOCKS)),
            ]
            + scratch,
        ),
        out_shape=[jax.ShapeDtypeStruct((rows, kinds * heads * 128), half)]
        + [jax.ShapeDtypeStruct((16, heads * 128), single)] * len(tops),
        compiler_params=pltpu.CompilerParams(vmem_limit_bytes=48 * 1024 * 1024),
        cost_estimate=cost,
        name=name,
    )(inv, slopes, *([joined] * 24), *extra)


def attn_forward(joined, inv, slopes, heads, scale):
    kernel = functools.partial(attn_fwd_kernel, scale)
    cost = hint(20 * 10**9, joined.shape[0] * heads * 128 * 8)
    return attn_call(
        kernel, 1, joined, [], [], [], inv, slopes, heads, cost, "attn_forward"
    )[0]


def attn_backward(joined, grad, inv, slopes, heads, scale):
    kernel = functools.partial(attn_bwd_kernel, scale)
    cost = hint(40 * 10**9, joined.shape[0] * heads * 128 * 14)
    sums = [pltpu.VMEM((joined.shape[0] // 2, 128), single)] * 2
    return attn_call(
        kernel,
        3,
        joined,
        [grad] * 8,
        block_specs(0),
        sums,
        inv,
        slopes,
        heads,
        cost,
        "attn_backward",
    )


HINT = 0.001


def block_of(x):
    return x if isinstance(x, tuple) else (x, x.shape[0], 0)


def hint(flops, bytes_accessed):
    return pl.CostEstimate(
        flops=int(HINT * flops), bytes_accessed=int(HINT * bytes_accessed), transcendentals=0
    )


def rows_kernel(dot, epilogue, count, extra, *refs):
    left, w_ref = refs[:count], refs[count]
    extras = refs[count + 1 : count + 1 + extra]
    outs = refs[count + 1 + extra :]
    for i in range(count):
        epilogue(i, dot(left[i][...], w_ref[...]), extras, outs)


def rows_matmul(blocks, w, transposed, extras, outs, epilogue, name, tile=512):
    blocks = [block_of(x) for x in blocks]
    extras = [block_of(x) for x in extras]
    n = w.shape[0] if transposed else w.shape[1]
    k = w.shape[1] if transposed else w.shape[0]
    t = math.gcd(n, tile)
    w_spec = (
        pl.BlockSpec((t, k), lambda i: (i, 0)) if transposed else pl.BlockSpec((k, t), lambda i: (0, i))
    )
    rows = sum(x[1] for x in blocks)
    return pl.pallas_call(
        functools.partial(
            rows_kernel, dot_nt if transposed else dot_nn, epilogue, len(blocks), len(extras)
        ),
        grid=(n // t,),
        in_specs=[pl.BlockSpec((x[1], k), lambda i, at=x[2]: (at, 0)) for x in blocks]
        + [w_spec]
        + [pl.BlockSpec((x[1], t), lambda i, at=x[2]: (at, i)) for x in extras],
        out_specs=[pl.BlockSpec((r, t), lambda i: (0, i)) for r, _ in outs],
        out_shape=[jax.ShapeDtypeStruct((r, n), d) for r, d in outs],
        compiler_params=pltpu.CompilerParams(vmem_limit_bytes=52 * 1024 * 1024),
        cost_estimate=hint(2 * rows * n * k, 2 * n * k + 4 * rows * (n + k)),
        name=name,
    )(*[x[0] for x in blocks], w, *[x[0] for x in extras])


def plain(blocks, w, transposed, dtype, name):
    def epilogue(i, x, extras, outs):
        outs[i][...] = x.astype(dtype)

    outs = [(block_of(x)[1], dtype) for x in blocks]
    return rows_matmul(blocks, w, transposed, [], outs, epilogue, name)


def joined_rows(blocks, w, bias, name):
    sizes = [block_of(x)[1] for x in blocks]

    def epilogue(i, x, extras, outs):
        at = sum(sizes[:i])
        outs[0][at : at + sizes[i], :] = (x + extras[0][...]).astype(half)

    bias = bias.reshape(1, -1)
    return rows_matmul(blocks, w, False, [bias], [(sum(sizes), half)], epilogue, name)[0]


def up_gelu(blocks, w, bias, name):
    count = len(blocks)

    def epilogue(i, x, extras, outs):
        value, slope = gelu_both(x + extras[0][...])
        outs[i][...] = value.astype(half)
        outs[count + i][...] = slope.astype(half)

    outs = [(block_of(x)[1], half) for x in blocks] * 2
    out = rows_matmul(blocks, w, False, [bias.reshape(1, -1)], outs, epilogue, name)
    return out[:count], out[count:]


def hidden_back(blocks, w, slopes, name):
    def epilogue(i, x, extras, outs):
        x = x.astype(half).astype(single) * extras[i][...].astype(single)
        outs[i][...] = x.astype(half)

    outs = [(block_of(x)[1], half) for x in blocks]
    return rows_matmul(blocks, w, True, slopes, outs, epilogue, name)


def outer_kernel(count, *refs):
    out = refs[-1]
    total = None
    for i in range(count):
        x = dot_tn(refs[i][...], refs[count + i][...])
        total = x if total is None else total + x
    out[...] = total.astype(half)


def outer(left, right, name):
    left = [block_of(x) for x in left]
    right = [block_of(x) for x in right]
    m, n = left[0][0].shape[1], right[0][0].shape[1]
    tm = math.gcd(m, 1024)
    tn = n // 2 if n % 256 == 0 and n > 1024 else n
    rows = sum(x[1] for x in left)
    return pl.pallas_call(
        functools.partial(outer_kernel, len(left)),
        grid=(m // tm, n // tn),
        in_specs=[pl.BlockSpec((x[1], tm), lambda i, j, at=x[2]: (at, i)) for x in left]
        + [pl.BlockSpec((x[1], tn), lambda i, j, at=x[2]: (at, j)) for x in right],
        out_specs=pl.BlockSpec((tm, tn), lambda i, j: (i, j)),
        out_shape=jax.ShapeDtypeStruct((m, n), half),
        compiler_params=pltpu.CompilerParams(vmem_limit_bytes=52 * 1024 * 1024),
        cost_estimate=hint(2 * rows * m * n, 2 * rows * (m + n) + 2 * m * n),
        name=name,
    )(*[x[0] for x in left], *[x[0] for x in right])


def partner(mask):
    c = lax.axis_index("ctx")
    if mask == 1:
        return c + 1 - 2 * lax.rem(c, 2)
    return lax.rem(c + 2, 4) if mask == 2 else 3 - c


def greet(masks):
    barrier = pltpu.get_barrier_semaphore()
    for mask in masks:
        pl.semaphore_signal(
            barrier,
            inc=1,
            device_id={"ctx": partner(mask)},
            device_id_type=pl.DeviceIdType.MESH,
        )
    pl.semaphore_wait(barrier, len(masks))


class Moves:
    def __init__(self, send_sem, recv_sem):
        self.send_sem, self.recv_sem, self.used = send_sem, recv_sem, 0

    def start(self, src, dst, mask):
        copy = pltpu.make_async_remote_copy(
            src_ref=src,
            dst_ref=dst,
            send_sem=self.send_sem.at[self.used],
            recv_sem=self.recv_sem.at[self.used],
            device_id={"ctx": partner(mask)},
            device_id_type=pl.DeviceIdType.MESH,
        )
        self.used += 1
        copy.start()
        return copy


def multiply(lefts, w, transposed, extras, outs, epilogue, tile=512):
    k = lefts[0].shape[1]
    n = w.shape[0] if transposed else w.shape[1]
    t = math.gcd(n, tile)
    w_spec = (
        pl.BlockSpec((t, k), lambda i: (i, 0)) if transposed else pl.BlockSpec((k, t), lambda i: (0, i))
    )
    dot = dot_nt if transposed else dot_nn

    def body(*refs):
        rows_kernel(dot, epilogue, len(lefts), len(extras), *refs)

    pltpu.emit_pipeline(
        body,
        grid=(n // t,),
        in_specs=[pl.BlockSpec((x.shape[0], k), lambda i: (0, 0)) for x in lefts]
        + [w_spec]
        + [pl.BlockSpec((x.shape[0], t), lambda i: (0, i)) for x in extras],
        out_specs=[pl.BlockSpec((x.shape[0], t), lambda i: (0, i)) for x in outs],
    )(*lefts, w, *extras, *outs)


def store(i, x, extras, outs):
    outs[i][...] = x.astype(outs[i].dtype)


def store_sum(i, x, extras, outs):
    outs[i][...] = (x + extras[i][...].astype(single)).astype(outs[i].dtype)


def store_passed(i, x, extras, outs):
    if i in (1, 2):
        x = x + extras[i - 1][...].astype(single)
    outs[i][...] = x.astype(outs[i].dtype)


def store_hidden(i, x, extras, outs):
    outs[i][...] = (x.astype(half).astype(single) * extras[i][...].astype(single)).astype(half)


def outer_on(lefts, rights, out):
    m, n = out.shape
    tm = math.gcd(m, 1024)
    tn = n // 2 if n % 256 == 0 and n > 1024 else n

    def body(*refs):
        outer_kernel(len(lefts), *refs)

    pltpu.emit_pipeline(
        body,
        grid=(m // tm, n // tn),
        in_specs=[pl.BlockSpec((x.shape[0], tm), lambda i, j: (0, i)) for x in lefts]
        + [pl.BlockSpec((x.shape[0], tn), lambda i, j: (0, j)) for x in rights],
        out_specs=[pl.BlockSpec((tm, tn), lambda i, j: (i, j))],
    )(*lefts, *rights, out)


def halves(ref):
    n = ref.shape[0] // 2
    return ref.at[pl.ds(0, n)], ref.at[pl.ds(n, n)]


def moving_call(kernel, operands, outs, moves, call, flops, name):
    anywhere = pl.BlockSpec(memory_space=pl.ANY)
    sems = pltpu.SemaphoreType.DMA((moves,))
    return pl.pallas_call(
        kernel,
        in_specs=[anywhere] * len(operands),
        out_specs=[anywhere] * len(outs),
        out_shape=[jax.ShapeDtypeStruct(shape, dtype) for shape, dtype in outs],
        scratch_shapes=[sems, sems],
        compiler_params=pltpu.CompilerParams(
            collective_id=call, has_side_effects=True, vmem_limit_bytes=52 * 1024 * 1024
        ),
        cost_estimate=hint(flops, 0),
        name=name,
    )(*operands)


def store_biased(i, x, extras, outs):
    outs[i][...] = (x + extras[0][...]).astype(half)


def qkv_kernel(*refs):
    tok, gain, shift, a1, w_qkv, bias = refs[0:2], refs[2], refs[3], refs[4:7], refs[7], refs[8]
    dz_lo, dz_hi = refs[9:11]
    joined, far, one_lo, two_hi = refs[11], refs[12:14], refs[14], refs[15]
    moves = Moves(*refs[16:18])
    n, width = tok[0].shape
    greet((1, 2))
    copies = [moves.start(dz_lo, one_lo, 1), moves.start(dz_hi, two_hi, 2)]

    def norm(x_lo, x_hi, g, s, o_lo, o_hi):
        for x, o in ((x_lo, o_lo), (x_hi, o_hi)):
            normed, _ = norm_parts(x[...].astype(single))
            o[...] = (normed * g[...] + s[...]).astype(half)

    t = math.gcd(n, 64)
    block = pl.BlockSpec((t, width), lambda i: (i, 0))
    row = pl.BlockSpec((1, width), lambda i: (0, 0))
    pltpu.emit_pipeline(
        norm, grid=(n // t,), in_specs=[block, block, row, row], out_specs=[block, block]
    )(*tok, gain, shift, *far)
    lefts, outs, at = [*a1, *far], [], 0
    for x in lefts:
        outs.append(joined.at[pl.ds(at, x.shape[0])])
        at += x.shape[0]
    multiply(lefts, w_qkv, False, [bias], outs, store_biased)
    for copy in copies:
        copy.wait()


def qkv_forward(tok, gain, shift, a1, w_qkv, bias, dz_lo, dz_hi):
    n, width = tok[0].shape
    k = w_qkv.shape[1]
    outs = [((8 * n, k), half)] + [((n, width), half)] * 4
    out = moving_call(
        qkv_kernel,
        [*tok, gain.reshape(1, -1), shift.reshape(1, -1), *a1, w_qkv, bias.reshape(1, -1), dz_lo, dz_hi],
        outs,
        2,
        7,
        16 * n * width * k,
        "qkv",
    )
    return out[0], out[1:3], out[3:5]


def feed_pass(dz, slope, w_down, w_up, du, total, sums):
    n, width = dz[0].shape
    wide = w_down.shape[0]
    t = math.gcd(wide, 512)
    total[...] = jnp.zeros_like(total)

    def body(dz_lo, dz_hi, down, up, slope_lo, slope_hi, du_lo, du_hi):
        for i, x, s, d in ((0, dz_lo, slope_lo, du_lo), (1, dz_hi, slope_hi, du_hi)):
            grad = dot_nt(x[...], down[...]).astype(half).astype(single)
            grad = (grad * s[...].astype(single)).astype(half)
            d[...] = grad
            at = pl.ds(pl.multiple_of(pl.program_id(0) * t, t), t)
            sums[0:1, at] += jnp.sum(grad.astype(single), axis=0, keepdims=True)
            total[i * n : (i + 1) * n, :] += dot_nt(grad, up[...])

    pltpu.emit_pipeline(
        body,
        grid=(wide // t,),
        in_specs=[pl.BlockSpec((n, width), lambda i: (0, 0))] * 2
        + [pl.BlockSpec((t, width), lambda i: (i, 0)), pl.BlockSpec((width, t), lambda i: (0, i))]
        + [pl.BlockSpec((n, t), lambda i: (0, i))] * 2,
        out_specs=[pl.BlockSpec((n, t), lambda i: (0, i))] * 2,
    )(*dz, w_down, w_up, *slope, *du)


def feed_back_kernel(*refs):
    dz, slope, (w_down, w_up) = refs[0:8], refs[8:13], refs[13:15]
    a2, gb_far = refs[15:20], refs[20:22]
    du, own, land1, land2, up_grad, mix_x, mix_y, bias = refs[22:27], *refs[27:34]
    total, far, near, rest, from_x, from_y, mixed, sums = refs[34:42]
    moves = Moves(*refs[42:44])
    local = refs[44]
    sums[...] = jnp.zeros_like(sums)
    n = from_x.shape[0]
    lo, hi = pl.ds(0, n), pl.ds(n, n)
    (s1_lo, s1_hi), (s2_lo, s2_hi) = halves(slope[1]), halves(slope[2])
    (d1_lo, d1_hi), (d2_lo, d2_hi) = halves(du[1]), halves(du[2])
    (land1_lo, land1_hi), (land2_lo, land2_hi) = halves(land1), halves(land2)
    greet((1, 2))
    wide, width = w_down.shape
    t = math.gcd(width, 512)

    def mix(x_lo, x_hi, w):
        at = pl.ds(pl.multiple_of(pl.program_id(0) * t, t), t)
        mixed[0:n, at] = dot_nn(x_lo[...], w[...]).astype(half)
        mixed[n : 2 * n, at] = dot_nn(x_hi[...], w[...]).astype(half)

    pltpu.emit_pipeline(
        mix,
        grid=(width // t,),
        in_specs=[pl.BlockSpec((n, wide), lambda i: (0, 0))] * 2
        + [pl.BlockSpec((wide, t), lambda i: (0, i))],
    )(*gb_far, w_down)
    second = [moves.start(mixed.at[lo], mix_x, 1), moves.start(mixed.at[hi], mix_y, 2)]
    feed_pass(dz[6:8], slope[3:5], w_down, w_up, du[3:5], total, sums)
    far[...] = total[...].astype(half)
    first = [moves.start(far.at[lo], from_x, 1), moves.start(far.at[hi], from_y, 2)]
    feed_pass([dz[2], dz[5]], [s1_lo, s2_hi], w_down, w_up, [d1_lo, d2_hi], total, sums)
    near[...] = total[...].astype(half)
    second += [moves.start(near.at[lo], land1_lo, 1), moves.start(near.at[hi], land2_hi, 2)]
    feed_pass([dz[3], dz[4]], [s1_hi, s2_lo], w_down, w_up, [d1_hi, d2_lo], total, sums)
    for copy in first:
        copy.wait()
    rest[lo] = (total[lo] + from_y[...].astype(single)).astype(half)
    rest[hi] = (total[hi] + from_x[...].astype(single)).astype(half)
    second += [moves.start(rest.at[lo], land1_hi, 1), moves.start(rest.at[hi], land2_lo, 2)]
    feed_pass(dz[0:2], halves(slope[0]), w_down, w_up, halves(du[0]), total, sums)
    stores = [
        pltpu.make_async_copy(total, own, local.at[0]),
        pltpu.make_async_copy(sums, bias, local.at[1]),
    ]
    for copy in stores:
        copy.start()
    outer_on(a2, du, up_grad)
    for copy in stores + second:
        copy.wait()


def feed_back(dz, slope, w_down, w_up, a2, gb_far):
    n, width = dz[0].shape
    rows, wide = 2 * n, w_down.shape[0]
    anywhere = pl.BlockSpec(memory_space=pl.ANY)
    outs = [((r, wide), half) for r in (rows, rows, rows, n, n)]
    outs += [((rows, width), single)] + [((rows, width), half)] * 2
    outs += [((width, wide), half)] + [((n, width), half)] * 2 + [((8, wide), single)]
    sems = pltpu.SemaphoreType.DMA((8,))
    out = pl.pallas_call(
        feed_back_kernel,
        in_specs=[anywhere] * 22,
        out_specs=[anywhere] * len(outs),
        out_shape=[jax.ShapeDtypeStruct(shape, dtype) for shape, dtype in outs],
        scratch_shapes=[pltpu.VMEM((rows, width), single)]
        + [pltpu.VMEM((rows, width), half)] * 3
        + [pltpu.VMEM((n, width), half)] * 2
        + [pltpu.VMEM((rows, width), half), pltpu.VMEM((8, wide), single)]
        + [sems, sems, pltpu.SemaphoreType.DMA((2,))],
        compiler_params=pltpu.CompilerParams(
            collective_id=3, has_side_effects=True, vmem_limit_bytes=56 * 1024 * 1024
        ),
        cost_estimate=hint(26 * rows * width * wide, 0),
        name="feed_back",
    )(*dz, *slope, w_down, w_up, *a2, *gb_far)
    return out[5:8], out[8], out[9:11], out[11][0]


def heads_back_kernel(part, *refs):
    own, land1, land2, cot, y1, gain, w_out = refs[0:7]
    ob, gb1, gb2, w_down, mix_x, mix_y, down = refs[7:14]
    dy1, dz1, sums, got, out_grad = refs[14:19]
    mix, down1, down2 = refs[19:23], refs[23], refs[24]
    dz, w, stage = refs[25:28]
    moves = Moves(*refs[28:30])
    local = refs[30]
    rows, width = own.shape
    greet((1, 2, 3))
    load = pltpu.make_async_copy(w_out, w, local.at[0])
    load.start()
    copies = [moves.start(down, down1, 1), moves.start(down, down2, 2)]
    t = math.gcd(rows, 64)

    def norm(own, one, two, cot, y1, gain, dy1, dz1, sums):
        step = pl.program_id(0)
        grad = own[...] + one[...].astype(single) + two[...].astype(single)
        normed, inv = norm_parts(y1[...])
        dy = cot[...] + norm_back(normed, inv, gain[...], grad)
        low = dy.astype(half)
        dy1[...] = dy
        dz1[...] = low
        dz[pl.ds(pl.multiple_of(step * t, t), t), :] = low

        @pl.when(step == 0)
        def _():
            sums[...] = jnp.zeros_like(sums)

        sums[0:1] += jnp.sum(grad * normed, axis=0, keepdims=True)
        sums[1:2] += jnp.sum(grad, axis=0, keepdims=True)
        sums[2:3] += jnp.sum(low.astype(single), axis=0, keepdims=True)

    block = pl.BlockSpec((t, width), lambda i: (i, 0))
    pltpu.emit_pipeline(
        norm,
        grid=(rows // t,),
        in_specs=[block] * 5 + [pl.BlockSpec((1, width), lambda i: (0, 0))],
        out_specs=[block] * 2 + [pl.BlockSpec((8, width), lambda i: (0, 0))],
    )(own, land1, land2, cot, y1, gain, dy1, dz1, sums)
    load.wait()
    for mask in (3, 1, 2, 0):
        of = partner(mask) if mask else lax.axis_index("ctx")
        heads = w[pl.ds(pl.multiple_of(of * part, part), part), :]
        stage[mask] = dot_nt(dz[...], heads).astype(half)
        at = got.at[pl.ds(mask * rows, rows)]
        if mask:
            copies.append(moves.start(stage.at[mask], at, mask))
        else:
            keep = pltpu.make_async_copy(stage.at[0], at, local.at[1])
            keep.start()
    outer_on([ob], [dz1], out_grad)
    multiply(
        [*halves(gb1), *halves(gb2)],
        w_down,
        False,
        [mix_y, mix_x],
        mix,
        store_passed,
    )
    keep.wait()
    for copy in copies:
        copy.wait()


def heads_back(terms, cot, y1, gain, w_out, ob, gb1, gb2, w_down, mix_first, down):
    rows, width = cot.shape
    part = width // 4
    anywhere = pl.BlockSpec(memory_space=pl.ANY)
    sems = pltpu.SemaphoreType.DMA((5,))
    outs = [((rows, width), single), ((rows, width), half), ((8, width), single)]
    outs += [((4 * rows, part), half), ((width, width), half)]
    outs += [((rows // 2, width), half)] * 4 + [(down.shape, half)] * 2
    out = pl.pallas_call(
        functools.partial(heads_back_kernel, part),
        in_specs=[anywhere] * 14,
        out_specs=[anywhere] * len(outs),
        out_shape=[jax.ShapeDtypeStruct(shape, dtype) for shape, dtype in outs],
        scratch_shapes=[
            pltpu.VMEM((rows, width), half),
            pltpu.VMEM((width, width), half),
            pltpu.VMEM((4, rows, part), half),
            sems,
            sems,
            pltpu.SemaphoreType.DMA((2,)),
        ],
        compiler_params=pltpu.CompilerParams(
            collective_id=4, has_side_effects=True, vmem_limit_bytes=56 * 1024 * 1024
        ),
        cost_estimate=hint(10 * rows * width * width, 0),
        name="heads_back",
    )(*terms, cot, y1, gain.reshape(1, -1), w_out, ob, gb1, gb2, w_down, *mix_first, down)
    return out[0], out[2], out[3], out[4], out[5:9], out[9:11]


def qkv_back_kernel(*refs):
    dqkv, w_qkv = refs[0:2]
    a1, gb_own, w_down, one_hi, two_hi = refs[2:7], *refs[7:11]
    own, p3, p1, p2, from_x, from_y, land1, land2, qkv_grad, mix_own = refs[11:21]
    x_hi, y_hi = refs[21:23]
    moves = Moves(*refs[23:25])
    rows = own.shape[0]
    n = rows // 2

    def block(k):
        return dqkv.at[pl.ds(k * n, n)]

    greet((1, 2))
    output = [moves.start(one_hi, x_hi, 1), moves.start(two_hi, y_hi, 2)]
    (p3_lo, p3_hi), (p1_lo, p1_hi), (p2_lo, p2_hi) = halves(p3), halves(p1), halves(p2)
    (land1_lo, land1_hi), (land2_lo, land2_hi) = halves(land1), halves(land2)
    multiply([block(6), block(7)], w_qkv, True, [], [p3_lo, p3_hi], store)
    first = [moves.start(p3_lo, from_x, 1), moves.start(p3_hi, from_y, 2)]
    multiply([block(2), block(5)], w_qkv, True, [], [p1_lo, p2_hi], store)
    second = [moves.start(p1_lo, land1_lo, 1), moves.start(p2_hi, land2_hi, 2)]
    multiply([dqkv.at[pl.ds(0, rows)]], w_qkv, True, [], [own], store)
    multiply([gb_own], w_down, False, [], [mix_own], store)
    for copy in first:
        copy.wait()
    multiply([block(3), block(4)], w_qkv, True, [from_y, from_x], [p1_hi, p2_lo], store_sum)
    second += [moves.start(p1_hi, land1_hi, 1), moves.start(p2_lo, land2_lo, 2)]
    rights, at = [], 0
    for x in a1:
        rights.append(dqkv.at[pl.ds(at, x.shape[0])])
        at += x.shape[0]
    outer_on(a1, rights, qkv_grad)
    for copy in output + second:
        copy.wait()


def qkv_back(dqkv, w_qkv, a1, gb_own, w_down, one_hi, two_hi):
    rows, width = a1[0].shape
    wide = gb_own.shape[1]
    n = rows // 2
    outs = [((rows, width), single)] + [((rows, width), half)] * 3
    outs += [((n, width), half)] * 2 + [((rows, width), half)] * 2
    outs += [((width, dqkv.shape[1]), half), ((rows, width), single)] + [((n, width), half)] * 2
    out = moving_call(
        qkv_back_kernel,
        [dqkv, w_qkv, *a1, gb_own, w_down, one_hi, two_hi],
        outs,
        8,
        5,
        16 * rows * width * dqkv.shape[1] + 2 * rows * width * wide,
        "qkv_back",
    )
    return out[0], out[6:8], out[8], out[9], out[10:12]


def lay_out_kernel(axis, layout, c_ref, *refs):
    out = refs[-1]
    for (j, row), ref in zip(layout, refs):
        x = ref[...].astype(single)
        r, w = x.shape
        if axis == 0:
            n = sum(ref.shape[0] for (k, _), ref in zip(layout, refs) if k == j)
            out[pl.ds(pl.multiple_of((c_ref[0] ^ j) * n + row, r), r), :] = x
        else:
            out[row : row + r, pl.ds(pl.multiple_of((c_ref[0] ^ j) * w, w), w)] = x


def lay_out(axis, pieces, c, groups):
    count = len(pieces)
    r = sum(x.shape[0] for x in pieces[0])
    n = pieces[0][0].shape[1]
    w = n // groups
    if w % 128:
        whole = xor_order([jnp.concatenate(p, axis=0).astype(single) for p in pieces], c)
        whole = jnp.stack([p.reshape(r, groups, w) for p in whole], axis=2)
        return whole.reshape(r, count * n)
    layout, blocks = [], []
    for j, p in enumerate(pieces):
        row = 0
        for x in p:
            layout.append((j, row))
            blocks.append(x)
            row += x.shape[0]
    out = (count * r, w) if axis == 0 else (r, count * w)
    return pl.pallas_call(
        functools.partial(lay_out_kernel, axis, layout),
        grid_spec=pltpu.PrefetchScalarGridSpec(
            num_scalar_prefetch=1,
            grid=(groups,),
            in_specs=[pl.BlockSpec((x.shape[0], w), lambda k, c: (0, k)) for x in blocks],
            out_specs=pl.BlockSpec(out, lambda k, c: (0, k)),
        ),
        out_shape=jax.ShapeDtypeStruct((out[0], out[1] * groups), single),
        compiler_params=pltpu.CompilerParams(vmem_limit_bytes=48 * 1024 * 1024),
        cost_estimate=hint(0, 6 * r * n * count),
        name="lay_out",
    )(c.reshape(1), *blocks)


def gather_small_kernel(nf, x_ref, o_ref, send_sem, recv_sem):
    f = lax.axis_index("fsdp")
    barrier = pltpu.get_barrier_semaphore()
    for d in range(1, nf):
        pl.semaphore_signal(
            barrier,
            inc=1,
            device_id={"fsdp": lax.rem(f + d, nf)},
            device_id_type=pl.DeviceIdType.MESH,
        )
    pl.semaphore_wait(barrier, nf - 1)
    copies = []
    for d in range(1, nf):
        copies.append(
            pltpu.make_async_remote_copy(
                src_ref=x_ref,
                dst_ref=o_ref.at[f],
                send_sem=send_sem.at[d],
                recv_sem=recv_sem.at[d],
                device_id={"fsdp": lax.rem(f + d, nf)},
                device_id_type=pl.DeviceIdType.MESH,
            )
        )
        copies[-1].start()
    o_ref[f] = x_ref[...]
    for copy in copies:
        copy.wait()


def gather_small(x, nf):
    return pl.pallas_call(
        functools.partial(gather_small_kernel, nf),
        out_shape=jax.ShapeDtypeStruct((nf,) + x.shape, single),
        in_specs=[pl.BlockSpec(memory_space=pltpu.VMEM)],
        out_specs=pl.BlockSpec(memory_space=pltpu.VMEM),
        scratch_shapes=[pltpu.SemaphoreType.DMA((nf,)), pltpu.SemaphoreType.DMA((nf,))],
        compiler_params=pltpu.CompilerParams(collective_id=1, has_side_effects=True),
        name="gather_small",
    )(x)


def reduce_small_kernel(nf, nc, x_ref, o_ref, land, stage, send_sem, recv_sem):
    f = lax.axis_index("fsdp")
    c = lax.axis_index("ctx")
    barrier = pltpu.get_barrier_semaphore()
    for d in range(1, nf):
        pl.semaphore_signal(
            barrier,
            inc=1,
            device_id={"fsdp": lax.rem(f + d, nf)},
            device_id_type=pl.DeviceIdType.MESH,
        )
    for d in range(1, nc):
        pl.semaphore_signal(
            barrier,
            inc=1,
            device_id={"ctx": lax.rem(c + d, nc)},
            device_id_type=pl.DeviceIdType.MESH,
        )
    pl.semaphore_wait(barrier, nf + nc - 2)
    copies = []
    for d in range(1, nf):
        to = lax.rem(f + d, nf)
        copies.append(
            pltpu.make_async_remote_copy(
                src_ref=x_ref.at[to],
                dst_ref=land.at[d],
                send_sem=send_sem.at[d],
                recv_sem=recv_sem.at[d],
                device_id={"fsdp": to},
                device_id_type=pl.DeviceIdType.MESH,
            )
        )
        copies[-1].start()
    total = x_ref[f]
    for d in range(1, nf):
        copies[d - 1].wait()
        total = total + land[d]
    stage[0] = total
    copies = []
    for d in range(1, nc):
        copies.append(
            pltpu.make_async_remote_copy(
                src_ref=stage.at[0],
                dst_ref=stage.at[d],
                send_sem=send_sem.at[nf + d],
                recv_sem=recv_sem.at[nf + d],
                device_id={"ctx": lax.rem(c + d, nc)},
                device_id_type=pl.DeviceIdType.MESH,
            )
        )
        copies[-1].start()
    for d in range(1, nc):
        copies[d - 1].wait()
        total = total + stage[d]
    o_ref[...] = total


def reduce_small(x, nf, nc, call):
    block = x.shape[1:]
    sems = pltpu.SemaphoreType.DMA((nf + nc,))
    return pl.pallas_call(
        functools.partial(reduce_small_kernel, nf, nc),
        out_shape=jax.ShapeDtypeStruct(block, single),
        in_specs=[pl.BlockSpec(memory_space=pltpu.VMEM)],
        out_specs=pl.BlockSpec(memory_space=pltpu.VMEM),
        scratch_shapes=[
            pltpu.VMEM((nf,) + block, single),
            pltpu.VMEM((nc,) + block, single),
            sems,
            sems,
        ],
        compiler_params=pltpu.CompilerParams(collective_id=call, has_side_effects=True),
        name="reduce_small",
    )(x)


def per_device(
    tokens,
    cotangent,
    lengths,
    span_place,
    ln1_gain,
    ln1_shift,
    qkv_weight,
    q_bias,
    v_bias,
    out_weight,
    out_bias,
    ln2_gain,
    ln2_shift,
    up_weight,
    up_bias,
    down_weight,
    down_bias,
):
    rows, width = tokens.shape
    CTX = lax.axis_size("ctx")
    c = lax.axis_index("ctx")
    f = lax.axis_index("fsdp")
    nf = lax.axis_size("fsdp")
    wide = up_weight.shape[1]
    part = width // CTX
    heads = HEADS // CTX
    scale = 1.0 / math.sqrt(width // HEADS)
    shard = width // nf
    fpart = wide // nf // CTX
    wpart = wide // CTX

    def columns(x, width_each, stride, count):
        return jnp.concatenate(
            [
                lax.dynamic_slice_in_dim(x, k * stride + c * width_each, width_each, axis=1)
                for k in range(count)
            ],
            axis=1,
        )

    def after(x, *others):
        return lax.optimization_barrier((x, others))[0]

    def pick(x, axis):
        return lax.dynamic_index_in_dim(x, c, axis, keepdims=False)

    def gather_f(x):
        return lax.all_gather(x, "fsdp", axis=0, tiled=True)

    qkv_own = columns(qkv_weight, part, width, 3)
    up_own = columns(up_weight, fpart, wide // nf, nf)
    down_own = lax.dynamic_slice_in_dim(down_weight, c * fpart, fpart, axis=0)
    w_qkv = gather_f(qkv_own.astype(half))
    up_own, down_own = up_own.astype(half), down_own.astype(half)
    small = jnp.concatenate(
        [ln1_gain, ln1_shift, q_bias, v_bias, out_bias, ln2_gain, ln2_shift, down_bias, up_bias]
    )
    small_len = small.shape[0]
    small = jnp.pad(small, (0, -small_len % 1024)).reshape(-1, 128)
    small_all = gather_small(small, nf).reshape(nf, -1)[:, :small_len]
    small_all = small_all.astype(half).astype(single)

    def vector(k):
        return small_all[:, k * shard : (k + 1) * shard].reshape(width)

    gain1, shift1, bias_q, bias_v, bias_o, gain2, shift2, bias_d = [vector(k) for k in range(8)]
    bias_u = pick(small_all[:, 8 * shard :].reshape(nf, CTX, fpart), 1).reshape(wpart)
    bias_qkv = jnp.concatenate(
        [pick(bias_q.reshape(CTX, part), 0), jnp.zeros((part,), single), pick(bias_v.reshape(CTX, part), 0)]
    )
    w_out = gather_f(out_weight.astype(half))

    per = rows // SPAN
    table = jnp.arange(CTX * per, dtype=jnp.int32)
    source = ((table // per) ^ c) * per + table % per
    place = jnp.sum(jnp.where(source[:, None] == table[None, :], span_place[0][None, :], 0), axis=1)
    inv = jnp.sum(jnp.where(place[None, :] == table[:, None], table[None, :], 0), axis=1)
    slopes = 2.0 ** (-8.0 * ((c * heads + jnp.arange(heads)).astype(single) + 1.0) / HEADS)

    def flat(pieces):
        return [x for p in pieces for x in p]

    def scatter_f(x):
        return lax.psum_scatter(x, "fsdp", scatter_dimension=0, tiled=True)

    far = CTX - 1
    mid = list(range(1, far))

    def first_norm(x):
        normed, _ = norm_parts(x.astype(single))
        return (normed * gain1 + shift1).astype(half)

    n = rows // 2
    dz2_lo, dz2_hi = cotangent[:n].astype(half), cotangent[n:].astype(half)
    early = (small_all, place, inv, slopes, up_own, down_own, dz2_lo, dz2_hi)
    early, tok_near = after((early, gather_first(tokens)))
    small_all, place, inv, slopes, up_own, down_own, dz2_lo, dz2_hi = early
    tok = gather_second(tokens, tok_near)
    near = [[first_norm(x) for x in p] for p in tok[:far]]
    tok = after(tok, near)
    if CTX != 4:
        dz2_own = jnp.concatenate([dz2_lo, dz2_hi], axis=0)
        dz2_rest = gather_first(dz2_own)
    w_up = gather_f(after(up_own, tok))
    a1 = flat(near)
    if CTX == 4:
        joined, a1_far, dz2_first = qkv_forward(
            tok[far], gain1, shift1, a1, w_qkv, bias_qkv, dz2_lo, dz2_hi
        )
        a1 = a1 + list(a1_far)
        dz2_rest = after((dz2_hi, dz2_lo), joined)
        dz2_rest = [swap(dz2_rest[0], 1), swap(dz2_rest[1], 2)]
    else:
        a1 = a1 + [first_norm(x) for x in tok[far]]
        joined = joined_rows(a1, w_qkv, bias_qkv, "qkv")
    w_down = gather_f(after(down_own, joined))
    attended = attn_forward(joined, inv, slopes, heads, scale)
    mine = [attended[j * rows : (j + 1) * rows] for j in range(CTX)]
    mine = after(mine, dz2_rest)
    mine = [mine[0]] + [swap(mine[j], j) for j in range(1, CTX)]
    ob = jnp.concatenate(xor_order(mine, c), axis=1)
    y1 = tokens.astype(single) + dot_nn(ob, w_out) + bias_o

    normed2, inv2 = norm_parts(y1)
    a2_own = (normed2 * gain2 + shift2).astype(half)
    gb, slope = [None] * CTX, [None] * CTX
    gb[0], slope[0] = up_gelu([a2_own], w_up, bias_u, "up_gelu_0")
    last = gb[0]
    a2_near = gather_first(a2_own)
    a2 = gather_second(a2_own, a2_near)
    if CTX == 4:
        one_lo, two_hi = after(dz2_first, a2_near)
        one_hi, two_lo = dz2_rest
        dz2 = [[dz2_lo, dz2_hi], [one_lo, one_hi], [two_lo, two_hi], [swap(one_lo, 2), swap(two_hi, 1)]]
    else:
        dz2 = [[dz2_own]] + [[x] for x in dz2_rest]
    for j in range(1, CTX):
        gb[j], slope[j] = up_gelu(after(a2[j], last), w_up, bias_u, f"up_gelu_{j}")
        last = gb[j]
    gb_blocks = flat(gb)
    if CTX == 4:
        gb_blocks = [(g[0], n, i) for g in gb[:far] for i in (0, 1)] + list(gb[far])
    down_grad = outer(gb_blocks, flat(dz2), "down_grad")
    down_part = scatter_f(down_grad)
    w_down = after(w_down, down_grad)

    du, dh2, mix = [None] * CTX, [None] * CTX, [None] * CTX
    if CTX == 4:
        dh2, up_grad, mix_first, up_bias_grad = feed_back(
            flat(dz2), flat(slope), w_down, w_up, flat(a2), gb[far]
        )
    else:
        for j in range(CTX):
            du[j] = hidden_back(dz2[j], w_down, slope[j], f"du_{j}")
            dh2[j] = plain(du[j], w_up, True, half if j else single, f"dh2_{j}")[0]
        arrived = scatter_send(dh2[1:])
        dh2 = dh2[0]
        up_grad = outer(flat(a2), flat(du), "up_grad")
        up_bias_grad = sum(jnp.sum(x.astype(single), axis=0) for x in flat(du))
        mix[far] = plain(gb[far], w_down, False, half, "mix_far")[0]
        dh2 = total_of(dh2, arrived)
    up_part = scatter_f(up_grad)
    if CTX == 4:
        dy1, sums2, dattn, out_grad, mix, down_near = heads_back(
            dh2, cotangent, y1, gain2, w_out, ob, gb[1][0], gb[2][0], w_down, mix_first, down_part
        )
        one_lo, one_hi, two_lo, two_hi = mix
        gain2_grad, shift2_grad, out_bias_grad = sums2[0], sums2[1], sums2[2]
    else:
        gain2_grad = jnp.sum(dh2 * normed2, axis=0)
        shift2_grad = jnp.sum(dh2, axis=0)
        dy1 = cotangent + norm_back(normed2, inv2, gain2, dh2)
        dz1 = dy1.astype(half)
        dattn = dot_nt(dz1, w_out).astype(half)
        out_bias_grad = jnp.sum(dz1.astype(single), axis=0)
        dattn = xor_order([dattn[:, s * part : (s + 1) * part] for s in range(CTX)], c)
        dattn = [dattn[0]] + [swap(dattn[j], j) for j in range(1, CTX)]
        dattn = jnp.concatenate(dattn, axis=0)
        out_grad = outer([ob], [dz1], "out_grad")
        for j in mid:
            mix[j] = plain(gb[j], w_down, False, half, f"mix_{j}")[0]
        down_near = gather_first(down_part)
    out_part = scatter_f(out_grad)
    dqkv, sum_q, sum_v = attn_backward(joined, dattn, inv, slopes, heads, scale)
    sum_q, sum_v = sum_q[0] + sum_q[8], sum_v[0] + sum_v[8]
    if CTX == 4:
        lows = [swap(one_lo, 1), swap(two_lo, 2)]
        down_out = gather_second(down_part, down_near)
        dqkv = after(dqkv, lows, up_part, down_out)
        dh1, arrived, qkv_grad, mix_own, highs = qkv_back(
            dqkv, w_qkv, a1, gb[0][0], w_down, one_hi, two_hi
        )
    else:
        dh1 = [
            plain([(dqkv, rows, j)], w_qkv, True, half if j else single, f"dh1_{j}")[0]
            for j in range(CTX)
        ]
        arrived = scatter_send(dh1[1:])
        dh1 = dh1[0]
        qkv_grad = outer(a1, [(dqkv, rows, j) for j in range(CTX)], "qkv_grad")
        mix_own = plain(gb[0], w_down, False, single, "mix_0")[0]
        down_out = gather_second(down_part, down_near)
    qkv_part = scatter_f(qkv_grad)

    up_own = after(up_part, arrived)
    up_near = gather_first(up_own)
    out_first = []
    if CTX == 4:
        k = out_part.shape[0] // 2
        out_lo, out_hi = after(out_part, arrived)[:k], after(out_part, arrived)[k:]
        out_first = [swap(out_lo, 1), swap(out_hi, 2)]
    waiting = (dh1, mix_own, flat(dz2[:1]), down_out)
    dh1, mix_own, dz2_own, down_out = after(waiting, out_part)
    down_out = lay_out(0, down_out, c, width // min(width, 512))
    dh1 = total_of(dh1, arrived)
    if CTX == 4:
        mixed = y1 + bias_d + mix_own
        mixed = jnp.concatenate([total_of(mixed[:n], lows), total_of(mixed[n:], highs)])
    else:
        mixed = total_of(y1 + bias_d + mix_own, scatter_send(mix[1:]))
    down_bias_grad = sum(jnp.sum(x.astype(single), axis=0) for x in dz2_own)
    normed1_own, inv1_own = norm_parts(tokens.astype(single))
    gain1_grad = jnp.sum(dh1 * normed1_own, axis=0)
    shift1_grad = jnp.sum(dh1, axis=0)
    input_grad = dy1 + norm_back(normed1_own, inv1_own, gain1, dh1)

    done = (down_out, input_grad, mixed, down_bias_grad, gain1_grad, shift1_grad)
    up_near, out_first = after((up_near, out_first), done)
    if CTX == 4:
        out_lo = (out_lo.astype(single) + out_first[0].astype(single)).astype(half)
        out_hi = (out_hi.astype(single) + out_first[1].astype(single)).astype(half)
        out_lo, out_hi, up_near = after((out_lo, out_hi, up_near))
        out_second = [(out_lo, swap(out_lo, 2)), (out_hi, swap(out_hi, 1))]
    up_out = gather_second(up_own, up_near)
    up_out = lay_out(1, up_out, c, nf)
    def spread(x, inner):
        x = x.reshape(-1, 1, inner)
        mask = (jnp.arange(CTX) == c)[None, :, None]
        return jnp.where(mask, x, 0.0).reshape(-1)

    def reduced(items, call):
        sizes = [x.shape[0] // nf for x in items]
        x = jnp.concatenate([x.reshape(nf, -1) for x in items], axis=1)
        x = jnp.pad(x, ((0, 0), (0, -x.shape[1] % 1024))).reshape(nf, -1, 128)
        x = reduce_small(x, nf, CTX, call).reshape(-1)
        out, at = [], 0
        for n in sizes:
            out.append(x[at : at + n])
            at += n
        return out

    sums_in = [out_bias_grad, gain2_grad, shift2_grad, down_bias_grad, spread(up_bias_grad, fpart)]
    sums_in += [gain1_grad, shift1_grad, spread(sum_q, part), spread(sum_v, part)]
    qkv_part = after(qkv_part, up_out)
    qkv_near = gather_first(qkv_part)
    sums_in[5] = after(sums_in[5], qkv_part)
    sums_out = reduced(sums_in, 2)
    if CTX == 4:
        out_second = after(out_second, sums_out)
        out_out = [x.astype(single) + y.astype(single) for x, y in out_second]
        out_out = jnp.concatenate(out_out, axis=0)
    else:
        bit = 1
        while bit < CTX:
            out_out = out_part.astype(single) + swap(out_part, bit).astype(single)
            out_part = out_out.astype(half)
            bit *= 2

    qkv_near = after(qkv_near, sums_out)
    qkv_out = lay_out(1, gather_second(qkv_part, qkv_near), c, 3)
    out_bias_out, gain2_out, shift2_out, down_bias_out, up_bias_out = sums_out[:5]
    gain1_out, shift1_out, q_bias_out, v_bias_out = sums_out[5:]
    return (
        mixed,
        input_grad,
        gain1_out,
        shift1_out,
        qkv_out,
        q_bias_out,
        v_bias_out,
        out_out,
        out_bias_out,
        gain2_out,
        shift2_out,
        up_out,
        up_bias_out,
        down_out,
        down_bias_out,
    )


def solution(mesh):
    rows, flat = P(("ctx", "fsdp"), None), P("fsdp")
    mat = P("fsdp", None)
    in_specs = (
        rows,
        rows,
        mat,
        mat,
        flat,
        flat,
        mat,
        flat,
        flat,
        mat,
        flat,
        flat,
        flat,
        mat,
        flat,
        mat,
        flat,
    )
    out_specs = (
        rows,
        rows,
        flat,
        flat,
        mat,
        flat,
        flat,
        mat,
        flat,
        flat,
        flat,
        mat,
        flat,
        mat,
        flat,
    )
    return jax.shard_map(
        per_device, mesh=mesh, in_specs=in_specs, out_specs=out_specs, check_vma=False
    )
```

```python
import functools
import math

import jax
import jax.numpy as jnp
from jax import lax
from jax.experimental import pallas as pl
from jax.experimental.pallas import tpu as pltpu
from jax.sharding import PartitionSpec as P

HEADS = 16
SPAN = 128
SEQ_BLOCKS = 8

norm_eps = 1e-05
gelu_coef = 0.7978845608028654
LOG2E = 1.4426950408889634

half = jnp.bfloat16
single = jnp.float32


def dot_nn(a, b):
    return lax.dot_general(a, b, (((1,), (0,)), ((), ())), preferred_element_type=single)


def dot_nt(a, b):
    return lax.dot_general(a, b, (((1,), (1,)), ((), ())), preferred_element_type=single)


def dot_tn(a, b):
    return lax.dot_general(a, b, (((0,), (0,)), ((), ())), preferred_element_type=single)


def norm_parts(values):
    center = values - jnp.mean(values, axis=-1, keepdims=True)
    spread = jnp.mean(center * center, axis=-1, keepdims=True)
    inv = lax.rsqrt(spread + norm_eps)
    return center * inv, inv


def norm_back(normed, inv, gain, grad):
    dn = grad * gain
    return inv * (
        dn
        - jnp.mean(dn, axis=-1, keepdims=True)
        - normed * jnp.mean(dn * normed, axis=-1, keepdims=True)
    )


def gelu_both(v):
    t = jnp.tanh(gelu_coef * (v + 0.044715 * v * v * v))
    value = 0.5 * v * (1.0 + t)
    slope = 0.5 * (1.0 + t) + 0.5 * v * (1.0 - t * t) * gelu_coef * (1.0 + 3 * 0.044715 * v * v)
    return value, slope


def swap(x, mask):
    n = lax.axis_size("ctx")
    return lax.ppermute(x, "ctx", [(i, i ^ mask) for i in range(n)])


def gather_first(x):
    count = lax.axis_size("ctx")
    return [swap(x, j) for j in range(1, 3 if count == 4 else count)]


def gather_second(x, arrived):
    if lax.axis_size("ctx") != 4:
        return [[x]] + [[p] for p in arrived]
    one, two = arrived
    n = x.shape[0] // 2
    return [[x], [one], [two], [swap(one[:n], 2), swap(two[n:], 1)]]


def gather_ctx(x):
    return gather_second(x, gather_first(x))


def scatter_first(far):
    if lax.axis_size("ctx") != 4:
        return None
    return swap(far[0], 1), swap(far[1], 2)


def scatter_second(pieces, first):
    if first is None:
        return pieces[1:]
    p1, p2 = pieces[1], pieces[2]
    n = p1.shape[0] // 2
    from_x, from_y = first
    p1 = jnp.concatenate(
        [p1[:n], (p1[n:].astype(single) + from_y.astype(single)).astype(half)], axis=0
    )
    p2 = jnp.concatenate(
        [(p2[:n].astype(single) + from_x.astype(single)).astype(half), p2[n:]], axis=0
    )
    return [p1, p2]


def scatter_send(sent):
    return [swap(x, j + 1) for j, x in enumerate(sent)]


def total_of(own, arrived):
    for x in arrived:
        own = own + x.astype(single)
    return own


def xor_order(items, c):
    bit = 1
    while bit < len(items):
        on = (c & bit) == bit
        items = [jnp.where(on, items[i ^ bit], items[i]) for i in range(len(items))]
        bit *= 2
    return items


TILE = 256


def attn_scores(q_refs, k_refs, i, scale, slope):
    q = jnp.concatenate([q_refs[2 * i][...], q_refs[2 * i + 1][...]], axis=0)
    k = jnp.concatenate([r[...] for r in k_refs[: 2 * i + 2]], axis=0)
    n = TILE * (i + 1)
    col = lax.broadcasted_iota(jnp.int32, (1, n), 1) - (n - 1)
    s = dot_nt(q, k) * (scale * LOG2E) + (slope * LOG2E) * col.astype(single)
    row_at = lax.broadcasted_iota(jnp.int32, (TILE, TILE), 0)
    col_at = lax.broadcasted_iota(jnp.int32, (TILE, TILE), 1)
    last = jnp.where(col_at <= row_at, s[:, n - TILE :], -1e30)
    s = last if i == 0 else jnp.concatenate([s[:, : n - TILE], last], axis=1)
    e = jnp.exp2(s - jnp.max(s, axis=1, keepdims=True))
    return q, k, e, 1.0 / jnp.sum(e, axis=1, keepdims=True)


class Rows:
    def __init__(self, inv_ref, stage, out, sems, kinds):
        self.inv, self.stage, self.out, self.sems, self.kinds = inv_ref, stage, out, sems, kinds
        self.heads = pl.num_programs(1)
        self.step = pl.program_id(0) * self.heads + pl.program_id(1)
        self.slot = lax.rem(self.step, 2)

    def copies(self, step):
        slot = lax.rem(step, 2)
        seq, head = step // self.heads, lax.rem(step, self.heads)
        for kind in range(self.kinds):
            col = pl.multiple_of((kind * self.heads + head) * 128, 128)
            for j in range(SEQ_BLOCKS):
                row = pl.multiple_of(self.inv[seq * SEQ_BLOCKS + j] * SPAN, SPAN)
                yield pltpu.make_async_copy(
                    self.stage.at[slot, kind, pl.ds(j * SPAN, SPAN)],
                    self.out.at[pl.ds(row, SPAN), pl.ds(col, 128)],
                    self.sems.at[slot, kind * SEQ_BLOCKS + j],
                )

    def wait(self, step):
        for copy in self.copies(step):
            copy.wait()

    def open(self):
        @pl.when(self.step >= 2)
        def _():
            self.wait(self.step - 2)

    def close(self):
        for copy in self.copies(self.step):
            copy.start()

        @pl.when(self.step == 2 * self.heads - 1)
        def _():
            self.wait(self.step - 1)
            self.wait(self.step)


def attn_fwd_kernel(scale, inv_ref, slope_ref, *refs):
    q_refs, k_refs, v_refs = refs[:8], refs[8:16], refs[16:24]
    out, stage, sems = refs[24:]
    slope = slope_ref[pl.program_id(1)]
    rows = Rows(inv_ref, stage, out, sems, 1)
    rows.open()
    for i in range(4):
        q, k, e, r = attn_scores(q_refs, k_refs, i, scale, slope)
        v = jnp.concatenate([x[...] for x in v_refs[: 2 * i + 2]], axis=0)
        o = dot_nn((e * r).astype(half), v)
        stage[rows.slot, 0, TILE * i : TILE * (i + 1), :] = o.astype(half)
    rows.close()


def attn_bwd_kernel(scale, inv_ref, slope_ref, *refs):
    q_refs, k_refs, v_refs, g_refs = refs[:8], refs[8:16], refs[16:24], refs[24:32]
    out, sum_q, sum_v, stage, sems, dk_acc, dv_acc = refs[32:]
    slope = slope_ref[pl.program_id(1)]
    rows = Rows(inv_ref, stage, out, sems, 3)
    rows.open()
    total_q = jnp.zeros((1, 128), single)
    for i in (3, 2, 1, 0):
        q, k, e, r = attn_scores(q_refs, k_refs, i, scale, slope)
        n = TILE * (i + 1)
        v = jnp.concatenate([x[...] for x in v_refs[: 2 * i + 2]], axis=0)
        g = jnp.concatenate([g_refs[2 * i][...], g_refs[2 * i + 1][...]], axis=0)
        p = e * r
        dp = dot_nt(g, v)
        delta = jnp.sum(p * dp, axis=1, keepdims=True)
        ds = (p * (dp - delta)).astype(half)
        pb = p.astype(half)
        dq = (dot_nn(ds, k) * scale).astype(half)
        stage[rows.slot, 0, TILE * i : TILE * (i + 1), :] = dq
        total_q = total_q + jnp.sum(dq.astype(single), axis=0, keepdims=True)
        dk = dot_tn(ds, q)
        dv = dot_tn(pb, g)
        if i == 3:
            dk_acc[...] = dk
            dv_acc[...] = dv
        else:
            dk_acc[:n, :] += dk
            dv_acc[:n, :] += dv
    stage[rows.slot, 1] = (dk_acc[...] * scale).astype(half)
    dv = dv_acc[...].astype(half)
    stage[rows.slot, 2] = dv
    total_v = jnp.sum(dv.astype(single), axis=0, keepdims=True)
    sum_q[...] = jnp.broadcast_to(total_q, sum_q.shape)
    sum_v[...] = jnp.broadcast_to(total_v, sum_v.shape)
    rows.close()


def block_specs(offset):
    def one(j):
        return pl.BlockSpec(
            (SPAN, 128), lambda s, h, inv, slope: (inv[s * SEQ_BLOCKS + j], offset + h)
        )

    return [one(j) for j in range(SEQ_BLOCKS)]


def attn_call(kernel, kinds, joined, extra, extra_specs, scratch, inv, slopes, heads, cost, name):
    rows = joined.shape[0]
    tops = [pl.BlockSpec((8, 128), lambda s, h, inv, slope: (s, h))] * (2 if kinds == 3 else 0)
    specs = block_specs(0) + block_specs(heads) + block_specs(2 * heads) + extra_specs
    return pl.pallas_call(
        kernel,
        grid_spec=pltpu.PrefetchScalarGridSpec(
            num_scalar_prefetch=2,
            grid=(2, heads),
            in_specs=specs,
            out_specs=[pl.BlockSpec(memory_space=pl.ANY)] + tops,
            scratch_shapes=[
                pltpu.VMEM((2, kinds, rows // 2, 128), half),
                pltpu.SemaphoreType.DMA((2, kinds * SEQ_BLOCKS)),
            ]
            + scratch,
        ),
        out_shape=[jax.ShapeDtypeStruct((rows, kinds * heads * 128), half)]
        + [jax.ShapeDtypeStruct((16, heads * 128), single)] * len(tops),
        compiler_params=pltpu.CompilerParams(vmem_limit_bytes=48 * 1024 * 1024),
        cost_estimate=cost,
        name=name,
    )(inv, slopes, *([joined] * 24), *extra)


def attn_forward(joined, inv, slopes, heads, scale):
    kernel = functools.partial(attn_fwd_kernel, scale)
    cost = hint(20 * 10**9, joined.shape[0] * heads * 128 * 8)
    return attn_call(
        kernel, 1, joined, [], [], [], inv, slopes, heads, cost, "attn_forward"
    )[0]


def attn_backward(joined, grad, inv, slopes, heads, scale):
    kernel = functools.partial(attn_bwd_kernel, scale)
    cost = hint(40 * 10**9, joined.shape[0] * heads * 128 * 14)
    sums = [pltpu.VMEM((joined.shape[0] // 2, 128), single)] * 2
    return attn_call(
        kernel,
        3,
        joined,
        [grad] * 8,
        block_specs(0),
        sums,
        inv,
        slopes,
        heads,
        cost,
        "attn_backward",
    )


HINT = 0.001


def block_of(x):
    return x if isinstance(x, tuple) else (x, x.shape[0], 0)


def hint(flops, bytes_accessed):
    return pl.CostEstimate(
        flops=int(HINT * flops), bytes_accessed=int(HINT * bytes_accessed), transcendentals=0
    )


def rows_kernel(dot, epilogue, count, extra, *refs):
    left, w_ref = refs[:count], refs[count]
    extras = refs[count + 1 : count + 1 + extra]
    outs = refs[count + 1 + extra :]
    for i in range(count):
        epilogue(i, dot(left[i][...], w_ref[...]), extras, outs)


def rows_matmul(blocks, w, transposed, extras, outs, epilogue, name, tile=512):
    blocks = [block_of(x) for x in blocks]
    extras = [block_of(x) for x in extras]
    n = w.shape[0] if transposed else w.shape[1]
    k = w.shape[1] if transposed else w.shape[0]
    t = math.gcd(n, tile)
    w_spec = (
        pl.BlockSpec((t, k), lambda i: (i, 0)) if transposed else pl.BlockSpec((k, t), lambda i: (0, i))
    )
    rows = sum(x[1] for x in blocks)
    return pl.pallas_call(
        functools.partial(
            rows_kernel, dot_nt if transposed else dot_nn, epilogue, len(blocks), len(extras)
        ),
        grid=(n // t,),
        in_specs=[pl.BlockSpec((x[1], k), lambda i, at=x[2]: (at, 0)) for x in blocks]
        + [w_spec]
        + [pl.BlockSpec((x[1], t), lambda i, at=x[2]: (at, i)) for x in extras],
        out_specs=[pl.BlockSpec((r, t), lambda i: (0, i)) for r, _ in outs],
        out_shape=[jax.ShapeDtypeStruct((r, n), d) for r, d in outs],
        compiler_params=pltpu.CompilerParams(vmem_limit_bytes=52 * 1024 * 1024),
        cost_estimate=hint(2 * rows * n * k, 2 * n * k + 4 * rows * (n + k)),
        name=name,
    )(*[x[0] for x in blocks], w, *[x[0] for x in extras])


def plain(blocks, w, transposed, dtype, name):
    def epilogue(i, x, extras, outs):
        outs[i][...] = x.astype(dtype)

    outs = [(block_of(x)[1], dtype) for x in blocks]
    return rows_matmul(blocks, w, transposed, [], outs, epilogue, name)


def joined_rows(blocks, w, bias, name):
    sizes = [block_of(x)[1] for x in blocks]

    def epilogue(i, x, extras, outs):
        at = sum(sizes[:i])
        outs[0][at : at + sizes[i], :] = (x + extras[0][...]).astype(half)

    bias = bias.reshape(1, -1)
    return rows_matmul(blocks, w, False, [bias], [(sum(sizes), half)], epilogue, name)[0]


def up_gelu(blocks, w, bias, name):
    count = len(blocks)

    def epilogue(i, x, extras, outs):
        value, slope = gelu_both(x + extras[0][...])
        outs[i][...] = value.astype(half)
        outs[count + i][...] = slope.astype(half)

    outs = [(block_of(x)[1], half) for x in blocks] * 2
    out = rows_matmul(blocks, w, False, [bias.reshape(1, -1)], outs, epilogue, name)
    return out[:count], out[count:]


def hidden_back(blocks, w, slopes, name):
    def epilogue(i, x, extras, outs):
        x = x.astype(half).astype(single) * extras[i][...].astype(single)
        outs[i][...] = x.astype(half)

    outs = [(block_of(x)[1], half) for x in blocks]
    return rows_matmul(blocks, w, True, slopes, outs, epilogue, name)


def outer_kernel(count, *refs):
    out = refs[-1]
    total = None
    for i in range(count):
        x = dot_tn(refs[i][...], refs[count + i][...])
        total = x if total is None else total + x
    out[...] = total.astype(half)


def outer(left, right, name):
    left = [block_of(x) for x in left]
    right = [block_of(x) for x in right]
    m, n = left[0][0].shape[1], right[0][0].shape[1]
    tm = math.gcd(m, 1024)
    tn = n // 2 if n % 256 == 0 and n > 1024 else n
    rows = sum(x[1] for x in left)
    return pl.pallas_call(
        functools.partial(outer_kernel, len(left)),
        grid=(m // tm, n // tn),
        in_specs=[pl.BlockSpec((x[1], tm), lambda i, j, at=x[2]: (at, i)) for x in left]
        + [pl.BlockSpec((x[1], tn), lambda i, j, at=x[2]: (at, j)) for x in right],
        out_specs=pl.BlockSpec((tm, tn), lambda i, j: (i, j)),
        out_shape=jax.ShapeDtypeStruct((m, n), half),
        compiler_params=pltpu.CompilerParams(vmem_limit_bytes=52 * 1024 * 1024),
        cost_estimate=hint(2 * rows * m * n, 2 * rows * (m + n) + 2 * m * n),
        name=name,
    )(*[x[0] for x in left], *[x[0] for x in right])


def partner(mask):
    c = lax.axis_index("ctx")
    if mask == 1:
        return c + 1 - 2 * lax.rem(c, 2)
    return lax.rem(c + 2, 4) if mask == 2 else 3 - c


def greet(masks):
    barrier = pltpu.get_barrier_semaphore()
    for mask in masks:
        pl.semaphore_signal(
            barrier,
            inc=1,
            device_id={"ctx": partner(mask)},
            device_id_type=pl.DeviceIdType.MESH,
        )
    pl.semaphore_wait(barrier, len(masks))


class Moves:
    def __init__(self, send_sem, recv_sem):
        self.send_sem, self.recv_sem, self.used = send_sem, recv_sem, 0

    def start(self, src, dst, mask):
        copy = pltpu.make_async_remote_copy(
            src_ref=src,
            dst_ref=dst,
            send_sem=self.send_sem.at[self.used],
            recv_sem=self.recv_sem.at[self.used],
            device_id={"ctx": partner(mask)},
            device_id_type=pl.DeviceIdType.MESH,
        )
        self.used += 1
        copy.start()
        return copy


def multiply(lefts, w, transposed, extras, outs, epilogue, tile=512):
    k = lefts[0].shape[1]
    n = w.shape[0] if transposed else w.shape[1]
    t = math.gcd(n, tile)
    w_spec = (
        pl.BlockSpec((t, k), lambda i: (i, 0)) if transposed else pl.BlockSpec((k, t), lambda i: (0, i))
    )
    dot = dot_nt if transposed else dot_nn

    def body(*refs):
        rows_kernel(dot, epilogue, len(lefts), len(extras), *refs)

    pltpu.emit_pipeline(
        body,
        grid=(n // t,),
        in_specs=[pl.BlockSpec((x.shape[0], k), lambda i: (0, 0)) for x in lefts]
        + [w_spec]
        + [pl.BlockSpec((x.shape[0], t), lambda i: (0, i)) for x in extras],
        out_specs=[pl.BlockSpec((x.shape[0], t), lambda i: (0, i)) for x in outs],
    )(*lefts, w, *extras, *outs)


def store(i, x, extras, outs):
    outs[i][...] = x.astype(outs[i].dtype)


def store_sum(i, x, extras, outs):
    outs[i][...] = (x + extras[i][...].astype(single)).astype(outs[i].dtype)


def store_passed(i, x, extras, outs):
    if i in (1, 2):
        x = x + extras[i - 1][...].astype(single)
    outs[i][...] = x.astype(outs[i].dtype)


def store_hidden(i, x, extras, outs):
    outs[i][...] = (x.astype(half).astype(single) * extras[i][...].astype(single)).astype(half)


def outer_on(lefts, rights, out):
    m, n = out.shape
    tm = math.gcd(m, 1024)
    tn = n // 2 if n % 256 == 0 and n > 1024 else n

    def body(*refs):
        outer_kernel(len(lefts), *refs)

    pltpu.emit_pipeline(
        body,
        grid=(m // tm, n // tn),
        in_specs=[pl.BlockSpec((x.shape[0], tm), lambda i, j: (0, i)) for x in lefts]
        + [pl.BlockSpec((x.shape[0], tn), lambda i, j: (0, j)) for x in rights],
        out_specs=[pl.BlockSpec((tm, tn), lambda i, j: (i, j))],
    )(*lefts, *rights, out)


def halves(ref):
    n = ref.shape[0] // 2
    return ref.at[pl.ds(0, n)], ref.at[pl.ds(n, n)]


def moving_call(kernel, operands, outs, moves, call, flops, name):
    anywhere = pl.BlockSpec(memory_space=pl.ANY)
    sems = pltpu.SemaphoreType.DMA((moves,))
    return pl.pallas_call(
        kernel,
        in_specs=[anywhere] * len(operands),
        out_specs=[anywhere] * len(outs),
        out_shape=[jax.ShapeDtypeStruct(shape, dtype) for shape, dtype in outs],
        scratch_shapes=[sems, sems],
        compiler_params=pltpu.CompilerParams(
            collective_id=call, has_side_effects=True, vmem_limit_bytes=52 * 1024 * 1024
        ),
        cost_estimate=hint(flops, 0),
        name=name,
    )(*operands)


def store_biased(i, x, extras, outs):
    outs[i][...] = (x + extras[0][...]).astype(half)


def qkv_kernel(*refs):
    tok, gain, shift, a1, w_qkv, bias = refs[0:2], refs[2], refs[3], refs[4:7], refs[7], refs[8]
    dz_lo, dz_hi = refs[9:11]
    joined, far, one_lo, two_hi = refs[11], refs[12:14], refs[14], refs[15]
    moves = Moves(*refs[16:18])
    n, width = tok[0].shape
    greet((1, 2))
    copies = [moves.start(dz_lo, one_lo, 1), moves.start(dz_hi, two_hi, 2)]

    def norm(x_lo, x_hi, g, s, o_lo, o_hi):
        for x, o in ((x_lo, o_lo), (x_hi, o_hi)):
            normed, _ = norm_parts(x[...].astype(single))
            o[...] = (normed * g[...] + s[...]).astype(half)

    t = math.gcd(n, 64)
    block = pl.BlockSpec((t, width), lambda i: (i, 0))
    row = pl.BlockSpec((1, width), lambda i: (0, 0))
    pltpu.emit_pipeline(
        norm, grid=(n // t,), in_specs=[block, block, row, row], out_specs=[block, block]
    )(*tok, gain, shift, *far)
    lefts, outs, at = [*a1, *far], [], 0
    for x in lefts:
        outs.append(joined.at[pl.ds(at, x.shape[0])])
        at += x.shape[0]
    multiply(lefts, w_qkv, False, [bias], outs, store_biased)
    for copy in copies:
        copy.wait()


def qkv_forward(tok, gain, shift, a1, w_qkv, bias, dz_lo, dz_hi):
    n, width = tok[0].shape
    k = w_qkv.shape[1]
    outs = [((8 * n, k), half)] + [((n, width), half)] * 4
    out = moving_call(
        qkv_kernel,
        [*tok, gain.reshape(1, -1), shift.reshape(1, -1), *a1, w_qkv, bias.reshape(1, -1), dz_lo, dz_hi],
        outs,
        2,
        7,
        16 * n * width * k,
        "qkv",
    )
    return out[0], out[1:3], out[3:5]


def feed_pass(dz, slope, w_down, w_up, du, total, sums):
    m, (n, width) = len(dz), dz[0].shape
    wide = w_down.shape[0]
    t = math.gcd(wide, 512)
    total[0 : m * n] = jnp.zeros((m * n, width), single)

    def body(*refs):
        down, up = refs[m : m + 2]
        at = pl.ds(pl.multiple_of(pl.program_id(0) * t, t), t)
        for i in range(m):
            x, s, d = refs[i], refs[m + 2 + i], refs[2 * m + 2 + i]
            grad = dot_nt(x[...], down[...]).astype(half).astype(single)
            grad = (grad * s[...].astype(single)).astype(half)
            d[...] = grad
            sums[0:1, at] += jnp.sum(grad.astype(single), axis=0, keepdims=True)
            total[i * n : (i + 1) * n, :] += dot_nt(grad, up[...])

    pltpu.emit_pipeline(
        body,
        grid=(wide // t,),
        in_specs=[pl.BlockSpec((n, width), lambda i: (0, 0))] * m
        + [pl.BlockSpec((t, width), lambda i: (i, 0)), pl.BlockSpec((width, t), lambda i: (0, i))]
        + [pl.BlockSpec((n, t), lambda i: (0, i))] * m,
        out_specs=[pl.BlockSpec((n, t), lambda i: (0, i))] * m,
    )(*dz, w_down, w_up, *slope, *du)


def feed_back_kernel(*refs):
    dz, slope, (w_down, w_up) = refs[0:8], refs[8:13], refs[13:15]
    a2, gb_far = refs[15:20], refs[20:22]
    du, own, land1, land2, up_grad, mix_x, mix_y, bias = refs[22:27], *refs[27:34]
    total, far, near, rest, from_x, from_y, mixed, sums = refs[34:42]
    moves = Moves(*refs[42:44])
    local = refs[44]
    sums[...] = jnp.zeros_like(sums)
    n = from_x.shape[0]
    lo, hi = pl.ds(0, n), pl.ds(n, n)
    (s1_lo, s1_hi), (s2_lo, s2_hi) = halves(slope[1]), halves(slope[2])
    (d1_lo, d1_hi), (d2_lo, d2_hi) = halves(du[1]), halves(du[2])
    (land1_lo, land1_hi), (land2_lo, land2_hi) = halves(land1), halves(land2)
    greet((1, 2))
    wide, width = w_down.shape
    t = math.gcd(width, 512)

    second = []
    for part, src, dst, mask in ((lo, gb_far[0], mix_x, 1), (hi, gb_far[1], mix_y, 2)):

        def mix(x, w, part=part):
            at = pl.ds(pl.multiple_of(pl.program_id(0) * t, t), t)
            mixed[part, at] = dot_nn(x[...], w[...]).astype(half)

        pltpu.emit_pipeline(
            mix,
            grid=(width // t,),
            in_specs=[
                pl.BlockSpec((n, wide), lambda i: (0, 0)),
                pl.BlockSpec((wide, t), lambda i: (0, i)),
            ],
        )(src, w_down)
        second.append(moves.start(mixed.at[part], dst, mask))
    feed_pass(dz[6:8], slope[3:5], w_down, w_up, du[3:5], total, sums)
    far[...] = total[0 : 2 * n].astype(half)
    first = [moves.start(far.at[lo], from_x, 1), moves.start(far.at[hi], from_y, 2)]
    feed_pass([dz[2], dz[5]], [s1_lo, s2_hi], w_down, w_up, [d1_lo, d2_hi], total, sums)
    near[...] = total[0 : 2 * n].astype(half)
    second += [moves.start(near.at[lo], land1_lo, 1), moves.start(near.at[hi], land2_hi, 2)]
    feed_pass(
        [dz[3], dz[4], dz[0], dz[1]],
        [s1_hi, s2_lo, *halves(slope[0])],
        w_down,
        w_up,
        [d1_hi, d2_lo, *halves(du[0])],
        total,
        sums,
    )
    for copy in first:
        copy.wait()
    rest[lo] = (total[lo] + from_y[...].astype(single)).astype(half)
    rest[hi] = (total[hi] + from_x[...].astype(single)).astype(half)
    second += [moves.start(rest.at[lo], land1_hi, 1), moves.start(rest.at[hi], land2_lo, 2)]
    stores = [
        pltpu.make_async_copy(total.at[pl.ds(2 * n, 2 * n)], own, local.at[0]),
        pltpu.make_async_copy(sums, bias, local.at[1]),
    ]
    for copy in stores:
        copy.start()
    outer_on(a2, du, up_grad)
    for copy in stores + second:
        copy.wait()


def feed_back(dz, slope, w_down, w_up, a2, gb_far):
    n, width = dz[0].shape
    rows, wide = 2 * n, w_down.shape[0]
    anywhere = pl.BlockSpec(memory_space=pl.ANY)
    outs = [((r, wide), half) for r in (rows, rows, rows, n, n)]
    outs += [((rows, width), single)] + [((rows, width), half)] * 2
    outs += [((width, wide), half)] + [((n, width), half)] * 2 + [((8, wide), single)]
    sems = pltpu.SemaphoreType.DMA((8,))
    out = pl.pallas_call(
        feed_back_kernel,
        in_specs=[anywhere] * 22,
        out_specs=[anywhere] * len(outs),
        out_shape=[jax.ShapeDtypeStruct(shape, dtype) for shape, dtype in outs],
        scratch_shapes=[pltpu.VMEM((2 * rows, width), single)]
        + [pltpu.VMEM((rows, width), half)] * 3
        + [pltpu.VMEM((n, width), half)] * 2
        + [pltpu.VMEM((rows, width), half), pltpu.VMEM((8, wide), single)]
        + [sems, sems, pltpu.SemaphoreType.DMA((2,))],
        compiler_params=pltpu.CompilerParams(
            collective_id=3, has_side_effects=True, vmem_limit_bytes=56 * 1024 * 1024
        ),
        cost_estimate=hint(26 * rows * width * wide, 0),
        name="feed_back",
    )(*dz, *slope, w_down, w_up, *a2, *gb_far)
    return out[5:8], out[8], out[9:11], out[11][0]


def heads_back_kernel(part, *refs):
    own, land1, land2, cot, y1, gain, w_out = refs[0:7]
    ob, gb1, gb2, w_down, mix_x, mix_y, down = refs[7:14]
    dy1, dz1, sums, got, out_grad = refs[14:19]
    mix, (one_lo, one_hi, two_lo, two_hi) = refs[19:23], refs[23:27]
    dz, w, stage = refs[27:30]
    moves = Moves(*refs[30:32])
    local = refs[32]
    rows, width = own.shape
    greet((1, 2, 3))
    load = pltpu.make_async_copy(w_out, w, local.at[0])
    load.start()
    down_lo, down_hi = halves(down)
    copies = [moves.start(down_lo, one_lo, 1), moves.start(down_hi, two_hi, 2)]
    copies += [moves.start(down_hi, one_hi, 1), moves.start(down_lo, two_lo, 2)]
    t = math.gcd(rows, 64)

    def norm(own, one, two, cot, y1, gain, dy1, dz1, sums):
        step = pl.program_id(0)
        grad = own[...] + one[...].astype(single) + two[...].astype(single)
        normed, inv = norm_parts(y1[...])
        dy = cot[...] + norm_back(normed, inv, gain[...], grad)
        low = dy.astype(half)
        dy1[...] = dy
        dz1[...] = low
        dz[pl.ds(pl.multiple_of(step * t, t), t), :] = low

        @pl.when(step == 0)
        def _():
            sums[...] = jnp.zeros_like(sums)

        sums[0:1] += jnp.sum(grad * normed, axis=0, keepdims=True)
        sums[1:2] += jnp.sum(grad, axis=0, keepdims=True)
        sums[2:3] += jnp.sum(low.astype(single), axis=0, keepdims=True)

    block = pl.BlockSpec((t, width), lambda i: (i, 0))
    pltpu.emit_pipeline(
        norm,
        grid=(rows // t,),
        in_specs=[block] * 5 + [pl.BlockSpec((1, width), lambda i: (0, 0))],
        out_specs=[block] * 2 + [pl.BlockSpec((8, width), lambda i: (0, 0))],
    )(own, land1, land2, cot, y1, gain, dy1, dz1, sums)
    load.wait()
    for mask in (3, 1, 2, 0):
        of = partner(mask) if mask else lax.axis_index("ctx")
        heads = w[pl.ds(pl.multiple_of(of * part, part), part), :]
        stage[mask] = dot_nt(dz[...], heads).astype(half)
        at = got.at[pl.ds(mask * rows, rows)]
        if mask:
            copies.append(moves.start(stage.at[mask], at, mask))
        else:
            keep = pltpu.make_async_copy(stage.at[0], at, local.at[1])
            keep.start()
    outer_on([ob], [dz1], out_grad)
    multiply(
        [*halves(gb1), *halves(gb2)],
        w_down,
        False,
        [mix_y, mix_x],
        mix,
        store_passed,
    )
    keep.wait()
    for copy in copies:
        copy.wait()


def heads_back(terms, cot, y1, gain, w_out, ob, gb1, gb2, w_down, mix_first, down):
    rows, width = cot.shape
    part = width // 4
    anywhere = pl.BlockSpec(memory_space=pl.ANY)
    sems = pltpu.SemaphoreType.DMA((7,))
    outs = [((rows, width), single), ((rows, width), half), ((8, width), single)]
    outs += [((4 * rows, part), half), ((width, width), half)]
    outs += [((rows // 2, width), half)] * 4 + [((down.shape[0] // 2, width), half)] * 4
    out = pl.pallas_call(
        functools.partial(heads_back_kernel, part),
        in_specs=[anywhere] * 14,
        out_specs=[anywhere] * len(outs),
        out_shape=[jax.ShapeDtypeStruct(shape, dtype) for shape, dtype in outs],
        scratch_shapes=[
            pltpu.VMEM((rows, width), half),
            pltpu.VMEM((width, width), half),
            pltpu.VMEM((4, rows, part), half),
            sems,
            sems,
            pltpu.SemaphoreType.DMA((2,)),
        ],
        compiler_params=pltpu.CompilerParams(
            collective_id=4, has_side_effects=True, vmem_limit_bytes=56 * 1024 * 1024
        ),
        cost_estimate=hint(10 * rows * width * width, 0),
        name="heads_back",
    )(*terms, cot, y1, gain.reshape(1, -1), w_out, ob, gb1, gb2, w_down, *mix_first, down)
    return out[0], out[2], out[3], out[4], out[5:9], out[9:13]


def qkv_back_kernel(*refs):
    dqkv, w_qkv = refs[0:2]
    a1, gb_own, w_down, one_hi, two_hi = refs[2:7], *refs[7:11]
    own, p3, p1, p2, from_x, from_y, land1, land2, qkv_grad, mix_own = refs[11:21]
    x_hi, y_hi = refs[21:23]
    moves = Moves(*refs[23:25])
    rows = own.shape[0]
    n = rows // 2

    def block(k):
        return dqkv.at[pl.ds(k * n, n)]

    greet((1, 2))
    output = [moves.start(one_hi, x_hi, 1), moves.start(two_hi, y_hi, 2)]
    (p3_lo, p3_hi), (p1_lo, p1_hi), (p2_lo, p2_hi) = halves(p3), halves(p1), halves(p2)
    (land1_lo, land1_hi), (land2_lo, land2_hi) = halves(land1), halves(land2)
    multiply([block(6), block(7)], w_qkv, True, [], [p3_lo, p3_hi], store)
    first = [moves.start(p3_lo, from_x, 1), moves.start(p3_hi, from_y, 2)]
    multiply([block(2), block(5)], w_qkv, True, [], [p1_lo, p2_hi], store)
    second = [moves.start(p1_lo, land1_lo, 1), moves.start(p2_hi, land2_hi, 2)]
    multiply([dqkv.at[pl.ds(0, rows)]], w_qkv, True, [], [own], store)
    multiply([gb_own], w_down, False, [], [mix_own], store)
    for copy in first:
        copy.wait()
    multiply([block(3), block(4)], w_qkv, True, [from_y, from_x], [p1_hi, p2_lo], store_sum)
    second += [moves.start(p1_hi, land1_hi, 1), moves.start(p2_lo, land2_lo, 2)]
    rights, at = [], 0
    for x in a1:
        rights.append(dqkv.at[pl.ds(at, x.shape[0])])
        at += x.shape[0]
    outer_on(a1, rights, qkv_grad)
    for copy in output + second:
        copy.wait()


def qkv_back(dqkv, w_qkv, a1, gb_own, w_down, one_hi, two_hi):
    rows, width = a1[0].shape
    wide = gb_own.shape[1]
    n = rows // 2
    outs = [((rows, width), single)] + [((rows, width), half)] * 3
    outs += [((n, width), half)] * 2 + [((rows, width), half)] * 2
    outs += [((width, dqkv.shape[1]), half), ((rows, width), single)] + [((n, width), half)] * 2
    out = moving_call(
        qkv_back_kernel,
        [dqkv, w_qkv, *a1, gb_own, w_down, one_hi, two_hi],
        outs,
        8,
        5,
        16 * rows * width * dqkv.shape[1] + 2 * rows * width * wide,
        "qkv_back",
    )
    return out[0], out[6:8], out[8], out[9], out[10:12]


def lay_out_kernel(axis, layout, c_ref, *refs):
    out = refs[-1]
    for (j, row), ref in zip(layout, refs):
        x = ref[...].astype(single)
        r, w = x.shape
        if axis == 0:
            n = sum(ref.shape[0] for (k, _), ref in zip(layout, refs) if k == j)
            out[pl.ds(pl.multiple_of((c_ref[0] ^ j) * n + row, r), r), :] = x
        else:
            out[row : row + r, pl.ds(pl.multiple_of((c_ref[0] ^ j) * w, w), w)] = x


def lay_out(axis, pieces, c, groups):
    count = len(pieces)
    r = sum(x.shape[0] for x in pieces[0])
    n = pieces[0][0].shape[1]
    w = n // groups
    if w % 128:
        whole = xor_order([jnp.concatenate(p, axis=0).astype(single) for p in pieces], c)
        whole = jnp.stack([p.reshape(r, groups, w) for p in whole], axis=2)
        return whole.reshape(r, count * n)
    layout, blocks = [], []
    for j, p in enumerate(pieces):
        row = 0
        for x in p:
            layout.append((j, row))
            blocks.append(x)
            row += x.shape[0]
    out = (count * r, w) if axis == 0 else (r, count * w)
    return pl.pallas_call(
        functools.partial(lay_out_kernel, axis, layout),
        grid_spec=pltpu.PrefetchScalarGridSpec(
            num_scalar_prefetch=1,
            grid=(groups,),
            in_specs=[pl.BlockSpec((x.shape[0], w), lambda k, c: (0, k)) for x in blocks],
            out_specs=pl.BlockSpec(out, lambda k, c: (0, k)),
        ),
        out_shape=jax.ShapeDtypeStruct((out[0], out[1] * groups), single),
        compiler_params=pltpu.CompilerParams(vmem_limit_bytes=48 * 1024 * 1024),
        cost_estimate=hint(0, 6 * r * n * count),
        name="lay_out",
    )(c.reshape(1), *blocks)


def gather_small_kernel(nf, x_ref, o_ref, send_sem, recv_sem):
    f = lax.axis_index("fsdp")
    barrier = pltpu.get_barrier_semaphore()
    for d in range(1, nf):
        pl.semaphore_signal(
            barrier,
            inc=1,
            device_id={"fsdp": lax.rem(f + d, nf)},
            device_id_type=pl.DeviceIdType.MESH,
        )
    pl.semaphore_wait(barrier, nf - 1)
    copies = []
    for d in range(1, nf):
        copies.append(
            pltpu.make_async_remote_copy(
                src_ref=x_ref,
                dst_ref=o_ref.at[f],
                send_sem=send_sem.at[d],
                recv_sem=recv_sem.at[d],
                device_id={"fsdp": lax.rem(f + d, nf)},
                device_id_type=pl.DeviceIdType.MESH,
            )
        )
        copies[-1].start()
    o_ref[f] = x_ref[...]
    for copy in copies:
        copy.wait()


def gather_small(x, nf):
    return pl.pallas_call(
        functools.partial(gather_small_kernel, nf),
        out_shape=jax.ShapeDtypeStruct((nf,) + x.shape, single),
        in_specs=[pl.BlockSpec(memory_space=pltpu.VMEM)],
        out_specs=pl.BlockSpec(memory_space=pltpu.VMEM),
        scratch_shapes=[pltpu.SemaphoreType.DMA((nf,)), pltpu.SemaphoreType.DMA((nf,))],
        compiler_params=pltpu.CompilerParams(collective_id=1, has_side_effects=True),
        name="gather_small",
    )(x)


def reduce_small_kernel(nf, nc, x_ref, o_ref, land, stage, send_sem, recv_sem):
    f = lax.axis_index("fsdp")
    c = lax.axis_index("ctx")
    barrier = pltpu.get_barrier_semaphore()
    for d in range(1, nf):
        pl.semaphore_signal(
            barrier,
            inc=1,
            device_id={"fsdp": lax.rem(f + d, nf)},
            device_id_type=pl.DeviceIdType.MESH,
        )
    for d in range(1, nc):
        pl.semaphore_signal(
            barrier,
            inc=1,
            device_id={"ctx": lax.rem(c + d, nc)},
            device_id_type=pl.DeviceIdType.MESH,
        )
    pl.semaphore_wait(barrier, nf + nc - 2)
    copies = []
    for d in range(1, nf):
        to = lax.rem(f + d, nf)
        copies.append(
            pltpu.make_async_remote_copy(
                src_ref=x_ref.at[to],
                dst_ref=land.at[d],
                send_sem=send_sem.at[d],
                recv_sem=recv_sem.at[d],
                device_id={"fsdp": to},
                device_id_type=pl.DeviceIdType.MESH,
            )
        )
        copies[-1].start()
    total = x_ref[f]
    for d in range(1, nf):
        copies[d - 1].wait()
        total = total + land[d]
    stage[0] = total
    copies = []
    for d in range(1, nc):
        copies.append(
            pltpu.make_async_remote_copy(
                src_ref=stage.at[0],
                dst_ref=stage.at[d],
                send_sem=send_sem.at[nf + d],
                recv_sem=recv_sem.at[nf + d],
                device_id={"ctx": lax.rem(c + d, nc)},
                device_id_type=pl.DeviceIdType.MESH,
            )
        )
        copies[-1].start()
    for d in range(1, nc):
        copies[d - 1].wait()
        total = total + stage[d]
    o_ref[...] = total


def reduce_small(x, nf, nc, call):
    block = x.shape[1:]
    sems = pltpu.SemaphoreType.DMA((nf + nc,))
    return pl.pallas_call(
        functools.partial(reduce_small_kernel, nf, nc),
        out_shape=jax.ShapeDtypeStruct(block, single),
        in_specs=[pl.BlockSpec(memory_space=pltpu.VMEM)],
        out_specs=pl.BlockSpec(memory_space=pltpu.VMEM),
        scratch_shapes=[
            pltpu.VMEM((nf,) + block, single),
            pltpu.VMEM((nc,) + block, single),
            sems,
            sems,
        ],
        compiler_params=pltpu.CompilerParams(collective_id=call, has_side_effects=True),
        name="reduce_small",
    )(x)


def per_device(
    tokens,
    cotangent,
    lengths,
    span_place,
    ln1_gain,
    ln1_shift,
    qkv_weight,
    q_bias,
    v_bias,
    out_weight,
    out_bias,
    ln2_gain,
    ln2_shift,
    up_weight,
    up_bias,
    down_weight,
    down_bias,
):
    rows, width = tokens.shape
    CTX = lax.axis_size("ctx")
    c = lax.axis_index("ctx")
    f = lax.axis_index("fsdp")
    nf = lax.axis_size("fsdp")
    wide = up_weight.shape[1]
    part = width // CTX
    heads = HEADS // CTX
    scale = 1.0 / math.sqrt(width // HEADS)
    shard = width // nf
    fpart = wide // nf // CTX
    wpart = wide // CTX

    def columns(x, width_each, stride, count):
        return jnp.concatenate(
            [
                lax.dynamic_slice_in_dim(x, k * stride + c * width_each, width_each, axis=1)
                for k in range(count)
            ],
            axis=1,
        )

    def after(x, *others):
        return lax.optimization_barrier((x, others))[0]

    def pick(x, axis):
        return lax.dynamic_index_in_dim(x, c, axis, keepdims=False)

    def gather_f(x):
        return lax.all_gather(x, "fsdp", axis=0, tiled=True)

    qkv_own = columns(qkv_weight, part, width, 3)
    up_own = columns(up_weight, fpart, wide // nf, nf)
    down_own = lax.dynamic_slice_in_dim(down_weight, c * fpart, fpart, axis=0)
    w_qkv = gather_f(qkv_own.astype(half))
    up_own, down_own = up_own.astype(half), down_own.astype(half)
    small = jnp.concatenate(
        [ln1_gain, ln1_shift, q_bias, v_bias, out_bias, ln2_gain, ln2_shift, down_bias, up_bias]
    )
    small_len = small.shape[0]
    small = jnp.pad(small, (0, -small_len % 1024)).reshape(-1, 128)
    small_all = gather_small(small, nf).reshape(nf, -1)[:, :small_len]
    small_all = small_all.astype(half).astype(single)

    def vector(k):
        return small_all[:, k * shard : (k + 1) * shard].reshape(width)

    gain1, shift1, bias_q, bias_v, bias_o, gain2, shift2, bias_d = [vector(k) for k in range(8)]
    bias_u = pick(small_all[:, 8 * shard :].reshape(nf, CTX, fpart), 1).reshape(wpart)
    bias_qkv = jnp.concatenate(
        [pick(bias_q.reshape(CTX, part), 0), jnp.zeros((part,), single), pick(bias_v.reshape(CTX, part), 0)]
    )
    w_out = gather_f(out_weight.astype(half))

    per = rows // SPAN
    table = jnp.arange(CTX * per, dtype=jnp.int32)
    source = ((table // per) ^ c) * per + table % per
    place = jnp.sum(jnp.where(source[:, None] == table[None, :], span_place[0][None, :], 0), axis=1)
    inv = jnp.sum(jnp.where(place[None, :] == table[:, None], table[None, :], 0), axis=1)
    slopes = 2.0 ** (-8.0 * ((c * heads + jnp.arange(heads)).astype(single) + 1.0) / HEADS)

    def flat(pieces):
        return [x for p in pieces for x in p]

    def scatter_f(x):
        return lax.psum_scatter(x, "fsdp", scatter_dimension=0, tiled=True)

    far = CTX - 1
    mid = list(range(1, far))

    def first_norm(x):
        normed, _ = norm_parts(x.astype(single))
        return (normed * gain1 + shift1).astype(half)

    n = rows // 2
    dz2_lo, dz2_hi = cotangent[:n].astype(half), cotangent[n:].astype(half)
    early = (small_all, place, inv, slopes, up_own, down_own, dz2_lo, dz2_hi)
    early, tok_near = after((early, gather_first(tokens)))
    small_all, place, inv, slopes, up_own, down_own, dz2_lo, dz2_hi = early
    tok = gather_second(tokens, tok_near)
    near = [[first_norm(x) for x in p] for p in tok[:far]]
    tok = after(tok, near)
    if CTX != 4:
        dz2_own = jnp.concatenate([dz2_lo, dz2_hi], axis=0)
        dz2_rest = gather_first(dz2_own)
    w_up = gather_f(after(up_own, tok))
    a1 = flat(near)
    if CTX == 4:
        joined, a1_far, dz2_first = qkv_forward(
            tok[far], gain1, shift1, a1, w_qkv, bias_qkv, dz2_lo, dz2_hi
        )
        a1 = a1 + list(a1_far)
        dz2_rest = after((dz2_hi, dz2_lo), joined)
        dz2_rest = [swap(dz2_rest[0], 1), swap(dz2_rest[1], 2)]
    else:
        a1 = a1 + [first_norm(x) for x in tok[far]]
        joined = joined_rows(a1, w_qkv, bias_qkv, "qkv")
    w_down = gather_f(after(down_own, joined))
    attended = attn_forward(joined, inv, slopes, heads, scale)
    mine = [attended[j * rows : (j + 1) * rows] for j in range(CTX)]
    mine = after(mine, dz2_rest)
    mine = [mine[0]] + [swap(mine[j], j) for j in range(1, CTX)]
    ob = after(jnp.concatenate(xor_order(mine, c), axis=1))
    y1 = tokens.astype(single) + dot_nn(ob, w_out) + bias_o

    normed2, inv2 = norm_parts(y1)
    a2_own = (normed2 * gain2 + shift2).astype(half)
    gb, slope = [None] * CTX, [None] * CTX
    gb[0], slope[0] = up_gelu([a2_own], w_up, bias_u, "up_gelu_0")
    last = gb[0]
    a2_near = gather_first(a2_own)
    a2 = gather_second(a2_own, a2_near)
    if CTX == 4:
        one_lo, two_hi = after(dz2_first, a2_near)
        one_hi, two_lo = dz2_rest
        dz2 = [[dz2_lo, dz2_hi], [one_lo, one_hi], [two_lo, two_hi], [swap(one_lo, 2), swap(two_hi, 1)]]
    else:
        dz2 = [[dz2_own]] + [[x] for x in dz2_rest]
    for j in range(1, CTX):
        gb[j], slope[j] = up_gelu(after(a2[j], last), w_up, bias_u, f"up_gelu_{j}")
        last = gb[j]
    gb_blocks = flat(gb)
    if CTX == 4:
        gb_blocks = [(g[0], n, i) for g in gb[:far] for i in (0, 1)] + list(gb[far])
    down_grad = outer(gb_blocks, flat(dz2), "down_grad")
    down_part = scatter_f(down_grad)
    w_down = after(w_down, down_grad)

    du, dh2, mix = [None] * CTX, [None] * CTX, [None] * CTX
    if CTX == 4:
        dh2, up_grad, mix_first, up_bias_grad = feed_back(
            flat(dz2), flat(slope), w_down, w_up, flat(a2), gb[far]
        )
    else:
        for j in range(CTX):
            du[j] = hidden_back(dz2[j], w_down, slope[j], f"du_{j}")
            dh2[j] = plain(du[j], w_up, True, half if j else single, f"dh2_{j}")[0]
        arrived = scatter_send(dh2[1:])
        dh2 = dh2[0]
        up_grad = outer(flat(a2), flat(du), "up_grad")
        up_bias_grad = sum(jnp.sum(x.astype(single), axis=0) for x in flat(du))
        mix[far] = plain(gb[far], w_down, False, half, "mix_far")[0]
        dh2 = total_of(dh2, arrived)
    up_part = scatter_f(up_grad)
    if CTX == 4:
        dy1, sums2, dattn, out_grad, mix, down_near = heads_back(
            dh2, cotangent, y1, gain2, w_out, ob, gb[1][0], gb[2][0], w_down, mix_first, down_part
        )
        one_lo, one_hi, two_lo, two_hi = mix
        gain2_grad, shift2_grad, out_bias_grad = sums2[0], sums2[1], sums2[2]
    else:
        gain2_grad = jnp.sum(dh2 * normed2, axis=0)
        shift2_grad = jnp.sum(dh2, axis=0)
        dy1 = cotangent + norm_back(normed2, inv2, gain2, dh2)
        dz1 = dy1.astype(half)
        dattn = dot_nt(dz1, w_out).astype(half)
        out_bias_grad = jnp.sum(dz1.astype(single), axis=0)
        dattn = xor_order([dattn[:, s * part : (s + 1) * part] for s in range(CTX)], c)
        dattn = [dattn[0]] + [swap(dattn[j], j) for j in range(1, CTX)]
        dattn = jnp.concatenate(dattn, axis=0)
        out_grad = outer([ob], [dz1], "out_grad")
        for j in mid:
            mix[j] = plain(gb[j], w_down, False, half, f"mix_{j}")[0]
        down_near = gather_first(down_part)
    out_part = scatter_f(out_grad)
    dqkv, sum_q, sum_v = attn_backward(joined, dattn, inv, slopes, heads, scale)
    sum_q, sum_v = sum_q[0] + sum_q[8], sum_v[0] + sum_v[8]
    if CTX == 4:
        lows = [swap(one_lo, 1), swap(two_lo, 2)]
        down_far = [swap(down_near[0], 2), swap(down_near[3], 1)]
        down_out = [[down_part], list(down_near[0:2]), list(down_near[2:4]), down_far]
        dqkv = after(dqkv, lows, up_part, down_far)
        dh1, arrived, qkv_grad, mix_own, highs = qkv_back(
            dqkv, w_qkv, a1, gb[0][0], w_down, one_hi, two_hi
        )
    else:
        dh1 = [
            plain([(dqkv, rows, j)], w_qkv, True, half if j else single, f"dh1_{j}")[0]
            for j in range(CTX)
        ]
        arrived = scatter_send(dh1[1:])
        dh1 = dh1[0]
        qkv_grad = outer(a1, [(dqkv, rows, j) for j in range(CTX)], "qkv_grad")
        mix_own = plain(gb[0], w_down, False, single, "mix_0")[0]
        down_out = gather_second(down_part, down_near)
    qkv_part = scatter_f(qkv_grad)

    up_own = after(up_part, arrived)
    up_near = gather_first(up_own)
    out_first = []
    if CTX == 4:
        k = out_part.shape[0] // 2
        out_lo, out_hi = after(out_part, arrived)[:k], after(out_part, arrived)[k:]
        out_first = [swap(out_lo, 1), swap(out_hi, 2)]
    waiting = (dh1, mix_own, flat(dz2[:1]), down_out)
    dh1, mix_own, dz2_own, down_out = after(waiting, out_part)
    down_out = lay_out(0, down_out, c, width // min(width, 512))
    dh1 = total_of(dh1, arrived)
    if CTX == 4:
        mixed = y1 + bias_d + mix_own
        mixed = jnp.concatenate([total_of(mixed[:n], lows), total_of(mixed[n:], highs)])
    else:
        mixed = total_of(y1 + bias_d + mix_own, scatter_send(mix[1:]))
    down_bias_grad = sum(jnp.sum(x.astype(single), axis=0) for x in dz2_own)
    normed1_own, inv1_own = norm_parts(tokens.astype(single))
    gain1_grad = jnp.sum(dh1 * normed1_own, axis=0)
    shift1_grad = jnp.sum(dh1, axis=0)
    input_grad = dy1 + norm_back(normed1_own, inv1_own, gain1, dh1)

    done = (down_out, input_grad, mixed, down_bias_grad, gain1_grad, shift1_grad)
    up_near, out_first = after((up_near, out_first), done)
    if CTX == 4:
        out_lo = (out_lo.astype(single) + out_first[0].astype(single)).astype(half)
        out_hi = (out_hi.astype(single) + out_first[1].astype(single)).astype(half)
        out_lo, out_hi, up_near = after((out_lo, out_hi, up_near))
        out_second = [(out_lo, swap(out_lo, 2)), (out_hi, swap(out_hi, 1))]
    up_out = gather_second(up_own, up_near)
    up_out = lay_out(1, up_out, c, nf)
    def spread(x, inner):
        x = x.reshape(-1, 1, inner)
        mask = (jnp.arange(CTX) == c)[None, :, None]
        return jnp.where(mask, x, 0.0).reshape(-1)

    def reduced(items, call):
        sizes = [x.shape[0] // nf for x in items]
        x = jnp.concatenate([x.reshape(nf, -1) for x in items], axis=1)
        x = jnp.pad(x, ((0, 0), (0, -x.shape[1] % 1024))).reshape(nf, -1, 128)
        x = reduce_small(x, nf, CTX, call).reshape(-1)
        out, at = [], 0
        for n in sizes:
            out.append(x[at : at + n])
            at += n
        return out

    sums_in = [out_bias_grad, gain2_grad, shift2_grad, down_bias_grad, spread(up_bias_grad, fpart)]
    sums_in += [gain1_grad, shift1_grad, spread(sum_q, part), spread(sum_v, part)]
    qkv_part = after(qkv_part, up_out)
    qkv_near = gather_first(qkv_part)
    sums_in[5] = after(sums_in[5], qkv_part)
    sums_out = reduced(sums_in, 2)
    if CTX == 4:
        out_second = after(out_second, sums_out)
        out_out = [x.astype(single) + y.astype(single) for x, y in out_second]
        out_out = jnp.concatenate(out_out, axis=0)
    else:
        bit = 1
        while bit < CTX:
            out_out = out_part.astype(single) + swap(out_part, bit).astype(single)
            out_part = out_out.astype(half)
            bit *= 2

    qkv_near = after(qkv_near, sums_out)
    qkv_out = lay_out(1, gather_second(qkv_part, qkv_near), c, 3)
    out_bias_out, gain2_out, shift2_out, down_bias_out, up_bias_out = sums_out[:5]
    gain1_out, shift1_out, q_bias_out, v_bias_out = sums_out[5:]
    return (
        mixed,
        input_grad,
        gain1_out,
        shift1_out,
        qkv_out,
        q_bias_out,
        v_bias_out,
        out_out,
        out_bias_out,
        gain2_out,
        shift2_out,
        up_out,
        up_bias_out,
        down_out,
        down_bias_out,
    )


def solution(mesh):
    rows, flat = P(("ctx", "fsdp"), None), P("fsdp")
    mat = P("fsdp", None)
    in_specs = (
        rows,
        rows,
        mat,
        mat,
        flat,
        flat,
        mat,
        flat,
        flat,
        mat,
        flat,
        flat,
        flat,
        mat,
        flat,
        mat,
        flat,
    )
    out_specs = (
        rows,
        rows,
        flat,
        flat,
        mat,
        flat,
        flat,
        mat,
        flat,
        flat,
        flat,
        mat,
        flat,
        mat,
        flat,
    )
    return jax.shard_map(
        per_device, mesh=mesh, in_specs=in_specs, out_specs=out_specs, check_vma=False
    )
```

```python
import functools
import math

import jax
import jax.numpy as jnp
from jax import lax
from jax.experimental import pallas as pl
from jax.experimental.pallas import tpu as pltpu
from jax.sharding import PartitionSpec as P

HEADS = 16
SPAN = 128
SEQ_BLOCKS = 8

norm_eps = 1e-05
gelu_coef = 0.7978845608028654
LOG2E = 1.4426950408889634

half = jnp.bfloat16
single = jnp.float32


def dot_nn(a, b):
    return lax.dot_general(a, b, (((1,), (0,)), ((), ())), preferred_element_type=single)


def dot_nt(a, b):
    return lax.dot_general(a, b, (((1,), (1,)), ((), ())), preferred_element_type=single)


def dot_tn(a, b):
    return lax.dot_general(a, b, (((0,), (0,)), ((), ())), preferred_element_type=single)


def norm_parts(values):
    center = values - jnp.mean(values, axis=-1, keepdims=True)
    spread = jnp.mean(center * center, axis=-1, keepdims=True)
    inv = lax.rsqrt(spread + norm_eps)
    return center * inv, inv


def norm_back(normed, inv, gain, grad):
    dn = grad * gain
    return inv * (
        dn
        - jnp.mean(dn, axis=-1, keepdims=True)
        - normed * jnp.mean(dn * normed, axis=-1, keepdims=True)
    )


def gelu_both(v):
    t = jnp.tanh(gelu_coef * (v + 0.044715 * v * v * v))
    value = 0.5 * v * (1.0 + t)
    slope = 0.5 * (1.0 + t) + 0.5 * v * (1.0 - t * t) * gelu_coef * (1.0 + 3 * 0.044715 * v * v)
    return value, slope


def swap(x, mask):
    n = lax.axis_size("ctx")
    return lax.ppermute(x, "ctx", [(i, i ^ mask) for i in range(n)])


def gather_first(x):
    count = lax.axis_size("ctx")
    return [swap(x, j) for j in range(1, 3 if count == 4 else count)]


def gather_second(x, arrived):
    if lax.axis_size("ctx") != 4:
        return [[x]] + [[p] for p in arrived]
    one, two = arrived
    n = x.shape[0] // 2
    return [[x], [one], [two], [swap(one[:n], 2), swap(two[n:], 1)]]


def gather_ctx(x):
    return gather_second(x, gather_first(x))


def scatter_first(far):
    if lax.axis_size("ctx") != 4:
        return None
    return swap(far[0], 1), swap(far[1], 2)


def scatter_second(pieces, first):
    if first is None:
        return pieces[1:]
    p1, p2 = pieces[1], pieces[2]
    n = p1.shape[0] // 2
    from_x, from_y = first
    p1 = jnp.concatenate(
        [p1[:n], (p1[n:].astype(single) + from_y.astype(single)).astype(half)], axis=0
    )
    p2 = jnp.concatenate(
        [(p2[:n].astype(single) + from_x.astype(single)).astype(half), p2[n:]], axis=0
    )
    return [p1, p2]


def scatter_send(sent):
    return [swap(x, j + 1) for j, x in enumerate(sent)]


def total_of(own, arrived):
    for x in arrived:
        own = own + x.astype(single)
    return own


def xor_order(items, c):
    bit = 1
    while bit < len(items):
        on = (c & bit) == bit
        items = [jnp.where(on, items[i ^ bit], items[i]) for i in range(len(items))]
        bit *= 2
    return items


TILE = 256


def attn_scores(q_refs, k_refs, i, scale, slope):
    q = jnp.concatenate([q_refs[2 * i][...], q_refs[2 * i + 1][...]], axis=0)
    k = jnp.concatenate([r[...] for r in k_refs[: 2 * i + 2]], axis=0)
    n = TILE * (i + 1)
    col = lax.broadcasted_iota(jnp.int32, (1, n), 1) - (n - 1)
    s = dot_nt(q, k) * (scale * LOG2E) + (slope * LOG2E) * col.astype(single)
    row_at = lax.broadcasted_iota(jnp.int32, (TILE, TILE), 0)
    col_at = lax.broadcasted_iota(jnp.int32, (TILE, TILE), 1)
    last = jnp.where(col_at <= row_at, s[:, n - TILE :], -1e30)
    s = last if i == 0 else jnp.concatenate([s[:, : n - TILE], last], axis=1)
    e = jnp.exp2(s - jnp.max(s, axis=1, keepdims=True))
    return q, k, e, 1.0 / jnp.sum(e, axis=1, keepdims=True)


class Rows:
    def __init__(self, inv_ref, stage, out, sems, kinds):
        self.inv, self.stage, self.out, self.sems, self.kinds = inv_ref, stage, out, sems, kinds
        self.heads = pl.num_programs(1)
        self.step = pl.program_id(0) * self.heads + pl.program_id(1)
        self.slot = lax.rem(self.step, 2)

    def copies(self, step):
        slot = lax.rem(step, 2)
        seq, head = step // self.heads, lax.rem(step, self.heads)
        for kind in range(self.kinds):
            col = pl.multiple_of((kind * self.heads + head) * 128, 128)
            for j in range(SEQ_BLOCKS):
                row = pl.multiple_of(self.inv[seq * SEQ_BLOCKS + j] * SPAN, SPAN)
                yield pltpu.make_async_copy(
                    self.stage.at[slot, kind, pl.ds(j * SPAN, SPAN)],
                    self.out.at[pl.ds(row, SPAN), pl.ds(col, 128)],
                    self.sems.at[slot, kind * SEQ_BLOCKS + j],
                )

    def wait(self, step):
        for copy in self.copies(step):
            copy.wait()

    def open(self):
        @pl.when(self.step >= 2)
        def _():
            self.wait(self.step - 2)

    def close(self):
        for copy in self.copies(self.step):
            copy.start()

        @pl.when(self.step == 2 * self.heads - 1)
        def _():
            self.wait(self.step - 1)
            self.wait(self.step)


def attn_fwd_kernel(scale, inv_ref, slope_ref, *refs):
    q_refs, k_refs, v_refs = refs[:8], refs[8:16], refs[16:24]
    out, stage, sems = refs[24:]
    slope = slope_ref[pl.program_id(1)]
    rows = Rows(inv_ref, stage, out, sems, 1)
    rows.open()
    for i in range(4):
        q, k, e, r = attn_scores(q_refs, k_refs, i, scale, slope)
        v = jnp.concatenate([x[...] for x in v_refs[: 2 * i + 2]], axis=0)
        o = dot_nn((e * r).astype(half), v)
        stage[rows.slot, 0, TILE * i : TILE * (i + 1), :] = o.astype(half)
    rows.close()


def attn_bwd_kernel(scale, inv_ref, slope_ref, *refs):
    q_refs, k_refs, v_refs, g_refs = refs[:8], refs[8:16], refs[16:24], refs[24:32]
    out, sum_q, sum_v, stage, sems, dk_acc, dv_acc = refs[32:]
    slope = slope_ref[pl.program_id(1)]
    rows = Rows(inv_ref, stage, out, sems, 3)
    rows.open()
    total_q = jnp.zeros((1, 128), single)
    for i in (3, 2, 1, 0):
        q, k, e, r = attn_scores(q_refs, k_refs, i, scale, slope)
        n = TILE * (i + 1)
        v = jnp.concatenate([x[...] for x in v_refs[: 2 * i + 2]], axis=0)
        g = jnp.concatenate([g_refs[2 * i][...], g_refs[2 * i + 1][...]], axis=0)
        p = e * r
        dp = dot_nt(g, v)
        delta = jnp.sum(p * dp, axis=1, keepdims=True)
        ds = (p * (dp - delta)).astype(half)
        pb = p.astype(half)
        dq = (dot_nn(ds, k) * scale).astype(half)
        stage[rows.slot, 0, TILE * i : TILE * (i + 1), :] = dq
        total_q = total_q + jnp.sum(dq.astype(single), axis=0, keepdims=True)
        dk = dot_tn(ds, q)
        dv = dot_tn(pb, g)
        if i == 3:
            dk_acc[...] = dk
            dv_acc[...] = dv
        else:
            dk_acc[:n, :] += dk
            dv_acc[:n, :] += dv
    stage[rows.slot, 1] = (dk_acc[...] * scale).astype(half)
    dv = dv_acc[...].astype(half)
    stage[rows.slot, 2] = dv
    total_v = jnp.sum(dv.astype(single), axis=0, keepdims=True)
    sum_q[...] = jnp.broadcast_to(total_q, sum_q.shape)
    sum_v[...] = jnp.broadcast_to(total_v, sum_v.shape)
    rows.close()


def block_specs(offset):
    def one(j):
        return pl.BlockSpec(
            (SPAN, 128), lambda s, h, inv, slope: (inv[s * SEQ_BLOCKS + j], offset + h)
        )

    return [one(j) for j in range(SEQ_BLOCKS)]


def attn_call(kernel, kinds, joined, extra, extra_specs, scratch, inv, slopes, heads, cost, name):
    rows = joined.shape[0]
    tops = [pl.BlockSpec((8, 128), lambda s, h, inv, slope: (s, h))] * (2 if kinds == 3 else 0)
    specs = block_specs(0) + block_specs(heads) + block_specs(2 * heads) + extra_specs
    return pl.pallas_call(
        kernel,
        grid_spec=pltpu.PrefetchScalarGridSpec(
            num_scalar_prefetch=2,
            grid=(2, heads),
            in_specs=specs,
            out_specs=[pl.BlockSpec(memory_space=pl.ANY)] + tops,
            scratch_shapes=[
                pltpu.VMEM((2, kinds, rows // 2, 128), half),
                pltpu.SemaphoreType.DMA((2, kinds * SEQ_BLOCKS)),
            ]
            + scratch,
        ),
        out_shape=[jax.ShapeDtypeStruct((rows, kinds * heads * 128), half)]
        + [jax.ShapeDtypeStruct((16, heads * 128), single)] * len(tops),
        compiler_params=pltpu.CompilerParams(vmem_limit_bytes=48 * 1024 * 1024),
        cost_estimate=cost,
        name=name,
    )(inv, slopes, *([joined] * 24), *extra)


def attn_forward(joined, inv, slopes, heads, scale):
    kernel = functools.partial(attn_fwd_kernel, scale)
    cost = hint(20 * 10**9, joined.shape[0] * heads * 128 * 8)
    return attn_call(
        kernel, 1, joined, [], [], [], inv, slopes, heads, cost, "attn_forward"
    )[0]


def attn_backward(joined, grad, inv, slopes, heads, scale):
    kernel = functools.partial(attn_bwd_kernel, scale)
    cost = hint(40 * 10**9, joined.shape[0] * heads * 128 * 14)
    sums = [pltpu.VMEM((joined.shape[0] // 2, 128), single)] * 2
    return attn_call(
        kernel,
        3,
        joined,
        [grad] * 8,
        block_specs(0),
        sums,
        inv,
        slopes,
        heads,
        cost,
        "attn_backward",
    )


HINT = 0.001


def block_of(x):
    return x if isinstance(x, tuple) else (x, x.shape[0], 0)


def hint(flops, bytes_accessed):
    return pl.CostEstimate(
        flops=int(HINT * flops), bytes_accessed=int(HINT * bytes_accessed), transcendentals=0
    )


def rows_kernel(dot, epilogue, count, extra, *refs):
    left, w_ref = refs[:count], refs[count]
    extras = refs[count + 1 : count + 1 + extra]
    outs = refs[count + 1 + extra :]
    for i in range(count):
        epilogue(i, dot(left[i][...], w_ref[...]), extras, outs)


def rows_matmul(blocks, w, transposed, extras, outs, epilogue, name, tile=512):
    blocks = [block_of(x) for x in blocks]
    extras = [block_of(x) for x in extras]
    n = w.shape[0] if transposed else w.shape[1]
    k = w.shape[1] if transposed else w.shape[0]
    t = math.gcd(n, tile)
    w_spec = (
        pl.BlockSpec((t, k), lambda i: (i, 0)) if transposed else pl.BlockSpec((k, t), lambda i: (0, i))
    )
    rows = sum(x[1] for x in blocks)
    return pl.pallas_call(
        functools.partial(
            rows_kernel, dot_nt if transposed else dot_nn, epilogue, len(blocks), len(extras)
        ),
        grid=(n // t,),
        in_specs=[pl.BlockSpec((x[1], k), lambda i, at=x[2]: (at, 0)) for x in blocks]
        + [w_spec]
        + [pl.BlockSpec((x[1], t), lambda i, at=x[2]: (at, i)) for x in extras],
        out_specs=[pl.BlockSpec((r, t), lambda i: (0, i)) for r, _ in outs],
        out_shape=[jax.ShapeDtypeStruct((r, n), d) for r, d in outs],
        compiler_params=pltpu.CompilerParams(vmem_limit_bytes=52 * 1024 * 1024),
        cost_estimate=hint(2 * rows * n * k, 2 * n * k + 4 * rows * (n + k)),
        name=name,
    )(*[x[0] for x in blocks], w, *[x[0] for x in extras])


def plain(blocks, w, transposed, dtype, name):
    def epilogue(i, x, extras, outs):
        outs[i][...] = x.astype(dtype)

    outs = [(block_of(x)[1], dtype) for x in blocks]
    return rows_matmul(blocks, w, transposed, [], outs, epilogue, name)


def joined_rows(blocks, w, bias, name):
    sizes = [block_of(x)[1] for x in blocks]

    def epilogue(i, x, extras, outs):
        at = sum(sizes[:i])
        outs[0][at : at + sizes[i], :] = (x + extras[0][...]).astype(half)

    bias = bias.reshape(1, -1)
    return rows_matmul(blocks, w, False, [bias], [(sum(sizes), half)], epilogue, name)[0]


def up_gelu(blocks, w, bias, name):
    count = len(blocks)

    def epilogue(i, x, extras, outs):
        value, slope = gelu_both(x + extras[0][...])
        outs[i][...] = value.astype(half)
        outs[count + i][...] = slope.astype(half)

    outs = [(block_of(x)[1], half) for x in blocks] * 2
    out = rows_matmul(blocks, w, False, [bias.reshape(1, -1)], outs, epilogue, name)
    return out[:count], out[count:]


def hidden_back(blocks, w, slopes, name):
    def epilogue(i, x, extras, outs):
        x = x.astype(half).astype(single) * extras[i][...].astype(single)
        outs[i][...] = x.astype(half)

    outs = [(block_of(x)[1], half) for x in blocks]
    return rows_matmul(blocks, w, True, slopes, outs, epilogue, name)


def outer_kernel(count, *refs):
    out = refs[-1]
    total = None
    for i in range(count):
        x = dot_tn(refs[i][...], refs[count + i][...])
        total = x if total is None else total + x
    out[...] = total.astype(half)


def outer(left, right, name):
    left = [block_of(x) for x in left]
    right = [block_of(x) for x in right]
    m, n = left[0][0].shape[1], right[0][0].shape[1]
    tm = math.gcd(m, 1024)
    tn = n // 2 if n % 256 == 0 and n > 1024 else n
    rows = sum(x[1] for x in left)
    return pl.pallas_call(
        functools.partial(outer_kernel, len(left)),
        grid=(m // tm, n // tn),
        in_specs=[pl.BlockSpec((x[1], tm), lambda i, j, at=x[2]: (at, i)) for x in left]
        + [pl.BlockSpec((x[1], tn), lambda i, j, at=x[2]: (at, j)) for x in right],
        out_specs=pl.BlockSpec((tm, tn), lambda i, j: (i, j)),
        out_shape=jax.ShapeDtypeStruct((m, n), half),
        compiler_params=pltpu.CompilerParams(vmem_limit_bytes=52 * 1024 * 1024),
        cost_estimate=hint(2 * rows * m * n, 2 * rows * (m + n) + 2 * m * n),
        name=name,
    )(*[x[0] for x in left], *[x[0] for x in right])


def partner(mask):
    c = lax.axis_index("ctx")
    if mask == 1:
        return c + 1 - 2 * lax.rem(c, 2)
    return lax.rem(c + 2, 4) if mask == 2 else 3 - c


def greet(masks):
    barrier = pltpu.get_barrier_semaphore()
    for mask in masks:
        pl.semaphore_signal(
            barrier,
            inc=1,
            device_id={"ctx": partner(mask)},
            device_id_type=pl.DeviceIdType.MESH,
        )
    pl.semaphore_wait(barrier, len(masks))


class Moves:
    def __init__(self, send_sem, recv_sem):
        self.send_sem, self.recv_sem, self.used = send_sem, recv_sem, 0

    def start(self, src, dst, mask):
        copy = pltpu.make_async_remote_copy(
            src_ref=src,
            dst_ref=dst,
            send_sem=self.send_sem.at[self.used],
            recv_sem=self.recv_sem.at[self.used],
            device_id={"ctx": partner(mask)},
            device_id_type=pl.DeviceIdType.MESH,
        )
        self.used += 1
        copy.start()
        return copy


def multiply(lefts, w, transposed, extras, outs, epilogue, tile=512):
    k = lefts[0].shape[1]
    n = w.shape[0] if transposed else w.shape[1]
    t = math.gcd(n, tile)
    w_spec = (
        pl.BlockSpec((t, k), lambda i: (i, 0)) if transposed else pl.BlockSpec((k, t), lambda i: (0, i))
    )
    dot = dot_nt if transposed else dot_nn

    def body(*refs):
        rows_kernel(dot, epilogue, len(lefts), len(extras), *refs)

    pltpu.emit_pipeline(
        body,
        grid=(n // t,),
        in_specs=[pl.BlockSpec((x.shape[0], k), lambda i: (0, 0)) for x in lefts]
        + [w_spec]
        + [pl.BlockSpec((x.shape[0], t), lambda i: (0, i)) for x in extras],
        out_specs=[pl.BlockSpec((x.shape[0], t), lambda i: (0, i)) for x in outs],
    )(*lefts, w, *extras, *outs)


def store(i, x, extras, outs):
    outs[i][...] = x.astype(outs[i].dtype)


def store_sum(i, x, extras, outs):
    outs[i][...] = (x + extras[i][...].astype(single)).astype(outs[i].dtype)


def store_passed(i, x, extras, outs):
    if i in (1, 2):
        x = x + extras[i - 1][...].astype(single)
    outs[i][...] = x.astype(outs[i].dtype)


def store_hidden(i, x, extras, outs):
    outs[i][...] = (x.astype(half).astype(single) * extras[i][...].astype(single)).astype(half)


def outer_on(lefts, rights, out):
    m, n = out.shape
    tm = math.gcd(m, 1024)
    tn = n // 2 if n % 256 == 0 and n > 1024 else n

    def body(*refs):
        outer_kernel(len(lefts), *refs)

    pltpu.emit_pipeline(
        body,
        grid=(m // tm, n // tn),
        in_specs=[pl.BlockSpec((x.shape[0], tm), lambda i, j: (0, i)) for x in lefts]
        + [pl.BlockSpec((x.shape[0], tn), lambda i, j: (0, j)) for x in rights],
        out_specs=[pl.BlockSpec((tm, tn), lambda i, j: (i, j))],
    )(*lefts, *rights, out)


def halves(ref):
    n = ref.shape[0] // 2
    return ref.at[pl.ds(0, n)], ref.at[pl.ds(n, n)]


def moving_call(kernel, operands, outs, moves, call, flops, name):
    anywhere = pl.BlockSpec(memory_space=pl.ANY)
    sems = pltpu.SemaphoreType.DMA((moves,))
    return pl.pallas_call(
        kernel,
        in_specs=[anywhere] * len(operands),
        out_specs=[anywhere] * len(outs),
        out_shape=[jax.ShapeDtypeStruct(shape, dtype) for shape, dtype in outs],
        scratch_shapes=[sems, sems],
        compiler_params=pltpu.CompilerParams(
            collective_id=call, has_side_effects=True, vmem_limit_bytes=52 * 1024 * 1024
        ),
        cost_estimate=hint(flops, 0),
        name=name,
    )(*operands)


def store_biased(i, x, extras, outs):
    outs[i][...] = (x + extras[0][...]).astype(half)


def qkv_kernel(*refs):
    tok, gain, shift, a1, w_qkv, bias = refs[0:2], refs[2], refs[3], refs[4:7], refs[7], refs[8]
    dz_lo, dz_hi = refs[9:11]
    joined, far, one_lo, two_hi = refs[11], refs[12:14], refs[14], refs[15]
    moves = Moves(*refs[16:18])
    n, width = tok[0].shape
    greet((1, 2))
    copies = [moves.start(dz_lo, one_lo, 1), moves.start(dz_hi, two_hi, 2)]

    def norm(x_lo, x_hi, g, s, o_lo, o_hi):
        for x, o in ((x_lo, o_lo), (x_hi, o_hi)):
            normed, _ = norm_parts(x[...].astype(single))
            o[...] = (normed * g[...] + s[...]).astype(half)

    t = math.gcd(n, 64)
    block = pl.BlockSpec((t, width), lambda i: (i, 0))
    row = pl.BlockSpec((1, width), lambda i: (0, 0))
    pltpu.emit_pipeline(
        norm, grid=(n // t,), in_specs=[block, block, row, row], out_specs=[block, block]
    )(*tok, gain, shift, *far)
    lefts, outs, at = [*a1, *far], [], 0
    for x in lefts:
        outs.append(joined.at[pl.ds(at, x.shape[0])])
        at += x.shape[0]
    multiply(lefts, w_qkv, False, [bias], outs, store_biased)
    for copy in copies:
        copy.wait()


def qkv_forward(tok, gain, shift, a1, w_qkv, bias, dz_lo, dz_hi):
    n, width = tok[0].shape
    k = w_qkv.shape[1]
    outs = [((8 * n, k), half)] + [((n, width), half)] * 4
    out = moving_call(
        qkv_kernel,
        [*tok, gain.reshape(1, -1), shift.reshape(1, -1), *a1, w_qkv, bias.reshape(1, -1), dz_lo, dz_hi],
        outs,
        2,
        7,
        16 * n * width * k,
        "qkv",
    )
    return out[0], out[1:3], out[3:5]


def feed_pass(dz, slope, w_down, w_up, du, total, sums):
    n, width = dz[0].shape
    wide = w_down.shape[0]
    t = math.gcd(wide, 512)
    total[...] = jnp.zeros_like(total)

    def body(dz_lo, dz_hi, down, up, slope_lo, slope_hi, du_lo, du_hi):
        for i, x, s, d in ((0, dz_lo, slope_lo, du_lo), (1, dz_hi, slope_hi, du_hi)):
            grad = dot_nt(x[...], down[...]).astype(half).astype(single)
            grad = (grad * s[...].astype(single)).astype(half)
            d[...] = grad
            at = pl.ds(pl.multiple_of(pl.program_id(0) * t, t), t)
            sums[0:1, at] += jnp.sum(grad.astype(single), axis=0, keepdims=True)
            total[i * n : (i + 1) * n, :] += dot_nt(grad, up[...])

    pltpu.emit_pipeline(
        body,
        grid=(wide // t,),
        in_specs=[pl.BlockSpec((n, width), lambda i: (0, 0))] * 2
        + [pl.BlockSpec((t, width), lambda i: (i, 0)), pl.BlockSpec((width, t), lambda i: (0, i))]
        + [pl.BlockSpec((n, t), lambda i: (0, i))] * 2,
        out_specs=[pl.BlockSpec((n, t), lambda i: (0, i))] * 2,
    )(*dz, w_down, w_up, *slope, *du)


def feed_back_kernel(*refs):
    dz, slope, (w_down, w_up) = refs[0:8], refs[8:13], refs[13:15]
    a2, gb_far = refs[15:20], refs[20:22]
    du, own, land1, land2, up_grad, mix_x, mix_y, bias = refs[22:27], *refs[27:34]
    total, far, near, rest, from_x, from_y, mixed, sums = refs[34:42]
    moves = Moves(*refs[42:44])
    local = refs[44]
    sums[...] = jnp.zeros_like(sums)
    n = from_x.shape[0]
    lo, hi = pl.ds(0, n), pl.ds(n, n)
    (s1_lo, s1_hi), (s2_lo, s2_hi) = halves(slope[1]), halves(slope[2])
    (d1_lo, d1_hi), (d2_lo, d2_hi) = halves(du[1]), halves(du[2])
    (land1_lo, land1_hi), (land2_lo, land2_hi) = halves(land1), halves(land2)
    greet((1, 2))
    wide, width = w_down.shape
    t = math.gcd(width, 512)

    def mix(x_lo, x_hi, w):
        at = pl.ds(pl.multiple_of(pl.program_id(0) * t, t), t)
        mixed[0:n, at] = dot_nn(x_lo[...], w[...]).astype(half)
        mixed[n : 2 * n, at] = dot_nn(x_hi[...], w[...]).astype(half)

    pltpu.emit_pipeline(
        mix,
        grid=(width // t,),
        in_specs=[pl.BlockSpec((n, wide), lambda i: (0, 0))] * 2
        + [pl.BlockSpec((wide, t), lambda i: (0, i))],
    )(*gb_far, w_down)
    second = [moves.start(mixed.at[lo], mix_x, 1), moves.start(mixed.at[hi], mix_y, 2)]
    feed_pass(dz[6:8], slope[3:5], w_down, w_up, du[3:5], total, sums)
    far[...] = total[...].astype(half)
    first = [moves.start(far.at[lo], from_x, 1), moves.start(far.at[hi], from_y, 2)]
    feed_pass([dz[2], dz[5]], [s1_lo, s2_hi], w_down, w_up, [d1_lo, d2_hi], total, sums)
    near[...] = total[...].astype(half)
    second += [moves.start(near.at[lo], land1_lo, 1), moves.start(near.at[hi], land2_hi, 2)]
    feed_pass([dz[3], dz[4]], [s1_hi, s2_lo], w_down, w_up, [d1_hi, d2_lo], total, sums)
    for copy in first:
        copy.wait()
    rest[lo] = (total[lo] + from_y[...].astype(single)).astype(half)
    rest[hi] = (total[hi] + from_x[...].astype(single)).astype(half)
    second += [moves.start(rest.at[lo], land1_hi, 1), moves.start(rest.at[hi], land2_lo, 2)]
    feed_pass(dz[0:2], halves(slope[0]), w_down, w_up, halves(du[0]), total, sums)
    stores = [
        pltpu.make_async_copy(total, own, local.at[0]),
        pltpu.make_async_copy(sums, bias, local.at[1]),
    ]
    for copy in stores:
        copy.start()
    outer_on(a2, du, up_grad)
    for copy in stores + second:
        copy.wait()


def feed_back(dz, slope, w_down, w_up, a2, gb_far):
    n, width = dz[0].shape
    rows, wide = 2 * n, w_down.shape[0]
    anywhere = pl.BlockSpec(memory_space=pl.ANY)
    outs = [((r, wide), half) for r in (rows, rows, rows, n, n)]
    outs += [((rows, width), single)] + [((rows, width), half)] * 2
    outs += [((width, wide), half)] + [((n, width), half)] * 2 + [((8, wide), single)]
    sems = pltpu.SemaphoreType.DMA((8,))
    out = pl.pallas_call(
        feed_back_kernel,
        in_specs=[anywhere] * 22,
        out_specs=[anywhere] * len(outs),
        out_shape=[jax.ShapeDtypeStruct(shape, dtype) for shape, dtype in outs],
        scratch_shapes=[pltpu.VMEM((rows, width), single)]
        + [pltpu.VMEM((rows, width), half)] * 3
        + [pltpu.VMEM((n, width), half)] * 2
        + [pltpu.VMEM((rows, width), half), pltpu.VMEM((8, wide), single)]
        + [sems, sems, pltpu.SemaphoreType.DMA((2,))],
        compiler_params=pltpu.CompilerParams(
            collective_id=3, has_side_effects=True, vmem_limit_bytes=56 * 1024 * 1024
        ),
        cost_estimate=hint(26 * rows * width * wide, 0),
        name="feed_back",
    )(*dz, *slope, w_down, w_up, *a2, *gb_far)
    return out[5:8], out[8], out[9:11], out[11][0]


def heads_back_kernel(part, *refs):
    own, land1, land2, cot, y1, gain, w_out = refs[0:7]
    ob, gb1, gb2, w_down, mix_x, mix_y, down = refs[7:14]
    dy1, dz1, sums, got, out_grad = refs[14:19]
    mix, (one_lo, one_hi, two_lo, two_hi) = refs[19:23], refs[23:27]
    dz, w, stage = refs[27:30]
    moves = Moves(*refs[30:32])
    local = refs[32]
    rows, width = own.shape
    greet((1, 2, 3))
    load = pltpu.make_async_copy(w_out, w, local.at[0])
    load.start()
    down_lo, down_hi = halves(down)
    copies = [moves.start(down_lo, one_lo, 1), moves.start(down_hi, two_hi, 2)]
    copies += [moves.start(down_hi, one_hi, 1), moves.start(down_lo, two_lo, 2)]
    t = math.gcd(rows, 64)

    def norm(own, one, two, cot, y1, gain, dy1, dz1, sums):
        step = pl.program_id(0)
        grad = own[...] + one[...].astype(single) + two[...].astype(single)
        normed, inv = norm_parts(y1[...])
        dy = cot[...] + norm_back(normed, inv, gain[...], grad)
        low = dy.astype(half)
        dy1[...] = dy
        dz1[...] = low
        dz[pl.ds(pl.multiple_of(step * t, t), t), :] = low

        @pl.when(step == 0)
        def _():
            sums[...] = jnp.zeros_like(sums)

        sums[0:1] += jnp.sum(grad * normed, axis=0, keepdims=True)
        sums[1:2] += jnp.sum(grad, axis=0, keepdims=True)
        sums[2:3] += jnp.sum(low.astype(single), axis=0, keepdims=True)

    block = pl.BlockSpec((t, width), lambda i: (i, 0))
    pltpu.emit_pipeline(
        norm,
        grid=(rows // t,),
        in_specs=[block] * 5 + [pl.BlockSpec((1, width), lambda i: (0, 0))],
        out_specs=[block] * 2 + [pl.BlockSpec((8, width), lambda i: (0, 0))],
    )(own, land1, land2, cot, y1, gain, dy1, dz1, sums)
    load.wait()
    for mask in (3, 1, 2, 0):
        of = partner(mask) if mask else lax.axis_index("ctx")
        heads = w[pl.ds(pl.multiple_of(of * part, part), part), :]
        stage[mask] = dot_nt(dz[...], heads).astype(half)
        at = got.at[pl.ds(mask * rows, rows)]
        if mask:
            copies.append(moves.start(stage.at[mask], at, mask))
        else:
            keep = pltpu.make_async_copy(stage.at[0], at, local.at[1])
            keep.start()
    outer_on([ob], [dz1], out_grad)
    multiply(
        [*halves(gb1), *halves(gb2)],
        w_down,
        False,
        [mix_y, mix_x],
        mix,
        store_passed,
    )
    keep.wait()
    for copy in copies:
        copy.wait()


def heads_back(terms, cot, y1, gain, w_out, ob, gb1, gb2, w_down, mix_first, down):
    rows, width = cot.shape
    part = width // 4
    anywhere = pl.BlockSpec(memory_space=pl.ANY)
    sems = pltpu.SemaphoreType.DMA((7,))
    outs = [((rows, width), single), ((rows, width), half), ((8, width), single)]
    outs += [((4 * rows, part), half), ((width, width), half)]
    outs += [((rows // 2, width), half)] * 4 + [((down.shape[0] // 2, width), half)] * 4
    out = pl.pallas_call(
        functools.partial(heads_back_kernel, part),
        in_specs=[anywhere] * 14,
        out_specs=[anywhere] * len(outs),
        out_shape=[jax.ShapeDtypeStruct(shape, dtype) for shape, dtype in outs],
        scratch_shapes=[
            pltpu.VMEM((rows, width), half),
            pltpu.VMEM((width, width), half),
            pltpu.VMEM((4, rows, part), half),
            sems,
            sems,
            pltpu.SemaphoreType.DMA((2,)),
        ],
        compiler_params=pltpu.CompilerParams(
            collective_id=4, has_side_effects=True, vmem_limit_bytes=56 * 1024 * 1024
        ),
        cost_estimate=hint(10 * rows * width * width, 0),
        name="heads_back",
    )(*terms, cot, y1, gain.reshape(1, -1), w_out, ob, gb1, gb2, w_down, *mix_first, down)
    return out[0], out[2], out[3], out[4], out[5:9], out[9:13]


def qkv_back_kernel(*refs):
    dqkv, w_qkv = refs[0:2]
    a1, gb_own, w_down, one_hi, two_hi = refs[2:7], *refs[7:11]
    own, p3, p1, p2, from_x, from_y, land1, land2, qkv_grad, mix_own = refs[11:21]
    x_hi, y_hi = refs[21:23]
    moves = Moves(*refs[23:25])
    rows = own.shape[0]
    n = rows // 2

    def block(k):
        return dqkv.at[pl.ds(k * n, n)]

    greet((1, 2))
    output = [moves.start(one_hi, x_hi, 1), moves.start(two_hi, y_hi, 2)]
    (p3_lo, p3_hi), (p1_lo, p1_hi), (p2_lo, p2_hi) = halves(p3), halves(p1), halves(p2)
    (land1_lo, land1_hi), (land2_lo, land2_hi) = halves(land1), halves(land2)
    multiply([block(6), block(7)], w_qkv, True, [], [p3_lo, p3_hi], store)
    first = [moves.start(p3_lo, from_x, 1), moves.start(p3_hi, from_y, 2)]
    multiply([block(2), block(5)], w_qkv, True, [], [p1_lo, p2_hi], store)
    second = [moves.start(p1_lo, land1_lo, 1), moves.start(p2_hi, land2_hi, 2)]
    multiply([dqkv.at[pl.ds(0, rows)]], w_qkv, True, [], [own], store)
    multiply([gb_own], w_down, False, [], [mix_own], store)
    for copy in first:
        copy.wait()
    multiply([block(3), block(4)], w_qkv, True, [from_y, from_x], [p1_hi, p2_lo], store_sum)
    second += [moves.start(p1_hi, land1_hi, 1), moves.start(p2_lo, land2_lo, 2)]
    rights, at = [], 0
    for x in a1:
        rights.append(dqkv.at[pl.ds(at, x.shape[0])])
        at += x.shape[0]
    outer_on(a1, rights, qkv_grad)
    for copy in output + second:
        copy.wait()


def qkv_back(dqkv, w_qkv, a1, gb_own, w_down, one_hi, two_hi):
    rows, width = a1[0].shape
    wide = gb_own.shape[1]
    n = rows // 2
    outs = [((rows, width), single)] + [((rows, width), half)] * 3
    outs += [((n, width), half)] * 2 + [((rows, width), half)] * 2
    outs += [((width, dqkv.shape[1]), half), ((rows, width), single)] + [((n, width), half)] * 2
    out = moving_call(
        qkv_back_kernel,
        [dqkv, w_qkv, *a1, gb_own, w_down, one_hi, two_hi],
        outs,
        8,
        5,
        16 * rows * width * dqkv.shape[1] + 2 * rows * width * wide,
        "qkv_back",
    )
    return out[0], out[6:8], out[8], out[9], out[10:12]


def lay_out_kernel(axis, layout, c_ref, *refs):
    out = refs[-1]
    for (j, row), ref in zip(layout, refs):
        x = ref[...].astype(single)
        r, w = x.shape
        if axis == 0:
            n = sum(ref.shape[0] for (k, _), ref in zip(layout, refs) if k == j)
            out[pl.ds(pl.multiple_of((c_ref[0] ^ j) * n + row, r), r), :] = x
        else:
            out[row : row + r, pl.ds(pl.multiple_of((c_ref[0] ^ j) * w, w), w)] = x


def lay_out(axis, pieces, c, groups):
    count = len(pieces)
    r = sum(x.shape[0] for x in pieces[0])
    n = pieces[0][0].shape[1]
    w = n // groups
    if w % 128:
        whole = xor_order([jnp.concatenate(p, axis=0).astype(single) for p in pieces], c)
        whole = jnp.stack([p.reshape(r, groups, w) for p in whole], axis=2)
        return whole.reshape(r, count * n)
    layout, blocks = [], []
    for j, p in enumerate(pieces):
        row = 0
        for x in p:
            layout.append((j, row))
            blocks.append(x)
            row += x.shape[0]
    out = (count * r, w) if axis == 0 else (r, count * w)
    return pl.pallas_call(
        functools.partial(lay_out_kernel, axis, layout),
        grid_spec=pltpu.PrefetchScalarGridSpec(
            num_scalar_prefetch=1,
            grid=(groups,),
            in_specs=[pl.BlockSpec((x.shape[0], w), lambda k, c: (0, k)) for x in blocks],
            out_specs=pl.BlockSpec(out, lambda k, c: (0, k)),
        ),
        out_shape=jax.ShapeDtypeStruct((out[0], out[1] * groups), single),
        compiler_params=pltpu.CompilerParams(vmem_limit_bytes=48 * 1024 * 1024),
        cost_estimate=hint(0, 6 * r * n * count),
        name="lay_out",
    )(c.reshape(1), *blocks)


def gather_small_kernel(nf, x_ref, o_ref, send_sem, recv_sem):
    f = lax.axis_index("fsdp")
    barrier = pltpu.get_barrier_semaphore()
    for d in range(1, nf):
        pl.semaphore_signal(
            barrier,
            inc=1,
            device_id={"fsdp": lax.rem(f + d, nf)},
            device_id_type=pl.DeviceIdType.MESH,
        )
    pl.semaphore_wait(barrier, nf - 1)
    copies = []
    for d in range(1, nf):
        copies.append(
            pltpu.make_async_remote_copy(
                src_ref=x_ref,
                dst_ref=o_ref.at[f],
                send_sem=send_sem.at[d],
                recv_sem=recv_sem.at[d],
                device_id={"fsdp": lax.rem(f + d, nf)},
                device_id_type=pl.DeviceIdType.MESH,
            )
        )
        copies[-1].start()
    o_ref[f] = x_ref[...]
    for copy in copies:
        copy.wait()


def gather_small(x, nf):
    return pl.pallas_call(
        functools.partial(gather_small_kernel, nf),
        out_shape=jax.ShapeDtypeStruct((nf,) + x.shape, single),
        in_specs=[pl.BlockSpec(memory_space=pltpu.VMEM)],
        out_specs=pl.BlockSpec(memory_space=pltpu.VMEM),
        scratch_shapes=[pltpu.SemaphoreType.DMA((nf,)), pltpu.SemaphoreType.DMA((nf,))],
        compiler_params=pltpu.CompilerParams(collective_id=1, has_side_effects=True),
        name="gather_small",
    )(x)


def reduce_small_kernel(nf, nc, x_ref, o_ref, land, stage, send_sem, recv_sem):
    f = lax.axis_index("fsdp")
    c = lax.axis_index("ctx")
    barrier = pltpu.get_barrier_semaphore()
    for d in range(1, nf):
        pl.semaphore_signal(
            barrier,
            inc=1,
            device_id={"fsdp": lax.rem(f + d, nf)},
            device_id_type=pl.DeviceIdType.MESH,
        )
    for d in range(1, nc):
        pl.semaphore_signal(
            barrier,
            inc=1,
            device_id={"ctx": lax.rem(c + d, nc)},
            device_id_type=pl.DeviceIdType.MESH,
        )
    pl.semaphore_wait(barrier, nf + nc - 2)
    copies = []
    for d in range(1, nf):
        to = lax.rem(f + d, nf)
        copies.append(
            pltpu.make_async_remote_copy(
                src_ref=x_ref.at[to],
                dst_ref=land.at[d],
                send_sem=send_sem.at[d],
                recv_sem=recv_sem.at[d],
                device_id={"fsdp": to},
                device_id_type=pl.DeviceIdType.MESH,
            )
        )
        copies[-1].start()
    total = x_ref[f]
    for d in range(1, nf):
        copies[d - 1].wait()
        total = total + land[d]
    stage[0] = total
    copies = []
    for d in range(1, nc):
        copies.append(
            pltpu.make_async_remote_copy(
                src_ref=stage.at[0],
                dst_ref=stage.at[d],
                send_sem=send_sem.at[nf + d],
                recv_sem=recv_sem.at[nf + d],
                device_id={"ctx": lax.rem(c + d, nc)},
                device_id_type=pl.DeviceIdType.MESH,
            )
        )
        copies[-1].start()
    for d in range(1, nc):
        copies[d - 1].wait()
        total = total + stage[d]
    o_ref[...] = total


def reduce_small(x, nf, nc, call):
    block = x.shape[1:]
    sems = pltpu.SemaphoreType.DMA((nf + nc,))
    return pl.pallas_call(
        functools.partial(reduce_small_kernel, nf, nc),
        out_shape=jax.ShapeDtypeStruct(block, single),
        in_specs=[pl.BlockSpec(memory_space=pltpu.VMEM)],
        out_specs=pl.BlockSpec(memory_space=pltpu.VMEM),
        scratch_shapes=[
            pltpu.VMEM((nf,) + block, single),
            pltpu.VMEM((nc,) + block, single),
            sems,
            sems,
        ],
        compiler_params=pltpu.CompilerParams(collective_id=call, has_side_effects=True),
        name="reduce_small",
    )(x)


def per_device(
    tokens,
    cotangent,
    lengths,
    span_place,
    ln1_gain,
    ln1_shift,
    qkv_weight,
    q_bias,
    v_bias,
    out_weight,
    out_bias,
    ln2_gain,
    ln2_shift,
    up_weight,
    up_bias,
    down_weight,
    down_bias,
):
    rows, width = tokens.shape
    CTX = lax.axis_size("ctx")
    c = lax.axis_index("ctx")
    f = lax.axis_index("fsdp")
    nf = lax.axis_size("fsdp")
    wide = up_weight.shape[1]
    part = width // CTX
    heads = HEADS // CTX
    scale = 1.0 / math.sqrt(width // HEADS)
    shard = width // nf
    fpart = wide // nf // CTX
    wpart = wide // CTX

    def columns(x, width_each, stride, count):
        return jnp.concatenate(
            [
                lax.dynamic_slice_in_dim(x, k * stride + c * width_each, width_each, axis=1)
                for k in range(count)
            ],
            axis=1,
        )

    def after(x, *others):
        return lax.optimization_barrier((x, others))[0]

    def pick(x, axis):
        return lax.dynamic_index_in_dim(x, c, axis, keepdims=False)

    def gather_f(x):
        return lax.all_gather(x, "fsdp", axis=0, tiled=True)

    qkv_own = columns(qkv_weight, part, width, 3)
    up_own = columns(up_weight, fpart, wide // nf, nf)
    down_own = lax.dynamic_slice_in_dim(down_weight, c * fpart, fpart, axis=0)
    w_qkv = gather_f(qkv_own.astype(half))
    up_own, down_own = up_own.astype(half), down_own.astype(half)
    small = jnp.concatenate(
        [ln1_gain, ln1_shift, q_bias, v_bias, out_bias, ln2_gain, ln2_shift, down_bias, up_bias]
    )
    small_len = small.shape[0]
    small = jnp.pad(small, (0, -small_len % 1024)).reshape(-1, 128)
    small_all = gather_small(small, nf).reshape(nf, -1)[:, :small_len]
    small_all = small_all.astype(half).astype(single)

    def vector(k):
        return small_all[:, k * shard : (k + 1) * shard].reshape(width)

    gain1, shift1, bias_q, bias_v, bias_o, gain2, shift2, bias_d = [vector(k) for k in range(8)]
    bias_u = pick(small_all[:, 8 * shard :].reshape(nf, CTX, fpart), 1).reshape(wpart)
    bias_qkv = jnp.concatenate(
        [pick(bias_q.reshape(CTX, part), 0), jnp.zeros((part,), single), pick(bias_v.reshape(CTX, part), 0)]
    )
    w_out = gather_f(out_weight.astype(half))

    per = rows // SPAN
    table = jnp.arange(CTX * per, dtype=jnp.int32)
    source = ((table // per) ^ c) * per + table % per
    place = jnp.sum(jnp.where(source[:, None] == table[None, :], span_place[0][None, :], 0), axis=1)
    inv = jnp.sum(jnp.where(place[None, :] == table[:, None], table[None, :], 0), axis=1)
    slopes = 2.0 ** (-8.0 * ((c * heads + jnp.arange(heads)).astype(single) + 1.0) / HEADS)

    def flat(pieces):
        return [x for p in pieces for x in p]

    def scatter_f(x):
        return lax.psum_scatter(x, "fsdp", scatter_dimension=0, tiled=True)

    far = CTX - 1
    mid = list(range(1, far))

    def first_norm(x):
        normed, _ = norm_parts(x.astype(single))
        return (normed * gain1 + shift1).astype(half)

    n = rows // 2
    dz2_lo, dz2_hi = cotangent[:n].astype(half), cotangent[n:].astype(half)
    early = (small_all, place, inv, slopes, up_own, down_own, dz2_lo, dz2_hi)
    early, tok_near = after((early, gather_first(tokens)))
    small_all, place, inv, slopes, up_own, down_own, dz2_lo, dz2_hi = early
    tok = gather_second(tokens, tok_near)
    near = [[first_norm(x) for x in p] for p in tok[:far]]
    tok = after(tok, near)
    if CTX != 4:
        dz2_own = jnp.concatenate([dz2_lo, dz2_hi], axis=0)
        dz2_rest = gather_first(dz2_own)
    w_up = gather_f(after(up_own, tok))
    a1 = flat(near)
    if CTX == 4:
        joined, a1_far, dz2_first = qkv_forward(
            tok[far], gain1, shift1, a1, w_qkv, bias_qkv, dz2_lo, dz2_hi
        )
        a1 = a1 + list(a1_far)
        dz2_rest = after((dz2_hi, dz2_lo), joined)
        dz2_rest = [swap(dz2_rest[0], 1), swap(dz2_rest[1], 2)]
    else:
        a1 = a1 + [first_norm(x) for x in tok[far]]
        joined = joined_rows(a1, w_qkv, bias_qkv, "qkv")
    w_down = gather_f(after(down_own, joined))
    attended = attn_forward(joined, inv, slopes, heads, scale)
    mine = [attended[j * rows : (j + 1) * rows] for j in range(CTX)]
    mine = after(mine, dz2_rest)
    mine = [mine[0]] + [swap(mine[j], j) for j in range(1, CTX)]
    ob = after(jnp.concatenate(xor_order(mine, c), axis=1))
    y1 = tokens.astype(single) + dot_nn(ob, w_out) + bias_o

    normed2, inv2 = norm_parts(y1)
    a2_own = (normed2 * gain2 + shift2).astype(half)
    gb, slope = [None] * CTX, [None] * CTX
    gb[0], slope[0] = up_gelu([a2_own], w_up, bias_u, "up_gelu_0")
    last = gb[0]
    a2_near = gather_first(a2_own)
    a2 = gather_second(a2_own, a2_near)
    if CTX == 4:
        one_lo, two_hi = after(dz2_first, a2_near)
        one_hi, two_lo = dz2_rest
        dz2 = [[dz2_lo, dz2_hi], [one_lo, one_hi], [two_lo, two_hi], [swap(one_lo, 2), swap(two_hi, 1)]]
    else:
        dz2 = [[dz2_own]] + [[x] for x in dz2_rest]
    for j in range(1, CTX):
        gb[j], slope[j] = up_gelu(after(a2[j], last), w_up, bias_u, f"up_gelu_{j}")
        last = gb[j]
    gb_blocks = flat(gb)
    if CTX == 4:
        gb_blocks = [(g[0], n, i) for g in gb[:far] for i in (0, 1)] + list(gb[far])
    down_grad = outer(gb_blocks, flat(dz2), "down_grad")
    down_part = scatter_f(down_grad)
    w_down = after(w_down, down_grad)

    du, dh2, mix = [None] * CTX, [None] * CTX, [None] * CTX
    if CTX == 4:
        dh2, up_grad, mix_first, up_bias_grad = feed_back(
            flat(dz2), flat(slope), w_down, w_up, flat(a2), gb[far]
        )
    else:
        for j in range(CTX):
            du[j] = hidden_back(dz2[j], w_down, slope[j], f"du_{j}")
            dh2[j] = plain(du[j], w_up, True, half if j else single, f"dh2_{j}")[0]
        arrived = scatter_send(dh2[1:])
        dh2 = dh2[0]
        up_grad = outer(flat(a2), flat(du), "up_grad")
        up_bias_grad = sum(jnp.sum(x.astype(single), axis=0) for x in flat(du))
        mix[far] = plain(gb[far], w_down, False, half, "mix_far")[0]
        dh2 = total_of(dh2, arrived)
    up_part = scatter_f(up_grad)
    if CTX == 4:
        dy1, sums2, dattn, out_grad, mix, down_near = heads_back(
            dh2, cotangent, y1, gain2, w_out, ob, gb[1][0], gb[2][0], w_down, mix_first, down_part
        )
        one_lo, one_hi, two_lo, two_hi = mix
        gain2_grad, shift2_grad, out_bias_grad = sums2[0], sums2[1], sums2[2]
    else:
        gain2_grad = jnp.sum(dh2 * normed2, axis=0)
        shift2_grad = jnp.sum(dh2, axis=0)
        dy1 = cotangent + norm_back(normed2, inv2, gain2, dh2)
        dz1 = dy1.astype(half)
        dattn = dot_nt(dz1, w_out).astype(half)
        out_bias_grad = jnp.sum(dz1.astype(single), axis=0)
        dattn = xor_order([dattn[:, s * part : (s + 1) * part] for s in range(CTX)], c)
        dattn = [dattn[0]] + [swap(dattn[j], j) for j in range(1, CTX)]
        dattn = jnp.concatenate(dattn, axis=0)
        out_grad = outer([ob], [dz1], "out_grad")
        for j in mid:
            mix[j] = plain(gb[j], w_down, False, half, f"mix_{j}")[0]
        down_near = gather_first(down_part)
    out_part = scatter_f(out_grad)
    dqkv, sum_q, sum_v = attn_backward(joined, dattn, inv, slopes, heads, scale)
    sum_q, sum_v = sum_q[0] + sum_q[8], sum_v[0] + sum_v[8]
    if CTX == 4:
        lows = [swap(one_lo, 1), swap(two_lo, 2)]
        down_far = [swap(down_near[0], 2), swap(down_near[3], 1)]
        down_out = [[down_part], list(down_near[0:2]), list(down_near[2:4]), down_far]
        dqkv = after(dqkv, lows, up_part, down_far)
        dh1, arrived, qkv_grad, mix_own, highs = qkv_back(
            dqkv, w_qkv, a1, gb[0][0], w_down, one_hi, two_hi
        )
    else:
        dh1 = [
            plain([(dqkv, rows, j)], w_qkv, True, half if j else single, f"dh1_{j}")[0]
            for j in range(CTX)
        ]
        arrived = scatter_send(dh1[1:])
        dh1 = dh1[0]
        qkv_grad = outer(a1, [(dqkv, rows, j) for j in range(CTX)], "qkv_grad")
        mix_own = plain(gb[0], w_down, False, single, "mix_0")[0]
        down_out = gather_second(down_part, down_near)
    qkv_part = scatter_f(qkv_grad)

    up_own = after(up_part, arrived)
    up_near = gather_first(up_own)
    out_first = []
    if CTX == 4:
        k = out_part.shape[0] // 2
        out_lo, out_hi = after(out_part, arrived)[:k], after(out_part, arrived)[k:]
        out_first = [swap(out_lo, 1), swap(out_hi, 2)]
    waiting = (dh1, mix_own, flat(dz2[:1]), down_out)
    dh1, mix_own, dz2_own, down_out = after(waiting, out_part)
    down_out = lay_out(0, down_out, c, width // min(width, 512))
    dh1 = total_of(dh1, arrived)
    if CTX == 4:
        mixed = y1 + bias_d + mix_own
        mixed = jnp.concatenate([total_of(mixed[:n], lows), total_of(mixed[n:], highs)])
    else:
        mixed = total_of(y1 + bias_d + mix_own, scatter_send(mix[1:]))
    down_bias_grad = sum(jnp.sum(x.astype(single), axis=0) for x in dz2_own)
    normed1_own, inv1_own = norm_parts(tokens.astype(single))
    gain1_grad = jnp.sum(dh1 * normed1_own, axis=0)
    shift1_grad = jnp.sum(dh1, axis=0)
    input_grad = dy1 + norm_back(normed1_own, inv1_own, gain1, dh1)

    done = (down_out, input_grad, mixed, down_bias_grad, gain1_grad, shift1_grad)
    up_near, out_first = after((up_near, out_first), done)
    if CTX == 4:
        out_lo = (out_lo.astype(single) + out_first[0].astype(single)).astype(half)
        out_hi = (out_hi.astype(single) + out_first[1].astype(single)).astype(half)
        out_lo, out_hi, up_near = after((out_lo, out_hi, up_near))
        out_second = [(out_lo, swap(out_lo, 2)), (out_hi, swap(out_hi, 1))]
    up_out = gather_second(up_own, up_near)
    up_out = lay_out(1, up_out, c, nf)
    def spread(x, inner):
        x = x.reshape(-1, 1, inner)
        mask = (jnp.arange(CTX) == c)[None, :, None]
        return jnp.where(mask, x, 0.0).reshape(-1)

    def reduced(items, call):
        sizes = [x.shape[0] // nf for x in items]
        x = jnp.concatenate([x.reshape(nf, -1) for x in items], axis=1)
        x = jnp.pad(x, ((0, 0), (0, -x.shape[1] % 1024))).reshape(nf, -1, 128)
        x = reduce_small(x, nf, CTX, call).reshape(-1)
        out, at = [], 0
        for n in sizes:
            out.append(x[at : at + n])
            at += n
        return out

    sums_in = [out_bias_grad, gain2_grad, shift2_grad, down_bias_grad, spread(up_bias_grad, fpart)]
    sums_in += [gain1_grad, shift1_grad, spread(sum_q, part), spread(sum_v, part)]
    qkv_part = after(qkv_part, up_out)
    qkv_near = gather_first(qkv_part)
    sums_in[5] = after(sums_in[5], qkv_part)
    sums_out = reduced(sums_in, 2)
    if CTX == 4:
        out_second = after(out_second, sums_out)
        out_out = [x.astype(single) + y.astype(single) for x, y in out_second]
        out_out = jnp.concatenate(out_out, axis=0)
    else:
        bit = 1
        while bit < CTX:
            out_out = out_part.astype(single) + swap(out_part, bit).astype(single)
            out_part = out_out.astype(half)
            bit *= 2

    qkv_near = after(qkv_near, sums_out)
    qkv_out = lay_out(1, gather_second(qkv_part, qkv_near), c, 3)
    out_bias_out, gain2_out, shift2_out, down_bias_out, up_bias_out = sums_out[:5]
    gain1_out, shift1_out, q_bias_out, v_bias_out = sums_out[5:]
    return (
        mixed,
        input_grad,
        gain1_out,
        shift1_out,
        qkv_out,
        q_bias_out,
        v_bias_out,
        out_out,
        out_bias_out,
        gain2_out,
        shift2_out,
        up_out,
        up_bias_out,
        down_out,
        down_bias_out,
    )


def solution(mesh):
    rows, flat = P(("ctx", "fsdp"), None), P("fsdp")
    mat = P("fsdp", None)
    in_specs = (
        rows,
        rows,
        mat,
        mat,
        flat,
        flat,
        mat,
        flat,
        flat,
        mat,
        flat,
        flat,
        flat,
        mat,
        flat,
        mat,
        flat,
    )
    out_specs = (
        rows,
        rows,
        flat,
        flat,
        mat,
        flat,
        flat,
        mat,
        flat,
        flat,
        flat,
        mat,
        flat,
        mat,
        flat,
    )
    return jax.shard_map(
        per_device, mesh=mesh, in_specs=in_specs, out_specs=out_specs, check_vma=False
    )
```

```python
import functools
import math

import jax
import jax.numpy as jnp
from jax import lax
from jax.experimental import pallas as pl
from jax.experimental.pallas import tpu as pltpu
from jax.sharding import PartitionSpec as P

HEADS = 16
SPAN = 128
SEQ_BLOCKS = 8

norm_eps = 1e-05
gelu_coef = 0.7978845608028654
LOG2E = 1.4426950408889634

half = jnp.bfloat16
single = jnp.float32


def dot_nn(a, b):
    return lax.dot_general(a, b, (((1,), (0,)), ((), ())), preferred_element_type=single)


def dot_nt(a, b):
    return lax.dot_general(a, b, (((1,), (1,)), ((), ())), preferred_element_type=single)


def dot_tn(a, b):
    return lax.dot_general(a, b, (((0,), (0,)), ((), ())), preferred_element_type=single)


def norm_parts(values):
    center = values - jnp.mean(values, axis=-1, keepdims=True)
    spread = jnp.mean(center * center, axis=-1, keepdims=True)
    inv = lax.rsqrt(spread + norm_eps)
    return center * inv, inv


def norm_back(normed, inv, gain, grad):
    dn = grad * gain
    return inv * (
        dn
        - jnp.mean(dn, axis=-1, keepdims=True)
        - normed * jnp.mean(dn * normed, axis=-1, keepdims=True)
    )


def gelu_both(v):
    t = jnp.tanh(gelu_coef * (v + 0.044715 * v * v * v))
    value = 0.5 * v * (1.0 + t)
    slope = 0.5 * (1.0 + t) + 0.5 * v * (1.0 - t * t) * gelu_coef * (1.0 + 3 * 0.044715 * v * v)
    return value, slope


def swap(x, mask):
    n = lax.axis_size("ctx")
    return lax.ppermute(x, "ctx", [(i, i ^ mask) for i in range(n)])


def gather_first(x):
    count = lax.axis_size("ctx")
    return [swap(x, j) for j in range(1, 3 if count == 4 else count)]


def gather_second(x, arrived):
    if lax.axis_size("ctx") != 4:
        return [[x]] + [[p] for p in arrived]
    one, two = arrived
    n = x.shape[0] // 2
    return [[x], [one], [two], [swap(one[:n], 2), swap(two[n:], 1)]]


def gather_ctx(x):
    return gather_second(x, gather_first(x))


def scatter_first(far):
    if lax.axis_size("ctx") != 4:
        return None
    return swap(far[0], 1), swap(far[1], 2)


def scatter_second(pieces, first):
    if first is None:
        return pieces[1:]
    p1, p2 = pieces[1], pieces[2]
    n = p1.shape[0] // 2
    from_x, from_y = first
    p1 = jnp.concatenate(
        [p1[:n], (p1[n:].astype(single) + from_y.astype(single)).astype(half)], axis=0
    )
    p2 = jnp.concatenate(
        [(p2[:n].astype(single) + from_x.astype(single)).astype(half), p2[n:]], axis=0
    )
    return [p1, p2]


def scatter_send(sent):
    return [swap(x, j + 1) for j, x in enumerate(sent)]


def total_of(own, arrived):
    for x in arrived:
        own = own + x.astype(single)
    return own


def xor_order(items, c):
    bit = 1
    while bit < len(items):
        on = (c & bit) == bit
        items = [jnp.where(on, items[i ^ bit], items[i]) for i in range(len(items))]
        bit *= 2
    return items


TILE = 256


def attn_scores(q_refs, k_refs, i, scale, slope):
    q = jnp.concatenate([q_refs[2 * i][...], q_refs[2 * i + 1][...]], axis=0)
    k = jnp.concatenate([r[...] for r in k_refs[: 2 * i + 2]], axis=0)
    n = TILE * (i + 1)
    col = lax.broadcasted_iota(jnp.int32, (1, n), 1) - (n - 1)
    s = dot_nt(q, k) * (scale * LOG2E) + (slope * LOG2E) * col.astype(single)
    row_at = lax.broadcasted_iota(jnp.int32, (TILE, TILE), 0)
    col_at = lax.broadcasted_iota(jnp.int32, (TILE, TILE), 1)
    last = jnp.where(col_at <= row_at, s[:, n - TILE :], -1e30)
    s = last if i == 0 else jnp.concatenate([s[:, : n - TILE], last], axis=1)
    e = jnp.exp2(s - jnp.max(s, axis=1, keepdims=True))
    return q, k, e, 1.0 / jnp.sum(e, axis=1, keepdims=True)


class Rows:
    def __init__(self, inv_ref, stage, out, sems, kinds):
        self.inv, self.stage, self.out, self.sems, self.kinds = inv_ref, stage, out, sems, kinds
        self.heads = pl.num_programs(1)
        self.step = pl.program_id(0) * self.heads + pl.program_id(1)
        self.slot = lax.rem(self.step, 2)

    def copies(self, step):
        slot = lax.rem(step, 2)
        seq, head = step // self.heads, lax.rem(step, self.heads)
        for kind in range(self.kinds):
            col = pl.multiple_of((kind * self.heads + head) * 128, 128)
            for j in range(SEQ_BLOCKS):
                row = pl.multiple_of(self.inv[seq * SEQ_BLOCKS + j] * SPAN, SPAN)
                yield pltpu.make_async_copy(
                    self.stage.at[slot, kind, pl.ds(j * SPAN, SPAN)],
                    self.out.at[pl.ds(row, SPAN), pl.ds(col, 128)],
                    self.sems.at[slot, kind * SEQ_BLOCKS + j],
                )

    def wait(self, step):
        for copy in self.copies(step):
            copy.wait()

    def open(self):
        @pl.when(self.step >= 2)
        def _():
            self.wait(self.step - 2)

    def close(self):
        for copy in self.copies(self.step):
            copy.start()

        @pl.when(self.step == 2 * self.heads - 1)
        def _():
            self.wait(self.step - 1)
            self.wait(self.step)


def attn_fwd_kernel(scale, inv_ref, slope_ref, *refs):
    q_refs, k_refs, v_refs = refs[:8], refs[8:16], refs[16:24]
    out, stage, sems = refs[24:]
    slope = slope_ref[pl.program_id(1)]
    rows = Rows(inv_ref, stage, out, sems, 1)
    rows.open()
    for i in range(4):
        q, k, e, r = attn_scores(q_refs, k_refs, i, scale, slope)
        v = jnp.concatenate([x[...] for x in v_refs[: 2 * i + 2]], axis=0)
        o = dot_nn((e * r).astype(half), v)
        stage[rows.slot, 0, TILE * i : TILE * (i + 1), :] = o.astype(half)
    rows.close()


def attn_bwd_kernel(scale, inv_ref, slope_ref, *refs):
    q_refs, k_refs, v_refs, g_refs = refs[:8], refs[8:16], refs[16:24], refs[24:32]
    out, sum_q, sum_v, stage, sems, dk_acc, dv_acc = refs[32:]
    slope = slope_ref[pl.program_id(1)]
    rows = Rows(inv_ref, stage, out, sems, 3)
    rows.open()
    total_q = jnp.zeros((1, 128), single)
    for i in (3, 2, 1, 0):
        q, k, e, r = attn_scores(q_refs, k_refs, i, scale, slope)
        n = TILE * (i + 1)
        v = jnp.concatenate([x[...] for x in v_refs[: 2 * i + 2]], axis=0)
        g = jnp.concatenate([g_refs[2 * i][...], g_refs[2 * i + 1][...]], axis=0)
        p = e * r
        dp = dot_nt(g, v)
        delta = jnp.sum(p * dp, axis=1, keepdims=True)
        ds = (p * (dp - delta)).astype(half)
        pb = p.astype(half)
        dq = (dot_nn(ds, k) * scale).astype(half)
        stage[rows.slot, 0, TILE * i : TILE * (i + 1), :] = dq
        total_q = total_q + jnp.sum(dq.astype(single), axis=0, keepdims=True)
        dk = dot_tn(ds, q)
        dv = dot_tn(pb, g)
        if i == 3:
            dk_acc[...] = dk
            dv_acc[...] = dv
        else:
            dk_acc[:n, :] += dk
            dv_acc[:n, :] += dv
    stage[rows.slot, 1] = (dk_acc[...] * scale).astype(half)
    dv = dv_acc[...].astype(half)
    stage[rows.slot, 2] = dv
    total_v = jnp.sum(dv.astype(single), axis=0, keepdims=True)
    sum_q[...] = jnp.broadcast_to(total_q, sum_q.shape)
    sum_v[...] = jnp.broadcast_to(total_v, sum_v.shape)
    rows.close()


def block_specs(offset):
    def one(j):
        return pl.BlockSpec(
            (SPAN, 128), lambda s, h, inv, slope: (inv[s * SEQ_BLOCKS + j], offset + h)
        )

    return [one(j) for j in range(SEQ_BLOCKS)]


def attn_call(kernel, kinds, joined, extra, extra_specs, scratch, inv, slopes, heads, cost, name):
    rows = joined.shape[0]
    tops = [pl.BlockSpec((8, 128), lambda s, h, inv, slope: (s, h))] * (2 if kinds == 3 else 0)
    specs = block_specs(0) + block_specs(heads) + block_specs(2 * heads) + extra_specs
    return pl.pallas_call(
        kernel,
        grid_spec=pltpu.PrefetchScalarGridSpec(
            num_scalar_prefetch=2,
            grid=(2, heads),
            in_specs=specs,
            out_specs=[pl.BlockSpec(memory_space=pl.ANY)] + tops,
            scratch_shapes=[
                pltpu.VMEM((2, kinds, rows // 2, 128), half),
                pltpu.SemaphoreType.DMA((2, kinds * SEQ_BLOCKS)),
            ]
            + scratch,
        ),
        out_shape=[jax.ShapeDtypeStruct((rows, kinds * heads * 128), half)]
        + [jax.ShapeDtypeStruct((16, heads * 128), single)] * len(tops),
        compiler_params=pltpu.CompilerParams(vmem_limit_bytes=48 * 1024 * 1024),
        cost_estimate=cost,
        name=name,
    )(inv, slopes, *([joined] * 24), *extra)


def attn_forward(joined, inv, slopes, heads, scale):
    kernel = functools.partial(attn_fwd_kernel, scale)
    cost = hint(20 * 10**9, joined.shape[0] * heads * 128 * 8)
    return attn_call(
        kernel, 1, joined, [], [], [], inv, slopes, heads, cost, "attn_forward"
    )[0]


def attn_backward(joined, grad, inv, slopes, heads, scale):
    kernel = functools.partial(attn_bwd_kernel, scale)
    cost = hint(40 * 10**9, joined.shape[0] * heads * 128 * 14)
    sums = [pltpu.VMEM((joined.shape[0] // 2, 128), single)] * 2
    return attn_call(
        kernel,
        3,
        joined,
        [grad] * 8,
        block_specs(0),
        sums,
        inv,
        slopes,
        heads,
        cost,
        "attn_backward",
    )


HINT = 0.001


def block_of(x):
    return x if isinstance(x, tuple) else (x, x.shape[0], 0)


def hint(flops, bytes_accessed):
    return pl.CostEstimate(
        flops=int(HINT * flops), bytes_accessed=int(HINT * bytes_accessed), transcendentals=0
    )


def rows_kernel(dot, epilogue, count, extra, *refs):
    left, w_ref = refs[:count], refs[count]
    extras = refs[count + 1 : count + 1 + extra]
    outs = refs[count + 1 + extra :]
    for i in range(count):
        epilogue(i, dot(left[i][...], w_ref[...]), extras, outs)


def rows_matmul(blocks, w, transposed, extras, outs, epilogue, name, tile=512):
    blocks = [block_of(x) for x in blocks]
    extras = [block_of(x) for x in extras]
    n = w.shape[0] if transposed else w.shape[1]
    k = w.shape[1] if transposed else w.shape[0]
    t = math.gcd(n, tile)
    w_spec = (
        pl.BlockSpec((t, k), lambda i: (i, 0)) if transposed else pl.BlockSpec((k, t), lambda i: (0, i))
    )
    rows = sum(x[1] for x in blocks)
    return pl.pallas_call(
        functools.partial(
            rows_kernel, dot_nt if transposed else dot_nn, epilogue, len(blocks), len(extras)
        ),
        grid=(n // t,),
        in_specs=[pl.BlockSpec((x[1], k), lambda i, at=x[2]: (at, 0)) for x in blocks]
        + [w_spec]
        + [pl.BlockSpec((x[1], t), lambda i, at=x[2]: (at, i)) for x in extras],
        out_specs=[pl.BlockSpec((r, t), lambda i: (0, i)) for r, _ in outs],
        out_shape=[jax.ShapeDtypeStruct((r, n), d) for r, d in outs],
        compiler_params=pltpu.CompilerParams(vmem_limit_bytes=52 * 1024 * 1024),
        cost_estimate=hint(2 * rows * n * k, 2 * n * k + 4 * rows * (n + k)),
        name=name,
    )(*[x[0] for x in blocks], w, *[x[0] for x in extras])


def plain(blocks, w, transposed, dtype, name):
    def epilogue(i, x, extras, outs):
        outs[i][...] = x.astype(dtype)

    outs = [(block_of(x)[1], dtype) for x in blocks]
    return rows_matmul(blocks, w, transposed, [], outs, epilogue, name)


def joined_rows(blocks, w, bias, name):
    sizes = [block_of(x)[1] for x in blocks]

    def epilogue(i, x, extras, outs):
        at = sum(sizes[:i])
        outs[0][at : at + sizes[i], :] = (x + extras[0][...]).astype(half)

    bias = bias.reshape(1, -1)
    return rows_matmul(blocks, w, False, [bias], [(sum(sizes), half)], epilogue, name)[0]


def up_gelu(blocks, w, bias, name):
    count = len(blocks)

    def epilogue(i, x, extras, outs):
        value, slope = gelu_both(x + extras[0][...])
        outs[i][...] = value.astype(half)
        outs[count + i][...] = slope.astype(half)

    outs = [(block_of(x)[1], half) for x in blocks] * 2
    out = rows_matmul(blocks, w, False, [bias.reshape(1, -1)], outs, epilogue, name)
    return out[:count], out[count:]


def hidden_back(blocks, w, slopes, name):
    def epilogue(i, x, extras, outs):
        x = x.astype(half).astype(single) * extras[i][...].astype(single)
        outs[i][...] = x.astype(half)

    outs = [(block_of(x)[1], half) for x in blocks]
    return rows_matmul(blocks, w, True, slopes, outs, epilogue, name)


def outer_kernel(count, *refs):
    out = refs[-1]
    total = None
    for i in range(count):
        x = dot_tn(refs[i][...], refs[count + i][...])
        total = x if total is None else total + x
    out[...] = total.astype(half)


def outer(left, right, name):
    left = [block_of(x) for x in left]
    right = [block_of(x) for x in right]
    m, n = left[0][0].shape[1], right[0][0].shape[1]
    tm = math.gcd(m, 1024)
    tn = n // 2 if n % 256 == 0 and n > 1024 else n
    rows = sum(x[1] for x in left)
    return pl.pallas_call(
        functools.partial(outer_kernel, len(left)),
        grid=(m // tm, n // tn),
        in_specs=[pl.BlockSpec((x[1], tm), lambda i, j, at=x[2]: (at, i)) for x in left]
        + [pl.BlockSpec((x[1], tn), lambda i, j, at=x[2]: (at, j)) for x in right],
        out_specs=pl.BlockSpec((tm, tn), lambda i, j: (i, j)),
        out_shape=jax.ShapeDtypeStruct((m, n), half),
        compiler_params=pltpu.CompilerParams(vmem_limit_bytes=52 * 1024 * 1024),
        cost_estimate=hint(2 * rows * m * n, 2 * rows * (m + n) + 2 * m * n),
        name=name,
    )(*[x[0] for x in left], *[x[0] for x in right])


def partner(mask):
    c = lax.axis_index("ctx")
    if mask == 1:
        return c + 1 - 2 * lax.rem(c, 2)
    return lax.rem(c + 2, 4) if mask == 2 else 3 - c


def greet(masks):
    barrier = pltpu.get_barrier_semaphore()
    for mask in masks:
        pl.semaphore_signal(
            barrier,
            inc=1,
            device_id={"ctx": partner(mask)},
            device_id_type=pl.DeviceIdType.MESH,
        )
    pl.semaphore_wait(barrier, len(masks))


class Moves:
    def __init__(self, send_sem, recv_sem):
        self.send_sem, self.recv_sem, self.used = send_sem, recv_sem, 0

    def start(self, src, dst, mask):
        copy = pltpu.make_async_remote_copy(
            src_ref=src,
            dst_ref=dst,
            send_sem=self.send_sem.at[self.used],
            recv_sem=self.recv_sem.at[self.used],
            device_id={"ctx": partner(mask)},
            device_id_type=pl.DeviceIdType.MESH,
        )
        self.used += 1
        copy.start()
        return copy


def multiply(lefts, w, transposed, extras, outs, epilogue, tile=512):
    k = lefts[0].shape[1]
    n = w.shape[0] if transposed else w.shape[1]
    t = math.gcd(n, tile)
    w_spec = (
        pl.BlockSpec((t, k), lambda i: (i, 0)) if transposed else pl.BlockSpec((k, t), lambda i: (0, i))
    )
    dot = dot_nt if transposed else dot_nn

    def body(*refs):
        rows_kernel(dot, epilogue, len(lefts), len(extras), *refs)

    pltpu.emit_pipeline(
        body,
        grid=(n // t,),
        in_specs=[pl.BlockSpec((x.shape[0], k), lambda i: (0, 0)) for x in lefts]
        + [w_spec]
        + [pl.BlockSpec((x.shape[0], t), lambda i: (0, i)) for x in extras],
        out_specs=[pl.BlockSpec((x.shape[0], t), lambda i: (0, i)) for x in outs],
    )(*lefts, w, *extras, *outs)


def store(i, x, extras, outs):
    outs[i][...] = x.astype(outs[i].dtype)


def store_sum(i, x, extras, outs):
    outs[i][...] = (x + extras[i][...].astype(single)).astype(outs[i].dtype)


def store_passed(i, x, extras, outs):
    if i in (1, 2):
        x = x + extras[i - 1][...].astype(single)
    outs[i][...] = x.astype(outs[i].dtype)


def store_hidden(i, x, extras, outs):
    outs[i][...] = (x.astype(half).astype(single) * extras[i][...].astype(single)).astype(half)


def outer_on(lefts, rights, out):
    m, n = out.shape
    tm = math.gcd(m, 1024)
    tn = n // 2 if n % 256 == 0 and n > 1024 else n

    def body(*refs):
        outer_kernel(len(lefts), *refs)

    pltpu.emit_pipeline(
        body,
        grid=(m // tm, n // tn),
        in_specs=[pl.BlockSpec((x.shape[0], tm), lambda i, j: (0, i)) for x in lefts]
        + [pl.BlockSpec((x.shape[0], tn), lambda i, j: (0, j)) for x in rights],
        out_specs=[pl.BlockSpec((tm, tn), lambda i, j: (i, j))],
    )(*lefts, *rights, out)


def halves(ref):
    n = ref.shape[0] // 2
    return ref.at[pl.ds(0, n)], ref.at[pl.ds(n, n)]


def moving_call(kernel, operands, outs, moves, call, flops, name):
    anywhere = pl.BlockSpec(memory_space=pl.ANY)
    sems = pltpu.SemaphoreType.DMA((moves,))
    return pl.pallas_call(
        kernel,
        in_specs=[anywhere] * len(operands),
        out_specs=[anywhere] * len(outs),
        out_shape=[jax.ShapeDtypeStruct(shape, dtype) for shape, dtype in outs],
        scratch_shapes=[sems, sems],
        compiler_params=pltpu.CompilerParams(
            collective_id=call, has_side_effects=True, vmem_limit_bytes=52 * 1024 * 1024
        ),
        cost_estimate=hint(flops, 0),
        name=name,
    )(*operands)


def store_biased(i, x, extras, outs):
    outs[i][...] = (x + extras[0][...]).astype(half)


def qkv_kernel(*refs):
    tok, gain, shift, a1, w_qkv, bias = refs[0:2], refs[2], refs[3], refs[4:7], refs[7], refs[8]
    dz_lo, dz_hi = refs[9:11]
    joined, far, one_lo, two_hi = refs[11], refs[12:14], refs[14], refs[15]
    moves = Moves(*refs[16:18])
    n, width = tok[0].shape
    greet((1, 2))
    copies = [moves.start(dz_lo, one_lo, 1), moves.start(dz_hi, two_hi, 2)]

    def norm(x_lo, x_hi, g, s, o_lo, o_hi):
        for x, o in ((x_lo, o_lo), (x_hi, o_hi)):
            normed, _ = norm_parts(x[...].astype(single))
            o[...] = (normed * g[...] + s[...]).astype(half)

    t = math.gcd(n, 64)
    block = pl.BlockSpec((t, width), lambda i: (i, 0))
    row = pl.BlockSpec((1, width), lambda i: (0, 0))
    pltpu.emit_pipeline(
        norm, grid=(n // t,), in_specs=[block, block, row, row], out_specs=[block, block]
    )(*tok, gain, shift, *far)
    lefts, outs, at = [*a1, *far], [], 0
    for x in lefts:
        outs.append(joined.at[pl.ds(at, x.shape[0])])
        at += x.shape[0]
    multiply(lefts, w_qkv, False, [bias], outs, store_biased)
    for copy in copies:
        copy.wait()


def qkv_forward(tok, gain, shift, a1, w_qkv, bias, dz_lo, dz_hi):
    n, width = tok[0].shape
    k = w_qkv.shape[1]
    outs = [((8 * n, k), half)] + [((n, width), half)] * 4
    out = moving_call(
        qkv_kernel,
        [*tok, gain.reshape(1, -1), shift.reshape(1, -1), *a1, w_qkv, bias.reshape(1, -1), dz_lo, dz_hi],
        outs,
        2,
        7,
        16 * n * width * k,
        "qkv",
    )
    return out[0], out[1:3], out[3:5]


def feed_pass(dz, slope, w_down, w_up, du, total, sums):
    n, width = dz[0].shape
    wide = w_down.shape[0]
    t = math.gcd(wide, 512)
    total[...] = jnp.zeros_like(total)

    def body(dz_lo, dz_hi, down, up, slope_lo, slope_hi, du_lo, du_hi):
        for i, x, s, d in ((0, dz_lo, slope_lo, du_lo), (1, dz_hi, slope_hi, du_hi)):
            grad = dot_nt(x[...], down[...]).astype(half).astype(single)
            grad = (grad * s[...].astype(single)).astype(half)
            d[...] = grad
            at = pl.ds(pl.multiple_of(pl.program_id(0) * t, t), t)
            sums[0:1, at] += jnp.sum(grad.astype(single), axis=0, keepdims=True)
            total[i * n : (i + 1) * n, :] += dot_nt(grad, up[...])

    pltpu.emit_pipeline(
        body,
        grid=(wide // t,),
        in_specs=[pl.BlockSpec((n, width), lambda i: (0, 0))] * 2
        + [pl.BlockSpec((t, width), lambda i: (i, 0)), pl.BlockSpec((width, t), lambda i: (0, i))]
        + [pl.BlockSpec((n, t), lambda i: (0, i))] * 2,
        out_specs=[pl.BlockSpec((n, t), lambda i: (0, i))] * 2,
    )(*dz, w_down, w_up, *slope, *du)


def feed_back_kernel(*refs):
    dz, slope, (w_down, w_up) = refs[0:8], refs[8:13], refs[13:15]
    a2, gb_far = refs[15:20], refs[20:22]
    du, own, land1, land2, up_grad, mix_x, mix_y, bias = refs[22:27], *refs[27:34]
    total, far, near, rest, from_x, from_y, mixed, sums = refs[34:42]
    moves = Moves(*refs[42:44])
    local = refs[44]
    sums[...] = jnp.zeros_like(sums)
    n = from_x.shape[0]
    lo, hi = pl.ds(0, n), pl.ds(n, n)
    (s1_lo, s1_hi), (s2_lo, s2_hi) = halves(slope[1]), halves(slope[2])
    (d1_lo, d1_hi), (d2_lo, d2_hi) = halves(du[1]), halves(du[2])
    (land1_lo, land1_hi), (land2_lo, land2_hi) = halves(land1), halves(land2)
    greet((1, 2))
    wide, width = w_down.shape
    t = math.gcd(width, 512)

    def mix(x_lo, x_hi, w):
        at = pl.ds(pl.multiple_of(pl.program_id(0) * t, t), t)
        mixed[0:n, at] = dot_nn(x_lo[...], w[...]).astype(half)
        mixed[n : 2 * n, at] = dot_nn(x_hi[...], w[...]).astype(half)

    pltpu.emit_pipeline(
        mix,
        grid=(width // t,),
        in_specs=[pl.BlockSpec((n, wide), lambda i: (0, 0))] * 2
        + [pl.BlockSpec((wide, t), lambda i: (0, i))],
    )(*gb_far, w_down)
    second = [moves.start(mixed.at[lo], mix_x, 1), moves.start(mixed.at[hi], mix_y, 2)]
    feed_pass(dz[6:8], slope[3:5], w_down, w_up, du[3:5], total, sums)
    far[...] = total[...].astype(half)
    first = [moves.start(far.at[lo], from_x, 1), moves.start(far.at[hi], from_y, 2)]
    feed_pass([dz[2], dz[5]], [s1_lo, s2_hi], w_down, w_up, [d1_lo, d2_hi], total, sums)
    near[...] = total[...].astype(half)
    second += [moves.start(near.at[lo], land1_lo, 1), moves.start(near.at[hi], land2_hi, 2)]
    feed_pass([dz[3], dz[4]], [s1_hi, s2_lo], w_down, w_up, [d1_hi, d2_lo], total, sums)
    for copy in first:
        copy.wait()
    rest[lo] = (total[lo] + from_y[...].astype(single)).astype(half)
    rest[hi] = (total[hi] + from_x[...].astype(single)).astype(half)
    second += [moves.start(rest.at[lo], land1_hi, 1), moves.start(rest.at[hi], land2_lo, 2)]
    feed_pass(dz[0:2], halves(slope[0]), w_down, w_up, halves(du[0]), total, sums)
    stores = [
        pltpu.make_async_copy(total, own, local.at[0]),
        pltpu.make_async_copy(sums, bias, local.at[1]),
    ]
    for copy in stores:
        copy.start()
    outer_on(a2, du, up_grad)
    for copy in stores + second:
        copy.wait()


def feed_back(dz, slope, w_down, w_up, a2, gb_far):
    n, width = dz[0].shape
    rows, wide = 2 * n, w_down.shape[0]
    anywhere = pl.BlockSpec(memory_space=pl.ANY)
    outs = [((r, wide), half) for r in (rows, rows, rows, n, n)]
    outs += [((rows, width), single)] + [((rows, width), half)] * 2
    outs += [((width, wide), half)] + [((n, width), half)] * 2 + [((8, wide), single)]
    sems = pltpu.SemaphoreType.DMA((8,))
    out = pl.pallas_call(
        feed_back_kernel,
        in_specs=[anywhere] * 22,
        out_specs=[anywhere] * len(outs),
        out_shape=[jax.ShapeDtypeStruct(shape, dtype) for shape, dtype in outs],
        scratch_shapes=[pltpu.VMEM((rows, width), single)]
        + [pltpu.VMEM((rows, width), half)] * 3
        + [pltpu.VMEM((n, width), half)] * 2
        + [pltpu.VMEM((rows, width), half), pltpu.VMEM((8, wide), single)]
        + [sems, sems, pltpu.SemaphoreType.DMA((2,))],
        compiler_params=pltpu.CompilerParams(
            collective_id=3, has_side_effects=True, vmem_limit_bytes=56 * 1024 * 1024
        ),
        cost_estimate=hint(26 * rows * width * wide, 0),
        name="feed_back",
    )(*dz, *slope, w_down, w_up, *a2, *gb_far)
    return out[5:8], out[8], out[9:11], out[11][0]


def heads_back_kernel(part, *refs):
    own, land1, land2, cot, y1, gain, w_out = refs[0:7]
    ob, gb1, gb2, w_down, mix_x, mix_y, down = refs[7:14]
    dy1, dz1, sums, got, out_grad = refs[14:19]
    mix, (one_lo, one_hi, two_lo, two_hi) = refs[19:23], refs[23:27]
    dz, w, stage = refs[27:30]
    moves = Moves(*refs[30:32])
    local = refs[32]
    rows, width = own.shape
    greet((1, 2, 3))
    load = pltpu.make_async_copy(w_out, w, local.at[0])
    load.start()
    down_lo, down_hi = halves(down)
    copies = [moves.start(down_lo, one_lo, 1), moves.start(down_hi, two_hi, 2)]
    copies += [moves.start(down_hi, one_hi, 1), moves.start(down_lo, two_lo, 2)]
    t = math.gcd(rows, 64)

    def norm(own, one, two, cot, y1, gain, dy1, dz1, sums):
        step = pl.program_id(0)
        grad = own[...] + one[...].astype(single) + two[...].astype(single)
        normed, inv = norm_parts(y1[...])
        dy = cot[...] + norm_back(normed, inv, gain[...], grad)
        low = dy.astype(half)
        dy1[...] = dy
        dz1[...] = low
        dz[pl.ds(pl.multiple_of(step * t, t), t), :] = low

        @pl.when(step == 0)
        def _():
            sums[...] = jnp.zeros_like(sums)

        sums[0:1] += jnp.sum(grad * normed, axis=0, keepdims=True)
        sums[1:2] += jnp.sum(grad, axis=0, keepdims=True)
        sums[2:3] += jnp.sum(low.astype(single), axis=0, keepdims=True)

    block = pl.BlockSpec((t, width), lambda i: (i, 0))
    pltpu.emit_pipeline(
        norm,
        grid=(rows // t,),
        in_specs=[block] * 5 + [pl.BlockSpec((1, width), lambda i: (0, 0))],
        out_specs=[block] * 2 + [pl.BlockSpec((8, width), lambda i: (0, 0))],
    )(own, land1, land2, cot, y1, gain, dy1, dz1, sums)
    load.wait()
    for mask in (3, 1, 2, 0):
        of = partner(mask) if mask else lax.axis_index("ctx")
        heads = w[pl.ds(pl.multiple_of(of * part, part), part), :]
        stage[mask] = dot_nt(dz[...], heads).astype(half)
        at = got.at[pl.ds(mask * rows, rows)]
        if mask:
            copies.append(moves.start(stage.at[mask], at, mask))
        else:
            keep = pltpu.make_async_copy(stage.at[0], at, local.at[1])
            keep.start()
    outer_on([ob], [dz1], out_grad)
    multiply(
        [*halves(gb1), *halves(gb2)],
        w_down,
        False,
        [mix_y, mix_x],
        mix,
        store_passed,
    )
    keep.wait()
    for copy in copies:
        copy.wait()


def heads_back(terms, cot, y1, gain, w_out, ob, gb1, gb2, w_down, mix_first, down):
    rows, width = cot.shape
    part = width // 4
    anywhere = pl.BlockSpec(memory_space=pl.ANY)
    sems = pltpu.SemaphoreType.DMA((7,))
    outs = [((rows, width), single), ((rows, width), half), ((8, width), single)]
    outs += [((4 * rows, part), half), ((width, width), half)]
    outs += [((rows // 2, width), half)] * 4 + [((down.shape[0] // 2, width), half)] * 4
    out = pl.pallas_call(
        functools.partial(heads_back_kernel, part),
        in_specs=[anywhere] * 14,
        out_specs=[anywhere] * len(outs),
        out_shape=[jax.ShapeDtypeStruct(shape, dtype) for shape, dtype in outs],
        scratch_shapes=[
            pltpu.VMEM((rows, width), half),
            pltpu.VMEM((width, width), half),
            pltpu.VMEM((4, rows, part), half),
            sems,
            sems,
            pltpu.SemaphoreType.DMA((2,)),
        ],
        compiler_params=pltpu.CompilerParams(
            collective_id=4, has_side_effects=True, vmem_limit_bytes=56 * 1024 * 1024
        ),
        cost_estimate=hint(10 * rows * width * width, 0),
        name="heads_back",
    )(*terms, cot, y1, gain.reshape(1, -1), w_out, ob, gb1, gb2, w_down, *mix_first, down)
    return out[0], out[2], out[3], out[4], out[5:9], out[9:13]


def qkv_back_kernel(*refs):
    dqkv, w_qkv = refs[0:2]
    a1, gb_own, w_down, one_hi, two_hi = refs[2:7], *refs[7:11]
    own, p3, p1, p2, from_x, from_y, land1, land2, qkv_grad, mix_own = refs[11:21]
    x_hi, y_hi = refs[21:23]
    moves = Moves(*refs[23:25])
    rows = own.shape[0]
    n = rows // 2

    def block(k):
        return dqkv.at[pl.ds(k * n, n)]

    greet((1, 2))
    output = [moves.start(one_hi, x_hi, 1), moves.start(two_hi, y_hi, 2)]
    (p3_lo, p3_hi), (p1_lo, p1_hi), (p2_lo, p2_hi) = halves(p3), halves(p1), halves(p2)
    (land1_lo, land1_hi), (land2_lo, land2_hi) = halves(land1), halves(land2)
    multiply([block(6), block(7)], w_qkv, True, [], [p3_lo, p3_hi], store)
    first = [moves.start(p3_lo, from_x, 1), moves.start(p3_hi, from_y, 2)]
    multiply([block(2), block(5)], w_qkv, True, [], [p1_lo, p2_hi], store)
    second = [moves.start(p1_lo, land1_lo, 1), moves.start(p2_hi, land2_hi, 2)]
    multiply([dqkv.at[pl.ds(0, rows)]], w_qkv, True, [], [own], store)
    multiply([gb_own], w_down, False, [], [mix_own], store)
    for copy in first:
        copy.wait()
    multiply([block(3), block(4)], w_qkv, True, [from_y, from_x], [p1_hi, p2_lo], store_sum)
    second += [moves.start(p1_hi, land1_hi, 1), moves.start(p2_lo, land2_lo, 2)]
    rights, at = [], 0
    for x in a1:
        rights.append(dqkv.at[pl.ds(at, x.shape[0])])
        at += x.shape[0]
    outer_on(a1, rights, qkv_grad)
    for copy in output + second:
        copy.wait()


def qkv_back(dqkv, w_qkv, a1, gb_own, w_down, one_hi, two_hi):
    rows, width = a1[0].shape
    wide = gb_own.shape[1]
    n = rows // 2
    outs = [((rows, width), single)] + [((rows, width), half)] * 3
    outs += [((n, width), half)] * 2 + [((rows, width), half)] * 2
    outs += [((width, dqkv.shape[1]), half), ((rows, width), single)] + [((n, width), half)] * 2
    out = moving_call(
        qkv_back_kernel,
        [dqkv, w_qkv, *a1, gb_own, w_down, one_hi, two_hi],
        outs,
        8,
        5,
        16 * rows * width * dqkv.shape[1] + 2 * rows * width * wide,
        "qkv_back",
    )
    return out[0], out[6:8], out[8], out[9], out[10:12]


def lay_out_kernel(axis, layout, c_ref, *refs):
    out = refs[-1]
    for (j, row), ref in zip(layout, refs):
        x = ref[...].astype(single)
        r, w = x.shape
        if axis == 0:
            n = sum(ref.shape[0] for (k, _), ref in zip(layout, refs) if k == j)
            out[pl.ds(pl.multiple_of((c_ref[0] ^ j) * n + row, r), r), :] = x
        else:
            out[row : row + r, pl.ds(pl.multiple_of((c_ref[0] ^ j) * w, w), w)] = x


def lay_out(axis, pieces, c, groups):
    count = len(pieces)
    r = sum(x.shape[0] for x in pieces[0])
    n = pieces[0][0].shape[1]
    w = n // groups
    if w % 128:
        whole = xor_order([jnp.concatenate(p, axis=0).astype(single) for p in pieces], c)
        whole = jnp.stack([p.reshape(r, groups, w) for p in whole], axis=2)
        return whole.reshape(r, count * n)
    layout, blocks = [], []
    for j, p in enumerate(pieces):
        row = 0
        for x in p:
            layout.append((j, row))
            blocks.append(x)
            row += x.shape[0]
    out = (count * r, w) if axis == 0 else (r, count * w)
    return pl.pallas_call(
        functools.partial(lay_out_kernel, axis, layout),
        grid_spec=pltpu.PrefetchScalarGridSpec(
            num_scalar_prefetch=1,
            grid=(groups,),
            in_specs=[pl.BlockSpec((x.shape[0], w), lambda k, c: (0, k)) for x in blocks],
            out_specs=pl.BlockSpec(out, lambda k, c: (0, k)),
        ),
        out_shape=jax.ShapeDtypeStruct((out[0], out[1] * groups), single),
        compiler_params=pltpu.CompilerParams(vmem_limit_bytes=48 * 1024 * 1024),
        cost_estimate=hint(0, 6 * r * n * count),
        name="lay_out",
    )(c.reshape(1), *blocks)


def gather_small_kernel(nf, x_ref, o_ref, send_sem, recv_sem):
    f = lax.axis_index("fsdp")
    barrier = pltpu.get_barrier_semaphore()
    for d in range(1, nf):
        pl.semaphore_signal(
            barrier,
            inc=1,
            device_id={"fsdp": lax.rem(f + d, nf)},
            device_id_type=pl.DeviceIdType.MESH,
        )
    pl.semaphore_wait(barrier, nf - 1)
    copies = []
    for d in range(1, nf):
        copies.append(
            pltpu.make_async_remote_copy(
                src_ref=x_ref,
                dst_ref=o_ref.at[f],
                send_sem=send_sem.at[d],
                recv_sem=recv_sem.at[d],
                device_id={"fsdp": lax.rem(f + d, nf)},
                device_id_type=pl.DeviceIdType.MESH,
            )
        )
        copies[-1].start()
    o_ref[f] = x_ref[...]
    for copy in copies:
        copy.wait()


def gather_small(x, nf):
    return pl.pallas_call(
        functools.partial(gather_small_kernel, nf),
        out_shape=jax.ShapeDtypeStruct((nf,) + x.shape, single),
        in_specs=[pl.BlockSpec(memory_space=pltpu.VMEM)],
        out_specs=pl.BlockSpec(memory_space=pltpu.VMEM),
        scratch_shapes=[pltpu.SemaphoreType.DMA((nf,)), pltpu.SemaphoreType.DMA((nf,))],
        compiler_params=pltpu.CompilerParams(collective_id=1, has_side_effects=True),
        name="gather_small",
    )(x)


def reduce_small_kernel(nf, nc, x_ref, o_ref, land, stage, send_sem, recv_sem):
    f = lax.axis_index("fsdp")
    c = lax.axis_index("ctx")
    barrier = pltpu.get_barrier_semaphore()
    for d in range(1, nf):
        pl.semaphore_signal(
            barrier,
            inc=1,
            device_id={"fsdp": lax.rem(f + d, nf)},
            device_id_type=pl.DeviceIdType.MESH,
        )
    for d in range(1, nc):
        pl.semaphore_signal(
            barrier,
            inc=1,
            device_id={"ctx": lax.rem(c + d, nc)},
            device_id_type=pl.DeviceIdType.MESH,
        )
    pl.semaphore_wait(barrier, nf + nc - 2)
    copies = []
    for d in range(1, nf):
        to = lax.rem(f + d, nf)
        copies.append(
            pltpu.make_async_remote_copy(
                src_ref=x_ref.at[to],
                dst_ref=land.at[d],
                send_sem=send_sem.at[d],
                recv_sem=recv_sem.at[d],
                device_id={"fsdp": to},
                device_id_type=pl.DeviceIdType.MESH,
            )
        )
        copies[-1].start()
    total = x_ref[f]
    for d in range(1, nf):
        copies[d - 1].wait()
        total = total + land[d]
    stage[0] = total
    copies = []
    for d in range(1, nc):
        copies.append(
            pltpu.make_async_remote_copy(
                src_ref=stage.at[0],
                dst_ref=stage.at[d],
                send_sem=send_sem.at[nf + d],
                recv_sem=recv_sem.at[nf + d],
                device_id={"ctx": lax.rem(c + d, nc)},
                device_id_type=pl.DeviceIdType.MESH,
            )
        )
        copies[-1].start()
    for d in range(1, nc):
        copies[d - 1].wait()
        total = total + stage[d]
    o_ref[...] = total


def reduce_small(x, nf, nc, call):
    block = x.shape[1:]
    sems = pltpu.SemaphoreType.DMA((nf + nc,))
    return pl.pallas_call(
        functools.partial(reduce_small_kernel, nf, nc),
        out_shape=jax.ShapeDtypeStruct(block, single),
        in_specs=[pl.BlockSpec(memory_space=pltpu.VMEM)],
        out_specs=pl.BlockSpec(memory_space=pltpu.VMEM),
        scratch_shapes=[
            pltpu.VMEM((nf,) + block, single),
            pltpu.VMEM((nc,) + block, single),
            sems,
            sems,
        ],
        compiler_params=pltpu.CompilerParams(collective_id=call, has_side_effects=True),
        name="reduce_small",
    )(x)


def per_device(
    tokens,
    cotangent,
    lengths,
    span_place,
    ln1_gain,
    ln1_shift,
    qkv_weight,
    q_bias,
    v_bias,
    out_weight,
    out_bias,
    ln2_gain,
    ln2_shift,
    up_weight,
    up_bias,
    down_weight,
    down_bias,
):
    rows, width = tokens.shape
    CTX = lax.axis_size("ctx")
    c = lax.axis_index("ctx")
    f = lax.axis_index("fsdp")
    nf = lax.axis_size("fsdp")
    wide = up_weight.shape[1]
    part = width // CTX
    heads = HEADS // CTX
    scale = 1.0 / math.sqrt(width // HEADS)
    shard = width // nf
    fpart = wide // nf // CTX
    wpart = wide // CTX

    def columns(x, width_each, stride, count):
        return jnp.concatenate(
            [
                lax.dynamic_slice_in_dim(x, k * stride + c * width_each, width_each, axis=1)
                for k in range(count)
            ],
            axis=1,
        )

    def after(x, *others):
        return lax.optimization_barrier((x, others))[0]

    def pick(x, axis):
        return lax.dynamic_index_in_dim(x, c, axis, keepdims=False)

    def gather_f(x):
        return lax.all_gather(x, "fsdp", axis=0, tiled=True)

    qkv_own = columns(qkv_weight, part, width, 3)
    up_own = columns(up_weight, fpart, wide // nf, nf)
    down_own = lax.dynamic_slice_in_dim(down_weight, c * fpart, fpart, axis=0)
    w_qkv = gather_f(qkv_own.astype(half))
    up_own, down_own = up_own.astype(half), down_own.astype(half)
    small = jnp.concatenate(
        [ln1_gain, ln1_shift, q_bias, v_bias, out_bias, ln2_gain, ln2_shift, down_bias, up_bias]
    )
    small_len = small.shape[0]
    small = jnp.pad(small, (0, -small_len % 1024)).reshape(-1, 128)
    small_all = gather_small(small, nf).reshape(nf, -1)[:, :small_len]
    small_all = small_all.astype(half).astype(single)

    def vector(k):
        return small_all[:, k * shard : (k + 1) * shard].reshape(width)

    gain1, shift1, bias_q, bias_v, bias_o, gain2, shift2, bias_d = [vector(k) for k in range(8)]
    bias_u = pick(small_all[:, 8 * shard :].reshape(nf, CTX, fpart), 1).reshape(wpart)
    bias_qkv = jnp.concatenate(
        [pick(bias_q.reshape(CTX, part), 0), jnp.zeros((part,), single), pick(bias_v.reshape(CTX, part), 0)]
    )
    w_out = gather_f(out_weight.astype(half))

    per = rows // SPAN
    table = jnp.arange(CTX * per, dtype=jnp.int32)
    source = ((table // per) ^ c) * per + table % per
    place = jnp.sum(jnp.where(source[:, None] == table[None, :], span_place[0][None, :], 0), axis=1)
    inv = jnp.sum(jnp.where(place[None, :] == table[:, None], table[None, :], 0), axis=1)
    slopes = 2.0 ** (-8.0 * ((c * heads + jnp.arange(heads)).astype(single) + 1.0) / HEADS)

    def flat(pieces):
        return [x for p in pieces for x in p]

    def scatter_f(x):
        return lax.psum_scatter(x, "fsdp", scatter_dimension=0, tiled=True)

    far = CTX - 1
    mid = list(range(1, far))

    def first_norm(x):
        normed, _ = norm_parts(x.astype(single))
        return (normed * gain1 + shift1).astype(half)

    n = rows // 2
    dz2_lo, dz2_hi = cotangent[:n].astype(half), cotangent[n:].astype(half)
    early = (small_all, place, inv, slopes, up_own, down_own, dz2_lo, dz2_hi)
    early, tok_near = after((early, gather_first(tokens)))
    small_all, place, inv, slopes, up_own, down_own, dz2_lo, dz2_hi = early
    tok = gather_second(tokens, tok_near)
    near = [[first_norm(x) for x in p] for p in tok[:far]]
    tok = after(tok, near)
    if CTX != 4:
        dz2_own = jnp.concatenate([dz2_lo, dz2_hi], axis=0)
        dz2_rest = gather_first(dz2_own)
    w_up = gather_f(after(up_own, tok))
    a1 = flat(near)
    if CTX == 4:
        joined, a1_far, dz2_first = qkv_forward(
            tok[far], gain1, shift1, a1, w_qkv, bias_qkv, dz2_lo, dz2_hi
        )
        a1 = a1 + list(a1_far)
        dz2_rest = after((dz2_hi, dz2_lo), joined)
        dz2_rest = [swap(dz2_rest[0], 1), swap(dz2_rest[1], 2)]
    else:
        a1 = a1 + [first_norm(x) for x in tok[far]]
        joined = joined_rows(a1, w_qkv, bias_qkv, "qkv")
    w_down = gather_f(after(down_own, joined))
    attended = attn_forward(joined, inv, slopes, heads, scale)
    mine = [attended[j * rows : (j + 1) * rows] for j in range(CTX)]
    mine = after(mine, dz2_rest)
    mine = [mine[0]] + [swap(mine[j], j) for j in range(1, CTX)]
    ob = after(jnp.concatenate(xor_order(mine, c), axis=1))
    y1 = tokens.astype(single) + dot_nn(ob, w_out) + bias_o

    normed2, inv2 = norm_parts(y1)
    a2_own = (normed2 * gain2 + shift2).astype(half)
    gb, slope = [None] * CTX, [None] * CTX
    gb[0], slope[0] = up_gelu([a2_own], w_up, bias_u, "up_gelu_0")
    last = gb[0]
    a2_near = gather_first(a2_own)
    a2 = gather_second(a2_own, a2_near)
    if CTX == 4:
        one_lo, two_hi = after(dz2_first, a2_near)
        one_hi, two_lo = dz2_rest
        dz2 = [[dz2_lo, dz2_hi], [one_lo, one_hi], [two_lo, two_hi], [swap(one_lo, 2), swap(two_hi, 1)]]
    else:
        dz2 = [[dz2_own]] + [[x] for x in dz2_rest]
    for j in range(1, CTX):
        gb[j], slope[j] = up_gelu(after(a2[j], last), w_up, bias_u, f"up_gelu_{j}")
        last = gb[j]
    gb_blocks = flat(gb)
    if CTX == 4:
        gb_blocks = [(g[0], n, i) for g in gb[:far] for i in (0, 1)] + list(gb[far])
    down_grad = outer(gb_blocks, flat(dz2), "down_grad")
    down_part = scatter_f(down_grad)
    w_down = after(w_down, down_grad)

    du, dh2, mix = [None] * CTX, [None] * CTX, [None] * CTX
    if CTX == 4:
        dh2, up_grad, mix_first, up_bias_grad = feed_back(
            flat(dz2), flat(slope), w_down, w_up, flat(a2), gb[far]
        )
    else:
        for j in range(CTX):
            du[j] = hidden_back(dz2[j], w_down, slope[j], f"du_{j}")
            dh2[j] = plain(du[j], w_up, True, half if j else single, f"dh2_{j}")[0]
        arrived = scatter_send(dh2[1:])
        dh2 = dh2[0]
        up_grad = outer(flat(a2), flat(du), "up_grad")
        up_bias_grad = sum(jnp.sum(x.astype(single), axis=0) for x in flat(du))
        mix[far] = plain(gb[far], w_down, False, half, "mix_far")[0]
        dh2 = total_of(dh2, arrived)
    up_part = scatter_f(up_grad)
    if CTX == 4:
        dy1, sums2, dattn, out_grad, mix, down_near = heads_back(
            dh2, cotangent, y1, gain2, w_out, ob, gb[1][0], gb[2][0], w_down, mix_first, down_part
        )
        one_lo, one_hi, two_lo, two_hi = mix
        gain2_grad, shift2_grad, out_bias_grad = sums2[0], sums2[1], sums2[2]
    else:
        gain2_grad = jnp.sum(dh2 * normed2, axis=0)
        shift2_grad = jnp.sum(dh2, axis=0)
        dy1 = cotangent + norm_back(normed2, inv2, gain2, dh2)
        dz1 = dy1.astype(half)
        dattn = dot_nt(dz1, w_out).astype(half)
        out_bias_grad = jnp.sum(dz1.astype(single), axis=0)
        dattn = xor_order([dattn[:, s * part : (s + 1) * part] for s in range(CTX)], c)
        dattn = [dattn[0]] + [swap(dattn[j], j) for j in range(1, CTX)]
        dattn = jnp.concatenate(dattn, axis=0)
        out_grad = outer([ob], [dz1], "out_grad")
        for j in mid:
            mix[j] = plain(gb[j], w_down, False, half, f"mix_{j}")[0]
        down_near = gather_first(down_part)
    out_part = scatter_f(out_grad)
    dqkv, sum_q, sum_v = attn_backward(joined, dattn, inv, slopes, heads, scale)
    sum_q, sum_v = sum_q[0] + sum_q[8], sum_v[0] + sum_v[8]
    if CTX == 4:
        lows = [swap(one_lo, 1), swap(two_lo, 2)]
        down_far = [swap(down_near[0], 2), swap(down_near[3], 1)]
        down_out = [[down_part], list(down_near[0:2]), list(down_near[2:4]), down_far]
        dqkv = after(dqkv, lows, up_part, down_far)
        dh1, arrived, qkv_grad, mix_own, highs = qkv_back(
            dqkv, w_qkv, a1, gb[0][0], w_down, one_hi, two_hi
        )
    else:
        dh1 = [
            plain([(dqkv, rows, j)], w_qkv, True, half if j else single, f"dh1_{j}")[0]
            for j in range(CTX)
        ]
        arrived = scatter_send(dh1[1:])
        dh1 = dh1[0]
        qkv_grad = outer(a1, [(dqkv, rows, j) for j in range(CTX)], "qkv_grad")
        mix_own = plain(gb[0], w_down, False, single, "mix_0")[0]
        down_out = gather_second(down_part, down_near)
    qkv_part = scatter_f(qkv_grad)

    up_own = after(up_part, arrived)
    up_near = gather_first(up_own)
    out_first = []
    if CTX == 4:
        k = out_part.shape[0] // 2
        out_lo, out_hi = after(out_part, arrived)[:k], after(out_part, arrived)[k:]
        out_first = [swap(out_lo, 1), swap(out_hi, 2)]
    waiting = (dh1, mix_own, flat(dz2[:1]), down_out)
    dh1, mix_own, dz2_own, down_out = after(waiting, out_part)
    down_out = lay_out(0, down_out, c, width // min(width, 512))
    dh1 = total_of(dh1, arrived)
    if CTX == 4:
        mixed = y1 + bias_d + mix_own
        mixed = jnp.concatenate([total_of(mixed[:n], lows), total_of(mixed[n:], highs)])
    else:
        mixed = total_of(y1 + bias_d + mix_own, scatter_send(mix[1:]))
    down_bias_grad = sum(jnp.sum(x.astype(single), axis=0) for x in dz2_own)
    normed1_own, inv1_own = norm_parts(tokens.astype(single))
    gain1_grad = jnp.sum(dh1 * normed1_own, axis=0)
    shift1_grad = jnp.sum(dh1, axis=0)
    input_grad = dy1 + norm_back(normed1_own, inv1_own, gain1, dh1)

    done = (down_out, input_grad, mixed, down_bias_grad, gain1_grad, shift1_grad)
    up_near, out_first = after((up_near, out_first), done)
    if CTX == 4:
        out_lo = (out_lo.astype(single) + out_first[0].astype(single)).astype(half)
        out_hi = (out_hi.astype(single) + out_first[1].astype(single)).astype(half)
        out_lo, out_hi, up_near = after((out_lo, out_hi, up_near))
        out_second = [(out_lo, swap(out_lo, 2)), (out_hi, swap(out_hi, 1))]
    up_out = gather_second(up_own, up_near)
    up_out = lay_out(1, up_out, c, nf)
    def spread(x, inner):
        x = x.reshape(-1, 1, inner)
        mask = (jnp.arange(CTX) == c)[None, :, None]
        return jnp.where(mask, x, 0.0).reshape(-1)

    def reduced(items, call):
        sizes = [x.shape[0] // nf for x in items]
        x = jnp.concatenate([x.reshape(nf, -1) for x in items], axis=1)
        x = jnp.pad(x, ((0, 0), (0, -x.shape[1] % 1024))).reshape(nf, -1, 128)
        x = reduce_small(x, nf, CTX, call)
        near = after(qkv_near, x)
        x = after(x, near).reshape(-1)
        out, at = [], 0
        for n in sizes:
            out.append(x[at : at + n])
            at += n
        return out, near

    sums_in = [out_bias_grad, gain2_grad, shift2_grad, down_bias_grad, spread(up_bias_grad, fpart)]
    sums_in += [gain1_grad, shift1_grad, spread(sum_q, part), spread(sum_v, part)]
    qkv_part = after(qkv_part, up_out)
    qkv_near = gather_first(qkv_part)
    sums_in[5] = after(sums_in[5], qkv_part)
    sums_out, qkv_near = reduced(sums_in, 2)
    if CTX == 4:
        out_second = after(out_second, qkv_near)
        out_out = [x.astype(single) + y.astype(single) for x, y in out_second]
        out_out = jnp.concatenate(out_out, axis=0)
    else:
        bit = 1
        while bit < CTX:
            out_out = out_part.astype(single) + swap(out_part, bit).astype(single)
            out_part = out_out.astype(half)
            bit *= 2

    qkv_out = lay_out(1, gather_second(qkv_part, qkv_near), c, 3)
    out_bias_out, gain2_out, shift2_out, down_bias_out, up_bias_out = sums_out[:5]
    gain1_out, shift1_out, q_bias_out, v_bias_out = sums_out[5:]
    return (
        mixed,
        input_grad,
        gain1_out,
        shift1_out,
        qkv_out,
        q_bias_out,
        v_bias_out,
        out_out,
        out_bias_out,
        gain2_out,
        shift2_out,
        up_out,
        up_bias_out,
        down_out,
        down_bias_out,
    )


def solution(mesh):
    rows, flat = P(("ctx", "fsdp"), None), P("fsdp")
    mat = P("fsdp", None)
    in_specs = (
        rows,
        rows,
        mat,
        mat,
        flat,
        flat,
        mat,
        flat,
        flat,
        mat,
        flat,
        flat,
        flat,
        mat,
        flat,
        mat,
        flat,
    )
    out_specs = (
        rows,
        rows,
        flat,
        flat,
        mat,
        flat,
        flat,
        mat,
        flat,
        flat,
        flat,
        mat,
        flat,
        mat,
        flat,
    )
    return jax.shard_map(
        per_device, mesh=mesh, in_specs=in_specs, out_specs=out_specs, check_vma=False
    )
```
